32 devices in a mesh: slot: 2 (over x), tile: 16 (over z, y, core).
Axes of the slice: x: 2, y: 2, z: 4, core: 2. Of those that a mesh axis runs over, the one named last changes fastest.
Arguments:
- control: float32 [2, 4, 2, 256, 512], P('slot', None, None, 'tile'), may hold values from -28 to 28
- background: bfloat16 [4, 2, 256, 512], P(None, None, 'tile'), may hold values from -6 to 6
- self_weight: bfloat16 [512, 512], replicated, may hold values from -0.25 to 0.25
- neighbour_weight: bfloat16 [512, 512], replicated, may hold values from -0.25 to 0.25
- output_weight: bfloat16 [512, 512], replicated, may hold values from -0.25 to 0.25
- norm_gain: float32 [512], replicated, may hold values from 0.1 to 1.9
- readout: bfloat16 [512, 128], replicated, may hold values from -0.25 to 0.25
- error_weight: float32 [512], replicated, may hold values from 0.3 to 3
- report_owner: int32 [2, 2, 512, 1], P('slot', None, 'tile'), may hold values from 0 to 15, as said below
- report_stencil: int32 [2, 2, 512, 4], P('slot', None, 'tile'), may hold values from 0 to 31
- report_weights: bfloat16 [2, 2, 512, 4], P('slot', None, 'tile'), may hold values from 0.049804688 to 1
- report_values: bfloat16 [2, 2, 512, 128], P('slot', None, 'tile'), may hold values from -6 to 6
- report_precision: bfloat16 [2, 2, 512], P('slot', None, 'tile'), may hold values from 0.049804688 to 0.5
Outputs:
- gradient: float32 [2, 4, 2, 256, 512], P('slot', None, None, 'tile')
The draws below stay inside these ranges and needn't reach their ends.
Inputs may be any that keep to these rules, and one draw needn't show every extreme that they name: `report_owner`: within the rows of one device for one slot and step (aligned blocks of 32 rows) no owner tile is named more than 5 times; in every slot and step one owner tile is named exactly 5 times by every device of the slot. `report_stencil`: A cell of the owner tile, numbered latitude row * 16 + column within the tile.
All inputs are finite; a program needn't handle non-finite values.
Results may differ from the reference program's by a relative error of at most 0.006.
Values may be sent and summed in bfloat16 or wider, within the bound.
No kernel may reach another device: no remote copies, remote signals or barrier semaphores. Data moves between devices by JAX's collectives and lax.ppermute only.
A program may use at most 64 MiB of HBM per device.

```python
import math
import jax
import jax.numpy as jnp
from jax import lax

C = 512
OBSV = 128
LAT_T = 2
LON_T = 16
MEMBERS = 4
STEPS = 2
CAP = 5
LON = 256
OBS_DEV = 32
OBS_ROWS = 512
N_SLOT = 2
N_TILE = 16


def draw_control(key, part):
    key_base, key_channel, key_cell = jax.random.split(jax.random.fold_in(key, 7), 3)
    full_shape = (N_SLOT, MEMBERS, LAT_T, LON, C)
    gaussian = jnp.clip(jax.random.normal(key_base, full_shape, jnp.float32), -4.0, 4.0)
    channel_scale = jnp.exp(jax.random.uniform(key_channel, (C,), jnp.float32, -1.15, 1.15))
    cell_scale = jnp.exp(jax.random.uniform(key_cell, (1, 1, LAT_T, LON, 1), jnp.float32, -0.7, 0.7))
    return gaussian * channel_scale * cell_scale


def draw_report_owner(key, part):
    key_heavy, key_rows = jax.random.split(jax.random.fold_in(key, 13))
    heavy_tiles = jax.random.randint(key_heavy, (N_SLOT * STEPS,), 0, N_TILE, dtype=jnp.int32)
    block_heavy = jnp.repeat(heavy_tiles, N_TILE)
    offset_pool = jnp.repeat(jnp.arange(1, N_TILE, dtype=jnp.int32), CAP)
    block_keys = jax.random.split(key_rows, N_SLOT * STEPS * N_TILE)

    def block_rows(block_key, heavy_tile):
        key_pick, key_order = jax.random.split(block_key)
        offsets = jax.random.permutation(key_pick, offset_pool)[:OBS_DEV - CAP]
        listed = jnp.concatenate([jnp.full((CAP,), heavy_tile, jnp.int32), (heavy_tile + offsets) % N_TILE])
        return jax.random.permutation(key_order, listed)
    owners = jax.vmap(block_rows)(block_keys, block_heavy)
    return owners.reshape(N_SLOT, STEPS, OBS_ROWS, 1).astype(jnp.int32)


def plant(entries, stream_key, least, high):
    longest = entries.shape.index(max(entries.shape))
    spots = []
    for shift in (0, 1):
        where = [jax.random.randint(jax.random.fold_in(stream_key, axis), (), 0, length) for axis, length in enumerate(entries.shape)]
        where[longest] = (where[longest] + shift) % entries.shape[longest]
        spots.append(tuple(where))
    return entries.at[spots[0]].set(least).at[spots[1]].set(high)


def shard_levels(stream_key, shape, cuts, low, largest):
    def one(position, parts):
        steps = jax.random.uniform(jax.random.fold_in(jax.random.fold_in(stream_key, 6), position), (parts,), jnp.float32, low / len(cuts), largest / len(cuts))
        return jnp.repeat(jnp.exp(steps), shape[position] // parts).reshape((-1,) + (1,) * (len(shape) - position - 1))

    factor_of = one(*cuts[0])
    for cut in cuts[1:]:
        factor_of = factor_of * one(*cut)
    return factor_of


def noise(own_key, dims, scale, bound, shards=(), held_as=jnp.bfloat16):
    entries = jax.random.normal(own_key, dims, jnp.float32) * scale
    if len(shards) > 0:
        entries = shard_levels(own_key, dims, shards, -0.22, 0.18) * entries
    return jnp.clip(entries, min=-bound, max=bound).astype(held_as)


def setup_inputs(seed: int = 0) -> dict:
    seeds = jax.random.split(jax.random.key(seed), 14)
    control = draw_control(jax.random.fold_in(seeds[13], 71), 0)
    background = noise(seeds[1], (MEMBERS, LAT_T, LON, C), 1.0, 6.0, ((2, 16),))
    self_weight = noise(seeds[2], (C, C), C ** -0.5, 0.25)
    neighbour_weight = noise(seeds[3], (C, C), C ** -0.5, 0.25)
    output_weight = noise(seeds[4], (C, C), C ** -0.5, 0.25)
    norm_gain = jnp.clip(1.0 + 0.18 * jax.random.normal(seeds[5], (C,), jnp.float32), 0.1, 1.9)
    readout = noise(seeds[6], (C, OBSV), C ** -0.5, 0.25)
    error_weight = jnp.clip(jnp.exp(jax.random.uniform(seeds[7], (C,), jnp.float32, math.log(0.3), math.log(3.0))), 0.3, 3.0)
    report_owner = draw_report_owner(jax.random.fold_in(seeds[13], 71), 0)
    report_stencil = plant(jax.random.randint(seeds[9], (N_SLOT, STEPS, OBS_ROWS, 4), 0, LAT_T * LON_T), jax.random.fold_in(seeds[9], 1), 0, (LAT_T * LON_T) - 1).astype(jnp.int32)
    report_weights = jnp.clip(0.049804688 + 0.9501953 * jax.random.uniform(seeds[10], (N_SLOT, STEPS, OBS_ROWS, 4), jnp.float32) ** shard_levels(seeds[10], (N_SLOT, STEPS, OBS_ROWS, 4), ((0, 2), (2, 16)), -0.2, 0.2), 0.049804688, 1.0).astype(jnp.bfloat16)
    report_values = noise(seeds[11], (N_SLOT, STEPS, OBS_ROWS, OBSV), 1.0, 6.0, ((0, 2), (2, 16)))
    report_precision = jnp.clip(jnp.exp(math.log(0.5) - 2.306499 * jax.random.uniform(seeds[12], (N_SLOT, STEPS, OBS_ROWS), jnp.float32) ** shard_levels(seeds[12], (N_SLOT, STEPS, OBS_ROWS), ((0, 2), (2, 16)), -0.2, 0.2)), 0.049804688, 0.5).astype(jnp.bfloat16)
    return {"control": control, "background": background, "self_weight": self_weight, "neighbour_weight": neighbour_weight, "output_weight": output_weight, "norm_gain": norm_gain, "readout": readout, "error_weight": error_weight, "report_owner": report_owner, "report_stencil": report_stencil, "report_weights": report_weights, "report_values": report_values, "report_precision": report_precision}


EPSILON = 1e-06

def matmul(operand, matrix):
    flattened = jnp.dot(operand.reshape(-1, operand.shape[-1]), matrix, preferred_element_type=jnp.float32)
    return flattened.reshape(operand.shape[:-1] + (matrix.shape[-1],))

def matmul_back(operand, matrix):
    flattened = jnp.dot(operand.reshape(-1, operand.shape[-1]), matrix.T, preferred_element_type=jnp.float32)
    return flattened.reshape(operand.shape[:-1] + (matrix.shape[0],))

def neighbour_sum(values):
    widened = values.astype(jnp.float32)
    zero_row = jnp.zeros_like(widened[:, :1])
    northern = jnp.concatenate([zero_row, widened[:, :-1]], axis=1)
    southern = jnp.concatenate([widened[:, 1:], zero_row], axis=1)
    return northern + southern + jnp.roll(widened, 1, axis=2) + jnp.roll(widened, -1, axis=2)

def normalize(current, norm_gain):
    inverse_rms = lax.rsqrt(lax.optimization_barrier(jnp.mean(current * current, axis=-1, keepdims=True)) + EPSILON)
    return ((current * inverse_rms * norm_gain).astype(jnp.bfloat16), inverse_rms)

def pre_activation(current, norm_gain, self_weight, neighbour_weight):
    normed, inverse_rms = normalize(current, norm_gain)
    mixed_mean = (0.25 * neighbour_sum(normed)).astype(jnp.bfloat16)
    return (inverse_rms, matmul(normed, self_weight) + matmul(mixed_mean, neighbour_weight))

def adjoint(current, inverse_rms, linear_sum, cotangent, norm_gain, self_weight, neighbour_weight, output_weight):
    grad_active = matmul_back(cotangent.astype(jnp.bfloat16), output_weight)
    sigmoid_value = jax.nn.sigmoid(linear_sum)
    grad_input = (grad_active * sigmoid_value * (1.0 + linear_sum * (1.0 - sigmoid_value))).astype(jnp.bfloat16)
    grad_mixed = matmul_back(grad_input, neighbour_weight).astype(jnp.bfloat16)
    grad_normed = matmul_back(grad_input, self_weight) + 0.25 * neighbour_sum(grad_mixed)
    scaled = norm_gain * grad_normed
    cubed_rms = inverse_rms * inverse_rms * inverse_rms
    return cotangent + inverse_rms * scaled - current * cubed_rms * lax.optimization_barrier(jnp.mean(current * scaled, axis=-1, keepdims=True))

def observe(current, owners, stencils, weights, values, precision, readout):
    members = current.shape[0]
    cell_count = LAT_T * LON_T
    flattened = current.astype(jnp.bfloat16).reshape(-1, C)
    readout_field = jnp.dot(flattened, readout, preferred_element_type=jnp.float32)
    readout_field = readout_field.reshape(members, LAT_T, N_TILE, LON_T, OBSV).transpose(0, 2, 1, 3, 4)
    readout_field = readout_field.reshape(members, N_TILE * cell_count, OBSV)
    cell_index = (owners * cell_count + stencils).astype(jnp.int32)
    stencil_weights = weights.astype(jnp.float32)
    predicted = lax.optimization_barrier(jnp.sum(readout_field[:, cell_index, :] * stencil_weights[None, :, :, None], axis=2))
    misfit = precision.astype(jnp.float32)[None, :, None] * (predicted - values.astype(jnp.float32)[None])

    def spread_member(member_misfit):
        weighted_terms = (member_misfit[:, None, :] * stencil_weights[:, :, None]).reshape(-1, OBSV)
        return jax.ops.segment_sum(weighted_terms, cell_index.reshape(-1), num_segments=N_TILE * cell_count)
    spread = jax.vmap(spread_member)(misfit).astype(jnp.bfloat16)
    spread = spread.reshape(members, N_TILE, LAT_T, LON_T, OBSV).transpose(0, 2, 1, 3, 4).reshape(-1, OBSV)
    pulled = jnp.dot(spread, readout.T, preferred_element_type=jnp.float32)
    return pulled.reshape(current.shape)

def slot_rows(table, slot, step_index):
    return lax.dynamic_index_in_dim(table, slot, 0, keepdims=False)[step_index]

def reference(control, background, self_weight, neighbour_weight, output_weight, norm_gain, readout, error_weight, report_owner, report_stencil, report_weights, report_values, report_precision):

    def slot_gradient(earlier_final, slot):
        current = lax.dynamic_index_in_dim(control, slot, 0, keepdims=False)
        later = jnp.minimum(slot + 1, N_SLOT - 1).astype(jnp.int32)
        following = lax.dynamic_index_in_dim(control, later, 0, keepdims=False)
        states = [current]
        kept = []
        for step_index in range(STEPS):
            inverse_rms, linear_sum = pre_activation(current, norm_gain, self_weight, neighbour_weight)
            kept.append((inverse_rms, linear_sum))
            current = current + matmul(jax.nn.silu(linear_sum).astype(jnp.bfloat16), output_weight)
            states.append(current)
        final_state = current.astype(jnp.bfloat16)
        own_misfit = error_weight * (states[0] - earlier_final.astype(jnp.float32))
        next_misfit = jnp.where(slot == N_SLOT - 1, 0.0, error_weight * (following - final_state.astype(jnp.float32)))
        pulls = []
        for step_index in range(STEPS):
            pulls.append(observe(states[step_index + 1], slot_rows(report_owner, slot, step_index), slot_rows(report_stencil, slot, step_index), slot_rows(report_weights, slot, step_index), slot_rows(report_values, slot, step_index), slot_rows(report_precision, slot, step_index), readout))
        cotangent = pulls[STEPS - 1] - next_misfit
        for step_index in reversed(range(STEPS)):
            inverse_rms, linear_sum = kept[step_index]
            cotangent = adjoint(states[step_index], inverse_rms, linear_sum, cotangent, norm_gain, self_weight, neighbour_weight, output_weight)
            if step_index > 0:
                cotangent = cotangent + pulls[step_index - 1]
        return (final_state, cotangent + own_misfit)
    unused_final, gradients = lax.scan(slot_gradient, background, jnp.arange(N_SLOT, dtype=jnp.int32))
    return gradients
```

```python
import functools
import jax
import jax.numpy as jnp
from jax import lax
from jax.experimental import pallas as pl
from jax.experimental.pallas import tpu as pltpu
from jax.sharding import PartitionSpec as P

EPSILON = 1e-06
F32 = jnp.float32
BF16 = jnp.bfloat16
LANES = 128
META = 16
WIDE = 40
SLIM = 24
VMEM_LIMIT = 28 * 1024 * 1024


def dot(a, b):
    return jnp.dot(a, b, preferred_element_type=F32)


def dot_t(a, b):
    return lax.dot_general(a, b, (((1,), (1,)), ((), ())), preferred_element_type=F32)


def sublane(shape):
    return lax.broadcasted_iota(jnp.int32, shape, 0)


def inverse_rms(x):
    return lax.rsqrt(jnp.mean(x * x, axis=-1, keepdims=True) + EPSILON)


def sigmoid(p):
    return 0.5 * jnp.tanh(0.5 * p) + 0.5


def neighbours(rows):
    width = rows[0].shape[0]
    return [
        0.25 * (rows[1 - i] + pltpu.roll(rows[i], 1, 0) + pltpu.roll(rows[i], width - 1, 0))
        for i in range(2)
    ]


def forward_step(u, n, mean, act, pre, d, gain, ws, wn, wo, width, members, out):
    both = 2 * width
    for m in range(members):
        base = m * both
        rows = []
        for lat in range(2):
            x = u[base + lat * width : base + (lat + 1) * width]
            rows.append((x * inverse_rms(x) * gain).astype(BF16).astype(F32))
        n[base : base + both] = jnp.concatenate(rows, axis=0).astype(BF16)
        mean[base : base + both] = jnp.concatenate(neighbours(rows), axis=0).astype(BF16)
    pre[...] = dot(n[...], ws[...]) + dot(mean[...], wn[...])
    for m in range(members):
        base = m * both
        p = pre[base : base + both]
        sig = sigmoid(p)
        act[base : base + both] = (p * sig).astype(BF16)
        if d is not None:
            pre[base : base + both] = sig * (1.0 + p * (1.0 - sig))
    if d is not None:
        for r in range(2 * members):
            slim_copy(d, pre, r)
    pre[...] = dot(act[...], wo[...])
    for r in range(2 * members):
        out(r, u[r * width : (r + 1) * width] + pre[r * width : (r + 1) * width])


def slim_copy(to, wide, r):
    to[r * SLIM : r * SLIM + 16] = wide[r * WIDE : r * WIDE + 16]
    low = wide[r * WIDE + 16 : r * WIDE + 24]
    high = wide[r * WIDE + 32 : r * WIDE + 40]
    to[r * SLIM + 16 : r * SLIM + 24] = jnp.where(sublane(low.shape) < 4, low, high)


def pack_kernel(owner, stencil, weights, precision, values, out, meta):
    steps, _, rows = owner.shape
    meta[...] = jnp.zeros_like(meta)
    for k in range(steps):
        meta[k * META : k * META + 1, 0:rows] = owner[k].astype(F32)
        meta[k * META + 1 : k * META + 5, 0:rows] = stencil[k].astype(F32)
        meta[k * META + 5 : k * META + 9, 0:rows] = weights[k].astype(F32)
        meta[k * META + 9 : k * META + 10, 0:rows] = precision[k : k + 1].astype(F32)
    out[0 : steps * rows] = values[...]
    out[steps * rows :] = meta[...].astype(BF16)


def forward_kernel(
    control, mate, oth, ws, wn, wo, gain,
    u0x, u1x, d0x, d1x, f2x, states,
    ua, ub, n, mean, act, pre, edge,
):
    members = control.shape[0] // 32
    even = lax.rem(lax.axis_index("tile"), 2) == 0
    tile_at = jnp.where(even, 24, 16)
    edge_at = jnp.where(even, 16, 32)
    far = oth[members * 32 :].astype(F32)
    for r in range(2 * members):
        ua[r * WIDE : r * WIDE + 16] = control[r * 16 : (r + 1) * 16]
        ua[pl.ds(pl.multiple_of(r * WIDE + tile_at, 8), 16)] = oth[r * 16 : (r + 1) * 16].astype(F32)
        near4 = mate[r * 4 : (r + 1) * 4]
        far2 = far[r * 2 : (r + 1) * 2]
        edge[...] = jnp.zeros_like(edge)
        edge[0:4] = near4
        edge[6:8] = far2
        edge[8:10] = far2
        edge[12:16] = near4
        ua[pl.ds(pl.multiple_of(r * WIDE + edge_at, 8), 8)] = jnp.where(even, edge[0:8], edge[8:16])
    for r in range(2 * members):
        slim_copy(u0x, ua, r)
    g = gain[...]

    def keep(ref):
        def store(r, value):
            ref[r * WIDE : (r + 1) * WIDE] = value

        return store

    def keep_states(ref, k):
        own = k * members * 32
        away = (2 + k) * members * 32
        for r in range(2 * members):
            states[own + r * 16 : own + (r + 1) * 16] = ref[r * WIDE : r * WIDE + 16].astype(BF16)
            taken = ref[pl.ds(pl.multiple_of(r * WIDE + tile_at, 8), 16)]
            states[away + r * 16 : away + (r + 1) * 16] = taken.astype(BF16)

    forward_step(ua, n, mean, act, pre, d0x, g, ws, wn, wo, WIDE, members, keep(ub))
    for r in range(2 * members):
        slim_copy(u1x, ub, r)
    keep_states(ub, 0)
    forward_step(ub, n, mean, act, pre, d1x, g, ws, wn, wo, WIDE, members, keep(ua))
    for r in range(2 * members):
        slim_copy(f2x, ua, r)
    keep_states(ua, 1)


def split(x):
    high = x.astype(BF16)
    return high, (x - high.astype(F32)).astype(BF16)


def observe_kernel(
    tiles, gathered, states, readout,
    pull1, pull2, message,
    th, tl, ph, plo, vals, field, spread,
):
    steps = 2
    members = states.shape[0] // 128
    per_device = gathered.shape[0] // tiles
    rows = (per_device - steps * META) // steps
    pieces = LANES // rows
    packs = tiles * steps * rows // LANES
    tile = lax.axis_index("tile")
    even = lax.rem(tile, 2) == 0
    other = jnp.where(even, lax.rem(tile + tiles - 1, tiles), lax.rem(tile + 1, tiles))
    me = tile.astype(F32)
    them = other.astype(F32)
    cells = sublane((32, LANES)).astype(F32)
    lane = lax.broadcasted_iota(jnp.int32, (1, LANES), 1)

    def table(p, carry):
        meta = None
        for j in range(pieces):
            index = p * pieces + j
            device = index // steps
            step = index % steps
            start = device * per_device
            piece = gathered[pl.ds(start + steps * rows + step * META, META)].astype(F32)
            if j > 0:
                piece = pltpu.roll(piece, j * rows, 1)
            meta = piece if meta is None else meta + piece
            vals[pl.ds(p * LANES + j * rows, rows)] = gathered[pl.ds(start + step * rows, rows)]
        weight = jnp.zeros((32, LANES), F32)
        for i in range(4):
            weight += jnp.where(cells == meta[1 + i : 2 + i], meta[5 + i : 6 + i], 0.0)
        scaled = weight * meta[9:10]
        wh, wl = split(weight)
        sh, sl = split(scaled)
        parts = ((th, wh.astype(F32)), (tl, wl.astype(F32)), (ph, sh.astype(F32)), (plo, sl.astype(F32)))
        at_step = (p * pieces + lane // rows) % steps
        for q in range(2 * steps):
            named = me if q < steps else them
            hit = jnp.logical_and(meta[0:1] == named, at_step == q % steps)
            for ref, value in parts:
                kept = jnp.where(hit, value, 0.0).astype(BF16)
                ref[q * 32 : (q + 1) * 32, pl.ds(p * LANES, LANES)] = kept
        return carry

    if packs <= 8:
        for p in range(packs):
            table(p, 0)
    else:
        lax.fori_loop(0, packs, table, 0)
    cross = dot_t(ph[...], th[...]) + dot_t(plo[...], th[...]) + dot_t(ph[...], tl[...])
    target = dot(ph[...], vals[...]) + dot(plo[...], vals[...])
    read = dot(states[...], readout[...])
    for q in range(2 * steps):
        for m in range(members):
            start = (q * members + m) * 32
            field[q * 32 : (q + 1) * 32, m * LANES : (m + 1) * LANES] = read[start : start + 32]
    ch, cl = split(cross)
    fh, fl = split(field[...])
    mixed = dot(ch, fh) + dot(cl, fh) + dot(ch, fl)
    for q in range(2 * steps):
        for m in range(members):
            start = (q * members + m) * 32
            value = mixed[q * 32 : (q + 1) * 32, m * LANES : (m + 1) * LANES] - target[q * 32 : (q + 1) * 32]
            spread[start : start + 32] = value.astype(BF16)
    pulled = dot_t(spread[...], readout[...])
    size = members * 32
    row8 = sublane((8, 1))
    for k, out in enumerate((pull1, pull2)):
        own = k * size
        away = (2 + k) * size
        for r in range(2 * members):
            out[r * SLIM : r * SLIM + 16] = pulled[own + r * 16 : own + (r + 1) * 16]
            low = pulled[away + r * 16 : away + r * 16 + 8]
            high = pulled[away + r * 16 + 8 : away + r * 16 + 16]
            group = jnp.where(
                even, jnp.where(row8 >= 4, high, 0.0), jnp.where(row8 < 4, low, 0.0)
            )
            out[r * SLIM + 16 : r * SLIM + 24] = group
        for r in range(2 * members):
            pair = spread[own + r * 16 : own + (r + 1) * 16].astype(F32)
            near = jnp.where(even, pair[8:16], pair[0:8])
            message[k * size // 2 + r * 8 : k * size // 2 + (r + 1) * 8] = near


def adjoint_step(u, cot, gb, gm, flat, d, add, out, gain, ws, wn, wo, members):
    both = 2 * SLIM
    gb[...] = cot[...].astype(BF16)
    flat[...] = dot_t(gb[...], wo[...])
    gb[...] = (flat[...] * d[...]).astype(BF16)
    gm[...] = dot_t(gb[...], wn[...])
    flat[...] = dot_t(gb[...], ws[...])
    for m in range(members):
        base = m * both
        rows = []
        for lat in range(2):
            start = base + lat * SLIM
            rows.append(gm[start : start + SLIM].astype(BF16).astype(F32))
        around = neighbours(rows)
        for lat in range(2):
            start = base + lat * SLIM
            x = u[start : start + SLIM]
            s = inverse_rms(x)
            scaled = gain * (flat[start : start + SLIM] + around[lat])
            inner = jnp.mean(x * scaled, axis=-1, keepdims=True)
            value = cot[start : start + SLIM] + s * scaled - x * (s * s * s * inner)
            if add is not None:
                value = value + add[start : start + SLIM]
            out[start : start + SLIM] = value


def backward_kernel(
    control, u0x, u1x, d0x, d1x, f2x, pull1, pull2, message,
    nxt, nxt_far, prv, prv_far, background, ws, wn, wo, gain, error, readout,
    result,
    cot, cot2, extra, gb, gm, flat, mate_pull, edge, ua, ub, n, mean, act, pre,
):
    members = control.shape[0] // 32
    size = members * 32
    even = lax.rem(lax.axis_index("tile"), 2) == 0
    slot = lax.axis_index("slot")
    later = jnp.where(slot == lax.axis_size("slot") - 1, 0.0, 1.0)
    gain = gain[...]
    error = error[...]
    weight = later * error
    row8 = sublane((8, 1))
    mate_pull[...] = dot_t(message[...].astype(BF16), readout[...])
    mate_side = jnp.where(even, 1, 0) == jnp.where(row8 < 4, 1, 0)

    def edges(near, far, r):
        edge[...] = jnp.zeros_like(edge)
        edge[0:2] = near[size + r * 2 : size + (r + 1) * 2]
        edge[6:8] = far[r * 2 : (r + 1) * 2]
        edge[8:10] = far[r * 2 : (r + 1) * 2]
        edge[14:16] = near[size + r * 2 : size + (r + 1) * 2]
        return jnp.where(even, edge[0:8], edge[8:16])

    for r in range(2 * members):
        a, b = r * SLIM, r * SLIM + 16
        cot[a:b] = pull2[a:b] - weight * (nxt[r * 16 : (r + 1) * 16] - f2x[a:b].astype(BF16).astype(F32))
        c, e = b, b + 8
        start = size // 2 + r * 8
        pulled = pull2[c:e] + jnp.where(mate_side, mate_pull[start : start + 8], 0.0)
        cot[c:e] = pulled - weight * (edges(nxt, nxt_far, r) - f2x[c:e].astype(BF16).astype(F32))
        extra[a:b] = pull1[a:b]
        extra[c:e] = pull1[c:e] + jnp.where(mate_side, mate_pull[r * 8 : (r + 1) * 8], 0.0)
    adjoint_step(u1x, cot, gb, gm, flat, d1x, extra, cot2, gain, ws, wn, wo, members)
    adjoint_step(u0x, cot2, gb, gm, flat, d0x, None, cot, gain, ws, wn, wo, members)
    for r in range(2 * members):
        a, b = r * SLIM, r * SLIM + 16
        ua[a:b] = prv[r * 16 : (r + 1) * 16]
        ua[b : b + 8] = edges(prv, prv_far, r)

    def keep(r, value):
        ub[r * SLIM : (r + 1) * SLIM] = value

    def finish(r, value):
        arrived = value[0:16].astype(BF16)
        before = jnp.where(slot == 0, background[r * 16 : (r + 1) * 16].astype(F32), arrived.astype(F32))
        now = control[r * 16 : (r + 1) * 16]
        result[r * 16 : (r + 1) * 16] = cot[r * SLIM : r * SLIM + 16] + error * (now - before)

    forward_step(ua, n, mean, act, pre, None, gain, ws, wn, wo, SLIM, members, keep)
    forward_step(ub, n, mean, act, pre, None, gain, ws, wn, wo, SLIM, members, finish)


def kernel_call(body, outs, scratch, flops, moved):
    return pl.pallas_call(
        body,
        out_shape=outs,
        scratch_shapes=scratch,
        compiler_params=pltpu.CompilerParams(vmem_limit_bytes=VMEM_LIMIT),
        cost_estimate=pl.CostEstimate(flops=flops, bytes_accessed=moved, transcendentals=0),
    )


def per_device(
    control,
    background,
    self_weight,
    neighbour_weight,
    output_weight,
    norm_gain,
    readout,
    error_weight,
    report_owner,
    report_stencil,
    report_weights,
    report_values,
    report_precision,
):
    tiles = lax.axis_size("tile")
    slots = lax.axis_size("slot")
    even = lax.rem(lax.axis_index("tile"), 2) == 0
    members, lats, cols, channels = control.shape[1:]
    groups = members * lats
    size = groups * cols
    steps = report_owner.shape[1]
    rows = report_owner.shape[2]
    gain = norm_gain.reshape(1, channels)
    error = error_weight.reshape(1, channels)
    grid = control.reshape(groups, cols, channels)
    flat = control.reshape(size, channels)

    def spec(count, dtype=F32, width=channels):
        return jax.ShapeDtypeStruct((count, width), dtype)

    def scratch(count, dtype=F32, width=channels):
        return pltpu.VMEM((count, width), dtype)

    mate_of = [(i, i ^ 1) for i in range(tiles)]
    other_of = [(i, (i - 1) % tiles if i % 2 == 0 else (i + 1) % tiles) for i in range(tiles)]

    def across(block, shift, route):
        pairs = [
            (((s + shift) % slots) * tiles + i, s * tiles + j)
            for s in range(slots)
            for i, j in route
        ]
        return lax.ppermute(block, ("slot", "tile"), pairs)

    near_mate = jnp.where(even, grid[:, cols - 4 :], grid[:, :4]).reshape(groups * 4, channels)
    mate = lax.ppermute(near_mate, "tile", mate_of)
    packed = kernel_call(
        pack_kernel,
        spec(steps * (rows + META), BF16, LANES),
        [scratch(steps * META, F32, LANES)],
        1000,
        100000,
    )(
        jnp.transpose(report_owner[0], (0, 2, 1)),
        jnp.transpose(report_stencil[0], (0, 2, 1)),
        jnp.transpose(report_weights[0], (0, 2, 1)),
        report_precision[0],
        report_values[0].reshape(steps * rows, LANES),
    )
    gathered = lax.all_gather(packed, "tile", tiled=True)
    mate_grid = mate.reshape(groups, 4, channels)
    mate2 = jnp.where(even, mate_grid[:, :2], mate_grid[:, 2:]).reshape(groups * 2, channels)
    sent = jnp.concatenate([flat, mate2], axis=0)
    oth = lax.ppermute(sent.astype(BF16), "tile", other_of)
    near_other = jnp.where(even, grid[:, :2], grid[:, cols - 2 :]).reshape(groups * 2, channels)
    straight = [(i, i) for i in range(tiles)]
    nxt = across(sent, 1, straight)
    nxt_far = across(near_other, 1, other_of)
    if slots == 2:
        prv, prv_far = nxt, nxt_far
    else:
        prv = across(sent, -1, straight)
        prv_far = across(near_other, -1, other_of)

    wide = groups * WIDE
    slim = groups * SLIM
    u0x, u1x, d0x, d1x, f2x, states = kernel_call(
        forward_kernel,
        [spec(slim)] * 5 + [spec(4 * size, BF16)],
        [scratch(wide), scratch(wide), scratch(wide, BF16), scratch(wide, BF16), scratch(wide, BF16)]
        + [scratch(wide), scratch(16)],
        12 * wide * channels * channels,
        4000000,
    )(flat, mate, oth, self_weight, neighbour_weight, output_weight, gain)
    total = tiles * steps * rows
    pull1, pull2, message = kernel_call(
        functools.partial(observe_kernel, tiles),
        [spec(slim), spec(slim), spec(size, F32, LANES)],
        [scratch(128, BF16, total)] * 4
        + [scratch(total, BF16, LANES), scratch(128, F32, members * LANES), scratch(4 * size, BF16, LANES)],
        10**9,
        2000000,
    )(gathered, states, readout)
    from_mate = lax.ppermute(message, "tile", mate_of)
    result = kernel_call(
        backward_kernel,
        spec(size),
        [scratch(slim), scratch(slim), scratch(slim), scratch(slim, BF16), scratch(slim), scratch(slim)]
        + [scratch(size), scratch(16), scratch(slim), scratch(slim)]
        + [scratch(slim, BF16), scratch(slim, BF16), scratch(slim, BF16), scratch(slim)],
        24 * slim * channels * channels,
        6000000,
    )(
        flat, u0x, u1x, d0x, d1x, f2x, pull1, pull2, from_mate,
        nxt, nxt_far, prv, prv_far, background.reshape(size, channels),
        self_weight, neighbour_weight, output_weight, gain, error, readout,
    )
    return result.reshape(control.shape)


def solution(mesh):
    in_specs = (
        P("slot", None, None, "tile", None),
        P(None, None, "tile", None),
        P(),
        P(),
        P(),
        P(),
        P(),
        P(),
        P("slot", None, "tile", None),
        P("slot", None, "tile", None),
        P("slot", None, "tile", None),
        P("slot", None, "tile", None),
        P("slot", None, "tile"),
    )
    out_specs = P("slot", None, None, "tile", None)
    return jax.shard_map(
        per_device, mesh=mesh, in_specs=in_specs, out_specs=out_specs, check_vma=False
    )
```

```python
import functools
import jax
import jax.numpy as jnp
from jax import lax
from jax.experimental import pallas as pl
from jax.experimental.pallas import tpu as pltpu
from jax.sharding import PartitionSpec as P

EPSILON = 1e-06
F32 = jnp.float32
BF16 = jnp.bfloat16
LANES = 128
CAP = 5
SLOTS = 4 * CAP
CHUNK = 32
META = 16
SENDERS = LANES // SLOTS
WIDE = 40
SLIM = 24
VMEM_LIMIT = 28 * 1024 * 1024


def dot(a, b):
    return jnp.dot(a, b, preferred_element_type=F32)


def dot_t(a, b):
    return lax.dot_general(a, b, (((1,), (1,)), ((), ())), preferred_element_type=F32)


def sublane(shape):
    return lax.broadcasted_iota(jnp.int32, shape, 0)


def inverse_rms(x):
    return lax.rsqrt(jnp.mean(x * x, axis=-1, keepdims=True) + EPSILON)


def sigmoid(p):
    return 0.5 * jnp.tanh(0.5 * p) + 0.5


def neighbours(rows):
    width = rows[0].shape[0]
    return [
        0.25 * (rows[1 - i] + pltpu.roll(rows[i], 1, 0) + pltpu.roll(rows[i], width - 1, 0))
        for i in range(2)
    ]


def forward_step(u, n, mean, act, pre, d, gain, ws, wn, wo, width, members, out):
    both = 2 * width
    for m in range(members):
        base = m * both
        rows = []
        for lat in range(2):
            x = u[base + lat * width : base + (lat + 1) * width]
            rows.append((x * inverse_rms(x) * gain).astype(BF16).astype(F32))
        n[base : base + both] = jnp.concatenate(rows, axis=0).astype(BF16)
        mean[base : base + both] = jnp.concatenate(neighbours(rows), axis=0).astype(BF16)
    pre[...] = dot(n[...], ws[...]) + dot(mean[...], wn[...])
    for m in range(members):
        base = m * both
        p = pre[base : base + both]
        sig = sigmoid(p)
        act[base : base + both] = (p * sig).astype(BF16)
        if d is not None:
            pre[base : base + both] = sig * (1.0 + p * (1.0 - sig))
    if d is not None:
        for r in range(2 * members):
            slim_copy(d, pre, r)
    pre[...] = dot(act[...], wo[...])
    for r in range(2 * members):
        out(r, u[r * width : (r + 1) * width] + pre[r * width : (r + 1) * width])


def slim_copy(to, wide, r):
    to[r * SLIM : r * SLIM + 16] = wide[r * WIDE : r * WIDE + 16]
    low = wide[r * WIDE + 16 : r * WIDE + 24]
    high = wide[r * WIDE + 32 : r * WIDE + 40]
    to[r * SLIM + 16 : r * SLIM + 24] = jnp.where(sublane(low.shape) < 4, low, high)


def pack_kernel(owner, stencil, weights, precision, values, out, key, meta, picked):
    steps, _, rows = owner.shape
    tiles = out.shape[0] // CHUNK
    total = steps * rows
    place = lax.axis_index("tile") % SENDERS * SLOTS
    earlier = lax.broadcasted_iota(jnp.int32, (rows, rows), 0) < lax.broadcasted_iota(jnp.int32, (rows, rows), 1)
    earlier = earlier.astype(F32).astype(BF16)
    meta[...] = jnp.zeros_like(meta)
    for k in range(steps):
        at = slice(k * rows, (k + 1) * rows)
        named = lax.broadcasted_iota(jnp.int32, (tiles, rows), 0) == owner[k]
        hits = named.astype(F32)
        before = dot(hits.astype(BF16), earlier)
        rank = jnp.sum(hits * before, axis=0, keepdims=True).astype(jnp.int32)
        key[0:1, at] = owner[k] * (2 * CAP) + k * CAP + rank
        meta[4:8, at] = stencil[k].astype(F32)
        meta[8:12, at] = weights[k].astype(F32)
        meta[12:13, at] = precision[k : k + 1].astype(F32)
    row = lax.broadcasted_iota(jnp.int32, (tiles * CHUNK, total), 0)
    tile = row // CHUNK
    slot = row % CHUNK
    other = jnp.where(tile % 2 == 0, (tile + tiles - 1) % tiles, (tile + 1) % tiles)
    mine = slot < 2 * CAP
    wanted = jnp.where(mine, tile * (2 * CAP) + slot, other * (2 * CAP) + slot - 2 * CAP)
    wanted = jnp.where(slot < SLOTS, wanted, -1)
    placement = (wanted == key[...]).astype(F32).astype(BF16)
    picked[...] = dot(placement, values[...])
    entries = dot_t(meta[...].astype(BF16), placement)
    lane = lax.broadcasted_iota(jnp.int32, (META, LANES), 1)
    used = jnp.logical_and(lane >= place, lane < place + SLOTS)
    per_tile = LANES // CHUNK
    for t in range(tiles):
        block = entries[:, t // per_tile * LANES : (t // per_tile + 1) * LANES]
        shift = (place + LANES - t % per_tile * CHUNK) % LANES
        block = jnp.where(used, pltpu.roll(block, shift, 1), 0.0)
        low = picked[t * CHUNK + 16 : (t + 1) * CHUNK]
        picked[t * CHUNK + 16 : (t + 1) * CHUNK] = jnp.where(sublane((META, 1)) < 4, low, block)
    out[...] = picked[...].astype(BF16)


def near_kernel(control, out):
    even = lax.rem(lax.axis_index("tile"), 2) == 0
    for r in range(control.shape[0] // 16):
        out[r * 4 : (r + 1) * 4] = jnp.where(
            even, control[r * 16 + 12 : (r + 1) * 16], control[r * 16 : r * 16 + 4]
        )


def near_two_kernel(control, out):
    even = lax.rem(lax.axis_index("tile"), 2) == 0
    for r in range(control.shape[0] // 16):
        out[r * 2 : (r + 1) * 2] = jnp.where(
            even, control[r * 16 + 14 : (r + 1) * 16], control[r * 16 : r * 16 + 2]
        )


def tile_kernel(control, mate, out, held):
    even = lax.rem(lax.axis_index("tile"), 2) == 0
    size = control.shape[0]
    out[0:size] = control[...].astype(BF16)
    for r in range(size // 16):
        held[r * 2 : (r + 1) * 2] = jnp.where(even, mate[r * 4 : r * 4 + 2], mate[r * 4 + 2 : (r + 1) * 4])
    out[size:] = held[...].astype(BF16)


def relay_kernel(oth, out, held, wide):
    even = lax.rem(lax.axis_index("tile"), 2) == 0
    size = oth.shape[0] * 8 // 9
    wide[...] = oth[0:size].astype(F32)
    for r in range(size // 16):
        held[r * 2 : (r + 1) * 2] = jnp.where(
            even, wide[r * 16 + 14 : (r + 1) * 16], wide[r * 16 : r * 16 + 2]
        )
    out[...] = held[...].astype(BF16)


def forward_kernel(
    control, mate, oth, ws, wn, wo, gain, readout,
    u0x, u1x, d0x, d1x, f2x, field,
    ua, ub, n, mean, act, pre, edge, states,
):
    members = control.shape[0] // 32
    even = lax.rem(lax.axis_index("tile"), 2) == 0
    tile_at = jnp.where(even, 24, 16)
    edge_at = jnp.where(even, 16, 32)
    far = oth[members * 32 :].astype(F32)
    for r in range(2 * members):
        ua[r * WIDE : r * WIDE + 16] = control[r * 16 : (r + 1) * 16]
        ua[pl.ds(pl.multiple_of(r * WIDE + tile_at, 8), 16)] = oth[r * 16 : (r + 1) * 16].astype(F32)
        near4 = mate[r * 4 : (r + 1) * 4]
        far2 = far[r * 2 : (r + 1) * 2]
        edge[...] = jnp.zeros_like(edge)
        edge[0:4] = near4
        edge[6:8] = far2
        edge[8:10] = far2
        edge[12:16] = near4
        ua[pl.ds(pl.multiple_of(r * WIDE + edge_at, 8), 8)] = jnp.where(even, edge[0:8], edge[8:16])
    for r in range(2 * members):
        slim_copy(u0x, ua, r)
    g = gain[...]

    def keep(ref):
        def store(r, value):
            ref[r * WIDE : (r + 1) * WIDE] = value

        return store

    def keep_states(ref, k):
        own = k * members * 32
        away = (2 + k) * members * 32
        for r in range(2 * members):
            states[own + r * 16 : own + (r + 1) * 16] = ref[r * WIDE : r * WIDE + 16].astype(BF16)
            taken = ref[pl.ds(pl.multiple_of(r * WIDE + tile_at, 8), 16)]
            states[away + r * 16 : away + (r + 1) * 16] = taken.astype(BF16)

    forward_step(ua, n, mean, act, pre, d0x, g, ws, wn, wo, WIDE, members, keep(ub))
    for r in range(2 * members):
        slim_copy(u1x, ub, r)
    keep_states(ub, 0)
    forward_step(ub, n, mean, act, pre, d1x, g, ws, wn, wo, WIDE, members, keep(ua))
    for r in range(2 * members):
        slim_copy(f2x, ua, r)
    keep_states(ua, 1)
    read = dot(states[...], readout[...])
    for q in range(4):
        for m in range(members):
            start = (q * members + m) * 32
            field[q * 32 : (q + 1) * 32, m * LANES : (m + 1) * LANES] = read[start : start + 32]


def split(x):
    high = x.astype(BF16)
    return high, (x - high.astype(F32)).astype(BF16)


def observe_kernel(
    tiles, arrived, field, readout,
    pull1, pull2, message,
    th, tl, ph, plo, vals, spread, wide,
):
    steps = 2
    members = field.shape[1] // LANES
    even = lax.rem(lax.axis_index("tile"), 2) == 0
    cells = sublane((32, LANES)).astype(F32)
    lane = lax.broadcasted_iota(jnp.int32, (1, LANES), 1)
    table_of = jnp.where(lane < SENDERS * SLOTS, lane % SLOTS // CAP, -1)
    wide[...] = arrived[...].astype(F32)
    vals[...] = jnp.zeros_like(vals)
    for p in range(th.shape[1] // LANES):
        meta = jnp.zeros((META, LANES), F32)
        for d in range(p * SENDERS, min((p + 1) * SENDERS, tiles)):
            meta += wide[d * CHUNK + 16 : (d + 1) * CHUNK]
            start = p * LANES + d % SENDERS * SLOTS
            vals[start : start + SLOTS] = wide[d * CHUNK : d * CHUNK + SLOTS]
        weight = jnp.zeros((32, LANES), F32)
        for i in range(4):
            weight += jnp.where(cells == meta[4 + i : 5 + i], meta[8 + i : 9 + i], 0.0)
        scaled = weight * meta[12:13]
        wh, wl = split(weight)
        sh, sl = split(scaled)
        parts = ((th, wh.astype(F32)), (tl, wl.astype(F32)), (ph, sh.astype(F32)), (plo, sl.astype(F32)))
        for q in range(2 * steps):
            hit = table_of == q
            for ref, value in parts:
                kept = jnp.where(hit, value, 0.0).astype(BF16)
                ref[q * 32 : (q + 1) * 32, p * LANES : (p + 1) * LANES] = kept
    cross = dot_t(ph[...], th[...]) + dot_t(plo[...], th[...]) + dot_t(ph[...], tl[...])
    taken = vals[...].astype(BF16)
    target = dot(ph[...], taken) + dot(plo[...], taken)
    ch, cl = split(cross)
    fh, fl = split(field[...])
    mixed = dot(ch, fh) + dot(cl, fh) + dot(ch, fl)
    for q in range(2 * steps):
        for m in range(members):
            start = (q * members + m) * 32
            value = mixed[q * 32 : (q + 1) * 32, m * LANES : (m + 1) * LANES] - target[q * 32 : (q + 1) * 32]
            spread[start : start + 32] = value.astype(BF16)
    pulled = dot_t(spread[...], readout[...])
    size = members * 32
    row8 = sublane((8, 1))
    for k, out in enumerate((pull1, pull2)):
        own = k * size
        away = (2 + k) * size
        for r in range(2 * members):
            out[r * SLIM : r * SLIM + 16] = pulled[own + r * 16 : own + (r + 1) * 16]
            low = pulled[away + r * 16 : away + r * 16 + 8]
            high = pulled[away + r * 16 + 8 : away + r * 16 + 16]
            group = jnp.where(
                even, jnp.where(row8 >= 4, high, 0.0), jnp.where(row8 < 4, low, 0.0)
            )
            out[r * SLIM + 16 : r * SLIM + 24] = group
        for r in range(2 * members):
            pair = spread[own + r * 16 : own + (r + 1) * 16].astype(F32)
            near = jnp.where(even, pair[8:16], pair[0:8])
            message[k * size // 2 + r * 8 : k * size // 2 + (r + 1) * 8] = near


def adjoint_step(u, cot, gb, gm, flat, d, add, out, gain, ws, wn, wo, members):
    both = 2 * SLIM
    gb[...] = cot[...].astype(BF16)
    flat[...] = dot_t(gb[...], wo[...])
    gb[...] = (flat[...] * d[...]).astype(BF16)
    gm[...] = dot_t(gb[...], wn[...])
    flat[...] = dot_t(gb[...], ws[...])
    for m in range(members):
        base = m * both
        rows = []
        for lat in range(2):
            start = base + lat * SLIM
            rows.append(gm[start : start + SLIM].astype(BF16).astype(F32))
        around = neighbours(rows)
        for lat in range(2):
            start = base + lat * SLIM
            x = u[start : start + SLIM]
            s = inverse_rms(x)
            scaled = gain * (flat[start : start + SLIM] + around[lat])
            inner = jnp.mean(x * scaled, axis=-1, keepdims=True)
            value = cot[start : start + SLIM] + s * scaled - x * (s * s * s * inner)
            if add is not None:
                value = value + add[start : start + SLIM]
            out[start : start + SLIM] = value


def edges(near, far, edge, r):
    even = lax.rem(lax.axis_index("tile"), 2) == 0
    near = near[r * 2 : (r + 1) * 2].astype(F32)
    far = far[r * 2 : (r + 1) * 2].astype(F32)
    edge[...] = jnp.zeros_like(edge)
    edge[0:2] = near
    edge[6:8] = far
    edge[8:10] = far
    edge[14:16] = near
    return jnp.where(even, edge[0:8], edge[8:16])


def previous_kernel(
    control, prv, prv_near, prv_far, background, ws, wn, wo, gain, error,
    misfit,
    ua, ub, n, mean, act, pre, edge, far,
):
    members = control.shape[0] // 32
    slot = lax.axis_index("slot")
    far[...] = prv_far[...].astype(F32)
    for r in range(2 * members):
        a, b = r * SLIM, r * SLIM + 16
        ua[a:b] = prv[r * 16 : (r + 1) * 16]
        ua[b : b + 8] = edges(prv_near, far, edge, r)

    def keep(r, value):
        ub[r * SLIM : (r + 1) * SLIM] = value

    def finish(r, value):
        arrived = value[0:16].astype(BF16).astype(F32)
        before = jnp.where(slot == 0, background[r * 16 : (r + 1) * 16].astype(F32), arrived)
        misfit[r * 16 : (r + 1) * 16] = error[...] * (control[r * 16 : (r + 1) * 16] - before)

    forward_step(ua, n, mean, act, pre, None, gain[...], ws, wn, wo, SLIM, members, keep)
    forward_step(ub, n, mean, act, pre, None, gain[...], ws, wn, wo, SLIM, members, finish)


def backward_kernel(
    u0x, u1x, d0x, d1x, f2x, pull1, pull2, message,
    nxt, nxt_near, nxt_far, misfit, ws, wn, wo, gain, error, readout,
    result,
    cot, cot2, extra, gb, gm, flat, mate_pull, edge, far,
):
    size = nxt.shape[0]
    members = size // 32
    even = lax.rem(lax.axis_index("tile"), 2) == 0
    slot = lax.axis_index("slot")
    later = jnp.where(slot == lax.axis_size("slot") - 1, 0.0, 1.0)
    gain = gain[...]
    weight = later * error[...]
    row8 = sublane((8, 1))
    mate_pull[...] = dot_t(message[...].astype(BF16), readout[...])
    mate_side = jnp.where(even, 1, 0) == jnp.where(row8 < 4, 1, 0)
    far[...] = nxt_far[...].astype(F32)
    for r in range(2 * members):
        a, b = r * SLIM, r * SLIM + 16
        cot[a:b] = pull2[a:b] - weight * (nxt[r * 16 : (r + 1) * 16] - f2x[a:b].astype(BF16).astype(F32))
        c, e = b, b + 8
        start = size // 2 + r * 8
        pulled = pull2[c:e] + jnp.where(mate_side, mate_pull[start : start + 8], 0.0)
        cot[c:e] = pulled - weight * (edges(nxt_near, far, edge, r) - f2x[c:e].astype(BF16).astype(F32))
        extra[a:b] = pull1[a:b]
        extra[c:e] = pull1[c:e] + jnp.where(mate_side, mate_pull[r * 8 : (r + 1) * 8], 0.0)
    adjoint_step(u1x, cot, gb, gm, flat, d1x, extra, cot2, gain, ws, wn, wo, members)
    adjoint_step(u0x, cot2, gb, gm, flat, d0x, None, cot, gain, ws, wn, wo, members)
    for r in range(2 * members):
        result[r * 16 : (r + 1) * 16] = cot[r * SLIM : r * SLIM + 16] + misfit[r * 16 : (r + 1) * 16]


def kernel_call(body, outs, scratch, flops, moved):
    return pl.pallas_call(
        body,
        out_shape=outs,
        scratch_shapes=scratch,
        compiler_params=pltpu.CompilerParams(vmem_limit_bytes=VMEM_LIMIT),
        cost_estimate=pl.CostEstimate(flops=flops, bytes_accessed=moved, transcendentals=0),
    )


def per_device(
    control,
    background,
    self_weight,
    neighbour_weight,
    output_weight,
    norm_gain,
    readout,
    error_weight,
    report_owner,
    report_stencil,
    report_weights,
    report_values,
    report_precision,
):
    tiles = lax.axis_size("tile")
    slots = lax.axis_size("slot")
    members, lats, cols, channels = control.shape[1:]
    groups = members * lats
    size = groups * cols
    steps = report_owner.shape[1]
    rows = report_owner.shape[2]
    gain = norm_gain.reshape(1, channels)
    error = error_weight.reshape(1, channels)
    flat = control.reshape(size, channels)

    def spec(count, dtype=F32, width=channels):
        return jax.ShapeDtypeStruct((count, width), dtype)

    def scratch(count, dtype=F32, width=channels):
        return pltpu.VMEM((count, width), dtype)

    mate_of = [(i, i ^ 1) for i in range(tiles)]
    other_of = [(i, (i - 1) % tiles if i % 2 == 0 else (i + 1) % tiles) for i in range(tiles)]

    def across(block, shift, route):
        pairs = [
            (((s + shift) % slots) * tiles + i, s * tiles + j)
            for s in range(slots)
            for i, j in route
        ]
        return lax.ppermute(block, ("slot", "tile"), pairs)

    straight = [(i, i) for i in range(tiles)]
    nxt = across(flat, 1, straight)
    prv = nxt if slots == 2 else across(flat, -1, straight)
    near_mate = kernel_call(near_kernel, spec(groups * 4), [], 1000, 300000)(flat)
    mate = lax.ppermute(near_mate, "tile", mate_of)
    packed = kernel_call(
        pack_kernel,
        spec(tiles * CHUNK, BF16, LANES),
        [
            pltpu.VMEM((1, steps * rows), jnp.int32),
            scratch(META, F32, steps * rows),
            scratch(tiles * CHUNK, F32, LANES),
        ],
        10**7,
        200000,
    )(
        jnp.transpose(report_owner[0], (0, 2, 1)),
        jnp.transpose(report_stencil[0], (0, 2, 1)),
        jnp.transpose(report_weights[0], (0, 2, 1)),
        report_precision[0],
        report_values[0].reshape(steps * rows, LANES),
    )
    sent = kernel_call(
        tile_kernel, spec(groups * (cols + 2), BF16), [scratch(groups * 2)], 1000, 400000
    )(flat, mate)
    oth = lax.ppermute(sent, "tile", other_of)
    arrived = lax.all_to_all(packed, "tile", split_axis=0, concat_axis=0, tiled=True)

    wide = groups * WIDE
    slim = groups * SLIM
    u0x, u1x, d0x, d1x, f2x, field = kernel_call(
        forward_kernel,
        [spec(slim)] * 5 + [spec(4 * lats * cols, F32, members * LANES)],
        [scratch(wide), scratch(wide), scratch(wide, BF16), scratch(wide, BF16), scratch(wide, BF16)]
        + [scratch(wide), scratch(16), scratch(4 * size, BF16)],
        12 * wide * channels * channels,
        4000000,
    )(flat, mate, oth, self_weight, neighbour_weight, output_weight, gain, readout)
    relayed = kernel_call(
        relay_kernel,
        spec(groups * 2, BF16),
        [scratch(groups * 2), scratch(size)],
        1000,
        300000,
    )(oth)
    nxt_far = across(relayed, 1, straight)

    def near_two(block):
        out = kernel_call(near_two_kernel, spec(groups * 2), [], 1000, 300000)(block)
        return lax.ppermute(out, "tile", mate_of)

    nxt_near = near_two(nxt)
    if slots == 2:
        prv_far, prv_near = nxt_far, nxt_near
    else:
        prv_far, prv_near = across(relayed, -1, straight), near_two(prv)
    total = -(-tiles // SENDERS) * LANES
    pull1, pull2, message = kernel_call(
        functools.partial(observe_kernel, tiles),
        [spec(slim), spec(slim), spec(size, F32, LANES)],
        [scratch(128, BF16, total)] * 4
        + [scratch(total, F32, LANES), scratch(4 * size, BF16, LANES), scratch(tiles * CHUNK, F32, LANES)],
        10**9,
        2000000,
    )(arrived, field, readout)
    from_mate = lax.ppermute(message, "tile", mate_of)
    misfit = kernel_call(
        previous_kernel,
        spec(size),
        [scratch(slim), scratch(slim), scratch(slim, BF16), scratch(slim, BF16), scratch(slim, BF16)]
        + [scratch(slim), scratch(16), scratch(groups * 2)],
        12 * slim * channels * channels,
        4000000,
    )(
        flat, prv, prv_near, prv_far, background.reshape(size, channels),
        self_weight, neighbour_weight, output_weight, gain, error,
    )
    result = kernel_call(
        backward_kernel,
        spec(size),
        [scratch(slim), scratch(slim), scratch(slim), scratch(slim, BF16), scratch(slim), scratch(slim)]
        + [scratch(size), scratch(16), scratch(groups * 2)],
        12 * slim * channels * channels,
        6000000,
    )(
        u0x, u1x, d0x, d1x, f2x, pull1, pull2, from_mate,
        nxt, nxt_near, nxt_far, misfit,
        self_weight, neighbour_weight, output_weight, gain, error, readout,
    )
    return result.reshape(control.shape)


def solution(mesh):
    in_specs = (
        P("slot", None, None, "tile", None),
        P(None, None, "tile", None),
        P(),
        P(),
        P(),
        P(),
        P(),
        P(),
        P("slot", None, "tile", None),
        P("slot", None, "tile", None),
        P("slot", None, "tile", None),
        P("slot", None, "tile", None),
        P("slot", None, "tile"),
    )
    out_specs = P("slot", None, None, "tile", None)
    return jax.shard_map(
        per_device, mesh=mesh, in_specs=in_specs, out_specs=out_specs, check_vma=False
    )
```

```python
import functools
import jax
import jax.numpy as jnp
from jax import lax
from jax.experimental import pallas as pl
from jax.experimental.pallas import tpu as pltpu
from jax.sharding import PartitionSpec as P

EPSILON = 1e-06
F32 = jnp.float32
BF16 = jnp.bfloat16
LANES = 128
CAP = 5
SLOTS = 4 * CAP
CHUNK = 32
META = 16
SENDERS = LANES // SLOTS
WIDE = 40
SLIM = 24
VMEM_LIMIT = 28 * 1024 * 1024


def dot(a, b):
    return jnp.dot(a, b, preferred_element_type=F32)


def dot_t(a, b):
    return lax.dot_general(a, b, (((1,), (1,)), ((), ())), preferred_element_type=F32)


def sublane(shape):
    return lax.broadcasted_iota(jnp.int32, shape, 0)


def inverse_rms(x):
    return lax.rsqrt(jnp.mean(x * x, axis=-1, keepdims=True) + EPSILON)


def sigmoid(p):
    return 0.5 * jnp.tanh(0.5 * p) + 0.5


def neighbours(rows):
    width = rows[0].shape[0]
    return [
        0.25 * (rows[1 - i] + pltpu.roll(rows[i], 1, 0) + pltpu.roll(rows[i], width - 1, 0))
        for i in range(2)
    ]


def forward_step(u, n, mean, act, pre, d, gain, ws, wn, wo, width, members, out):
    both = 2 * width
    for m in range(members):
        base = m * both
        rows = []
        for lat in range(2):
            x = u[base + lat * width : base + (lat + 1) * width]
            rows.append((x * inverse_rms(x) * gain).astype(BF16).astype(F32))
        n[base : base + both] = jnp.concatenate(rows, axis=0).astype(BF16)
        mean[base : base + both] = jnp.concatenate(neighbours(rows), axis=0).astype(BF16)
    pre[...] = dot(n[...], ws[...]) + dot(mean[...], wn[...])
    for m in range(members):
        base = m * both
        p = pre[base : base + both]
        sig = sigmoid(p)
        act[base : base + both] = (p * sig).astype(BF16)
        if d is not None:
            pre[base : base + both] = sig * (1.0 + p * (1.0 - sig))
    if d is not None:
        for m in range(members):
            slim_copy(d, pre, m)
    pre[...] = dot(act[...], wo[...])
    for r in range(2 * members):
        out(r, u[r * width : (r + 1) * width] + pre[r * width : (r + 1) * width])


def slim_edge(wide, r):
    low = wide[r * WIDE + 16 : r * WIDE + 24]
    high = wide[r * WIDE + 32 : r * WIDE + 40]
    return jnp.where(sublane(low.shape) < 4, low, high)


def slim_copy(to, wide, m):
    parts = []
    for r in (2 * m, 2 * m + 1):
        parts += [wide[r * WIDE : r * WIDE + 16], slim_edge(wide, r)]
    both = jnp.concatenate(parts, axis=0)
    to[m * 2 * SLIM : (m + 1) * 2 * SLIM] = both.astype(to.dtype)


def pack_kernel(owner, stencil, weights, precision, values, out, key, meta, picked):
    steps, _, rows = owner.shape
    tiles = out.shape[0] // CHUNK
    total = steps * rows
    place = lax.axis_index("tile") % SENDERS * SLOTS
    earlier = lax.broadcasted_iota(jnp.int32, (rows, rows), 0) < lax.broadcasted_iota(jnp.int32, (rows, rows), 1)
    earlier = earlier.astype(F32).astype(BF16)
    meta[...] = jnp.zeros_like(meta)
    for k in range(steps):
        at = slice(k * rows, (k + 1) * rows)
        named = lax.broadcasted_iota(jnp.int32, (tiles, rows), 0) == owner[k]
        hits = named.astype(F32)
        before = dot(hits.astype(BF16), earlier)
        rank = jnp.sum(hits * before, axis=0, keepdims=True).astype(jnp.int32)
        key[0:1, at] = owner[k] * (2 * CAP) + k * CAP + rank
        meta[4:8, at] = stencil[k].astype(F32)
        meta[8:12, at] = weights[k].astype(F32)
        meta[12:13, at] = precision[k : k + 1].astype(F32)
    row = lax.broadcasted_iota(jnp.int32, (tiles * CHUNK, total), 0)
    tile = row // CHUNK
    slot = row % CHUNK
    other = jnp.where(tile % 2 == 0, (tile + tiles - 1) % tiles, (tile + 1) % tiles)
    mine = slot < 2 * CAP
    wanted = jnp.where(mine, tile * (2 * CAP) + slot, other * (2 * CAP) + slot - 2 * CAP)
    wanted = jnp.where(slot < SLOTS, wanted, -1)
    placement = (wanted == key[...]).astype(F32).astype(BF16)
    picked[...] = dot(placement, values[...])
    entries = dot_t(meta[...].astype(BF16), placement)
    lane = lax.broadcasted_iota(jnp.int32, (META, LANES), 1)
    used = jnp.logical_and(lane >= place, lane < place + SLOTS)
    per_tile = LANES // CHUNK
    for t in range(tiles):
        block = entries[:, t // per_tile * LANES : (t // per_tile + 1) * LANES]
        shift = (place + LANES - t % per_tile * CHUNK) % LANES
        block = jnp.where(used, pltpu.roll(block, shift, 1), 0.0)
        low = picked[t * CHUNK + 16 : (t + 1) * CHUNK]
        picked[t * CHUNK + 16 : (t + 1) * CHUNK] = jnp.where(sublane((META, 1)) < 4, low, block)
    out[...] = picked[...].astype(BF16)


def near_kernel(control, held, out):
    held[...] = control[...]
    even = lax.rem(lax.axis_index("tile"), 2) == 0
    for r in range(control.shape[0] // 16):
        out[r * 4 : (r + 1) * 4] = jnp.where(
            even, control[r * 16 + 12 : (r + 1) * 16], control[r * 16 : r * 16 + 4]
        )


def near_two_kernel(control, out):
    even = lax.rem(lax.axis_index("tile"), 2) == 0
    for r in range(control.shape[0] // 16):
        out[r * 2 : (r + 1) * 2] = jnp.where(
            even, control[r * 16 + 14 : (r + 1) * 16], control[r * 16 : r * 16 + 2]
        )


def tile_kernel(control, mate, out, held):
    even = lax.rem(lax.axis_index("tile"), 2) == 0
    size = control.shape[0]
    out[0:size] = control[...].astype(BF16)
    for r in range(size // 16):
        held[r * 2 : (r + 1) * 2] = jnp.where(even, mate[r * 4 : r * 4 + 2], mate[r * 4 + 2 : (r + 1) * 4])
    out[size:] = held[...].astype(BF16)


def after_kernel(packed, sent, out):
    out[...] = packed[...]


def relay_kernel(oth, out, held, wide):
    even = lax.rem(lax.axis_index("tile"), 2) == 0
    size = oth.shape[0] * 8 // 9
    wide[...] = oth[0:size].astype(F32)
    for r in range(size // 16):
        held[r * 2 : (r + 1) * 2] = jnp.where(
            even, wide[r * 16 + 14 : (r + 1) * 16], wide[r * 16 : r * 16 + 2]
        )
    out[...] = held[...].astype(BF16)


def forward_kernel(
    control, mate, oth, ws, wn, wo, gain, readout,
    edge0, u1x, d0x, d1x, f2x, field,
    ua, ub, n, mean, act, pre, edge, states,
):
    members = control.shape[0] // 32
    even = lax.rem(lax.axis_index("tile"), 2) == 0
    tile_at = jnp.where(even, 24, 16)
    edge_at = jnp.where(even, 16, 32)
    far = oth[members * 32 :].astype(F32)
    for r in range(2 * members):
        ua[r * WIDE : r * WIDE + 16] = control[r * 16 : (r + 1) * 16]
        ua[pl.ds(pl.multiple_of(r * WIDE + tile_at, 8), 16)] = oth[r * 16 : (r + 1) * 16].astype(F32)
        near4 = mate[r * 4 : (r + 1) * 4]
        far2 = far[r * 2 : (r + 1) * 2]
        edge[...] = jnp.zeros_like(edge)
        edge[0:4] = near4
        edge[6:8] = far2
        edge[8:10] = far2
        edge[12:16] = near4
        ua[pl.ds(pl.multiple_of(r * WIDE + edge_at, 8), 8)] = jnp.where(even, edge[0:8], edge[8:16])
    for r in range(2 * members):
        edge0[r * 8 : (r + 1) * 8] = slim_edge(ua, r)
    g = gain[...]

    def keep(ref):
        def store(r, value):
            ref[r * WIDE : (r + 1) * WIDE] = value

        return store

    def keep_states(ref, k):
        own = k * members * 32
        away = (2 + k) * members * 32
        for r in range(2 * members):
            states[own + r * 16 : own + (r + 1) * 16] = ref[r * WIDE : r * WIDE + 16].astype(BF16)
            taken = ref[pl.ds(pl.multiple_of(r * WIDE + tile_at, 8), 16)]
            states[away + r * 16 : away + (r + 1) * 16] = taken.astype(BF16)

    forward_step(ua, n, mean, act, pre, d0x, g, ws, wn, wo, WIDE, members, keep(ub))
    for m in range(members):
        slim_copy(u1x, ub, m)
    keep_states(ub, 0)
    forward_step(ub, n, mean, act, pre, d1x, g, ws, wn, wo, WIDE, members, keep(ua))
    for m in range(members):
        slim_copy(f2x, ua, m)
    keep_states(ua, 1)
    read = dot(states[...], readout[...])
    for q in range(4):
        for m in range(members):
            start = (q * members + m) * 32
            field[q * 32 : (q + 1) * 32, m * LANES : (m + 1) * LANES] = read[start : start + 32]


def split(x):
    high = x.astype(BF16)
    return high, (x - high.astype(F32)).astype(BF16)


def observe_kernel(
    tiles, arrived, field, readout,
    pull1, pull2, message,
    th, tl, ph, plo, vals, spread, wide,
):
    steps = 2
    members = field.shape[1] // LANES
    even = lax.rem(lax.axis_index("tile"), 2) == 0
    cells = sublane((32, LANES)).astype(F32)
    lane = lax.broadcasted_iota(jnp.int32, (1, LANES), 1)
    table_of = jnp.where(lane < SENDERS * SLOTS, lane % SLOTS // CAP, -1)
    wide[...] = arrived[...].astype(F32)
    vals[...] = jnp.zeros_like(vals)
    for p in range(th.shape[1] // LANES):
        meta = jnp.zeros((META, LANES), F32)
        for d in range(p * SENDERS, min((p + 1) * SENDERS, tiles)):
            meta += wide[d * CHUNK + 16 : (d + 1) * CHUNK]
            start = p * LANES + d % SENDERS * SLOTS
            vals[start : start + SLOTS] = wide[d * CHUNK : d * CHUNK + SLOTS]
        weight = jnp.zeros((32, LANES), F32)
        for i in range(4):
            weight += jnp.where(cells == meta[4 + i : 5 + i], meta[8 + i : 9 + i], 0.0)
        scaled = weight * meta[12:13]
        wh, wl = split(weight)
        sh, sl = split(scaled)
        parts = ((th, wh.astype(F32)), (tl, wl.astype(F32)), (ph, sh.astype(F32)), (plo, sl.astype(F32)))
        for q in range(2 * steps):
            hit = table_of == q
            for ref, value in parts:
                kept = jnp.where(hit, value, 0.0).astype(BF16)
                ref[q * 32 : (q + 1) * 32, p * LANES : (p + 1) * LANES] = kept
    cross = dot_t(ph[...], th[...]) + dot_t(plo[...], th[...]) + dot_t(ph[...], tl[...])
    taken = vals[...].astype(BF16)
    target = dot(ph[...], taken) + dot(plo[...], taken)
    ch, cl = split(cross)
    fh, fl = split(field[...])
    mixed = dot(ch, fh) + dot(cl, fh) + dot(ch, fl)
    for q in range(2 * steps):
        for m in range(members):
            start = (q * members + m) * 32
            value = mixed[q * 32 : (q + 1) * 32, m * LANES : (m + 1) * LANES] - target[q * 32 : (q + 1) * 32]
            spread[start : start + 32] = value.astype(BF16)
    pulled = dot_t(spread[...], readout[...])
    size = members * 32
    row8 = sublane((8, 1))
    for k, out in enumerate((pull1, pull2)):
        own = k * size
        away = (2 + k) * size
        for r in range(2 * members):
            out[r * SLIM : r * SLIM + 16] = pulled[own + r * 16 : own + (r + 1) * 16]
            low = pulled[away + r * 16 : away + r * 16 + 8]
            high = pulled[away + r * 16 + 8 : away + r * 16 + 16]
            group = jnp.where(
                even, jnp.where(row8 >= 4, high, 0.0), jnp.where(row8 < 4, low, 0.0)
            )
            out[r * SLIM + 16 : r * SLIM + 24] = group
        for r in range(2 * members):
            pair = spread[own + r * 16 : own + (r + 1) * 16].astype(F32)
            near = jnp.where(even, pair[8:16], pair[0:8])
            message[k * size // 2 + r * 8 : k * size // 2 + (r + 1) * 8] = near


def adjoint_step(u, cot, gb, gm, flat, d, add, out, gain, ws, wn, wo, members):
    both = 2 * SLIM
    gb[...] = cot[...].astype(BF16)
    flat[...] = dot_t(gb[...], wo[...])
    gb[...] = (flat[...] * d[...]).astype(BF16)
    gm[...] = dot_t(gb[...], wn[...])
    flat[...] = dot_t(gb[...], ws[...])
    for m in range(members):
        base = m * both
        rows = []
        for lat in range(2):
            start = base + lat * SLIM
            rows.append(gm[start : start + SLIM].astype(BF16).astype(F32))
        around = neighbours(rows)
        for lat in range(2):
            start = base + lat * SLIM
            x = u[start : start + SLIM]
            s = inverse_rms(x)
            scaled = gain * (flat[start : start + SLIM] + around[lat])
            inner = jnp.mean(x * scaled, axis=-1, keepdims=True)
            value = cot[start : start + SLIM] + s * scaled - x * (s * s * s * inner)
            if add is not None:
                value = value + add[start : start + SLIM]
            out[start : start + SLIM] = value


def edges(near, far, edge, r):
    even = lax.rem(lax.axis_index("tile"), 2) == 0
    near = near[r * 2 : (r + 1) * 2].astype(F32)
    far = far[r * 2 : (r + 1) * 2].astype(F32)
    edge[...] = jnp.zeros_like(edge)
    edge[0:2] = near
    edge[6:8] = far
    edge[8:10] = far
    edge[14:16] = near
    return jnp.where(even, edge[0:8], edge[8:16])


def previous_kernel(
    control, prv, prv_near, prv_far, background, ws, wn, wo, gain, error,
    misfit,
    ua, ub, n, mean, act, pre, edge, far,
):
    members = control.shape[0] // 32
    slot = lax.axis_index("slot")
    far[...] = prv_far[...].astype(F32)
    for r in range(2 * members):
        a, b = r * SLIM, r * SLIM + 16
        ua[a:b] = prv[r * 16 : (r + 1) * 16]
        ua[b : b + 8] = edges(prv_near, far, edge, r)

    def keep(r, value):
        ub[r * SLIM : (r + 1) * SLIM] = value

    def finish(r, value):
        arrived = value[0:16].astype(BF16).astype(F32)
        before = jnp.where(slot == 0, background[r * 16 : (r + 1) * 16].astype(F32), arrived)
        misfit[r * 16 : (r + 1) * 16] = error[...] * (control[r * 16 : (r + 1) * 16] - before)

    forward_step(ua, n, mean, act, pre, None, gain[...], ws, wn, wo, SLIM, members, keep)
    forward_step(ub, n, mean, act, pre, None, gain[...], ws, wn, wo, SLIM, members, finish)


def backward_kernel(
    control, edge0, u1x, d0x, d1x, f2x, pull1, pull2, message,
    nxt, nxt_near, nxt_far, misfit, ws, wn, wo, gain, error, readout,
    result,
    cot, cot2, extra, gb, gm, flat, mate_pull, edge, far, u0x, final,
):
    size = nxt.shape[0]
    members = size // 32
    even = lax.rem(lax.axis_index("tile"), 2) == 0
    slot = lax.axis_index("slot")
    later = jnp.where(slot == lax.axis_size("slot") - 1, 0.0, 1.0)
    gain = gain[...]
    weight = later * error[...]
    row8 = sublane((8, 1))
    mate_pull[...] = dot_t(message[...].astype(BF16), readout[...])
    mate_side = jnp.where(even, 1, 0) == jnp.where(row8 < 4, 1, 0)
    far[...] = nxt_far[...].astype(F32)
    final[...] = f2x[...].astype(F32)
    for r in range(2 * members):
        a, b = r * SLIM, r * SLIM + 16
        u0x[a:b] = control[r * 16 : (r + 1) * 16]
        u0x[b : b + 8] = edge0[r * 8 : (r + 1) * 8]
        cot[a:b] = pull2[a:b] - weight * (nxt[r * 16 : (r + 1) * 16] - final[a:b])
        c, e = b, b + 8
        start = size // 2 + r * 8
        pulled = pull2[c:e] + jnp.where(mate_side, mate_pull[start : start + 8], 0.0)
        cot[c:e] = pulled - weight * (edges(nxt_near, far, edge, r) - final[c:e])
        extra[a:b] = pull1[a:b]
        extra[c:e] = pull1[c:e] + jnp.where(mate_side, mate_pull[r * 8 : (r + 1) * 8], 0.0)
    adjoint_step(u1x, cot, gb, gm, flat, d1x, extra, cot2, gain, ws, wn, wo, members)
    adjoint_step(u0x, cot2, gb, gm, flat, d0x, None, cot, gain, ws, wn, wo, members)
    for r in range(2 * members):
        result[r * 16 : (r + 1) * 16] = cot[r * SLIM : r * SLIM + 16] + misfit[r * 16 : (r + 1) * 16]


def kernel_call(body, outs, scratch, flops, moved):
    return pl.pallas_call(
        body,
        out_shape=outs,
        scratch_shapes=scratch,
        compiler_params=pltpu.CompilerParams(vmem_limit_bytes=VMEM_LIMIT),
        cost_estimate=pl.CostEstimate(flops=flops, bytes_accessed=moved, transcendentals=0),
    )


def per_device(
    control,
    background,
    self_weight,
    neighbour_weight,
    output_weight,
    norm_gain,
    readout,
    error_weight,
    report_owner,
    report_stencil,
    report_weights,
    report_values,
    report_precision,
):
    tiles = lax.axis_size("tile")
    slots = lax.axis_size("slot")
    members, lats, cols, channels = control.shape[1:]
    groups = members * lats
    size = groups * cols
    steps = report_owner.shape[1]
    rows = report_owner.shape[2]
    gain = norm_gain.reshape(1, channels)
    error = error_weight.reshape(1, channels)
    flat = control.reshape(size, channels)

    def spec(count, dtype=F32, width=channels):
        return jax.ShapeDtypeStruct((count, width), dtype)

    def scratch(count, dtype=F32, width=channels):
        return pltpu.VMEM((count, width), dtype)

    mate_of = [(i, i ^ 1) for i in range(tiles)]
    other_of = [(i, (i - 1) % tiles if i % 2 == 0 else (i + 1) % tiles) for i in range(tiles)]

    def across(block, shift, route):
        pairs = [
            (((s + shift) % slots) * tiles + i, s * tiles + j)
            for s in range(slots)
            for i, j in route
        ]
        return lax.ppermute(block, ("slot", "tile"), pairs)

    straight = [(i, i) for i in range(tiles)]
    nxt = across(flat, 1, straight)
    prv = nxt if slots == 2 else across(flat, -1, straight)
    held, near_mate = kernel_call(near_kernel, [spec(size), spec(groups * 4)], [], 1000, 300000)(flat)
    mate = lax.ppermute(near_mate, "tile", mate_of)
    packed = kernel_call(
        pack_kernel,
        spec(tiles * CHUNK, BF16, LANES),
        [
            pltpu.VMEM((1, steps * rows), jnp.int32),
            scratch(META, F32, steps * rows),
            scratch(tiles * CHUNK, F32, LANES),
        ],
        10**7,
        200000,
    )(
        jnp.transpose(report_owner[0], (0, 2, 1)),
        jnp.transpose(report_stencil[0], (0, 2, 1)),
        jnp.transpose(report_weights[0], (0, 2, 1)),
        report_precision[0],
        report_values[0].reshape(steps * rows, LANES),
    )
    sent = kernel_call(
        tile_kernel, spec(groups * (cols + 2), BF16), [scratch(groups * 2)], 1000, 400000
    )(held, mate)
    oth = lax.ppermute(sent, "tile", other_of)
    packed = kernel_call(after_kernel, spec(tiles * CHUNK, BF16, LANES), [], 1000, 200000)(packed, sent)
    arrived = lax.all_to_all(packed, "tile", split_axis=0, concat_axis=0, tiled=True)

    wide = groups * WIDE
    slim = groups * SLIM
    edge0, u1x, d0x, d1x, f2x, field = kernel_call(
        forward_kernel,
        [spec(groups * 8), spec(slim)] + [spec(slim, BF16)] * 3 + [spec(4 * lats * cols, F32, members * LANES)],
        [scratch(wide), scratch(wide), scratch(wide, BF16), scratch(wide, BF16), scratch(wide, BF16)]
        + [scratch(wide), scratch(16), scratch(4 * size, BF16)],
        12 * wide * channels * channels,
        4000000,
    )(held, mate, oth, self_weight, neighbour_weight, output_weight, gain, readout)
    relayed = kernel_call(
        relay_kernel,
        spec(groups * 2, BF16),
        [scratch(groups * 2), scratch(size)],
        1000,
        300000,
    )(oth)
    nxt_far = across(relayed, 1, straight)

    def near_two(block):
        out = kernel_call(near_two_kernel, spec(groups * 2), [], 1000, 300000)(block)
        return lax.ppermute(out, "tile", mate_of)

    nxt_near = near_two(nxt)
    if slots == 2:
        prv_far, prv_near = nxt_far, nxt_near
    else:
        prv_far, prv_near = across(relayed, -1, straight), near_two(prv)
    total = -(-tiles // SENDERS) * LANES
    pull1, pull2, message = kernel_call(
        functools.partial(observe_kernel, tiles),
        [spec(slim), spec(slim), spec(size, F32, LANES)],
        [scratch(128, BF16, total)] * 4
        + [scratch(total, F32, LANES), scratch(4 * size, BF16, LANES), scratch(tiles * CHUNK, F32, LANES)],
        10**9,
        2000000,
    )(arrived, field, readout)
    from_mate = lax.ppermute(message, "tile", mate_of)
    misfit = kernel_call(
        previous_kernel,
        spec(size),
        [scratch(slim), scratch(slim), scratch(slim, BF16), scratch(slim, BF16), scratch(slim, BF16)]
        + [scratch(slim), scratch(16), scratch(groups * 2)],
        12 * slim * channels * channels,
        4000000,
    )(
        flat, prv, prv_near, prv_far, background.reshape(size, channels),
        self_weight, neighbour_weight, output_weight, gain, error,
    )
    result = kernel_call(
        backward_kernel,
        spec(size),
        [scratch(slim), scratch(slim), scratch(slim), scratch(slim, BF16), scratch(slim), scratch(slim)]
        + [scratch(size), scratch(16), scratch(groups * 2), scratch(slim), scratch(slim)],
        12 * slim * channels * channels,
        6000000,
    )(
        flat, edge0, u1x, d0x, d1x, f2x, pull1, pull2, from_mate,
        nxt, nxt_near, nxt_far, misfit,
        self_weight, neighbour_weight, output_weight, gain, error, readout,
    )
    return result.reshape(control.shape)


def solution(mesh):
    in_specs = (
        P("slot", None, None, "tile", None),
        P(None, None, "tile", None),
        P(),
        P(),
        P(),
        P(),
        P(),
        P(),
        P("slot", None, "tile", None),
        P("slot", None, "tile", None),
        P("slot", None, "tile", None),
        P("slot", None, "tile", None),
        P("slot", None, "tile"),
    )
    out_specs = P("slot", None, None, "tile", None)
    return jax.shard_map(
        per_device, mesh=mesh, in_specs=in_specs, out_specs=out_specs, check_vma=False
    )
```

```python
import functools
import jax
import jax.numpy as jnp
from jax import lax
from jax.experimental import pallas as pl
from jax.experimental.pallas import tpu as pltpu
from jax.sharding import PartitionSpec as P

EPSILON = 1e-06
F32 = jnp.float32
BF16 = jnp.bfloat16
LANES = 128
CAP = 5
SLOTS = 4 * CAP
CHUNK = 32
META = 16
SENDERS = LANES // SLOTS
WIDE = 40
SLIM = 24
VMEM_LIMIT = 28 * 1024 * 1024


def dot(a, b):
    return jnp.dot(a, b, preferred_element_type=F32)


def dot_t(a, b):
    return lax.dot_general(a, b, (((1,), (1,)), ((), ())), preferred_element_type=F32)


def sublane(shape):
    return lax.broadcasted_iota(jnp.int32, shape, 0)


def inverse_rms(x):
    return lax.rsqrt(jnp.mean(x * x, axis=-1, keepdims=True) + EPSILON)


def sigmoid(p):
    return 0.5 * jnp.tanh(0.5 * p) + 0.5


def neighbours(rows):
    width = rows[0].shape[0]
    return [
        0.25 * (rows[1 - i] + pltpu.roll(rows[i], 1, 0) + pltpu.roll(rows[i], width - 1, 0))
        for i in range(2)
    ]


def forward_step(u, n, mean, act, pre, d, gain, ws, wn, wo, width, members, out, fetch=None):
    both = 2 * width
    for m in range(members):
        base = m * both
        rows = []
        for lat in range(2):
            x = u[base + lat * width : base + (lat + 1) * width]
            rows.append((x * inverse_rms(x) * gain).astype(BF16).astype(F32))
        n[base : base + both] = jnp.concatenate(rows, axis=0).astype(BF16)
        mean[base : base + both] = jnp.concatenate(neighbours(rows), axis=0).astype(BF16)
    pre[...] = dot(n[...], ws[...]) + dot(mean[...], wn[...])
    for m in range(members):
        base = m * both
        p = pre[base : base + both]
        sig = sigmoid(p)
        act[base : base + both] = (p * sig).astype(BF16)
        if d is not None:
            pre[base : base + both] = sig * (1.0 + p * (1.0 - sig))
    if d is not None:
        for m in range(members):
            slim_copy(d, pre, m)
    if fetch is not None:
        fetch.wait()
    pre[...] = dot(act[...], wo[...])
    for r in range(2 * members):
        out(r, u[r * width : (r + 1) * width] + pre[r * width : (r + 1) * width])


def slim_edge(wide, r):
    low = wide[r * WIDE + 16 : r * WIDE + 24]
    high = wide[r * WIDE + 32 : r * WIDE + 40]
    return jnp.where(sublane(low.shape) < 4, low, high)


def slim_copy(to, wide, m):
    parts = []
    for r in (2 * m, 2 * m + 1):
        parts += [wide[r * WIDE : r * WIDE + 16], slim_edge(wide, r)]
    both = jnp.concatenate(parts, axis=0)
    to[m * 2 * SLIM : (m + 1) * 2 * SLIM] = both.astype(to.dtype)


def first_kernel(
    control_hbm, owner_hbm, stencil_hbm, weights_hbm, precision_hbm, values_hbm,
    held, near, out,
    owner, stencil, weights, precision, values, key, meta, picked, sems,
):
    pairs = (
        (owner_hbm, owner), (stencil_hbm, stencil), (weights_hbm, weights),
        (precision_hbm, precision), (values_hbm, values), (control_hbm, held),
    )
    copies = [pltpu.make_async_copy(source, to, sems.at[i]) for i, (source, to) in enumerate(pairs)]
    for copy in copies:
        copy.start()
    for copy in copies[:-1]:
        copy.wait()
    pack(owner, stencil, weights, precision, values, out, key, meta, picked)
    copies[-1].wait()
    even = lax.rem(lax.axis_index("tile"), 2) == 0
    for r in range(held.shape[0] // 16):
        near[r * 4 : (r + 1) * 4] = jnp.where(
            even, held[r * 16 + 12 : (r + 1) * 16], held[r * 16 : r * 16 + 4]
        )


def pack(owner, stencil, weights, precision, values, out, key, meta, picked):
    steps, _, rows = owner.shape
    tiles = out.shape[0] // CHUNK
    total = steps * rows
    place = lax.axis_index("tile") % SENDERS * SLOTS
    earlier = lax.broadcasted_iota(jnp.int32, (rows, rows), 0) < lax.broadcasted_iota(jnp.int32, (rows, rows), 1)
    earlier = earlier.astype(F32).astype(BF16)
    meta[...] = jnp.zeros_like(meta)
    for k in range(steps):
        at = slice(k * rows, (k + 1) * rows)
        named = lax.broadcasted_iota(jnp.int32, (tiles, rows), 0) == owner[k]
        hits = named.astype(F32)
        before = dot(hits.astype(BF16), earlier)
        rank = jnp.sum(hits * before, axis=0, keepdims=True).astype(jnp.int32)
        key[0:1, at] = owner[k] * (2 * CAP) + k * CAP + rank
        meta[4:8, at] = stencil[k].astype(F32)
        meta[8:12, at] = weights[k].astype(F32)
        meta[12:13, at] = precision[k : k + 1].astype(F32)
    row = lax.broadcasted_iota(jnp.int32, (tiles * CHUNK, total), 0)
    tile = row // CHUNK
    slot = row % CHUNK
    other = jnp.where(tile % 2 == 0, (tile + tiles - 1) % tiles, (tile + 1) % tiles)
    mine = slot < 2 * CAP
    wanted = jnp.where(mine, tile * (2 * CAP) + slot, other * (2 * CAP) + slot - 2 * CAP)
    wanted = jnp.where(slot < SLOTS, wanted, -1)
    placement = (wanted == key[...]).astype(F32).astype(BF16)
    picked[...] = dot(placement, values[...])
    entries = dot_t(meta[...].astype(BF16), placement)
    lane = lax.broadcasted_iota(jnp.int32, (META, LANES), 1)
    used = jnp.logical_and(lane >= place, lane < place + SLOTS)
    per_tile = LANES // CHUNK
    for t in range(tiles):
        block = entries[:, t // per_tile * LANES : (t // per_tile + 1) * LANES]
        shift = (place + LANES - t % per_tile * CHUNK) % LANES
        block = jnp.where(used, pltpu.roll(block, shift, 1), 0.0)
        low = picked[t * CHUNK + 16 : (t + 1) * CHUNK]
        picked[t * CHUNK + 16 : (t + 1) * CHUNK] = jnp.where(sublane((META, 1)) < 4, low, block)
    out[...] = picked[...].astype(BF16)


def near_two_kernel(control, out):
    even = lax.rem(lax.axis_index("tile"), 2) == 0
    for r in range(control.shape[0] // 16):
        out[r * 2 : (r + 1) * 2] = jnp.where(
            even, control[r * 16 + 14 : (r + 1) * 16], control[r * 16 : r * 16 + 2]
        )


def tile_kernel(control, mate, out, held):
    even = lax.rem(lax.axis_index("tile"), 2) == 0
    size = control.shape[0]
    out[0:size] = control[...].astype(BF16)
    for r in range(size // 16):
        held[r * 2 : (r + 1) * 2] = jnp.where(even, mate[r * 4 : r * 4 + 2], mate[r * 4 + 2 : (r + 1) * 4])
    out[size:] = held[...].astype(BF16)


def after_kernel(packed, out):
    out[...] = packed[...]


def forward_kernel(
    wo_hbm, control, mate, oth, ws, wn, gain, readout,
    edge0, u1x, d0x, d1x, f2x, field, relayed,
    ua, ub, n, mean, act, pre, edge, states, held, wo, sem,
):
    fetch = pltpu.make_async_copy(wo_hbm, wo, sem)
    fetch.start()
    members = control.shape[0] // 32
    even = lax.rem(lax.axis_index("tile"), 2) == 0
    tile_at = jnp.where(even, 24, 16)
    edge_at = jnp.where(even, 16, 32)
    far = oth[members * 32 :].astype(F32)
    for r in range(2 * members):
        ua[r * WIDE : r * WIDE + 16] = control[r * 16 : (r + 1) * 16]
        ua[pl.ds(pl.multiple_of(r * WIDE + tile_at, 8), 16)] = oth[r * 16 : (r + 1) * 16].astype(F32)
        near4 = mate[r * 4 : (r + 1) * 4]
        far2 = far[r * 2 : (r + 1) * 2]
        edge[...] = jnp.zeros_like(edge)
        edge[0:4] = near4
        edge[6:8] = far2
        edge[8:10] = far2
        edge[12:16] = near4
        ua[pl.ds(pl.multiple_of(r * WIDE + edge_at, 8), 8)] = jnp.where(even, edge[0:8], edge[8:16])
    for r in range(2 * members):
        edge0[r * 8 : (r + 1) * 8] = slim_edge(ua, r)
        taken = ua[pl.ds(pl.multiple_of(r * WIDE + tile_at, 8), 16)]
        held[r * 2 : (r + 1) * 2] = jnp.where(even, taken[14:16], taken[0:2])
    relayed[...] = held[...].astype(BF16)
    g = gain[...]

    def keep(ref):
        def store(r, value):
            ref[r * WIDE : (r + 1) * WIDE] = value

        return store

    def keep_states(ref, k):
        own = k * members * 32
        away = (2 + k) * members * 32
        for r in range(2 * members):
            states[own + r * 16 : own + (r + 1) * 16] = ref[r * WIDE : r * WIDE + 16].astype(BF16)
            taken = ref[pl.ds(pl.multiple_of(r * WIDE + tile_at, 8), 16)]
            states[away + r * 16 : away + (r + 1) * 16] = taken.astype(BF16)

    forward_step(ua, n, mean, act, pre, d0x, g, ws, wn, wo, WIDE, members, keep(ub), fetch)
    for m in range(members):
        slim_copy(u1x, ub, m)
    keep_states(ub, 0)
    forward_step(ub, n, mean, act, pre, d1x, g, ws, wn, wo, WIDE, members, keep(ua))
    for m in range(members):
        slim_copy(f2x, ua, m)
    keep_states(ua, 1)
    read = dot(states[...], readout[...])
    for q in range(4):
        for m in range(members):
            start = (q * members + m) * 32
            field[q * 32 : (q + 1) * 32, m * LANES : (m + 1) * LANES] = read[start : start + 32]


def split(x):
    high = x.astype(BF16)
    return high, (x - high.astype(F32)).astype(BF16)


def observe_kernel(
    tiles, arrived, field, readout,
    pull1, pull2, message,
    th, tl, ph, plo, vals, spread, wide,
):
    steps = 2
    members = field.shape[1] // LANES
    even = lax.rem(lax.axis_index("tile"), 2) == 0
    cells = sublane((32, LANES)).astype(F32)
    lane = lax.broadcasted_iota(jnp.int32, (1, LANES), 1)
    table_of = jnp.where(lane < SENDERS * SLOTS, lane % SLOTS // CAP, -1)
    wide[...] = arrived[...].astype(F32)
    vals[...] = jnp.zeros_like(vals)
    for p in range(th.shape[1] // LANES):
        meta = jnp.zeros((META, LANES), F32)
        for d in range(p * SENDERS, min((p + 1) * SENDERS, tiles)):
            meta += wide[d * CHUNK + 16 : (d + 1) * CHUNK]
            start = p * LANES + d % SENDERS * SLOTS
            vals[start : start + SLOTS] = wide[d * CHUNK : d * CHUNK + SLOTS]
        weight = jnp.zeros((32, LANES), F32)
        for i in range(4):
            weight += jnp.where(cells == meta[4 + i : 5 + i], meta[8 + i : 9 + i], 0.0)
        scaled = weight * meta[12:13]
        wh, wl = split(weight)
        sh, sl = split(scaled)
        parts = ((th, wh.astype(F32)), (tl, wl.astype(F32)), (ph, sh.astype(F32)), (plo, sl.astype(F32)))
        for q in range(2 * steps):
            hit = table_of == q
            for ref, value in parts:
                kept = jnp.where(hit, value, 0.0).astype(BF16)
                ref[q * 32 : (q + 1) * 32, p * LANES : (p + 1) * LANES] = kept
    cross = dot_t(ph[...], th[...]) + dot_t(plo[...], th[...]) + dot_t(ph[...], tl[...])
    taken = vals[...].astype(BF16)
    target = dot(ph[...], taken) + dot(plo[...], taken)
    ch, cl = split(cross)
    fh, fl = split(field[...])
    mixed = dot(ch, fh) + dot(cl, fh) + dot(ch, fl)
    for q in range(2 * steps):
        for m in range(members):
            start = (q * members + m) * 32
            value = mixed[q * 32 : (q + 1) * 32, m * LANES : (m + 1) * LANES] - target[q * 32 : (q + 1) * 32]
            spread[start : start + 32] = value.astype(BF16)
    pulled = dot_t(spread[...], readout[...])
    size = members * 32
    row8 = sublane((8, 1))
    for k, out in enumerate((pull1, pull2)):
        own = k * size
        away = (2 + k) * size
        for r in range(2 * members):
            out[r * SLIM : r * SLIM + 16] = pulled[own + r * 16 : own + (r + 1) * 16]
            low = pulled[away + r * 16 : away + r * 16 + 8]
            high = pulled[away + r * 16 + 8 : away + r * 16 + 16]
            group = jnp.where(
                even, jnp.where(row8 >= 4, high, 0.0), jnp.where(row8 < 4, low, 0.0)
            )
            out[r * SLIM + 16 : r * SLIM + 24] = group
        for r in range(2 * members):
            pair = spread[own + r * 16 : own + (r + 1) * 16].astype(F32)
            near = jnp.where(even, pair[8:16], pair[0:8])
            message[k * size // 2 + r * 8 : k * size // 2 + (r + 1) * 8] = near


def adjoint_step(u, cot, gb, gm, flat, d, add, out, gain, ws, wn, wo, members):
    both = 2 * SLIM
    gb[...] = cot[...].astype(BF16)
    flat[...] = dot_t(gb[...], wo[...])
    gb[...] = (flat[...] * d[...]).astype(BF16)
    gm[...] = dot_t(gb[...], wn[...])
    flat[...] = dot_t(gb[...], ws[...])
    for m in range(members):
        base = m * both
        rows = []
        for lat in range(2):
            start = base + lat * SLIM
            rows.append(gm[start : start + SLIM].astype(BF16).astype(F32))
        around = neighbours(rows)
        for lat in range(2):
            start = base + lat * SLIM
            x = u[start : start + SLIM]
            s = inverse_rms(x)
            scaled = gain * (flat[start : start + SLIM] + around[lat])
            inner = jnp.mean(x * scaled, axis=-1, keepdims=True)
            value = cot[start : start + SLIM] + s * scaled - x * (s * s * s * inner)
            if add is not None:
                value = value + add[start : start + SLIM]
            out[start : start + SLIM] = value


def edges(near, far, edge, r):
    even = lax.rem(lax.axis_index("tile"), 2) == 0
    near = near[r * 2 : (r + 1) * 2].astype(F32)
    far = far[r * 2 : (r + 1) * 2].astype(F32)
    edge[...] = jnp.zeros_like(edge)
    edge[0:2] = near
    edge[6:8] = far
    edge[8:10] = far
    edge[14:16] = near
    return jnp.where(even, edge[0:8], edge[8:16])


def previous_kernel(
    control_hbm, background_hbm, prv, prv_near, prv_far, ws, wn, wo, gain, error,
    misfit,
    ua, ub, n, mean, act, pre, edge, far, control, background, sems,
):
    copies = [
        pltpu.make_async_copy(control_hbm, control, sems.at[0]),
        pltpu.make_async_copy(background_hbm, background, sems.at[1]),
    ]
    for copy in copies:
        copy.start()
    members = control.shape[0] // 32
    slot = lax.axis_index("slot")
    far[...] = prv_far[...].astype(F32)
    for r in range(2 * members):
        a, b = r * SLIM, r * SLIM + 16
        ua[a:b] = prv[r * 16 : (r + 1) * 16]
        ua[b : b + 8] = edges(prv_near, far, edge, r)

    def keep(r, value):
        ub[r * SLIM : (r + 1) * SLIM] = value

    def finish(r, value):
        arrived = value[0:16].astype(BF16).astype(F32)
        before = jnp.where(slot == 0, background[r * 16 : (r + 1) * 16].astype(F32), arrived)
        misfit[r * 16 : (r + 1) * 16] = error[...] * (control[r * 16 : (r + 1) * 16] - before)

    forward_step(ua, n, mean, act, pre, None, gain[...], ws, wn, wo, SLIM, members, keep)
    for copy in copies:
        copy.wait()
    forward_step(ub, n, mean, act, pre, None, gain[...], ws, wn, wo, SLIM, members, finish)


def backward_kernel(
    control_hbm, edge0, u1x, d0x, d1x, f2x, pull1, pull2, message,
    nxt, nxt_near, nxt_far, misfit, ws, wn, wo, gain, error, readout,
    result,
    cot, cot2, extra, gb, gm, flat, mate_pull, edge, far, u0x, final, control, sem,
):
    fetch = pltpu.make_async_copy(control_hbm, control, sem)
    fetch.start()
    size = nxt.shape[0]
    members = size // 32
    even = lax.rem(lax.axis_index("tile"), 2) == 0
    slot = lax.axis_index("slot")
    later = jnp.where(slot == lax.axis_size("slot") - 1, 0.0, 1.0)
    gain = gain[...]
    weight = later * error[...]
    row8 = sublane((8, 1))
    mate_pull[...] = dot_t(message[...].astype(BF16), readout[...])
    mate_side = jnp.where(even, 1, 0) == jnp.where(row8 < 4, 1, 0)
    far[...] = nxt_far[...].astype(F32)
    final[...] = f2x[...].astype(F32)
    for r in range(2 * members):
        a, b = r * SLIM, r * SLIM + 16
        cot[a:b] = pull2[a:b] - weight * (nxt[r * 16 : (r + 1) * 16] - final[a:b])
        c, e = b, b + 8
        start = size // 2 + r * 8
        pulled = pull2[c:e] + jnp.where(mate_side, mate_pull[start : start + 8], 0.0)
        cot[c:e] = pulled - weight * (edges(nxt_near, far, edge, r) - final[c:e])
        extra[a:b] = pull1[a:b]
        extra[c:e] = pull1[c:e] + jnp.where(mate_side, mate_pull[r * 8 : (r + 1) * 8], 0.0)
    adjoint_step(u1x, cot, gb, gm, flat, d1x, extra, cot2, gain, ws, wn, wo, members)
    fetch.wait()
    for r in range(2 * members):
        u0x[r * SLIM : r * SLIM + 16] = control[r * 16 : (r + 1) * 16]
        u0x[r * SLIM + 16 : (r + 1) * SLIM] = edge0[r * 8 : (r + 1) * 8]
    adjoint_step(u0x, cot2, gb, gm, flat, d0x, None, cot, gain, ws, wn, wo, members)
    for r in range(2 * members):
        result[r * 16 : (r + 1) * 16] = cot[r * SLIM : r * SLIM + 16] + misfit[r * 16 : (r + 1) * 16]


def kernel_call(body, outs, scratch, flops, moved, hbm=0):
    def call(*operands):
        operands = [pltpu.with_memory_space_constraint(x, pltpu.HBM) for x in operands[:hbm]] + list(operands[hbm:])
        places = [pltpu.HBM] * hbm + [pltpu.VMEM] * (len(operands) - hbm)
        return pl.pallas_call(
            body,
            out_shape=outs,
            in_specs=[pl.BlockSpec(memory_space=place) for place in places],
            scratch_shapes=scratch,
            compiler_params=pltpu.CompilerParams(vmem_limit_bytes=VMEM_LIMIT),
            cost_estimate=pl.CostEstimate(flops=flops, bytes_accessed=moved, transcendentals=0),
        )(*operands)

    return call


def per_device(
    control,
    background,
    self_weight,
    neighbour_weight,
    output_weight,
    norm_gain,
    readout,
    error_weight,
    report_owner,
    report_stencil,
    report_weights,
    report_values,
    report_precision,
):
    tiles = lax.axis_size("tile")
    slots = lax.axis_size("slot")
    members, lats, cols, channels = control.shape[1:]
    groups = members * lats
    size = groups * cols
    steps = report_owner.shape[1]
    rows = report_owner.shape[2]
    gain = norm_gain.reshape(1, channels)
    error = error_weight.reshape(1, channels)
    flat = control.reshape(size, channels)

    def spec(count, dtype=F32, width=channels):
        return jax.ShapeDtypeStruct((count, width), dtype)

    def scratch(count, dtype=F32, width=channels):
        return pltpu.VMEM((count, width), dtype)

    mate_of = [(i, i ^ 1) for i in range(tiles)]
    other_of = [(i, (i - 1) % tiles if i % 2 == 0 else (i + 1) % tiles) for i in range(tiles)]

    def across(block, shift, route):
        pairs = [
            (((s + shift) % slots) * tiles + i, s * tiles + j)
            for s in range(slots)
            for i, j in route
        ]
        return lax.ppermute(block, ("slot", "tile"), pairs)

    straight = [(i, i) for i in range(tiles)]
    nxt = across(flat, 1, straight)
    prv = nxt if slots == 2 else across(flat, -1, straight)
    held, near_mate, packed = kernel_call(
        first_kernel,
        [spec(size), spec(groups * 4), spec(tiles * CHUNK, BF16, LANES)],
        [
            pltpu.VMEM((steps, 1, rows), jnp.int32),
            pltpu.VMEM((steps, 4, rows), jnp.int32),
            pltpu.VMEM((steps, 4, rows), BF16),
            pltpu.VMEM((steps, rows), BF16),
            scratch(steps * rows, BF16, LANES),
            pltpu.VMEM((1, steps * rows), jnp.int32),
            scratch(META, F32, steps * rows),
            scratch(tiles * CHUNK, F32, LANES),
            pltpu.SemaphoreType.DMA((6,)),
        ],
        10**7,
        200000,
        hbm=6,
    )(
        flat,
        jnp.transpose(report_owner[0], (0, 2, 1)),
        jnp.transpose(report_stencil[0], (0, 2, 1)),
        jnp.transpose(report_weights[0], (0, 2, 1)),
        report_precision[0],
        report_values[0].reshape(steps * rows, LANES),
    )
    mate = lax.ppermute(near_mate, "tile", mate_of)
    sent = kernel_call(
        tile_kernel, spec(groups * (cols + 2), BF16), [scratch(groups * 2)], 1000, 400000
    )(held, mate)
    oth = lax.ppermute(sent, "tile", other_of)
    packed = kernel_call(after_kernel, spec(tiles * CHUNK, BF16, LANES), [], 1000, 200000)(packed)
    arrived = lax.all_to_all(packed, "tile", split_axis=0, concat_axis=0, tiled=True)

    wide = groups * WIDE
    slim = groups * SLIM
    edge0, u1x, d0x, d1x, f2x, field, relayed = kernel_call(
        forward_kernel,
        [spec(groups * 8), spec(slim)] + [spec(slim, BF16)] * 3
        + [spec(4 * lats * cols, F32, members * LANES), spec(groups * 2, BF16)],
        [scratch(wide), scratch(wide), scratch(wide, BF16), scratch(wide, BF16), scratch(wide, BF16)]
        + [scratch(wide), scratch(16), scratch(4 * size, BF16), scratch(groups * 2)]
        + [scratch(channels, BF16), pltpu.SemaphoreType.DMA],
        10**11,
        4000000,
        hbm=1,
    )(output_weight, held, mate, oth, self_weight, neighbour_weight, gain, readout)
    nxt_far = across(relayed, 1, straight)

    def near_two(block):
        out = kernel_call(near_two_kernel, spec(groups * 2), [], 1000, 300000)(block)
        return lax.ppermute(out, "tile", mate_of)

    nxt_near = near_two(nxt)
    if slots == 2:
        prv_far, prv_near = nxt_far, nxt_near
    else:
        prv_far, prv_near = across(relayed, -1, straight), near_two(prv)
    total = -(-tiles // SENDERS) * LANES
    pull1, pull2, message = kernel_call(
        functools.partial(observe_kernel, tiles),
        [spec(slim), spec(slim), spec(size, F32, LANES)],
        [scratch(128, BF16, total)] * 4
        + [scratch(total, F32, LANES), scratch(4 * size, BF16, LANES), scratch(tiles * CHUNK, F32, LANES)],
        10**9,
        2000000,
    )(arrived, field, readout)
    from_mate = lax.ppermute(message, "tile", mate_of)
    misfit = kernel_call(
        previous_kernel,
        spec(size),
        [scratch(slim), scratch(slim), scratch(slim, BF16), scratch(slim, BF16), scratch(slim, BF16)]
        + [scratch(slim), scratch(16), scratch(groups * 2), scratch(size), scratch(size, BF16)]
        + [pltpu.SemaphoreType.DMA((2,))],
        12 * slim * channels * channels,
        4000000,
        hbm=2,
    )(
        flat, background.reshape(size, channels), prv, prv_near, prv_far,
        self_weight, neighbour_weight, output_weight, gain, error,
    )
    result = kernel_call(
        backward_kernel,
        spec(size),
        [scratch(slim), scratch(slim), scratch(slim), scratch(slim, BF16), scratch(slim), scratch(slim)]
        + [scratch(size), scratch(16), scratch(groups * 2), scratch(slim), scratch(slim), scratch(size)]
        + [pltpu.SemaphoreType.DMA],
        12 * slim * channels * channels,
        6000000,
        hbm=1,
    )(
        flat, edge0, u1x, d0x, d1x, f2x, pull1, pull2, from_mate,
        nxt, nxt_near, nxt_far, misfit,
        self_weight, neighbour_weight, output_weight, gain, error, readout,
    )
    return result.reshape(control.shape)


def solution(mesh):
    in_specs = (
        P("slot", None, None, "tile", None),
        P(None, None, "tile", None),
        P(),
        P(),
        P(),
        P(),
        P(),
        P(),
        P("slot", None, "tile", None),
        P("slot", None, "tile", None),
        P("slot", None, "tile", None),
        P("slot", None, "tile", None),
        P("slot", None, "tile"),
    )
    out_specs = P("slot", None, None, "tile", None)
    return jax.shard_map(
        per_device, mesh=mesh, in_specs=in_specs, out_specs=out_specs, check_vma=False
    )
```

```python
import functools
import jax
import jax.numpy as jnp
from jax import lax
from jax.experimental import pallas as pl
from jax.experimental.pallas import tpu as pltpu
from jax.sharding import PartitionSpec as P

EPSILON = 1e-06
F32 = jnp.float32
BF16 = jnp.bfloat16
LANES = 128
CAP = 5
SLOTS = 4 * CAP
CHUNK = 32
META = 16
SENDERS = LANES // SLOTS
WIDE = 40
SLIM = 24
VMEM_LIMIT = 28 * 1024 * 1024


def dot(a, b):
    return jnp.dot(a, b, preferred_element_type=F32)


def dot_t(a, b):
    return lax.dot_general(a, b, (((1,), (1,)), ((), ())), preferred_element_type=F32)


def sublane(shape):
    return lax.broadcasted_iota(jnp.int32, shape, 0)


def inverse_rms(x):
    return lax.rsqrt(jnp.mean(x * x, axis=-1, keepdims=True) + EPSILON)


def sigmoid(p):
    return 0.5 * jnp.tanh(0.5 * p) + 0.5


def neighbours(rows):
    width = rows[0].shape[0]
    return [
        0.25 * (rows[1 - i] + pltpu.roll(rows[i], 1, 0) + pltpu.roll(rows[i], width - 1, 0))
        for i in range(2)
    ]


def forward_step(u, n, mean, act, pre, d, gain, ws, wn, wo, width, members, out, fetch=None):
    both = 2 * width
    for m in range(members):
        base = m * both
        rows = []
        for lat in range(2):
            x = u[base + lat * width : base + (lat + 1) * width]
            rows.append((x * inverse_rms(x) * gain).astype(BF16).astype(F32))
        n[base : base + both] = jnp.concatenate(rows, axis=0).astype(BF16)
        mean[base : base + both] = jnp.concatenate(neighbours(rows), axis=0).astype(BF16)
    pre[...] = dot(n[...], ws[...]) + dot(mean[...], wn[...])
    for m in range(members):
        base = m * both
        p = pre[base : base + both]
        sig = sigmoid(p)
        act[base : base + both] = (p * sig).astype(BF16)
        if d is not None:
            pre[base : base + both] = sig * (1.0 + p * (1.0 - sig))
    if d is not None:
        for m in range(members):
            slim_copy(d, pre, m)
    if fetch is not None:
        fetch.wait()
    pre[...] = dot(act[...], wo[...])
    for r in range(2 * members):
        out(r, u[r * width : (r + 1) * width] + pre[r * width : (r + 1) * width])


def slim_edge(wide, r):
    low = wide[r * WIDE + 16 : r * WIDE + 24]
    high = wide[r * WIDE + 32 : r * WIDE + 40]
    return jnp.where(sublane(low.shape) < 4, low, high)


def slim_copy(to, wide, m):
    parts = []
    for r in (2 * m, 2 * m + 1):
        parts += [wide[r * WIDE : r * WIDE + 16], slim_edge(wide, r)]
    both = jnp.concatenate(parts, axis=0)
    to[m * 2 * SLIM : (m + 1) * 2 * SLIM] = both.astype(to.dtype)


def first_kernel(
    control_hbm, owner_hbm, stencil_hbm, weights_hbm, precision_hbm, values_hbm,
    held, out_hbm,
    owner, stencil, weights, precision, values, key, meta, picked, out, sems,
):
    pairs = (
        (owner_hbm, owner), (stencil_hbm, stencil), (weights_hbm, weights),
        (precision_hbm, precision), (values_hbm, values), (control_hbm, held),
    )
    copies = [pltpu.make_async_copy(source, to, sems.at[i]) for i, (source, to) in enumerate(pairs)]
    for copy in copies:
        copy.start()
    for copy in copies[:-1]:
        copy.wait()
    pack(owner, stencil, weights, precision, values, out, key, meta, picked)
    store = pltpu.make_async_copy(out, out_hbm, sems.at[len(pairs)])
    store.start()
    copies[-1].wait()
    store.wait()


def pack(owner, stencil, weights, precision, values, out, key, meta, picked):
    steps, _, rows = owner.shape
    tiles = out.shape[0] // CHUNK
    total = steps * rows
    place = lax.axis_index("tile") % SENDERS * SLOTS
    earlier = lax.broadcasted_iota(jnp.int32, (rows, rows), 0) < lax.broadcasted_iota(jnp.int32, (rows, rows), 1)
    earlier = earlier.astype(F32).astype(BF16)
    meta[...] = jnp.zeros_like(meta)
    for k in range(steps):
        at = slice(k * rows, (k + 1) * rows)
        named = lax.broadcasted_iota(jnp.int32, (tiles, rows), 0) == owner[k]
        hits = named.astype(F32)
        before = dot(hits.astype(BF16), earlier)
        rank = jnp.sum(hits * before, axis=0, keepdims=True).astype(jnp.int32)
        key[0:1, at] = owner[k] * (2 * CAP) + k * CAP + rank
        meta[4:8, at] = stencil[k].astype(F32)
        meta[8:12, at] = weights[k].astype(F32)
        meta[12:13, at] = precision[k : k + 1].astype(F32)
    row = lax.broadcasted_iota(jnp.int32, (tiles * CHUNK, total), 0)
    tile = row // CHUNK
    slot = row % CHUNK
    other = jnp.where(tile % 2 == 0, (tile + tiles - 1) % tiles, (tile + 1) % tiles)
    mine = slot < 2 * CAP
    wanted = jnp.where(mine, tile * (2 * CAP) + slot, other * (2 * CAP) + slot - 2 * CAP)
    wanted = jnp.where(slot < SLOTS, wanted, -1)
    placement = (wanted == key[...]).astype(F32).astype(BF16)
    picked[...] = dot(placement, values[...])
    entries = dot_t(meta[...].astype(BF16), placement)
    lane = lax.broadcasted_iota(jnp.int32, (META, LANES), 1)
    used = jnp.logical_and(lane >= place, lane < place + SLOTS)
    per_tile = LANES // CHUNK
    for t in range(tiles):
        block = entries[:, t // per_tile * LANES : (t // per_tile + 1) * LANES]
        shift = (place + LANES - t % per_tile * CHUNK) % LANES
        block = jnp.where(used, pltpu.roll(block, shift, 1), 0.0)
        low = picked[t * CHUNK + 16 : (t + 1) * CHUNK]
        picked[t * CHUNK + 16 : (t + 1) * CHUNK] = jnp.where(sublane((META, 1)) < 4, low, block)
    out[...] = picked[...].astype(BF16)


def tile_kernel(control, mate, out, held):
    even = lax.rem(lax.axis_index("tile"), 2) == 0
    size = control.shape[0]
    out[0:size] = control[...].astype(BF16)
    for r in range(size // 16):
        held[r * 2 : (r + 1) * 2] = jnp.where(
            even, mate[r * 16 : r * 16 + 2], mate[r * 16 + 14 : (r + 1) * 16]
        )
    out[size:] = held[...].astype(BF16)


def relay_kernel(control, mate, oth, out, wide):
    even = lax.rem(lax.axis_index("tile"), 2) == 0
    size = control.shape[0]
    edge = size // 8
    out[0:size] = control[...]
    wide[...] = oth[0:size].astype(F32)
    for r in range(size // 16):
        a, b = r * 16, (r + 1) * 16
        out[size + r * 2 : size + (r + 1) * 2] = jnp.where(even, wide[b - 2 : b], wide[a : a + 2])
        start = size + edge + r * 2
        out[start : start + 2] = jnp.where(even, mate[a : a + 2], mate[b - 2 : b])


def forward_kernel(
    wo_hbm, control, mate, oth, ws, wn, gain, readout,
    edge0, u1x, d0x, d1x, f2x, field, final,
    ua, ub, n, mean, act, pre, edge, states, wo, sem,
):
    fetch = pltpu.make_async_copy(wo_hbm, wo, sem)
    fetch.start()
    members = control.shape[0] // 32
    even = lax.rem(lax.axis_index("tile"), 2) == 0
    tile_at = jnp.where(even, 24, 16)
    edge_at = jnp.where(even, 16, 32)
    far = oth[members * 32 :].astype(F32)
    for r in range(2 * members):
        ua[r * WIDE : r * WIDE + 16] = control[r * 16 : (r + 1) * 16]
        ua[pl.ds(pl.multiple_of(r * WIDE + tile_at, 8), 16)] = oth[r * 16 : (r + 1) * 16].astype(F32)
        near4 = jnp.where(even, mate[r * 16 : r * 16 + 4], mate[r * 16 + 12 : (r + 1) * 16])
        far2 = far[r * 2 : (r + 1) * 2]
        edge[...] = jnp.zeros_like(edge)
        edge[0:4] = near4
        edge[6:8] = far2
        edge[8:10] = far2
        edge[12:16] = near4
        ua[pl.ds(pl.multiple_of(r * WIDE + edge_at, 8), 8)] = jnp.where(even, edge[0:8], edge[8:16])
    for r in range(2 * members):
        edge0[r * 8 : (r + 1) * 8] = slim_edge(ua, r)
    g = gain[...]

    def keep(ref):
        def store(r, value):
            ref[r * WIDE : (r + 1) * WIDE] = value

        return store

    def keep_states(ref, k):
        own = k * members * 32
        away = (2 + k) * members * 32
        for r in range(2 * members):
            states[own + r * 16 : own + (r + 1) * 16] = ref[r * WIDE : r * WIDE + 16].astype(BF16)
            taken = ref[pl.ds(pl.multiple_of(r * WIDE + tile_at, 8), 16)]
            states[away + r * 16 : away + (r + 1) * 16] = taken.astype(BF16)

    forward_step(ua, n, mean, act, pre, d0x, g, ws, wn, wo, WIDE, members, keep(ub), fetch)
    for m in range(members):
        slim_copy(u1x, ub, m)
    keep_states(ub, 0)
    forward_step(ub, n, mean, act, pre, d1x, g, ws, wn, wo, WIDE, members, keep(ua))
    for m in range(members):
        slim_copy(f2x, ua, m)
    keep_states(ua, 1)
    final[...] = states[members * 32 : 2 * members * 32]
    read = dot(states[...], readout[...])
    for q in range(4):
        for m in range(members):
            start = (q * members + m) * 32
            field[q * 32 : (q + 1) * 32, m * LANES : (m + 1) * LANES] = read[start : start + 32]


def split(x):
    high = x.astype(BF16)
    return high, (x - high.astype(F32)).astype(BF16)


def observe_kernel(
    tiles, arrived, field, readout,
    pull1, pull2, message,
    th, tl, ph, plo, vals, spread, wide,
):
    steps = 2
    members = field.shape[1] // LANES
    even = lax.rem(lax.axis_index("tile"), 2) == 0
    cells = sublane((32, LANES)).astype(F32)
    lane = lax.broadcasted_iota(jnp.int32, (1, LANES), 1)
    table_of = jnp.where(lane < SENDERS * SLOTS, lane % SLOTS // CAP, -1)
    wide[...] = arrived[...].astype(F32)
    vals[...] = jnp.zeros_like(vals)
    for p in range(th.shape[1] // LANES):
        meta = jnp.zeros((META, LANES), F32)
        for d in range(p * SENDERS, min((p + 1) * SENDERS, tiles)):
            meta += wide[d * CHUNK + 16 : (d + 1) * CHUNK]
            start = p * LANES + d % SENDERS * SLOTS
            vals[start : start + SLOTS] = wide[d * CHUNK : d * CHUNK + SLOTS]
        weight = jnp.zeros((32, LANES), F32)
        for i in range(4):
            weight += jnp.where(cells == meta[4 + i : 5 + i], meta[8 + i : 9 + i], 0.0)
        scaled = weight * meta[12:13]
        wh, wl = split(weight)
        sh, sl = split(scaled)
        parts = ((th, wh.astype(F32)), (tl, wl.astype(F32)), (ph, sh.astype(F32)), (plo, sl.astype(F32)))
        for q in range(2 * steps):
            hit = table_of == q
            for ref, value in parts:
                kept = jnp.where(hit, value, 0.0).astype(BF16)
                ref[q * 32 : (q + 1) * 32, p * LANES : (p + 1) * LANES] = kept
    cross = dot_t(ph[...], th[...]) + dot_t(plo[...], th[...]) + dot_t(ph[...], tl[...])
    taken = vals[...].astype(BF16)
    target = dot(ph[...], taken) + dot(plo[...], taken)
    ch, cl = split(cross)
    fh, fl = split(field[...])
    mixed = dot(ch, fh) + dot(cl, fh) + dot(ch, fl)
    for q in range(2 * steps):
        for m in range(members):
            start = (q * members + m) * 32
            value = mixed[q * 32 : (q + 1) * 32, m * LANES : (m + 1) * LANES] - target[q * 32 : (q + 1) * 32]
            spread[start : start + 32] = value.astype(BF16)
    pulled = dot_t(spread[...], readout[...])
    size = members * 32
    row8 = sublane((8, 1))
    for k, out in enumerate((pull1, pull2)):
        own = k * size
        away = (2 + k) * size
        for r in range(2 * members):
            out[r * SLIM : r * SLIM + 16] = pulled[own + r * 16 : own + (r + 1) * 16]
            low = pulled[away + r * 16 : away + r * 16 + 8]
            high = pulled[away + r * 16 + 8 : away + r * 16 + 16]
            group = jnp.where(
                even, jnp.where(row8 >= 4, high, 0.0), jnp.where(row8 < 4, low, 0.0)
            )
            out[r * SLIM + 16 : r * SLIM + 24] = group
        for r in range(2 * members):
            pair = spread[own + r * 16 : own + (r + 1) * 16].astype(F32)
            near = jnp.where(even, pair[8:16], pair[0:8])
            message[k * size // 2 + r * 8 : k * size // 2 + (r + 1) * 8] = near


def adjoint_step(u, cot, gb, gm, flat, d, add, out, gain, ws, wn, wo, members):
    both = 2 * SLIM
    gb[...] = cot[...].astype(BF16)
    flat[...] = dot_t(gb[...], wo[...])
    gb[...] = (flat[...] * d[...]).astype(BF16)
    gm[...] = dot_t(gb[...], wn[...])
    flat[...] = dot_t(gb[...], ws[...])
    for m in range(members):
        base = m * both
        rows = []
        for lat in range(2):
            start = base + lat * SLIM
            rows.append(gm[start : start + SLIM].astype(BF16).astype(F32))
        around = neighbours(rows)
        for lat in range(2):
            start = base + lat * SLIM
            x = u[start : start + SLIM]
            s = inverse_rms(x)
            scaled = gain * (flat[start : start + SLIM] + around[lat])
            inner = jnp.mean(x * scaled, axis=-1, keepdims=True)
            value = cot[start : start + SLIM] + s * scaled - x * (s * s * s * inner)
            if add is not None:
                value = value + add[start : start + SLIM]
            out[start : start + SLIM] = value


def edges(nxt, size, edge, r):
    even = lax.rem(lax.axis_index("tile"), 2) == 0
    start = size + r * 2
    far = nxt[start : start + 2]
    start = size + size // 8 + r * 2
    near = nxt[start : start + 2]
    edge[...] = jnp.zeros_like(edge)
    edge[0:2] = near
    edge[6:8] = far
    edge[8:10] = far
    edge[14:16] = near
    return jnp.where(even, edge[0:8], edge[8:16])


def backward_kernel(
    control_hbm, background_hbm, edge0, u1x, d0x, d1x, f2x, pull1, pull2, message,
    nxt, ws, wn, wo, gain, error, readout,
    result, background,
    cot, cot2, extra, gb, gm, flat, mate_pull, edge, u0x, final, control, sems,
):
    fetches = [
        pltpu.make_async_copy(control_hbm, control, sems.at[0]),
        pltpu.make_async_copy(background_hbm, background, sems.at[1]),
    ]
    for fetch in fetches:
        fetch.start()
    size = control.shape[0]
    members = size // 32
    even = lax.rem(lax.axis_index("tile"), 2) == 0
    slot = lax.axis_index("slot")
    later = jnp.where(slot == lax.axis_size("slot") - 1, 0.0, 1.0)
    gain = gain[...]
    weight = later * error[...]
    row8 = sublane((8, 1))
    mate_pull[...] = dot_t(message[...].astype(BF16), readout[...])
    mate_side = jnp.where(even, 1, 0) == jnp.where(row8 < 4, 1, 0)
    final[...] = f2x[...].astype(F32)
    for r in range(2 * members):
        a, b = r * SLIM, r * SLIM + 16
        cot[a:b] = pull2[a:b] - weight * (nxt[r * 16 : (r + 1) * 16] - final[a:b])
        c, e = b, b + 8
        start = size // 2 + r * 8
        pulled = pull2[c:e] + jnp.where(mate_side, mate_pull[start : start + 8], 0.0)
        cot[c:e] = pulled - weight * (edges(nxt, size, edge, r) - final[c:e])
        extra[a:b] = pull1[a:b]
        extra[c:e] = pull1[c:e] + jnp.where(mate_side, mate_pull[r * 8 : (r + 1) * 8], 0.0)
    adjoint_step(u1x, cot, gb, gm, flat, d1x, extra, cot2, gain, ws, wn, wo, members)
    for fetch in fetches:
        fetch.wait()
    for r in range(2 * members):
        u0x[r * SLIM : r * SLIM + 16] = control[r * 16 : (r + 1) * 16]
        u0x[r * SLIM + 16 : (r + 1) * SLIM] = edge0[r * 8 : (r + 1) * 8]
    adjoint_step(u0x, cot2, gb, gm, flat, d0x, None, cot, gain, ws, wn, wo, members)
    for r in range(2 * members):
        a, b = r * 16, (r + 1) * 16
        result[a:b] = cot[r * SLIM : r * SLIM + 16] + error[...] * control[a:b]


def last_kernel(base, background, before, error, result):
    first = lax.axis_index("slot") == 0
    taken = jnp.where(first, background[...].astype(F32), before[...].astype(F32))
    result[...] = base[...] - error[...] * taken


def kernel_call(body, outs, scratch, flops, moved, hbm=0, out_places=None):
    def call(*operands):
        operands = [pltpu.with_memory_space_constraint(x, pltpu.HBM) for x in operands[:hbm]] + list(operands[hbm:])
        places = [pltpu.HBM] * hbm + [pltpu.VMEM] * (len(operands) - hbm)
        given = {} if out_places is None else {"out_specs": [pl.BlockSpec(memory_space=p) for p in out_places]}
        return pl.pallas_call(
            body,
            out_shape=outs,
            in_specs=[pl.BlockSpec(memory_space=place) for place in places],
            **given,
            scratch_shapes=scratch,
            compiler_params=pltpu.CompilerParams(vmem_limit_bytes=VMEM_LIMIT),
            cost_estimate=pl.CostEstimate(flops=flops, bytes_accessed=moved, transcendentals=0),
        )(*operands)

    return call


def per_device(
    control,
    background,
    self_weight,
    neighbour_weight,
    output_weight,
    norm_gain,
    readout,
    error_weight,
    report_owner,
    report_stencil,
    report_weights,
    report_values,
    report_precision,
):
    tiles = lax.axis_size("tile")
    slots = lax.axis_size("slot")
    members, lats, cols, channels = control.shape[1:]
    groups = members * lats
    size = groups * cols
    steps = report_owner.shape[1]
    rows = report_owner.shape[2]
    gain = norm_gain.reshape(1, channels)
    error = error_weight.reshape(1, channels)
    flat = control.reshape(size, channels)

    def spec(count, dtype=F32, width=channels):
        return jax.ShapeDtypeStruct((count, width), dtype)

    def scratch(count, dtype=F32, width=channels):
        return pltpu.VMEM((count, width), dtype)

    mate_of = [(i, i ^ 1) for i in range(tiles)]
    other_of = [(i, (i - 1) % tiles if i % 2 == 0 else (i + 1) % tiles) for i in range(tiles)]

    def across(block, shift, route):
        pairs = [
            (((s + shift) % slots) * tiles + i, s * tiles + j)
            for s in range(slots)
            for i, j in route
        ]
        return lax.ppermute(block, ("slot", "tile"), pairs)

    straight = [(i, i) for i in range(tiles)]
    mate = lax.ppermute(flat, "tile", mate_of)
    held, packed = kernel_call(
        first_kernel,
        [spec(size), spec(tiles * CHUNK, BF16, LANES)],
        [
            pltpu.VMEM((steps, 1, rows), jnp.int32),
            pltpu.VMEM((steps, 4, rows), jnp.int32),
            pltpu.VMEM((steps, 4, rows), BF16),
            pltpu.VMEM((steps, rows), BF16),
            scratch(steps * rows, BF16, LANES),
            pltpu.VMEM((1, steps * rows), jnp.int32),
            scratch(META, F32, steps * rows),
            scratch(tiles * CHUNK, F32, LANES),
            scratch(tiles * CHUNK, BF16, LANES),
            pltpu.SemaphoreType.DMA((7,)),
        ],
        10**7,
        200000,
        hbm=6,
        out_places=[pltpu.VMEM, pltpu.HBM],
    )(
        flat,
        jnp.transpose(report_owner[0], (0, 2, 1)),
        jnp.transpose(report_stencil[0], (0, 2, 1)),
        jnp.transpose(report_weights[0], (0, 2, 1)),
        report_precision[0],
        report_values[0].reshape(steps * rows, LANES),
    )
    sent = kernel_call(
        tile_kernel, spec(groups * (cols + 2), BF16), [scratch(groups * 2)], 1000, 400000
    )(held, mate)
    oth = lax.ppermute(sent, "tile", other_of)
    arrived = lax.all_to_all(packed, "tile", split_axis=0, concat_axis=0, tiled=True)

    message = kernel_call(
        relay_kernel, spec(size + 4 * groups), [scratch(size)], 1000, 700000
    )(held, mate, oth)
    nxt = across(message, 1, straight)
    wide = groups * WIDE
    slim = groups * SLIM
    edge0, u1x, d0x, d1x, f2x, field, final = kernel_call(
        forward_kernel,
        [spec(groups * 8), spec(slim)] + [spec(slim, BF16)] * 3
        + [spec(4 * lats * cols, F32, members * LANES), spec(size, BF16)],
        [scratch(wide), scratch(wide), scratch(wide, BF16), scratch(wide, BF16), scratch(wide, BF16)]
        + [scratch(wide), scratch(16), scratch(4 * size, BF16)]
        + [scratch(channels, BF16), pltpu.SemaphoreType.DMA],
        10**11,
        4000000,
        hbm=1,
    )(output_weight, held, mate, oth, self_weight, neighbour_weight, gain, readout)
    before = across(final, -1, straight)
    total = -(-tiles // SENDERS) * LANES
    pull1, pull2, message = kernel_call(
        functools.partial(observe_kernel, tiles),
        [spec(slim), spec(slim), spec(size, F32, LANES)],
        [scratch(128, BF16, total)] * 4
        + [scratch(total, F32, LANES), scratch(4 * size, BF16, LANES), scratch(tiles * CHUNK, F32, LANES)],
        10**9,
        2000000,
    )(arrived, field, readout)
    from_mate = lax.ppermute(message, "tile", mate_of)
    base, handed = kernel_call(
        backward_kernel,
        [spec(size), spec(size, BF16)],
        [scratch(slim), scratch(slim), scratch(slim), scratch(slim, BF16), scratch(slim), scratch(slim)]
        + [scratch(size), scratch(16), scratch(slim), scratch(slim), scratch(size)]
        + [pltpu.SemaphoreType.DMA((2,))],
        12 * slim * channels * channels,
        6000000,
        hbm=2,
    )(
        flat, background.reshape(size, channels), edge0, u1x, d0x, d1x, f2x, pull1, pull2, from_mate,
        nxt, self_weight, neighbour_weight, output_weight, gain, error, readout,
    )
    result = kernel_call(last_kernel, spec(size), [], 10**6, 900000)(base, handed, before, error)
    return result.reshape(control.shape)


def solution(mesh):
    in_specs = (
        P("slot", None, None, "tile", None),
        P(None, None, "tile", None),
        P(),
        P(),
        P(),
        P(),
        P(),
        P(),
        P("slot", None, "tile", None),
        P("slot", None, "tile", None),
        P("slot", None, "tile", None),
        P("slot", None, "tile", None),
        P("slot", None, "tile"),
    )
    out_specs = P("slot", None, None, "tile", None)
    return jax.shard_map(
        per_device, mesh=mesh, in_specs=in_specs, out_specs=out_specs, check_vma=False
    )
```

```python
import functools
import jax
import jax.numpy as jnp
from jax import lax
from jax.experimental import pallas as pl
from jax.experimental.pallas import tpu as pltpu
from jax.sharding import PartitionSpec as P

EPSILON = 1e-06
F32 = jnp.float32
BF16 = jnp.bfloat16
LANES = 128
CAP = 5
SLOTS = 4 * CAP
CHUNK = 32
META = 16
SENDERS = LANES // SLOTS
WIDE = 40
SLIM = 24
VMEM_LIMIT = 28 * 1024 * 1024


def dot(a, b):
    return jnp.dot(a, b, preferred_element_type=F32)


def dot_t(a, b):
    return lax.dot_general(a, b, (((1,), (1,)), ((), ())), preferred_element_type=F32)


def sublane(shape):
    return lax.broadcasted_iota(jnp.int32, shape, 0)


def inverse_rms(x):
    return lax.rsqrt(jnp.mean(x * x, axis=-1, keepdims=True) + EPSILON)


def sigmoid(p):
    return 0.5 * jnp.tanh(0.5 * p) + 0.5


def neighbours(rows):
    width = rows[0].shape[0]
    return [
        0.25 * (rows[1 - i] + pltpu.roll(rows[i], 1, 0) + pltpu.roll(rows[i], width - 1, 0))
        for i in range(2)
    ]


def forward_step(u, n, mean, act, pre, d, gain, ws, wn, wo, width, members, out, fetch=None):
    both = 2 * width
    for m in range(members):
        base = m * both
        rows = []
        for lat in range(2):
            x = u[base + lat * width : base + (lat + 1) * width]
            rows.append((x * inverse_rms(x) * gain).astype(BF16).astype(F32))
        n[base : base + both] = jnp.concatenate(rows, axis=0).astype(BF16)
        mean[base : base + both] = jnp.concatenate(neighbours(rows), axis=0).astype(BF16)
    pre[...] = dot(n[...], ws[...]) + dot(mean[...], wn[...])
    for m in range(members):
        base = m * both
        p = pre[base : base + both]
        sig = sigmoid(p)
        act[base : base + both] = (p * sig).astype(BF16)
        if d is not None:
            pre[base : base + both] = sig * (1.0 + p * (1.0 - sig))
    if d is not None:
        for m in range(members):
            slim_copy(d, pre, m)
    if fetch is not None:
        fetch.wait()
    pre[...] = dot(act[...], wo[...])
    for r in range(2 * members):
        out(r, u[r * width : (r + 1) * width] + pre[r * width : (r + 1) * width])


def slim_edge(wide, r):
    low = wide[r * WIDE + 16 : r * WIDE + 24]
    high = wide[r * WIDE + 32 : r * WIDE + 40]
    return jnp.where(sublane(low.shape) < 4, low, high)


def slim_copy(to, wide, m):
    parts = []
    for r in (2 * m, 2 * m + 1):
        parts += [wide[r * WIDE : r * WIDE + 16], slim_edge(wide, r)]
    both = jnp.concatenate(parts, axis=0)
    to[m * 2 * SLIM : (m + 1) * 2 * SLIM] = both.astype(to.dtype)


def first_kernel(
    control_hbm, owner_hbm, stencil_hbm, weights_hbm, precision_hbm, values_hbm,
    ws_hbm, wn_hbm, readout_hbm, gain_hbm,
    held, out_hbm, ws, wn, readout, gain,
    owner, stencil, weights, precision, values, key, meta, picked, out, sems,
):
    pairs = (
        (owner_hbm, owner), (stencil_hbm, stencil), (weights_hbm, weights),
        (precision_hbm, precision), (values_hbm, values), (control_hbm, held),
        (gain_hbm, gain), (ws_hbm, ws), (wn_hbm, wn), (readout_hbm, readout),
    )
    copies = [pltpu.make_async_copy(source, to, sems.at[i]) for i, (source, to) in enumerate(pairs)]
    for copy in copies:
        copy.start()
    for copy in copies[:5]:
        copy.wait()
    pack(owner, stencil, weights, precision, values, out, key, meta, picked)
    store = pltpu.make_async_copy(out, out_hbm, sems.at[len(pairs)])
    store.start()
    for copy in copies[5:]:
        copy.wait()
    store.wait()


def pack(owner, stencil, weights, precision, values, out, key, meta, picked):
    steps, _, rows = owner.shape
    tiles = out.shape[0] // CHUNK
    total = steps * rows
    place = lax.axis_index("tile") % SENDERS * SLOTS
    earlier = lax.broadcasted_iota(jnp.int32, (rows, rows), 0) < lax.broadcasted_iota(jnp.int32, (rows, rows), 1)
    earlier = earlier.astype(F32).astype(BF16)
    meta[...] = jnp.zeros_like(meta)
    for k in range(steps):
        at = slice(k * rows, (k + 1) * rows)
        named = lax.broadcasted_iota(jnp.int32, (tiles, rows), 0) == owner[k]
        hits = named.astype(F32)
        before = dot(hits.astype(BF16), earlier)
        rank = jnp.sum(hits * before, axis=0, keepdims=True).astype(jnp.int32)
        key[0:1, at] = owner[k] * (2 * CAP) + k * CAP + rank
        meta[4:8, at] = stencil[k].astype(F32)
        meta[8:12, at] = weights[k].astype(F32)
        meta[12:13, at] = precision[k : k + 1].astype(F32)
    row = lax.broadcasted_iota(jnp.int32, (tiles * CHUNK, total), 0)
    tile = row // CHUNK
    slot = row % CHUNK
    other = jnp.where(tile % 2 == 0, (tile + tiles - 1) % tiles, (tile + 1) % tiles)
    mine = slot < 2 * CAP
    wanted = jnp.where(mine, tile * (2 * CAP) + slot, other * (2 * CAP) + slot - 2 * CAP)
    wanted = jnp.where(slot < SLOTS, wanted, -1)
    placement = (wanted == key[...]).astype(F32).astype(BF16)
    picked[...] = dot(placement, values[...])
    entries = dot_t(meta[...].astype(BF16), placement)
    lane = lax.broadcasted_iota(jnp.int32, (META, LANES), 1)
    used = jnp.logical_and(lane >= place, lane < place + SLOTS)
    per_tile = LANES // CHUNK
    for t in range(tiles):
        block = entries[:, t // per_tile * LANES : (t // per_tile + 1) * LANES]
        shift = (place + LANES - t % per_tile * CHUNK) % LANES
        block = jnp.where(used, pltpu.roll(block, shift, 1), 0.0)
        low = picked[t * CHUNK + 16 : (t + 1) * CHUNK]
        picked[t * CHUNK + 16 : (t + 1) * CHUNK] = jnp.where(sublane((META, 1)) < 4, low, block)
    out[...] = picked[...].astype(BF16)


def tile_kernel(control, mate, out, held):
    even = lax.rem(lax.axis_index("tile"), 2) == 0
    size = control.shape[0]
    out[0:size] = control[...].astype(BF16)
    for r in range(size // 16):
        held[r * 2 : (r + 1) * 2] = jnp.where(
            even, mate[r * 16 : r * 16 + 2], mate[r * 16 + 14 : (r + 1) * 16]
        )
    out[size:] = held[...].astype(BF16)


def after_kernel(block, earlier, out):
    out[...] = block[...]


def relay_kernel(control, mate, oth_inner, oth_ends, out, oth, wide):
    tile = lax.axis_index("tile")
    end = jnp.logical_or(tile == 0, tile == lax.axis_size("tile") - 1)
    even = lax.rem(lax.axis_index("tile"), 2) == 0
    size = control.shape[0]
    edge = size // 8
    out[0:size] = control[...]
    wide[...] = jnp.where(end, oth_ends[...].astype(F32), oth_inner[...].astype(F32))
    oth[...] = wide[...].astype(BF16)
    for r in range(size // 16):
        a, b = r * 16, (r + 1) * 16
        out[size + r * 2 : size + (r + 1) * 2] = jnp.where(even, wide[b - 2 : b], wide[a : a + 2])
        start = size + edge + r * 2
        out[start : start + 2] = jnp.where(even, mate[a : a + 2], mate[b - 2 : b])


def forward_kernel(
    wo_hbm, control, mate, oth, ws, wn, gain, readout,
    edge0, u1x, d0x, d1x, f2x, field, final,
    ua, ub, n, mean, act, pre, edge, states, wo, sem,
):
    fetch = pltpu.make_async_copy(wo_hbm, wo, sem)
    fetch.start()
    members = control.shape[0] // 32
    even = lax.rem(lax.axis_index("tile"), 2) == 0
    tile_at = jnp.where(even, 24, 16)
    edge_at = jnp.where(even, 16, 32)
    far = oth[members * 32 :].astype(F32)
    for r in range(2 * members):
        ua[r * WIDE : r * WIDE + 16] = control[r * 16 : (r + 1) * 16]
        ua[pl.ds(pl.multiple_of(r * WIDE + tile_at, 8), 16)] = oth[r * 16 : (r + 1) * 16].astype(F32)
        near4 = jnp.where(even, mate[r * 16 : r * 16 + 4], mate[r * 16 + 12 : (r + 1) * 16])
        far2 = far[r * 2 : (r + 1) * 2]
        edge[...] = jnp.zeros_like(edge)
        edge[0:4] = near4
        edge[6:8] = far2
        edge[8:10] = far2
        edge[12:16] = near4
        ua[pl.ds(pl.multiple_of(r * WIDE + edge_at, 8), 8)] = jnp.where(even, edge[0:8], edge[8:16])
    for r in range(2 * members):
        edge0[r * 8 : (r + 1) * 8] = slim_edge(ua, r)
    g = gain[...]

    def keep(ref):
        def store(r, value):
            ref[r * WIDE : (r + 1) * WIDE] = value

        return store

    def keep_states(ref, k):
        own = k * members * 32
        away = (2 + k) * members * 32
        for r in range(2 * members):
            states[own + r * 16 : own + (r + 1) * 16] = ref[r * WIDE : r * WIDE + 16].astype(BF16)
            taken = ref[pl.ds(pl.multiple_of(r * WIDE + tile_at, 8), 16)]
            states[away + r * 16 : away + (r + 1) * 16] = taken.astype(BF16)

    forward_step(ua, n, mean, act, pre, d0x, g, ws, wn, wo, WIDE, members, keep(ub), fetch)
    for m in range(members):
        slim_copy(u1x, ub, m)
    keep_states(ub, 0)
    forward_step(ub, n, mean, act, pre, d1x, g, ws, wn, wo, WIDE, members, keep(ua))
    for m in range(members):
        slim_copy(f2x, ua, m)
    keep_states(ua, 1)
    final[...] = states[members * 32 : 2 * members * 32]
    read = dot(states[...], readout[...])
    for q in range(4):
        for m in range(members):
            start = (q * members + m) * 32
            field[q * 32 : (q + 1) * 32, m * LANES : (m + 1) * LANES] = read[start : start + 32]


def split(x):
    high = x.astype(BF16)
    return high, (x - high.astype(F32)).astype(BF16)


def observe_kernel(
    tiles,
    ws_hbm, wn_hbm, wo_hbm, readout_hbm, gain_hbm, error_hbm, control_hbm, background_hbm, arrived, field,
    pull1, pull2, message, ws, wn, wo, readout, gain, error, control, background,
    th, tl, ph, plo, vals, spread, wide, sems,
):
    pairs = (
        (readout_hbm, readout), (gain_hbm, gain), (error_hbm, error), (wo_hbm, wo), (wn_hbm, wn), (ws_hbm, ws),
        (control_hbm, control), (background_hbm, background),
    )
    copies = [pltpu.make_async_copy(source, to, sems.at[i]) for i, (source, to) in enumerate(pairs)]
    for copy in copies:
        copy.start()
    steps = 2
    members = field.shape[1] // LANES
    even = lax.rem(lax.axis_index("tile"), 2) == 0
    cells = sublane((32, LANES)).astype(F32)
    lane = lax.broadcasted_iota(jnp.int32, (1, LANES), 1)
    table_of = jnp.where(lane < SENDERS * SLOTS, lane % SLOTS // CAP, -1)
    wide[...] = arrived[...].astype(F32)
    vals[...] = jnp.zeros_like(vals)
    for p in range(th.shape[1] // LANES):
        meta = jnp.zeros((META, LANES), F32)
        for d in range(p * SENDERS, min((p + 1) * SENDERS, tiles)):
            meta += wide[d * CHUNK + 16 : (d + 1) * CHUNK]
            start = p * LANES + d % SENDERS * SLOTS
            vals[start : start + SLOTS] = wide[d * CHUNK : d * CHUNK + SLOTS]
        weight = jnp.zeros((32, LANES), F32)
        for i in range(4):
            weight += jnp.where(cells == meta[4 + i : 5 + i], meta[8 + i : 9 + i], 0.0)
        scaled = weight * meta[12:13]
        wh, wl = split(weight)
        sh, sl = split(scaled)
        parts = ((th, wh.astype(F32)), (tl, wl.astype(F32)), (ph, sh.astype(F32)), (plo, sl.astype(F32)))
        for q in range(2 * steps):
            hit = table_of == q
            for ref, value in parts:
                kept = jnp.where(hit, value, 0.0).astype(BF16)
                ref[q * 32 : (q + 1) * 32, p * LANES : (p + 1) * LANES] = kept
    cross = dot_t(ph[...], th[...]) + dot_t(plo[...], th[...]) + dot_t(ph[...], tl[...])
    taken = vals[...].astype(BF16)
    target = dot(ph[...], taken) + dot(plo[...], taken)
    ch, cl = split(cross)
    fh, fl = split(field[...])
    mixed = dot(ch, fh) + dot(cl, fh) + dot(ch, fl)
    for q in range(2 * steps):
        for m in range(members):
            start = (q * members + m) * 32
            value = mixed[q * 32 : (q + 1) * 32, m * LANES : (m + 1) * LANES] - target[q * 32 : (q + 1) * 32]
            spread[start : start + 32] = value.astype(BF16)
    copies[0].wait()
    pulled = dot_t(spread[...], readout[...])
    size = members * 32
    row8 = sublane((8, 1))
    for k, out in enumerate((pull1, pull2)):
        own = k * size
        away = (2 + k) * size
        for r in range(2 * members):
            out[r * SLIM : r * SLIM + 16] = pulled[own + r * 16 : own + (r + 1) * 16]
            low = pulled[away + r * 16 : away + r * 16 + 8]
            high = pulled[away + r * 16 + 8 : away + r * 16 + 16]
            group = jnp.where(
                even, jnp.where(row8 >= 4, high, 0.0), jnp.where(row8 < 4, low, 0.0)
            )
            out[r * SLIM + 16 : r * SLIM + 24] = group
        for r in range(2 * members):
            pair = spread[own + r * 16 : own + (r + 1) * 16].astype(F32)
            near = jnp.where(even, pair[8:16], pair[0:8])
            message[k * size // 2 + r * 8 : k * size // 2 + (r + 1) * 8] = near
    for copy in copies[1:]:
        copy.wait()


def adjoint_step(u, cot, gb, gm, flat, d, add, out, gain, ws, wn, wo, members):
    both = 2 * SLIM
    gb[...] = cot[...].astype(BF16)
    flat[...] = dot_t(gb[...], wo[...])
    gb[...] = (flat[...] * d[...]).astype(BF16)
    gm[...] = dot_t(gb[...], wn[...])
    flat[...] = dot_t(gb[...], ws[...])
    for m in range(members):
        base = m * both
        rows = []
        for lat in range(2):
            start = base + lat * SLIM
            rows.append(gm[start : start + SLIM].astype(BF16).astype(F32))
        around = neighbours(rows)
        for lat in range(2):
            start = base + lat * SLIM
            x = u[start : start + SLIM]
            s = inverse_rms(x)
            scaled = gain * (flat[start : start + SLIM] + around[lat])
            inner = jnp.mean(x * scaled, axis=-1, keepdims=True)
            value = cot[start : start + SLIM] + s * scaled - x * (s * s * s * inner)
            if add is not None:
                value = value + add[start : start + SLIM]
            out[start : start + SLIM] = value


def edges(nxt, size, edge, r):
    even = lax.rem(lax.axis_index("tile"), 2) == 0
    start = size + r * 2
    far = nxt[start : start + 2]
    start = size + size // 8 + r * 2
    near = nxt[start : start + 2]
    edge[...] = jnp.zeros_like(edge)
    edge[0:2] = near
    edge[6:8] = far
    edge[8:10] = far
    edge[14:16] = near
    return jnp.where(even, edge[0:8], edge[8:16])


def backward_kernel(
    control, edge0, u1x, d0x, d1x, f2x, pull1, pull2, message,
    nxt, ws, wn, wo, gain, error, readout,
    result,
    cot, cot2, extra, gb, gm, flat, mate_pull, edge, u0x, final,
):
    size = control.shape[0]
    members = size // 32
    even = lax.rem(lax.axis_index("tile"), 2) == 0
    slot = lax.axis_index("slot")
    later = jnp.where(slot == lax.axis_size("slot") - 1, 0.0, 1.0)
    gain = gain[...]
    weight = later * error[...]
    row8 = sublane((8, 1))
    mate_pull[...] = dot_t(message[...].astype(BF16), readout[...])
    mate_side = jnp.where(even, 1, 0) == jnp.where(row8 < 4, 1, 0)
    final[...] = f2x[...].astype(F32)
    for r in range(2 * members):
        a, b = r * SLIM, r * SLIM + 16
        cot[a:b] = pull2[a:b] - weight * (nxt[r * 16 : (r + 1) * 16] - final[a:b])
        c, e = b, b + 8
        start = size // 2 + r * 8
        pulled = pull2[c:e] + jnp.where(mate_side, mate_pull[start : start + 8], 0.0)
        cot[c:e] = pulled - weight * (edges(nxt, size, edge, r) - final[c:e])
        extra[a:b] = pull1[a:b]
        extra[c:e] = pull1[c:e] + jnp.where(mate_side, mate_pull[r * 8 : (r + 1) * 8], 0.0)
    adjoint_step(u1x, cot, gb, gm, flat, d1x, extra, cot2, gain, ws, wn, wo, members)
    for r in range(2 * members):
        u0x[r * SLIM : r * SLIM + 16] = control[r * 16 : (r + 1) * 16]
        u0x[r * SLIM + 16 : (r + 1) * SLIM] = edge0[r * 8 : (r + 1) * 8]
    adjoint_step(u0x, cot2, gb, gm, flat, d0x, None, cot, gain, ws, wn, wo, members)
    for r in range(2 * members):
        a, b = r * 16, (r + 1) * 16
        result[a:b] = cot[r * SLIM : r * SLIM + 16] + error[...] * control[a:b]


def last_kernel(base, background, before, error, result):
    first = lax.axis_index("slot") == 0
    taken = jnp.where(first, background[...].astype(F32), before[...].astype(F32))
    result[...] = base[...] - error[...] * taken


def kernel_call(body, outs, scratch, flops, moved, hbm=0, out_places=None):
    def call(*operands):
        operands = [pltpu.with_memory_space_constraint(x, pltpu.HBM) for x in operands[:hbm]] + list(operands[hbm:])
        places = [pltpu.HBM] * hbm + [pltpu.VMEM] * (len(operands) - hbm)
        given = {} if out_places is None else {"out_specs": [pl.BlockSpec(memory_space=p) for p in out_places]}
        return pl.pallas_call(
            body,
            out_shape=outs,
            in_specs=[pl.BlockSpec(memory_space=place) for place in places],
            **given,
            scratch_shapes=scratch,
            compiler_params=pltpu.CompilerParams(vmem_limit_bytes=VMEM_LIMIT),
            cost_estimate=pl.CostEstimate(flops=flops, bytes_accessed=moved, transcendentals=0),
        )(*operands)

    return call


def per_device(
    control,
    background,
    self_weight,
    neighbour_weight,
    output_weight,
    norm_gain,
    readout,
    error_weight,
    report_owner,
    report_stencil,
    report_weights,
    report_values,
    report_precision,
):
    tiles = lax.axis_size("tile")
    slots = lax.axis_size("slot")
    members, lats, cols, channels = control.shape[1:]
    groups = members * lats
    size = groups * cols
    steps = report_owner.shape[1]
    rows = report_owner.shape[2]
    gain = norm_gain.reshape(1, channels)
    error = error_weight.reshape(1, channels)
    flat = control.reshape(size, channels)

    def spec(count, dtype=F32, width=channels):
        return jax.ShapeDtypeStruct((count, width), dtype)

    def scratch(count, dtype=F32, width=channels):
        return pltpu.VMEM((count, width), dtype)

    mate_of = [(i, i ^ 1) for i in range(tiles)]
    other_of = [(i, (i - 1) % tiles if i % 2 == 0 else (i + 1) % tiles) for i in range(tiles)]

    def across(block, shift, route):
        pairs = [
            (((s + shift) % slots) * tiles + i, s * tiles + j)
            for s in range(slots)
            for i, j in route
        ]
        return lax.ppermute(block, ("slot", "tile"), pairs)

    straight = [(i, i) for i in range(tiles)]
    mate = lax.ppermute(flat, "tile", mate_of)
    held, packed, ws, wn, readout_first, gain_first = kernel_call(
        first_kernel,
        [spec(size), spec(tiles * CHUNK, BF16, LANES), spec(channels, BF16), spec(channels, BF16)]
        + [spec(channels, BF16, LANES), spec(1)],
        [
            pltpu.VMEM((steps, 1, rows), jnp.int32),
            pltpu.VMEM((steps, 4, rows), jnp.int32),
            pltpu.VMEM((steps, 4, rows), BF16),
            pltpu.VMEM((steps, rows), BF16),
            scratch(steps * rows, BF16, LANES),
            pltpu.VMEM((1, steps * rows), jnp.int32),
            scratch(META, F32, steps * rows),
            scratch(tiles * CHUNK, F32, LANES),
            scratch(tiles * CHUNK, BF16, LANES),
            pltpu.SemaphoreType.DMA((11,)),
        ],
        10**7,
        200000,
        hbm=10,
        out_places=[pltpu.VMEM, pltpu.HBM] + [pltpu.VMEM] * 4,
    )(
        flat,
        jnp.transpose(report_owner[0], (0, 2, 1)),
        jnp.transpose(report_stencil[0], (0, 2, 1)),
        jnp.transpose(report_weights[0], (0, 2, 1)),
        report_precision[0],
        report_values[0].reshape(steps * rows, LANES),
        self_weight,
        neighbour_weight,
        readout,
        gain,
    )
    sent = kernel_call(
        tile_kernel, spec(groups * (cols + 2), BF16), [scratch(groups * 2)], 1000, 400000
    )(held, mate)
    ends = (0, tiles - 1)
    oth_inner = lax.ppermute(sent, "tile", [(i, i if i in ends else j) for i, j in other_of])
    again = kernel_call(after_kernel, spec(groups * (cols + 2), BF16), [], 10**11, 300000)(sent, oth_inner)
    oth_ends = lax.ppermute(again, "tile", [(i, j if i in ends else i) for i, j in other_of])
    arrived = lax.all_to_all(packed, "tile", split_axis=0, concat_axis=0, tiled=True)

    message, oth = kernel_call(
        relay_kernel,
        [spec(size + 4 * groups), spec(groups * (cols + 2), BF16)],
        [scratch(groups * (cols + 2))],
        1000,
        700000,
    )(held, mate, oth_inner, oth_ends)
    nxt = across(message, 1, straight)
    wide = groups * WIDE
    slim = groups * SLIM
    edge0, u1x, d0x, d1x, f2x, field, final = kernel_call(
        forward_kernel,
        [spec(groups * 8), spec(slim)] + [spec(slim, BF16)] * 3
        + [spec(4 * lats * cols, F32, members * LANES), spec(size, BF16)],
        [scratch(wide), scratch(wide), scratch(wide, BF16), scratch(wide, BF16), scratch(wide, BF16)]
        + [scratch(wide), scratch(16), scratch(4 * size, BF16)]
        + [scratch(channels, BF16), pltpu.SemaphoreType.DMA],
        12 * wide * channels * channels,
        4000000,
        hbm=1,
    )(output_weight, held, mate, oth, ws, wn, gain_first, readout_first)
    before = across(final, -1, straight)
    total = -(-tiles // SENDERS) * LANES
    handed = [self_weight, neighbour_weight, output_weight, readout, gain, error]
    handed += [flat, background.reshape(size, channels)]
    pull1, pull2, message, *handed = kernel_call(
        functools.partial(observe_kernel, tiles),
        [spec(slim), spec(slim), spec(size, F32, LANES)]
        + [jax.ShapeDtypeStruct(block.shape, block.dtype) for block in handed],
        [scratch(128, BF16, total)] * 4
        + [scratch(total, F32, LANES), scratch(4 * size, BF16, LANES), scratch(tiles * CHUNK, F32, LANES)]
        + [pltpu.SemaphoreType.DMA((8,))],
        10**9,
        2000000,
        hbm=8,
    )(*handed, arrived, field)
    ws, wn, wo, readout, gain, error, held, background = handed
    from_mate = lax.ppermute(message, "tile", mate_of)
    base = kernel_call(
        backward_kernel,
        spec(size),
        [scratch(slim), scratch(slim), scratch(slim), scratch(slim, BF16), scratch(slim), scratch(slim)]
        + [scratch(size), scratch(16), scratch(slim), scratch(slim)],
        12 * slim * channels * channels,
        6000000,
    )(held, edge0, u1x, d0x, d1x, f2x, pull1, pull2, from_mate, nxt, ws, wn, wo, gain, error, readout)
    result = kernel_call(last_kernel, spec(size), [], 10**6, 900000)(base, background, before, error)
    return result.reshape(control.shape)


def solution(mesh):
    in_specs = (
        P("slot", None, None, "tile", None),
        P(None, None, "tile", None),
        P(),
        P(),
        P(),
        P(),
        P(),
        P(),
        P("slot", None, "tile", None),
        P("slot", None, "tile", None),
        P("slot", None, "tile", None),
        P("slot", None, "tile", None),
        P("slot", None, "tile"),
    )
    out_specs = P("slot", None, None, "tile", None)
    return jax.shard_map(
        per_device, mesh=mesh, in_specs=in_specs, out_specs=out_specs, check_vma=False
    )
```

```python
import functools
import jax
import jax.numpy as jnp
from jax import lax
from jax.experimental import pallas as pl
from jax.experimental.pallas import tpu as pltpu
from jax.sharding import PartitionSpec as P

EPSILON = 1e-06
F32 = jnp.float32
BF16 = jnp.bfloat16
LANES = 128
CAP = 5
SLOTS = 4 * CAP
CHUNK = 32
META = 16
SENDERS = LANES // SLOTS
WIDE = 40
SLIM = 24
VMEM_LIMIT = 28 * 1024 * 1024


def dot(a, b):
    return jnp.dot(a, b, preferred_element_type=F32)


def dot_t(a, b):
    return lax.dot_general(a, b, (((1,), (1,)), ((), ())), preferred_element_type=F32)


def sublane(shape):
    return lax.broadcasted_iota(jnp.int32, shape, 0)


def inverse_rms(x):
    return lax.rsqrt(jnp.mean(x * x, axis=-1, keepdims=True) + EPSILON)


def sigmoid(p):
    return 0.5 * jnp.tanh(0.5 * p) + 0.5


def neighbours(rows):
    width = rows[0].shape[0]
    return [
        0.25 * (rows[1 - i] + pltpu.roll(rows[i], 1, 0) + pltpu.roll(rows[i], width - 1, 0))
        for i in range(2)
    ]


def forward_step(u, n, mean, act, pre, d, gain, ws, wn, wo, width, members, out, copies=()):
    both = 2 * width
    for m in range(members):
        base = m * both
        rows = []
        for lat in range(2):
            x = u[base + lat * width : base + (lat + 1) * width]
            rows.append((x * inverse_rms(x) * gain).astype(BF16).astype(F32))
        n[base : base + both] = jnp.concatenate(rows, axis=0).astype(BF16)
        mean[base : base + both] = jnp.concatenate(neighbours(rows), axis=0).astype(BF16)
    for copy in copies[:2]:
        copy.wait()
    pre[...] = dot(n[...], ws[...]) + dot(mean[...], wn[...])
    for m in range(members):
        base = m * both
        p = pre[base : base + both]
        sig = sigmoid(p)
        act[base : base + both] = (p * sig).astype(BF16)
        if d is not None:
            pre[base : base + both] = sig * (1.0 + p * (1.0 - sig))
    if d is not None:
        for m in range(members):
            slim_copy(d, pre, m)
    for copy in copies[2:]:
        copy.wait()
    pre[...] = dot(act[...], wo[...])
    for r in range(2 * members):
        out(r, u[r * width : (r + 1) * width] + pre[r * width : (r + 1) * width])


def slim_edge(wide, r):
    low = wide[r * WIDE + 16 : r * WIDE + 24]
    high = wide[r * WIDE + 32 : r * WIDE + 40]
    return jnp.where(sublane(low.shape) < 4, low, high)


def slim_copy(to, wide, m):
    parts = []
    for r in (2 * m, 2 * m + 1):
        parts += [wide[r * WIDE : r * WIDE + 16], slim_edge(wide, r)]
    both = jnp.concatenate(parts, axis=0)
    to[m * 2 * SLIM : (m + 1) * 2 * SLIM] = both.astype(to.dtype)


def first_kernel(
    control_hbm, owner_hbm, stencil_hbm, weights_hbm, precision_hbm, values_hbm,
    held, out_hbm,
    owner, stencil, weights, precision, values, key, meta, picked, out, sems,
):
    pairs = (
        (owner_hbm, owner), (stencil_hbm, stencil), (weights_hbm, weights),
        (precision_hbm, precision), (values_hbm, values), (control_hbm, held),
    )
    copies = [pltpu.make_async_copy(source, to, sems.at[i]) for i, (source, to) in enumerate(pairs)]
    for copy in copies:
        copy.start()
    for copy in copies[:5]:
        copy.wait()
    pack(owner, stencil, weights, precision, values, out, key, meta, picked)
    store = pltpu.make_async_copy(out, out_hbm, sems.at[len(pairs)])
    store.start()
    for copy in copies[5:]:
        copy.wait()
    store.wait()


def pack(owner, stencil, weights, precision, values, out, key, meta, picked):
    steps, _, rows = owner.shape
    tiles = out.shape[0] // CHUNK
    total = steps * rows
    place = lax.axis_index("tile") % SENDERS * SLOTS
    earlier = lax.broadcasted_iota(jnp.int32, (rows, rows), 0) < lax.broadcasted_iota(jnp.int32, (rows, rows), 1)
    earlier = earlier.astype(F32).astype(BF16)
    meta[...] = jnp.zeros_like(meta)
    for k in range(steps):
        at = slice(k * rows, (k + 1) * rows)
        named = lax.broadcasted_iota(jnp.int32, (tiles, rows), 0) == owner[k]
        hits = named.astype(F32)
        before = dot(hits.astype(BF16), earlier)
        rank = jnp.sum(hits * before, axis=0, keepdims=True).astype(jnp.int32)
        key[0:1, at] = owner[k] * (2 * CAP) + k * CAP + rank
        meta[4:8, at] = stencil[k].astype(F32)
        meta[8:12, at] = weights[k].astype(F32)
        meta[12:13, at] = precision[k : k + 1].astype(F32)
    row = lax.broadcasted_iota(jnp.int32, (tiles * CHUNK, total), 0)
    tile = row // CHUNK
    slot = row % CHUNK
    other = jnp.where(tile % 2 == 0, (tile + tiles - 1) % tiles, (tile + 1) % tiles)
    mine = slot < 2 * CAP
    wanted = jnp.where(mine, tile * (2 * CAP) + slot, other * (2 * CAP) + slot - 2 * CAP)
    wanted = jnp.where(slot < SLOTS, wanted, -1)
    placement = (wanted == key[...]).astype(F32).astype(BF16)
    picked[...] = dot(placement, values[...])
    entries = dot_t(meta[...].astype(BF16), placement)
    lane = lax.broadcasted_iota(jnp.int32, (META, LANES), 1)
    used = jnp.logical_and(lane >= place, lane < place + SLOTS)
    per_tile = LANES // CHUNK
    for t in range(tiles):
        block = entries[:, t // per_tile * LANES : (t // per_tile + 1) * LANES]
        shift = (place + LANES - t % per_tile * CHUNK) % LANES
        block = jnp.where(used, pltpu.roll(block, shift, 1), 0.0)
        low = picked[t * CHUNK + 16 : (t + 1) * CHUNK]
        picked[t * CHUNK + 16 : (t + 1) * CHUNK] = jnp.where(sublane((META, 1)) < 4, low, block)
    out[...] = picked[...].astype(BF16)


def tile_kernel(control, mate, out, held):
    even = lax.rem(lax.axis_index("tile"), 2) == 0
    size = control.shape[0]
    out[0:size] = control[...].astype(BF16)
    for r in range(size // 16):
        held[r * 2 : (r + 1) * 2] = jnp.where(
            even, mate[r * 16 : r * 16 + 2], mate[r * 16 + 14 : (r + 1) * 16]
        )
    out[size:] = held[...].astype(BF16)


def relay_kernel(control, mate, oth, out, near4, wide):
    even = lax.rem(lax.axis_index("tile"), 2) == 0
    size = control.shape[0]
    edge = size // 8
    out[0:size] = control[...]
    wide[...] = oth[0:size].astype(F32)
    for r in range(size // 16):
        a, b = r * 16, (r + 1) * 16
        out[size + r * 2 : size + (r + 1) * 2] = jnp.where(even, wide[b - 2 : b], wide[a : a + 2])
        near4[r * 4 : (r + 1) * 4] = jnp.where(even, mate[a : a + 4], mate[b - 4 : b])
        start = size + edge + r * 2
        out[start : start + 2] = jnp.where(even, mate[a : a + 2], mate[b - 2 : b])


def forward_kernel(
    gain_hbm, ws_hbm, wn_hbm, wo_hbm, readout_hbm, control, mate, oth,
    edge0, u1x, d0x, d1x, f2x, field, final,
    ua, ub, n, mean, act, pre, edge, states, gain, ws, wn, wo, readout, sems,
):
    pairs = ((gain_hbm, gain), (ws_hbm, ws), (wn_hbm, wn), (wo_hbm, wo), (readout_hbm, readout))
    copies = [pltpu.make_async_copy(source, to, sems.at[i]) for i, (source, to) in enumerate(pairs)]
    for copy in copies:
        copy.start()
    members = final.shape[0] // 32
    even = lax.rem(lax.axis_index("tile"), 2) == 0
    tile_at = jnp.where(even, 24, 16)
    edge_at = jnp.where(even, 16, 32)
    far = oth[members * 32 :].astype(F32)
    for r in range(2 * members):
        ua[r * WIDE : r * WIDE + 16] = control[r * 16 : (r + 1) * 16]
        ua[pl.ds(pl.multiple_of(r * WIDE + tile_at, 8), 16)] = oth[r * 16 : (r + 1) * 16].astype(F32)
        near4 = mate[r * 4 : (r + 1) * 4]
        far2 = far[r * 2 : (r + 1) * 2]
        edge[...] = jnp.zeros_like(edge)
        edge[0:4] = near4
        edge[6:8] = far2
        edge[8:10] = far2
        edge[12:16] = near4
        ua[pl.ds(pl.multiple_of(r * WIDE + edge_at, 8), 8)] = jnp.where(even, edge[0:8], edge[8:16])
    for r in range(2 * members):
        edge0[r * 8 : (r + 1) * 8] = slim_edge(ua, r)
    copies[0].wait()
    g = gain[...]

    def keep(ref):
        def store(r, value):
            ref[r * WIDE : (r + 1) * WIDE] = value

        return store

    def keep_states(ref, k):
        own = k * members * 32
        away = (2 + k) * members * 32
        for r in range(2 * members):
            states[own + r * 16 : own + (r + 1) * 16] = ref[r * WIDE : r * WIDE + 16].astype(BF16)
            taken = ref[pl.ds(pl.multiple_of(r * WIDE + tile_at, 8), 16)]
            states[away + r * 16 : away + (r + 1) * 16] = taken.astype(BF16)

    forward_step(ua, n, mean, act, pre, d0x, g, ws, wn, wo, WIDE, members, keep(ub), copies[1:])
    for m in range(members):
        slim_copy(u1x, ub, m)
    keep_states(ub, 0)
    forward_step(ub, n, mean, act, pre, d1x, g, ws, wn, wo, WIDE, members, keep(ua))
    for m in range(members):
        slim_copy(f2x, ua, m)
    keep_states(ua, 1)
    final[...] = states[members * 32 : 2 * members * 32]
    read = dot(states[...], readout[...])
    for q in range(4):
        for m in range(members):
            start = (q * members + m) * 32
            field[q * 32 : (q + 1) * 32, m * LANES : (m + 1) * LANES] = read[start : start + 32]


def split(x):
    high = x.astype(BF16)
    return high, (x - high.astype(F32)).astype(BF16)


def observe_kernel(
    tiles,
    ws_hbm, wn_hbm, wo_hbm, readout_hbm, gain_hbm, error_hbm, control_hbm, background_hbm, arrived, field,
    pull1, pull2, message, ws, wn, wo, readout, gain, error, control, background,
    th, tl, ph, plo, vals, spread, wide, sems,
):
    pairs = (
        (readout_hbm, readout), (gain_hbm, gain), (error_hbm, error), (wo_hbm, wo), (wn_hbm, wn), (ws_hbm, ws),
        (control_hbm, control), (background_hbm, background),
    )
    copies = [pltpu.make_async_copy(source, to, sems.at[i]) for i, (source, to) in enumerate(pairs)]
    for copy in copies:
        copy.start()
    steps = 2
    members = field.shape[1] // LANES
    even = lax.rem(lax.axis_index("tile"), 2) == 0
    cells = sublane((32, LANES)).astype(F32)
    lane = lax.broadcasted_iota(jnp.int32, (1, LANES), 1)
    table_of = jnp.where(lane < SENDERS * SLOTS, lane % SLOTS // CAP, -1)
    wide[...] = arrived[...].astype(F32)
    vals[...] = jnp.zeros_like(vals)
    for p in range(th.shape[1] // LANES):
        meta = jnp.zeros((META, LANES), F32)
        for d in range(p * SENDERS, min((p + 1) * SENDERS, tiles)):
            meta += wide[d * CHUNK + 16 : (d + 1) * CHUNK]
            start = p * LANES + d % SENDERS * SLOTS
            vals[start : start + SLOTS] = wide[d * CHUNK : d * CHUNK + SLOTS]
        weight = jnp.zeros((32, LANES), F32)
        for i in range(4):
            weight += jnp.where(cells == meta[4 + i : 5 + i], meta[8 + i : 9 + i], 0.0)
        scaled = weight * meta[12:13]
        wh, wl = split(weight)
        sh, sl = split(scaled)
        parts = ((th, wh.astype(F32)), (tl, wl.astype(F32)), (ph, sh.astype(F32)), (plo, sl.astype(F32)))
        for q in range(2 * steps):
            hit = table_of == q
            for ref, value in parts:
                kept = jnp.where(hit, value, 0.0).astype(BF16)
                ref[q * 32 : (q + 1) * 32, p * LANES : (p + 1) * LANES] = kept
    cross = dot_t(ph[...], th[...]) + dot_t(plo[...], th[...]) + dot_t(ph[...], tl[...])
    taken = vals[...].astype(BF16)
    target = dot(ph[...], taken) + dot(plo[...], taken)
    ch, cl = split(cross)
    fh, fl = split(field[...])
    mixed = dot(ch, fh) + dot(cl, fh) + dot(ch, fl)
    for q in range(2 * steps):
        for m in range(members):
            start = (q * members + m) * 32
            value = mixed[q * 32 : (q + 1) * 32, m * LANES : (m + 1) * LANES] - target[q * 32 : (q + 1) * 32]
            spread[start : start + 32] = value.astype(BF16)
    copies[0].wait()
    pulled = dot_t(spread[...], readout[...])
    size = members * 32
    row8 = sublane((8, 1))
    for k, out in enumerate((pull1, pull2)):
        own = k * size
        away = (2 + k) * size
        for r in range(2 * members):
            out[r * SLIM : r * SLIM + 16] = pulled[own + r * 16 : own + (r + 1) * 16]
            low = pulled[away + r * 16 : away + r * 16 + 8]
            high = pulled[away + r * 16 + 8 : away + r * 16 + 16]
            group = jnp.where(
                even, jnp.where(row8 >= 4, high, 0.0), jnp.where(row8 < 4, low, 0.0)
            )
            out[r * SLIM + 16 : r * SLIM + 24] = group
        for r in range(2 * members):
            pair = spread[own + r * 16 : own + (r + 1) * 16].astype(F32)
            near = jnp.where(even, pair[8:16], pair[0:8])
            message[k * size // 2 + r * 8 : k * size // 2 + (r + 1) * 8] = near
    for copy in copies[1:]:
        copy.wait()


def adjoint_step(u, cot, gb, gm, flat, d, add, out, gain, ws, wn, wo, members):
    both = 2 * SLIM
    gb[...] = cot[...].astype(BF16)
    flat[...] = dot_t(gb[...], wo[...])
    gb[...] = (flat[...] * d[...]).astype(BF16)
    gm[...] = dot_t(gb[...], wn[...])
    flat[...] = dot_t(gb[...], ws[...])
    for m in range(members):
        base = m * both
        rows = []
        for lat in range(2):
            start = base + lat * SLIM
            rows.append(gm[start : start + SLIM].astype(BF16).astype(F32))
        around = neighbours(rows)
        for lat in range(2):
            start = base + lat * SLIM
            x = u[start : start + SLIM]
            s = inverse_rms(x)
            scaled = gain * (flat[start : start + SLIM] + around[lat])
            inner = jnp.mean(x * scaled, axis=-1, keepdims=True)
            value = cot[start : start + SLIM] + s * scaled - x * (s * s * s * inner)
            if add is not None:
                value = value + add[start : start + SLIM]
            out[start : start + SLIM] = value


def edges(nxt, size, edge, r):
    even = lax.rem(lax.axis_index("tile"), 2) == 0
    start = size + r * 2
    far = nxt[start : start + 2]
    start = size + size // 8 + r * 2
    near = nxt[start : start + 2]
    edge[...] = jnp.zeros_like(edge)
    edge[0:2] = near
    edge[6:8] = far
    edge[8:10] = far
    edge[14:16] = near
    return jnp.where(even, edge[0:8], edge[8:16])


def backward_kernel(
    control, edge0, u1x, d0x, d1x, f2x, pull1, pull2, message,
    nxt, ws, wn, wo, gain, error, readout,
    result,
    cot, cot2, extra, gb, gm, flat, mate_pull, edge, u0x, final,
):
    size = control.shape[0]
    members = size // 32
    even = lax.rem(lax.axis_index("tile"), 2) == 0
    slot = lax.axis_index("slot")
    later = jnp.where(slot == lax.axis_size("slot") - 1, 0.0, 1.0)
    gain = gain[...]
    weight = later * error[...]
    row8 = sublane((8, 1))
    mate_pull[...] = dot_t(message[...].astype(BF16), readout[...])
    mate_side = jnp.where(even, 1, 0) == jnp.where(row8 < 4, 1, 0)
    final[...] = f2x[...].astype(F32)
    for r in range(2 * members):
        a, b = r * SLIM, r * SLIM + 16
        cot[a:b] = pull2[a:b] - weight * (nxt[r * 16 : (r + 1) * 16] - final[a:b])
        c, e = b, b + 8
        start = size // 2 + r * 8
        pulled = pull2[c:e] + jnp.where(mate_side, mate_pull[start : start + 8], 0.0)
        cot[c:e] = pulled - weight * (edges(nxt, size, edge, r) - final[c:e])
        extra[a:b] = pull1[a:b]
        extra[c:e] = pull1[c:e] + jnp.where(mate_side, mate_pull[r * 8 : (r + 1) * 8], 0.0)
    adjoint_step(u1x, cot, gb, gm, flat, d1x, extra, cot2, gain, ws, wn, wo, members)
    for r in range(2 * members):
        u0x[r * SLIM : r * SLIM + 16] = control[r * 16 : (r + 1) * 16]
        u0x[r * SLIM + 16 : (r + 1) * SLIM] = edge0[r * 8 : (r + 1) * 8]
    adjoint_step(u0x, cot2, gb, gm, flat, d0x, None, cot, gain, ws, wn, wo, members)
    for r in range(2 * members):
        a, b = r * 16, (r + 1) * 16
        result[a:b] = cot[r * SLIM : r * SLIM + 16] + error[...] * control[a:b]


def last_kernel(base, background, before, error, result):
    first = lax.axis_index("slot") == 0
    taken = jnp.where(first, background[...].astype(F32), before[...].astype(F32))
    result[...] = base[...] - error[...] * taken


def kernel_call(body, outs, scratch, flops, moved, hbm=0, out_places=None):
    def call(*operands):
        operands = [pltpu.with_memory_space_constraint(x, pltpu.HBM) for x in operands[:hbm]] + list(operands[hbm:])
        places = [pltpu.HBM] * hbm + [pltpu.VMEM] * (len(operands) - hbm)
        given = {} if out_places is None else {"out_specs": [pl.BlockSpec(memory_space=p) for p in out_places]}
        return pl.pallas_call(
            body,
            out_shape=outs,
            in_specs=[pl.BlockSpec(memory_space=place) for place in places],
            **given,
            scratch_shapes=scratch,
            compiler_params=pltpu.CompilerParams(vmem_limit_bytes=VMEM_LIMIT),
            cost_estimate=pl.CostEstimate(flops=flops, bytes_accessed=moved, transcendentals=0),
        )(*operands)

    return call


def per_device(
    control,
    background,
    self_weight,
    neighbour_weight,
    output_weight,
    norm_gain,
    readout,
    error_weight,
    report_owner,
    report_stencil,
    report_weights,
    report_values,
    report_precision,
):
    tiles = lax.axis_size("tile")
    slots = lax.axis_size("slot")
    members, lats, cols, channels = control.shape[1:]
    groups = members * lats
    size = groups * cols
    steps = report_owner.shape[1]
    rows = report_owner.shape[2]
    gain = norm_gain.reshape(1, channels)
    error = error_weight.reshape(1, channels)
    flat = control.reshape(size, channels)

    def spec(count, dtype=F32, width=channels):
        return jax.ShapeDtypeStruct((count, width), dtype)

    def scratch(count, dtype=F32, width=channels):
        return pltpu.VMEM((count, width), dtype)

    mate_of = [(i, i ^ 1) for i in range(tiles)]
    other_of = [(i, (i - 1) % tiles if i % 2 == 0 else (i + 1) % tiles) for i in range(tiles)]

    def across(block, shift, route):
        pairs = [
            (((s + shift) % slots) * tiles + i, s * tiles + j)
            for s in range(slots)
            for i, j in route
        ]
        return lax.ppermute(block, ("slot", "tile"), pairs)

    straight = [(i, i) for i in range(tiles)]
    mate = lax.ppermute(flat, "tile", mate_of)
    held, packed = kernel_call(
        first_kernel,
        [spec(size), spec(tiles * CHUNK, BF16, LANES)],
        [
            pltpu.VMEM((steps, 1, rows), jnp.int32),
            pltpu.VMEM((steps, 4, rows), jnp.int32),
            pltpu.VMEM((steps, 4, rows), BF16),
            pltpu.VMEM((steps, rows), BF16),
            scratch(steps * rows, BF16, LANES),
            pltpu.VMEM((1, steps * rows), jnp.int32),
            scratch(META, F32, steps * rows),
            scratch(tiles * CHUNK, F32, LANES),
            scratch(tiles * CHUNK, BF16, LANES),
            pltpu.SemaphoreType.DMA((7,)),
        ],
        10**7,
        200000,
        hbm=6,
        out_places=[pltpu.VMEM, pltpu.HBM],
    )(
        flat,
        jnp.transpose(report_owner[0], (0, 2, 1)),
        jnp.transpose(report_stencil[0], (0, 2, 1)),
        jnp.transpose(report_weights[0], (0, 2, 1)),
        report_precision[0],
        report_values[0].reshape(steps * rows, LANES),
    )
    sent = kernel_call(
        tile_kernel, spec(groups * (cols + 2), BF16), [scratch(groups * 2)], 1000, 400000
    )(held, mate)
    oth = lax.ppermute(sent, "tile", other_of)
    arrived = lax.all_to_all(packed, "tile", split_axis=0, concat_axis=0, tiled=True)

    message, near4 = kernel_call(
        relay_kernel, [spec(size + 4 * groups), spec(4 * groups)], [scratch(size)], 1000, 700000
    )(held, mate, oth)
    nxt = across(message, 1, straight)
    wide = groups * WIDE
    slim = groups * SLIM
    edge0, u1x, d0x, d1x, f2x, field, final = kernel_call(
        forward_kernel,
        [spec(groups * 8), spec(slim)] + [spec(slim, BF16)] * 3
        + [spec(4 * lats * cols, F32, members * LANES), spec(size, BF16)],
        [scratch(wide), scratch(wide), scratch(wide, BF16), scratch(wide, BF16), scratch(wide, BF16)]
        + [scratch(wide), scratch(16), scratch(4 * size, BF16)]
        + [scratch(1), scratch(channels, BF16), scratch(channels, BF16), scratch(channels, BF16)]
        + [scratch(channels, BF16, LANES), pltpu.SemaphoreType.DMA((5,))],
        10**11,
        4000000,
        hbm=5,
    )(gain, self_weight, neighbour_weight, output_weight, readout, message, near4, oth)
    before = across(final, -1, straight)
    total = -(-tiles // SENDERS) * LANES
    handed = [self_weight, neighbour_weight, output_weight, readout, gain, error]
    handed += [flat, background.reshape(size, channels)]
    pull1, pull2, message, *handed = kernel_call(
        functools.partial(observe_kernel, tiles),
        [spec(slim), spec(slim), spec(size, F32, LANES)]
        + [jax.ShapeDtypeStruct(block.shape, block.dtype) for block in handed],
        [scratch(128, BF16, total)] * 4
        + [scratch(total, F32, LANES), scratch(4 * size, BF16, LANES), scratch(tiles * CHUNK, F32, LANES)]
        + [pltpu.SemaphoreType.DMA((8,))],
        10**9,
        2000000,
        hbm=8,
    )(*handed, arrived, field)
    ws, wn, wo, readout, gain, error, held, background = handed
    from_mate = lax.ppermute(message, "tile", mate_of)
    base = kernel_call(
        backward_kernel,
        spec(size),
        [scratch(slim), scratch(slim), scratch(slim), scratch(slim, BF16), scratch(slim), scratch(slim)]
        + [scratch(size), scratch(16), scratch(slim), scratch(slim)],
        12 * slim * channels * channels,
        6000000,
    )(held, edge0, u1x, d0x, d1x, f2x, pull1, pull2, from_mate, nxt, ws, wn, wo, gain, error, readout)
    result = kernel_call(last_kernel, spec(size), [], 10**6, 900000)(base, background, before, error)
    return result.reshape(control.shape)


def solution(mesh):
    in_specs = (
        P("slot", None, None, "tile", None),
        P(None, None, "tile", None),
        P(),
        P(),
        P(),
        P(),
        P(),
        P(),
        P("slot", None, "tile", None),
        P("slot", None, "tile", None),
        P("slot", None, "tile", None),
        P("slot", None, "tile", None),
        P("slot", None, "tile"),
    )
    out_specs = P("slot", None, None, "tile", None)
    return jax.shard_map(
        per_device, mesh=mesh, in_specs=in_specs, out_specs=out_specs, check_vma=False
    )
```

```python
import functools
import jax
import jax.numpy as jnp
from jax import lax
from jax.experimental import pallas as pl
from jax.experimental.pallas import tpu as pltpu
from jax.sharding import PartitionSpec as P

EPSILON = 1e-06
F32 = jnp.float32
BF16 = jnp.bfloat16
LANES = 128
CAP = 5
SLOTS = 4 * CAP
CHUNK = 32
META = 16
SENDERS = LANES // SLOTS
WIDE = 40
SLIM = 24
VMEM_LIMIT = 28 * 1024 * 1024


def dot(a, b):
    return jnp.dot(a, b, preferred_element_type=F32)


def dot_t(a, b):
    return lax.dot_general(a, b, (((1,), (1,)), ((), ())), preferred_element_type=F32)


def sublane(shape):
    return lax.broadcasted_iota(jnp.int32, shape, 0)


def inverse_rms(x):
    return lax.rsqrt(jnp.mean(x * x, axis=-1, keepdims=True) + EPSILON)


def sigmoid(p):
    return 0.5 * jnp.tanh(0.5 * p) + 0.5


def neighbours(rows):
    width = rows[0].shape[0]
    return [
        0.25 * (rows[1 - i] + pltpu.roll(rows[i], 1, 0) + pltpu.roll(rows[i], width - 1, 0))
        for i in range(2)
    ]


def forward_step(u, n, mean, act, pre, d, gain, ws, wn, wo, width, members, out, copies=()):
    both = 2 * width
    for m in range(members):
        base = m * both
        rows = []
        for lat in range(2):
            x = u[base + lat * width : base + (lat + 1) * width]
            rows.append((x * inverse_rms(x) * gain).astype(BF16).astype(F32))
        n[base : base + both] = jnp.concatenate(rows, axis=0).astype(BF16)
        mean[base : base + both] = jnp.concatenate(neighbours(rows), axis=0).astype(BF16)
    for copy in copies[:2]:
        copy.wait()
    pre[...] = dot(n[...], ws[...]) + dot(mean[...], wn[...])
    for m in range(members):
        base = m * both
        p = pre[base : base + both]
        sig = sigmoid(p)
        act[base : base + both] = (p * sig).astype(BF16)
        if d is not None:
            pre[base : base + both] = sig * (1.0 + p * (1.0 - sig))
    if d is not None:
        for m in range(members):
            slim_copy(d, pre, m)
    for copy in copies[2:]:
        copy.wait()
    pre[...] = dot(act[...], wo[...])
    for r in range(2 * members):
        out(r, u[r * width : (r + 1) * width] + pre[r * width : (r + 1) * width])


def slim_edge(wide, r):
    low = wide[r * WIDE + 16 : r * WIDE + 24]
    high = wide[r * WIDE + 32 : r * WIDE + 40]
    return jnp.where(sublane(low.shape) < 4, low, high)


def slim_copy(to, wide, m):
    parts = []
    for r in (2 * m, 2 * m + 1):
        parts += [wide[r * WIDE : r * WIDE + 16], slim_edge(wide, r)]
    both = jnp.concatenate(parts, axis=0)
    to[m * 2 * SLIM : (m + 1) * 2 * SLIM] = both.astype(to.dtype)


def first_kernel(
    control_hbm, owner_hbm, stencil_hbm, weights_hbm, precision_hbm, values_hbm,
    held, out_hbm,
    owner, stencil, weights, precision, values, key, meta, picked, out, sems,
):
    pairs = (
        (owner_hbm, owner), (stencil_hbm, stencil), (weights_hbm, weights),
        (precision_hbm, precision), (values_hbm, values), (control_hbm, held),
    )
    copies = [pltpu.make_async_copy(source, to, sems.at[i]) for i, (source, to) in enumerate(pairs)]
    for copy in copies:
        copy.start()
    for copy in copies[:5]:
        copy.wait()
    pack(owner, stencil, weights, precision, values, out, key, meta, picked)
    store = pltpu.make_async_copy(out, out_hbm, sems.at[len(pairs)])
    store.start()
    for copy in copies[5:]:
        copy.wait()
    store.wait()


def pack(owner, stencil, weights, precision, values, out, key, meta, picked):
    steps, _, rows = owner.shape
    tiles = out.shape[0] // CHUNK
    total = steps * rows
    place = lax.axis_index("tile") % SENDERS * SLOTS
    earlier = lax.broadcasted_iota(jnp.int32, (rows, rows), 0) < lax.broadcasted_iota(jnp.int32, (rows, rows), 1)
    earlier = earlier.astype(F32).astype(BF16)
    meta[...] = jnp.zeros_like(meta)
    for k in range(steps):
        at = slice(k * rows, (k + 1) * rows)
        named = lax.broadcasted_iota(jnp.int32, (tiles, rows), 0) == owner[k]
        hits = named.astype(F32)
        before = dot(hits.astype(BF16), earlier)
        rank = jnp.sum(hits * before, axis=0, keepdims=True).astype(jnp.int32)
        key[0:1, at] = owner[k] * (2 * CAP) + k * CAP + rank
        meta[4:8, at] = stencil[k].astype(F32)
        meta[8:12, at] = weights[k].astype(F32)
        meta[12:13, at] = precision[k : k + 1].astype(F32)
    row = lax.broadcasted_iota(jnp.int32, (tiles * CHUNK, total), 0)
    tile = row // CHUNK
    slot = row % CHUNK
    other = jnp.where(tile % 2 == 0, (tile + tiles - 1) % tiles, (tile + 1) % tiles)
    mine = slot < 2 * CAP
    wanted = jnp.where(mine, tile * (2 * CAP) + slot, other * (2 * CAP) + slot - 2 * CAP)
    wanted = jnp.where(slot < SLOTS, wanted, -1)
    placement = (wanted == key[...]).astype(F32).astype(BF16)
    picked[...] = dot(placement, values[...])
    entries = dot_t(meta[...].astype(BF16), placement)
    lane = lax.broadcasted_iota(jnp.int32, (META, LANES), 1)
    used = jnp.logical_and(lane >= place, lane < place + SLOTS)
    per_tile = LANES // CHUNK
    for t in range(tiles):
        block = entries[:, t // per_tile * LANES : (t // per_tile + 1) * LANES]
        shift = (place + LANES - t % per_tile * CHUNK) % LANES
        block = jnp.where(used, pltpu.roll(block, shift, 1), 0.0)
        low = picked[t * CHUNK + 16 : (t + 1) * CHUNK]
        picked[t * CHUNK + 16 : (t + 1) * CHUNK] = jnp.where(sublane((META, 1)) < 4, low, block)
    out[...] = picked[...].astype(BF16)


def tile_kernel(control, mate, out, held):
    even = lax.rem(lax.axis_index("tile"), 2) == 0
    size = control.shape[0]
    out[0:size] = control[...].astype(BF16)
    for r in range(size // 16):
        held[r * 2 : (r + 1) * 2] = jnp.where(
            even, mate[r * 16 : r * 16 + 2], mate[r * 16 + 14 : (r + 1) * 16]
        )
    out[size:] = held[...].astype(BF16)


def relay_kernel(control, mate, oth, out, near4, wide):
    even = lax.rem(lax.axis_index("tile"), 2) == 0
    size = control.shape[0]
    edge = size // 8
    out[0:size] = control[...]
    wide[...] = oth[0:size].astype(F32)
    for r in range(size // 16):
        a, b = r * 16, (r + 1) * 16
        out[size + r * 2 : size + (r + 1) * 2] = jnp.where(even, wide[b - 2 : b], wide[a : a + 2])
        near4[r * 4 : (r + 1) * 4] = jnp.where(even, mate[a : a + 4], mate[b - 4 : b])
        start = size + edge + r * 2
        out[start : start + 2] = jnp.where(even, mate[a : a + 2], mate[b - 2 : b])


def forward_kernel(
    gain_hbm, ws_hbm, wn_hbm, wo_hbm, readout_hbm, control, mate, oth,
    edge0, u1x, d0x, d1x, f2x, field, final,
    ua, ub, n, mean, act, pre, edge, states, gain, ws, wn, wo, readout, sems,
):
    pairs = ((gain_hbm, gain), (ws_hbm, ws), (wn_hbm, wn), (wo_hbm, wo), (readout_hbm, readout))
    copies = [pltpu.make_async_copy(source, to, sems.at[i]) for i, (source, to) in enumerate(pairs)]
    for copy in copies:
        copy.start()
    members = final.shape[0] // 32
    even = lax.rem(lax.axis_index("tile"), 2) == 0
    tile_at = jnp.where(even, 24, 16)
    edge_at = jnp.where(even, 16, 32)
    far = oth[members * 32 :].astype(F32)
    for r in range(2 * members):
        ua[r * WIDE : r * WIDE + 16] = control[r * 16 : (r + 1) * 16]
        ua[pl.ds(pl.multiple_of(r * WIDE + tile_at, 8), 16)] = oth[r * 16 : (r + 1) * 16].astype(F32)
        near4 = mate[r * 4 : (r + 1) * 4]
        far2 = far[r * 2 : (r + 1) * 2]
        edge[...] = jnp.zeros_like(edge)
        edge[0:4] = near4
        edge[6:8] = far2
        edge[8:10] = far2
        edge[12:16] = near4
        ua[pl.ds(pl.multiple_of(r * WIDE + edge_at, 8), 8)] = jnp.where(even, edge[0:8], edge[8:16])
    for r in range(2 * members):
        edge0[r * 8 : (r + 1) * 8] = slim_edge(ua, r)
    copies[0].wait()
    g = gain[...]

    def keep(ref):
        def store(r, value):
            ref[r * WIDE : (r + 1) * WIDE] = value

        return store

    def keep_states(ref, k):
        own = k * members * 32
        away = (2 + k) * members * 32
        for r in range(2 * members):
            states[own + r * 16 : own + (r + 1) * 16] = ref[r * WIDE : r * WIDE + 16].astype(BF16)
            taken = ref[pl.ds(pl.multiple_of(r * WIDE + tile_at, 8), 16)]
            states[away + r * 16 : away + (r + 1) * 16] = taken.astype(BF16)

    forward_step(ua, n, mean, act, pre, d0x, g, ws, wn, wo, WIDE, members, keep(ub), copies[1:])
    for m in range(members):
        slim_copy(u1x, ub, m)
    keep_states(ub, 0)
    forward_step(ub, n, mean, act, pre, d1x, g, ws, wn, wo, WIDE, members, keep(ua))
    for m in range(members):
        slim_copy(f2x, ua, m)
    keep_states(ua, 1)
    final[...] = states[members * 32 : 2 * members * 32]
    read = dot(states[...], readout[...])
    for q in range(4):
        for m in range(members):
            start = (q * members + m) * 32
            field[q * 32 : (q + 1) * 32, m * LANES : (m + 1) * LANES] = read[start : start + 32]


def split(x):
    high = x.astype(BF16)
    return high, (x - high.astype(F32)).astype(BF16)


def observe_kernel(
    tiles,
    readout_hbm, error_hbm, wo_hbm, arrived, field,
    spread, message, readout, error, wo,
    th, tl, ph, plo, vals, wide, sems,
):
    pairs = ((readout_hbm, readout), (error_hbm, error), (wo_hbm, wo))
    copies = [pltpu.make_async_copy(source, to, sems.at[i]) for i, (source, to) in enumerate(pairs)]
    for copy in copies:
        copy.start()
    steps = 2
    members = field.shape[1] // LANES
    even = lax.rem(lax.axis_index("tile"), 2) == 0
    cells = sublane((32, LANES)).astype(F32)
    lane = lax.broadcasted_iota(jnp.int32, (1, LANES), 1)
    table_of = jnp.where(lane < SENDERS * SLOTS, lane % SLOTS // CAP, -1)
    wide[...] = arrived[...].astype(F32)
    vals[...] = jnp.zeros_like(vals)
    for p in range(th.shape[1] // LANES):
        meta = jnp.zeros((META, LANES), F32)
        for d in range(p * SENDERS, min((p + 1) * SENDERS, tiles)):
            meta += wide[d * CHUNK + 16 : (d + 1) * CHUNK]
            start = p * LANES + d % SENDERS * SLOTS
            vals[start : start + SLOTS] = wide[d * CHUNK : d * CHUNK + SLOTS]
        weight = jnp.zeros((32, LANES), F32)
        for i in range(4):
            weight += jnp.where(cells == meta[4 + i : 5 + i], meta[8 + i : 9 + i], 0.0)
        scaled = weight * meta[12:13]
        wh, wl = split(weight)
        sh, sl = split(scaled)
        parts = ((th, wh.astype(F32)), (tl, wl.astype(F32)), (ph, sh.astype(F32)), (plo, sl.astype(F32)))
        for q in range(2 * steps):
            hit = table_of == q
            for ref, value in parts:
                kept = jnp.where(hit, value, 0.0).astype(BF16)
                ref[q * 32 : (q + 1) * 32, p * LANES : (p + 1) * LANES] = kept
    cross = dot_t(ph[...], th[...]) + dot_t(plo[...], th[...]) + dot_t(ph[...], tl[...])
    taken = vals[...].astype(BF16)
    target = dot(ph[...], taken) + dot(plo[...], taken)
    ch, cl = split(cross)
    fh, fl = split(field[...])
    mixed = dot(ch, fh) + dot(cl, fh) + dot(ch, fl)
    for q in range(2 * steps):
        for m in range(members):
            start = (q * members + m) * 32
            value = mixed[q * 32 : (q + 1) * 32, m * LANES : (m + 1) * LANES] - target[q * 32 : (q + 1) * 32]
            spread[start : start + 32] = value.astype(BF16)
    size = members * 32
    for k in range(steps):
        for m in range(members):
            start = k * size + m * 32
            pair = spread[start : start + 32].astype(F32)
            near = [jnp.where(even, pair[i + 8 : i + 16], pair[i : i + 8]) for i in (0, 16)]
            start = k * size // 2 + m * 16
            message[start : start + 16] = jnp.concatenate(near, axis=0).astype(BF16)
    for copy in copies:
        copy.wait()


def finish_adjoint(u, parts, add, out, gain, members):
    for m in range(members):
        rows = [parts(2 * m + lat) for lat in range(2)]
        around = neighbours([row[1].astype(BF16).astype(F32) for row in rows])
        for lat in range(2):
            r = 2 * m + lat
            start = r * SLIM
            x = u[start : start + SLIM]
            s = inverse_rms(x)
            scaled = gain * (rows[lat][2] + around[lat])
            inner = jnp.mean(x * scaled, axis=-1, keepdims=True)
            value = rows[lat][0] + s * scaled - x * (s * s * s * inner)
            if add is not None:
                value = value + add(r)
            out[start : start + SLIM] = value


def edges(nxt, size, edge, r):
    even = lax.rem(lax.axis_index("tile"), 2) == 0
    start = size + r * 2
    far = nxt[start : start + 2]
    start = size + size // 8 + r * 2
    near = nxt[start : start + 2]
    edge[...] = jnp.zeros_like(edge)
    edge[0:2] = near
    edge[6:8] = far
    edge[8:10] = far
    edge[14:16] = near
    return jnp.where(even, edge[0:8], edge[8:16])


def own_kernel(
    wn_hbm, ws_hbm, spread, readout, error, wo, nxt, f2x, d1x,
    cot_own, cot_edge, add_own, add_edge, gm_own, flat_own, wn, ws,
    pulled, final, gb, edge, d, sems,
):
    pairs = ((wn_hbm, wn), (ws_hbm, ws))
    copies = [pltpu.make_async_copy(source, to, sems.at[i]) for i, (source, to) in enumerate(pairs)]
    for copy in copies:
        copy.start()
    size = cot_own.shape[0]
    even = lax.rem(lax.axis_index("tile"), 2) == 0
    later = jnp.where(lax.axis_index("slot") == lax.axis_size("slot") - 1, 0.0, 1.0)
    weight = later * error[...]
    row8 = sublane((8, 1))
    pulled[...] = dot_t(spread[...], readout[...])
    final[...] = f2x[...].astype(F32)
    d[...] = d1x[...].astype(F32)

    def other_edge(k, r):
        start = (2 + k) * size + r * 16
        low = jnp.where(row8 < 4, pulled[start : start + 8], 0.0)
        high = jnp.where(row8 >= 4, pulled[start + 8 : start + 16], 0.0)
        return jnp.where(even, high, low)

    for r in range(size // 16):
        a, b = r * 16, (r + 1) * 16
        at = r * SLIM
        value = pulled[size + a : size + b] - weight * (nxt[a:b] - final[at : at + 16])
        cot_own[a:b] = value
        gb[a:b] = value.astype(BF16)
        misfit = weight * (edges(nxt, size, edge, r) - final[at + 16 : at + 24])
        cot_edge[r * 8 : (r + 1) * 8] = other_edge(1, r) - misfit
        add_own[a:b] = pulled[a:b]
        add_edge[r * 8 : (r + 1) * 8] = other_edge(0, r)
    flat_own[...] = dot_t(gb[...], wo[...])
    for r in range(size // 16):
        a, b = r * 16, (r + 1) * 16
        gb[a:b] = (flat_own[a:b] * d[r * SLIM : r * SLIM + 16]).astype(BF16)
    copies[0].wait()
    gm_own[...] = dot_t(gb[...], wn[...])
    copies[1].wait()
    flat_own[...] = dot_t(gb[...], ws[...])


def backward_kernel(
    gain_hbm, control_hbm, background_hbm, error, readout, wo, wn, ws, message, edge0, u1x, d0x, d1x,
    cot_own, cot_edge, add_own, add_edge, gm_own, flat_own,
    result, background,
    cot, gb, gm, flat, mate_pull, u0x, d, gain, control, cot_all, add_all, gb_edge, gm_edge, flat_edge, sems,
):
    pairs = ((gain_hbm, gain), (control_hbm, control), (background_hbm, background))
    copies = [pltpu.make_async_copy(source, to, sems.at[i]) for i, (source, to) in enumerate(pairs)]
    for copy in copies:
        copy.start()
    size = result.shape[0]
    members = size // 32
    half = size // 2
    even = lax.rem(lax.axis_index("tile"), 2) == 0
    row8 = sublane((8, 1))
    mate_side = jnp.where(even, 1, 0) == jnp.where(row8 < 4, 1, 0)
    mate_pull[...] = dot_t(message[...], readout[...])
    d[...] = d1x[...].astype(F32)
    for r in range(2 * members):
        a, b = r * 8, (r + 1) * 8
        cot_all[a:b] = cot_edge[a:b] + jnp.where(mate_side, mate_pull[half + a : half + b], 0.0)
        add_all[a:b] = add_edge[a:b] + jnp.where(mate_side, mate_pull[a:b], 0.0)
    gb_edge[...] = cot_all[...].astype(BF16)
    gm_edge[...] = dot_t(gb_edge[...], wo[...])
    for r in range(2 * members):
        a, b = r * 8, (r + 1) * 8
        gm_edge[a:b] = gm_edge[a:b] * d[r * SLIM + 16 : (r + 1) * SLIM]
    gb_edge[...] = gm_edge[...].astype(BF16)
    gm_edge[...] = dot_t(gb_edge[...], wn[...])
    flat_edge[...] = dot_t(gb_edge[...], ws[...])

    def joined(own, edge, r):
        return jnp.concatenate([own[r * 16 : (r + 1) * 16], edge[r * 8 : (r + 1) * 8]], axis=0)

    def first(r):
        return joined(cot_own, cot_all, r), joined(gm_own, gm_edge, r), joined(flat_own, flat_edge, r)

    copies[0].wait()
    finish_adjoint(u1x, first, lambda r: joined(add_own, add_all, r), cot, gain[...], members)
    for copy in copies[1:]:
        copy.wait()
    for r in range(2 * members):
        u0x[r * SLIM : r * SLIM + 16] = control[r * 16 : (r + 1) * 16]
        u0x[r * SLIM + 16 : (r + 1) * SLIM] = edge0[r * 8 : (r + 1) * 8]
    gb[...] = cot[...].astype(BF16)
    flat[...] = dot_t(gb[...], wo[...])
    gb[...] = (flat[...] * d0x[...].astype(F32)).astype(BF16)
    gm[...] = dot_t(gb[...], wn[...])
    flat[...] = dot_t(gb[...], ws[...])

    def second(r):
        at = slice(r * SLIM, (r + 1) * SLIM)
        return cot[at], gm[at], flat[at]

    finish_adjoint(u0x, second, None, cot, gain[...], members)
    for r in range(2 * members):
        a, b = r * 16, (r + 1) * 16
        result[a:b] = cot[r * SLIM : r * SLIM + 16] + error[...] * control[a:b]


def last_kernel(base, background, before, error, result):
    first = lax.axis_index("slot") == 0
    taken = jnp.where(first, background[...].astype(F32), before[...].astype(F32))
    result[...] = base[...] - error[...] * taken


def kernel_call(body, outs, scratch, flops, moved, hbm=0, out_places=None):
    def call(*operands):
        operands = [pltpu.with_memory_space_constraint(x, pltpu.HBM) for x in operands[:hbm]] + list(operands[hbm:])
        places = [pltpu.HBM] * hbm + [pltpu.VMEM] * (len(operands) - hbm)
        given = {} if out_places is None else {"out_specs": [pl.BlockSpec(memory_space=p) for p in out_places]}
        return pl.pallas_call(
            body,
            out_shape=outs,
            in_specs=[pl.BlockSpec(memory_space=place) for place in places],
            **given,
            scratch_shapes=scratch,
            compiler_params=pltpu.CompilerParams(vmem_limit_bytes=VMEM_LIMIT),
            cost_estimate=pl.CostEstimate(flops=flops, bytes_accessed=moved, transcendentals=0),
        )(*operands)

    return call


def per_device(
    control,
    background,
    self_weight,
    neighbour_weight,
    output_weight,
    norm_gain,
    readout,
    error_weight,
    report_owner,
    report_stencil,
    report_weights,
    report_values,
    report_precision,
):
    tiles = lax.axis_size("tile")
    slots = lax.axis_size("slot")
    members, lats, cols, channels = control.shape[1:]
    groups = members * lats
    size = groups * cols
    steps = report_owner.shape[1]
    rows = report_owner.shape[2]
    gain = norm_gain.reshape(1, channels)
    error = error_weight.reshape(1, channels)
    flat = control.reshape(size, channels)

    def spec(count, dtype=F32, width=channels):
        return jax.ShapeDtypeStruct((count, width), dtype)

    def scratch(count, dtype=F32, width=channels):
        return pltpu.VMEM((count, width), dtype)

    mate_of = [(i, i ^ 1) for i in range(tiles)]
    other_of = [(i, (i - 1) % tiles if i % 2 == 0 else (i + 1) % tiles) for i in range(tiles)]

    def across(block, shift, route):
        pairs = [
            (((s + shift) % slots) * tiles + i, s * tiles + j)
            for s in range(slots)
            for i, j in route
        ]
        return lax.ppermute(block, ("slot", "tile"), pairs)

    straight = [(i, i) for i in range(tiles)]
    mate = lax.ppermute(flat, "tile", mate_of)
    held, packed = kernel_call(
        first_kernel,
        [spec(size), spec(tiles * CHUNK, BF16, LANES)],
        [
            pltpu.VMEM((steps, 1, rows), jnp.int32),
            pltpu.VMEM((steps, 4, rows), jnp.int32),
            pltpu.VMEM((steps, 4, rows), BF16),
            pltpu.VMEM((steps, rows), BF16),
            scratch(steps * rows, BF16, LANES),
            pltpu.VMEM((1, steps * rows), jnp.int32),
            scratch(META, F32, steps * rows),
            scratch(tiles * CHUNK, F32, LANES),
            scratch(tiles * CHUNK, BF16, LANES),
            pltpu.SemaphoreType.DMA((7,)),
        ],
        10**7,
        200000,
        hbm=6,
        out_places=[pltpu.VMEM, pltpu.HBM],
    )(
        flat,
        jnp.transpose(report_owner[0], (0, 2, 1)),
        jnp.transpose(report_stencil[0], (0, 2, 1)),
        jnp.transpose(report_weights[0], (0, 2, 1)),
        report_precision[0],
        report_values[0].reshape(steps * rows, LANES),
    )
    sent = kernel_call(
        tile_kernel, spec(groups * (cols + 2), BF16), [scratch(groups * 2)], 1000, 400000
    )(held, mate)
    oth = lax.ppermute(sent, "tile", other_of)
    arrived = lax.all_to_all(packed, "tile", split_axis=0, concat_axis=0, tiled=True)

    message, near4 = kernel_call(
        relay_kernel, [spec(size + 4 * groups), spec(4 * groups)], [scratch(size)], 1000, 700000
    )(held, mate, oth)
    nxt = across(message, 1, straight)
    wide = groups * WIDE
    slim = groups * SLIM
    edge0, u1x, d0x, d1x, f2x, field, final = kernel_call(
        forward_kernel,
        [spec(groups * 8), spec(slim)] + [spec(slim, BF16)] * 3
        + [spec(4 * lats * cols, F32, members * LANES), spec(size, BF16)],
        [scratch(wide), scratch(wide), scratch(wide, BF16), scratch(wide, BF16), scratch(wide, BF16)]
        + [scratch(wide), scratch(16), scratch(4 * size, BF16)]
        + [scratch(1), scratch(channels, BF16), scratch(channels, BF16), scratch(channels, BF16)]
        + [scratch(channels, BF16, LANES), pltpu.SemaphoreType.DMA((5,))],
        10**11,
        4000000,
        hbm=5,
    )(gain, self_weight, neighbour_weight, output_weight, readout, message, near4, oth)
    before = across(final, -1, straight)
    total = -(-tiles // SENDERS) * LANES
    spread, near_spread, readout_held, error_held, wo = kernel_call(
        functools.partial(observe_kernel, tiles),
        [spec(4 * size, BF16, LANES), spec(size, BF16, LANES)]
        + [spec(channels, BF16, LANES), spec(1), spec(channels, BF16)],
        [scratch(128, BF16, total)] * 4
        + [scratch(total, F32, LANES), scratch(tiles * CHUNK, F32, LANES), pltpu.SemaphoreType.DMA((3,))],
        10**9,
        2000000,
        hbm=3,
    )(readout, error, output_weight, arrived, field)
    from_mate = lax.ppermute(near_spread, "tile", mate_of)
    *own, wn, ws = kernel_call(
        own_kernel,
        [spec(size), spec(size // 2), spec(size), spec(size // 2), spec(size), spec(size)]
        + [spec(channels, BF16), spec(channels, BF16)],
        [scratch(4 * size), scratch(slim), scratch(size, BF16), scratch(16), scratch(slim)]
        + [pltpu.SemaphoreType.DMA((2,))],
        10**9,
        3000000,
        hbm=2,
    )(neighbour_weight, self_weight, spread, readout_held, error_held, wo, nxt, f2x, d1x)
    base, background_held = kernel_call(
        backward_kernel,
        [spec(size), spec(size, BF16)],
        [scratch(slim), scratch(slim, BF16), scratch(slim), scratch(slim), scratch(size), scratch(slim)]
        + [scratch(slim), scratch(1), scratch(size), scratch(size // 2), scratch(size // 2)]
        + [scratch(size // 2, BF16), scratch(size // 2), scratch(size // 2), pltpu.SemaphoreType.DMA((3,))],
        12 * slim * channels * channels,
        6000000,
        hbm=3,
    )(
        gain, flat, background.reshape(size, channels), error_held, readout_held, wo, wn, ws, from_mate,
        edge0, u1x, d0x, d1x, *own,
    )
    result = kernel_call(last_kernel, spec(size), [], 10**6, 900000)(base, background_held, before, error_held)
    return result.reshape(control.shape)


def solution(mesh):
    in_specs = (
        P("slot", None, None, "tile", None),
        P(None, None, "tile", None),
        P(),
        P(),
        P(),
        P(),
        P(),
        P(),
        P("slot", None, "tile", None),
        P("slot", None, "tile", None),
        P("slot", None, "tile", None),
        P("slot", None, "tile", None),
        P("slot", None, "tile"),
    )
    out_specs = P("slot", None, None, "tile", None)
    return jax.shard_map(
        per_device, mesh=mesh, in_specs=in_specs, out_specs=out_specs, check_vma=False
    )
```

```python
import functools
import jax
import jax.numpy as jnp
from jax import lax
from jax.experimental import pallas as pl
from jax.experimental.pallas import tpu as pltpu
from jax.sharding import PartitionSpec as P

EPSILON = 1e-06
F32 = jnp.float32
BF16 = jnp.bfloat16
LANES = 128
CAP = 5
SLOTS = 4 * CAP
CHUNK = 32
META = 16
SENDERS = LANES // SLOTS
WIDE = 40
SLIM = 24
VMEM_LIMIT = 28 * 1024 * 1024


def dot(a, b):
    return jnp.dot(a, b, preferred_element_type=F32)


def dot_t(a, b):
    return lax.dot_general(a, b, (((1,), (1,)), ((), ())), preferred_element_type=F32)


def sublane(shape):
    return lax.broadcasted_iota(jnp.int32, shape, 0)


def inverse_rms(x):
    return lax.rsqrt(jnp.mean(x * x, axis=-1, keepdims=True) + EPSILON)


def sigmoid(p):
    return 0.5 * jnp.tanh(0.5 * p) + 0.5


def neighbours(rows):
    width = rows[0].shape[0]
    return [
        0.25 * (rows[1 - i] + pltpu.roll(rows[i], 1, 0) + pltpu.roll(rows[i], width - 1, 0))
        for i in range(2)
    ]


def forward_step(u, n, mean, act, pre, d, gain, ws, wn, wo, width, members, out, copies=()):
    both = 2 * width
    for m in range(members):
        base = m * both
        rows = []
        for lat in range(2):
            x = u[base + lat * width : base + (lat + 1) * width]
            rows.append((x * inverse_rms(x) * gain).astype(BF16).astype(F32))
        n[base : base + both] = jnp.concatenate(rows, axis=0).astype(BF16)
        mean[base : base + both] = jnp.concatenate(neighbours(rows), axis=0).astype(BF16)
    for copy in copies[:2]:
        copy.wait()
    pre[...] = dot(n[...], ws[...]) + dot(mean[...], wn[...])
    for m in range(members):
        base = m * both
        p = pre[base : base + both]
        sig = sigmoid(p)
        act[base : base + both] = (p * sig).astype(BF16)
        if d is not None:
            pre[base : base + both] = sig * (1.0 + p * (1.0 - sig))
    if d is not None:
        for m in range(members):
            slim_copy(d, pre, m)
    for copy in copies[2:]:
        copy.wait()
    pre[...] = dot(act[...], wo[...])
    for r in range(2 * members):
        out(r, u[r * width : (r + 1) * width] + pre[r * width : (r + 1) * width])


def slim_edge(wide, r):
    low = wide[r * WIDE + 16 : r * WIDE + 24]
    high = wide[r * WIDE + 32 : r * WIDE + 40]
    return jnp.where(sublane(low.shape) < 4, low, high)


def slim_copy(to, wide, m):
    parts = []
    for r in (2 * m, 2 * m + 1):
        parts += [wide[r * WIDE : r * WIDE + 16], slim_edge(wide, r)]
    both = jnp.concatenate(parts, axis=0)
    to[m * 2 * SLIM : (m + 1) * 2 * SLIM] = both.astype(to.dtype)


def reports(sources, out_hbm, buffers, key, meta, picked, out, sems):
    copies = [
        pltpu.make_async_copy(source, to, sems.at[i]) for i, (source, to) in enumerate(zip(sources, buffers))
    ]
    for copy in copies:
        copy.start()
    for copy in copies:
        copy.wait()
    pack(*buffers, out, key, meta, picked)
    store = pltpu.make_async_copy(out, out_hbm, sems.at[len(copies)])
    store.start()
    store.wait()


def early():
    return lax.axis_index("tile") < lax.axis_size("tile") // 2


def first_kernel(control_hbm, *refs):
    sources, (held, out_hbm), rest = refs[:5], refs[5:7], refs[7:]
    buffers, (key, meta, picked, out, sems, sem) = rest[:5], rest[5:]
    fetch = pltpu.make_async_copy(control_hbm, held, sem)
    fetch.start()

    @pl.when(early())
    def _():
        reports(sources, out_hbm, buffers, key, meta, picked, out, sems)

    fetch.wait()


def later_kernel(packed_hbm, *refs):
    sources, out_hbm, rest = refs[:5], refs[6], refs[7:]
    buffers, (key, meta, picked, out, sems) = rest[:5], rest[5:]

    @pl.when(jnp.logical_not(early()))
    def _():
        reports(sources, out_hbm, buffers, key, meta, picked, out, sems)


def pack(owner, stencil, weights, precision, values, out, key, meta, picked):
    steps, _, rows = owner.shape
    tiles = out.shape[0] // CHUNK
    total = steps * rows
    place = lax.axis_index("tile") % SENDERS * SLOTS
    earlier = lax.broadcasted_iota(jnp.int32, (rows, rows), 0) < lax.broadcasted_iota(jnp.int32, (rows, rows), 1)
    earlier = earlier.astype(F32).astype(BF16)
    meta[...] = jnp.zeros_like(meta)
    for k in range(steps):
        at = slice(k * rows, (k + 1) * rows)
        named = lax.broadcasted_iota(jnp.int32, (tiles, rows), 0) == owner[k]
        hits = named.astype(F32)
        before = dot(hits.astype(BF16), earlier)
        rank = jnp.sum(hits * before, axis=0, keepdims=True).astype(jnp.int32)
        key[0:1, at] = owner[k] * (2 * CAP) + k * CAP + rank
        meta[4:8, at] = stencil[k].astype(F32)
        meta[8:12, at] = weights[k].astype(F32)
        meta[12:13, at] = precision[k : k + 1].astype(F32)
    row = lax.broadcasted_iota(jnp.int32, (tiles * CHUNK, total), 0)
    tile = row // CHUNK
    slot = row % CHUNK
    other = jnp.where(tile % 2 == 0, (tile + tiles - 1) % tiles, (tile + 1) % tiles)
    mine = slot < 2 * CAP
    wanted = jnp.where(mine, tile * (2 * CAP) + slot, other * (2 * CAP) + slot - 2 * CAP)
    wanted = jnp.where(slot < SLOTS, wanted, -1)
    placement = (wanted == key[...]).astype(F32).astype(BF16)
    picked[...] = dot(placement, values[...])
    entries = dot_t(meta[...].astype(BF16), placement)
    lane = lax.broadcasted_iota(jnp.int32, (META, LANES), 1)
    used = jnp.logical_and(lane >= place, lane < place + SLOTS)
    per_tile = LANES // CHUNK
    for t in range(tiles):
        block = entries[:, t // per_tile * LANES : (t // per_tile + 1) * LANES]
        shift = (place + LANES - t % per_tile * CHUNK) % LANES
        block = jnp.where(used, pltpu.roll(block, shift, 1), 0.0)
        low = picked[t * CHUNK + 16 : (t + 1) * CHUNK]
        picked[t * CHUNK + 16 : (t + 1) * CHUNK] = jnp.where(sublane((META, 1)) < 4, low, block)
    out[...] = picked[...].astype(BF16)


def tile_kernel(control, mate, out, held):
    even = lax.rem(lax.axis_index("tile"), 2) == 0
    size = control.shape[0]
    out[0:size] = control[...].astype(BF16)
    for r in range(size // 16):
        held[r * 2 : (r + 1) * 2] = jnp.where(
            even, mate[r * 16 : r * 16 + 2], mate[r * 16 + 14 : (r + 1) * 16]
        )
    out[size:] = held[...].astype(BF16)


def relay_kernel(mate, oth, nxt, out, near4, wide):
    even = lax.rem(lax.axis_index("tile"), 2) == 0
    size = mate.shape[0]
    wide[...] = oth[0:size].astype(F32)
    for r in range(size // 16):
        a, b = r * 16, (r + 1) * 16
        out[r * 2 : (r + 1) * 2] = jnp.where(even, wide[b - 2 : b], wide[a : a + 2])
        near4[r * 4 : (r + 1) * 4] = jnp.where(even, mate[a : a + 4], mate[b - 4 : b])
        start = size // 8 + r * 2
        out[start : start + 2] = jnp.where(even, mate[a : a + 2], mate[b - 2 : b])


def forward_kernel(
    gain_hbm, ws_hbm, wn_hbm, wo_hbm, readout_hbm, control, mate, oth,
    edge0, u1x, d0x, d1x, f2x, field, final,
    ua, ub, n, mean, act, pre, edge, states, gain, ws, wn, wo, readout, sems,
):
    pairs = ((gain_hbm, gain), (ws_hbm, ws), (wn_hbm, wn), (wo_hbm, wo), (readout_hbm, readout))
    copies = [pltpu.make_async_copy(source, to, sems.at[i]) for i, (source, to) in enumerate(pairs)]
    for copy in copies:
        copy.start()
    members = final.shape[0] // 32
    even = lax.rem(lax.axis_index("tile"), 2) == 0
    tile_at = jnp.where(even, 24, 16)
    edge_at = jnp.where(even, 16, 32)
    far = oth[members * 32 :].astype(F32)
    for r in range(2 * members):
        ua[r * WIDE : r * WIDE + 16] = control[r * 16 : (r + 1) * 16]
        ua[pl.ds(pl.multiple_of(r * WIDE + tile_at, 8), 16)] = oth[r * 16 : (r + 1) * 16].astype(F32)
        near4 = mate[r * 4 : (r + 1) * 4]
        far2 = far[r * 2 : (r + 1) * 2]
        edge[...] = jnp.zeros_like(edge)
        edge[0:4] = near4
        edge[6:8] = far2
        edge[8:10] = far2
        edge[12:16] = near4
        ua[pl.ds(pl.multiple_of(r * WIDE + edge_at, 8), 8)] = jnp.where(even, edge[0:8], edge[8:16])
    for r in range(2 * members):
        edge0[r * 8 : (r + 1) * 8] = slim_edge(ua, r)
    copies[0].wait()
    g = gain[...]

    def keep(ref):
        def store(r, value):
            ref[r * WIDE : (r + 1) * WIDE] = value

        return store

    def keep_states(ref, k):
        own = k * members * 32
        away = (2 + k) * members * 32
        for r in range(2 * members):
            states[own + r * 16 : own + (r + 1) * 16] = ref[r * WIDE : r * WIDE + 16].astype(BF16)
            taken = ref[pl.ds(pl.multiple_of(r * WIDE + tile_at, 8), 16)]
            states[away + r * 16 : away + (r + 1) * 16] = taken.astype(BF16)

    forward_step(ua, n, mean, act, pre, d0x, g, ws, wn, wo, WIDE, members, keep(ub), copies[1:])
    for m in range(members):
        slim_copy(u1x, ub, m)
    keep_states(ub, 0)
    forward_step(ub, n, mean, act, pre, d1x, g, ws, wn, wo, WIDE, members, keep(ua))
    for m in range(members):
        slim_copy(f2x, ua, m)
    keep_states(ua, 1)
    final[...] = states[members * 32 : 2 * members * 32]
    read = dot(states[...], readout[...])
    for q in range(4):
        for m in range(members):
            start = (q * members + m) * 32
            field[q * 32 : (q + 1) * 32, m * LANES : (m + 1) * LANES] = read[start : start + 32]


def split(x):
    high = x.astype(BF16)
    return high, (x - high.astype(F32)).astype(BF16)


def observe_kernel(
    tiles,
    readout_hbm, error_hbm, arrived, field,
    spread, message, readout, error,
    th, tl, ph, plo, vals, wide, sems,
):
    pairs = ((readout_hbm, readout), (error_hbm, error))
    copies = [pltpu.make_async_copy(source, to, sems.at[i]) for i, (source, to) in enumerate(pairs)]
    for copy in copies:
        copy.start()
    steps = 2
    members = field.shape[1] // LANES
    even = lax.rem(lax.axis_index("tile"), 2) == 0
    cells = sublane((32, LANES)).astype(F32)
    lane = lax.broadcasted_iota(jnp.int32, (1, LANES), 1)
    table_of = jnp.where(lane < SENDERS * SLOTS, lane % SLOTS // CAP, -1)
    wide[...] = arrived[...].astype(F32)
    vals[...] = jnp.zeros_like(vals)
    for p in range(th.shape[1] // LANES):
        meta = jnp.zeros((META, LANES), F32)
        for d in range(p * SENDERS, min((p + 1) * SENDERS, tiles)):
            meta += wide[d * CHUNK + 16 : (d + 1) * CHUNK]
            start = p * LANES + d % SENDERS * SLOTS
            vals[start : start + SLOTS] = wide[d * CHUNK : d * CHUNK + SLOTS]
        weight = jnp.zeros((32, LANES), F32)
        for i in range(4):
            weight += jnp.where(cells == meta[4 + i : 5 + i], meta[8 + i : 9 + i], 0.0)
        scaled = weight * meta[12:13]
        wh, wl = split(weight)
        sh, sl = split(scaled)
        parts = ((th, wh.astype(F32)), (tl, wl.astype(F32)), (ph, sh.astype(F32)), (plo, sl.astype(F32)))
        for q in range(2 * steps):
            hit = table_of == q
            for ref, value in parts:
                kept = jnp.where(hit, value, 0.0).astype(BF16)
                ref[q * 32 : (q + 1) * 32, p * LANES : (p + 1) * LANES] = kept
    cross = dot_t(ph[...], th[...]) + dot_t(plo[...], th[...]) + dot_t(ph[...], tl[...])
    taken = vals[...].astype(BF16)
    target = dot(ph[...], taken) + dot(plo[...], taken)
    ch, cl = split(cross)
    fh, fl = split(field[...])
    mixed = dot(ch, fh) + dot(cl, fh) + dot(ch, fl)
    for q in range(2 * steps):
        for m in range(members):
            start = (q * members + m) * 32
            value = mixed[q * 32 : (q + 1) * 32, m * LANES : (m + 1) * LANES] - target[q * 32 : (q + 1) * 32]
            spread[start : start + 32] = value.astype(BF16)
    size = members * 32
    for k in range(steps):
        for m in range(members):
            start = k * size + m * 32
            pair = spread[start : start + 32].astype(F32)
            near = [jnp.where(even, pair[i + 8 : i + 16], pair[i : i + 8]) for i in (0, 16)]
            start = k * size // 2 + m * 16
            message[start : start + 16] = jnp.concatenate(near, axis=0).astype(BF16)
    for copy in copies:
        copy.wait()


def adjoint_step(u, cot, gb, gm, flat, d, add, out, gain, ws, wn, wo, members):
    both = 2 * SLIM
    gb[...] = cot[...].astype(BF16)
    flat[...] = dot_t(gb[...], wo[...])
    gb[...] = (flat[...] * d[...]).astype(BF16)
    gm[...] = dot_t(gb[...], wn[...])
    flat[...] = dot_t(gb[...], ws[...])
    for m in range(members):
        base = m * both
        rows = []
        for lat in range(2):
            start = base + lat * SLIM
            rows.append(gm[start : start + SLIM].astype(BF16).astype(F32))
        around = neighbours(rows)
        for lat in range(2):
            start = base + lat * SLIM
            x = u[start : start + SLIM]
            s = inverse_rms(x)
            scaled = gain * (flat[start : start + SLIM] + around[lat])
            inner = jnp.mean(x * scaled, axis=-1, keepdims=True)
            value = cot[start : start + SLIM] + s * scaled - x * (s * s * s * inner)
            if add is not None:
                value = value + add[start : start + SLIM]
            out[start : start + SLIM] = value


def edges(nxt, edge, r):
    even = lax.rem(lax.axis_index("tile"), 2) == 0
    far = nxt[r * 2 : (r + 1) * 2]
    start = nxt.shape[0] // 2 + r * 2
    near = nxt[start : start + 2]
    edge[...] = jnp.zeros_like(edge)
    edge[0:2] = near
    edge[6:8] = far
    edge[8:10] = far
    edge[14:16] = near
    return jnp.where(even, edge[0:8], edge[8:16])


def pull_kernel(
    wo_hbm, wn_hbm, ws_hbm, gain_hbm, control_hbm, background_hbm, spread, readout, error, nxt, nxt_edges, f2x, edge0,
    cot, extra, u0x, wo, wn, ws, gain, background,
    pulled, final, edge, control, sems,
):
    pairs = (
        (control_hbm, control), (wo_hbm, wo), (wn_hbm, wn), (ws_hbm, ws), (gain_hbm, gain),
        (background_hbm, background),
    )
    copies = [pltpu.make_async_copy(source, to, sems.at[i]) for i, (source, to) in enumerate(pairs)]
    for copy in copies:
        copy.start()
    size = nxt.shape[0]
    even = lax.rem(lax.axis_index("tile"), 2) == 0
    later = jnp.where(lax.axis_index("slot") == lax.axis_size("slot") - 1, 0.0, 1.0)
    weight = later * error[...]
    row8 = sublane((8, 1))
    pulled[...] = dot_t(spread[...], readout[...])
    final[...] = f2x[...].astype(F32)

    def other_edge(k, r):
        start = (2 + k) * size + r * 16
        low = jnp.where(row8 < 4, pulled[start : start + 8], 0.0)
        high = jnp.where(row8 >= 4, pulled[start + 8 : start + 16], 0.0)
        return jnp.where(even, high, low)

    for r in range(size // 16):
        a, b = r * 16, (r + 1) * 16
        c, d, e = r * SLIM, r * SLIM + 16, (r + 1) * SLIM
        cot[c:d] = pulled[size + a : size + b] - weight * (nxt[a:b] - final[c:d])
        cot[d:e] = other_edge(1, r) - weight * (edges(nxt_edges, edge, r) - final[d:e])
        extra[c:d] = pulled[a:b]
        extra[d:e] = other_edge(0, r)
    copies[0].wait()
    for r in range(size // 16):
        u0x[r * SLIM : r * SLIM + 16] = control[r * 16 : (r + 1) * 16]
        u0x[r * SLIM + 16 : (r + 1) * SLIM] = edge0[r * 8 : (r + 1) * 8]
    for copy in copies[1:]:
        copy.wait()


def backward_kernel(
    cot, extra, u0x, wo, wn, ws, gain, background, readout, error, message, u1x, d0x, d1x, before,
    result,
    cot2, cot1, add, gb, gm, flat, mate_pull,
):
    size = result.shape[0]
    members = size // 32
    even = lax.rem(lax.axis_index("tile"), 2) == 0
    first = lax.axis_index("slot") == 0
    row8 = sublane((8, 1))
    mate_side = jnp.where(even, 1, 0) == jnp.where(row8 < 4, 1, 0)
    mate_pull[...] = dot_t(message[...], readout[...])
    cot2[...] = cot[...]
    add[...] = extra[...]
    for r in range(2 * members):
        a, b = r * SLIM + 16, (r + 1) * SLIM
        start = size // 2 + r * 8
        cot2[a:b] = cot[a:b] + jnp.where(mate_side, mate_pull[start : start + 8], 0.0)
        add[a:b] = extra[a:b] + jnp.where(mate_side, mate_pull[r * 8 : (r + 1) * 8], 0.0)
    adjoint_step(u1x, cot2, gb, gm, flat, d1x, add, cot1, gain[...], ws, wn, wo, members)
    adjoint_step(u0x, cot1, gb, gm, flat, d0x, None, cot2, gain[...], ws, wn, wo, members)
    taken = jnp.where(first, background[...].astype(F32), before[...].astype(F32))
    for r in range(2 * members):
        a, b, start = r * 16, (r + 1) * 16, r * SLIM
        result[a:b] = cot2[start : start + 16] + error[...] * (u0x[start : start + 16] - taken[a:b])


def kernel_call(body, outs, scratch, flops, moved, hbm=0, out_places=None, aliases={}):
    def call(*operands):
        fixed = [i in range(hbm) and i not in aliases for i in range(len(operands))]
        operands = [
            pltpu.with_memory_space_constraint(x, pltpu.HBM) if fix else x for x, fix in zip(operands, fixed)
        ]
        places = [pltpu.HBM] * hbm + [pltpu.VMEM] * (len(operands) - hbm)
        given = {} if out_places is None else {"out_specs": [pl.BlockSpec(memory_space=p) for p in out_places]}
        return pl.pallas_call(
            body,
            out_shape=outs,
            in_specs=[pl.BlockSpec(memory_space=place) for place in places],
            **given,
            scratch_shapes=scratch,
            input_output_aliases=aliases,
            compiler_params=pltpu.CompilerParams(vmem_limit_bytes=VMEM_LIMIT),
            cost_estimate=pl.CostEstimate(flops=flops, bytes_accessed=moved, transcendentals=0),
        )(*operands)

    return call


def per_device(
    control,
    background,
    self_weight,
    neighbour_weight,
    output_weight,
    norm_gain,
    readout,
    error_weight,
    report_owner,
    report_stencil,
    report_weights,
    report_values,
    report_precision,
):
    tiles = lax.axis_size("tile")
    slots = lax.axis_size("slot")
    members, lats, cols, channels = control.shape[1:]
    groups = members * lats
    size = groups * cols
    steps = report_owner.shape[1]
    rows = report_owner.shape[2]
    gain = norm_gain.reshape(1, channels)
    error = error_weight.reshape(1, channels)
    flat = control.reshape(size, channels)

    def spec(count, dtype=F32, width=channels):
        return jax.ShapeDtypeStruct((count, width), dtype)

    def scratch(count, dtype=F32, width=channels):
        return pltpu.VMEM((count, width), dtype)

    mate_of = [(i, i ^ 1) for i in range(tiles)]
    other_of = [(i, (i - 1) % tiles if i % 2 == 0 else (i + 1) % tiles) for i in range(tiles)]

    def across(block, shift, route):
        pairs = [
            (((s + shift) % slots) * tiles + i, s * tiles + j)
            for s in range(slots)
            for i, j in route
        ]
        return lax.ppermute(block, ("slot", "tile"), pairs)

    straight = [(i, i) for i in range(tiles)]
    mate = lax.ppermute(flat, "tile", mate_of)
    nxt = across(flat, 1, straight)
    listed = (
        jnp.transpose(report_owner[0], (0, 2, 1)),
        jnp.transpose(report_stencil[0], (0, 2, 1)),
        jnp.transpose(report_weights[0], (0, 2, 1)),
        report_precision[0],
        report_values[0].reshape(steps * rows, LANES),
    )
    buffers = [
        pltpu.VMEM((steps, 1, rows), jnp.int32),
        pltpu.VMEM((steps, 4, rows), jnp.int32),
        pltpu.VMEM((steps, 4, rows), BF16),
        pltpu.VMEM((steps, rows), BF16),
        scratch(steps * rows, BF16, LANES),
        pltpu.VMEM((1, steps * rows), jnp.int32),
        scratch(META, F32, steps * rows),
        scratch(tiles * CHUNK, F32, LANES),
        scratch(tiles * CHUNK, BF16, LANES),
        pltpu.SemaphoreType.DMA((6,)),
    ]
    held, packed = kernel_call(
        first_kernel,
        [spec(size), spec(tiles * CHUNK, BF16, LANES)],
        buffers + [pltpu.SemaphoreType.DMA],
        10**7,
        200000,
        hbm=6,
        out_places=[pltpu.VMEM, pltpu.HBM],
    )(flat, *listed)
    sent = kernel_call(
        tile_kernel, spec(groups * (cols + 2), BF16), [scratch(groups * 2)], 1000, 400000
    )(held, mate)
    oth = lax.ppermute(sent, "tile", other_of)
    (packed,) = kernel_call(
        later_kernel,
        [spec(tiles * CHUNK, BF16, LANES)],
        buffers,
        10**7,
        200000,
        hbm=6,
        out_places=[pltpu.HBM],
        aliases={0: 0},
    )(packed, *listed, sent)
    arrived = lax.all_to_all(packed, "tile", split_axis=0, concat_axis=0, tiled=True)

    near2, near4 = kernel_call(
        relay_kernel, [spec(4 * groups), spec(4 * groups)], [scratch(size)], 1000, 700000
    )(mate, oth, nxt)
    nxt_edges = across(near2, 1, straight)
    wide = groups * WIDE
    slim = groups * SLIM
    edge0, u1x, d0x, d1x, f2x, field, final = kernel_call(
        forward_kernel,
        [spec(groups * 8), spec(slim)] + [spec(slim, BF16)] * 3
        + [spec(4 * lats * cols, F32, members * LANES), spec(size, BF16)],
        [scratch(wide), scratch(wide), scratch(wide, BF16), scratch(wide, BF16), scratch(wide, BF16)]
        + [scratch(wide), scratch(16), scratch(4 * size, BF16)]
        + [scratch(1), scratch(channels, BF16), scratch(channels, BF16), scratch(channels, BF16)]
        + [scratch(channels, BF16, LANES), pltpu.SemaphoreType.DMA((5,))],
        10**11,
        4000000,
        hbm=5,
    )(gain, self_weight, neighbour_weight, output_weight, readout, held, near4, oth)
    before = across(final, -1, straight)
    total = -(-tiles // SENDERS) * LANES
    spread, near_spread, readout_held, error_held = kernel_call(
        functools.partial(observe_kernel, tiles),
        [spec(4 * size, BF16, LANES), spec(size, BF16, LANES), spec(channels, BF16, LANES), spec(1)],
        [scratch(128, BF16, total)] * 4
        + [scratch(total, F32, LANES), scratch(tiles * CHUNK, F32, LANES), pltpu.SemaphoreType.DMA((2,))],
        10**9,
        2000000,
        hbm=2,
    )(readout, error, arrived, field)
    from_mate = lax.ppermute(near_spread, "tile", mate_of)
    handed = kernel_call(
        pull_kernel,
        [spec(slim), spec(slim), spec(slim), spec(channels, BF16), spec(channels, BF16), spec(channels, BF16)]
        + [spec(1), spec(size, BF16)],
        [scratch(4 * size), scratch(slim), scratch(16), scratch(size), pltpu.SemaphoreType.DMA((6,))],
        10**9,
        3000000,
        hbm=6,
    )(
        output_weight, neighbour_weight, self_weight, gain, flat, background.reshape(size, channels),
        spread, readout_held, error_held, nxt, nxt_edges, f2x, edge0,
    )
    result = kernel_call(
        backward_kernel,
        spec(size),
        [scratch(slim), scratch(slim), scratch(slim), scratch(slim, BF16), scratch(slim), scratch(slim)]
        + [scratch(size)],
        12 * slim * channels * channels,
        6000000,
    )(*handed, readout_held, error_held, from_mate, u1x, d0x, d1x, before)
    return result.reshape(control.shape)


def solution(mesh):
    in_specs = (
        P("slot", None, None, "tile", None),
        P(None, None, "tile", None),
        P(),
        P(),
        P(),
        P(),
        P(),
        P(),
        P("slot", None, "tile", None),
        P("slot", None, "tile", None),
        P("slot", None, "tile", None),
        P("slot", None, "tile", None),
        P("slot", None, "tile"),
    )
    out_specs = P("slot", None, None, "tile", None)
    return jax.shard_map(
        per_device, mesh=mesh, in_specs=in_specs, out_specs=out_specs, check_vma=False
    )
```

```python
import functools
import jax
import jax.numpy as jnp
from jax import lax
from jax.experimental import pallas as pl
from jax.experimental.pallas import tpu as pltpu
from jax.sharding import PartitionSpec as P

EPSILON = 1e-06
F32 = jnp.float32
BF16 = jnp.bfloat16
LANES = 128
CAP = 5
SLOTS = 4 * CAP
CHUNK = 32
META = 16
SENDERS = LANES // SLOTS
WIDE = 40
SLIM = 24
VMEM_LIMIT = 28 * 1024 * 1024


def dot(a, b):
    return jnp.dot(a, b, preferred_element_type=F32)


def dot_t(a, b):
    return lax.dot_general(a, b, (((1,), (1,)), ((), ())), preferred_element_type=F32)


def sublane(shape):
    return lax.broadcasted_iota(jnp.int32, shape, 0)


def inverse_rms(x):
    return lax.rsqrt(jnp.mean(x * x, axis=-1, keepdims=True) + EPSILON)


def sigmoid(p):
    return 0.5 * jnp.tanh(0.5 * p) + 0.5


def neighbours(rows):
    width = rows[0].shape[0]
    return [
        0.25 * (rows[1 - i] + pltpu.roll(rows[i], 1, 0) + pltpu.roll(rows[i], width - 1, 0))
        for i in range(2)
    ]


def forward_step(u, n, mean, act, pre, d, gain, ws, wn, wo, width, members, out, copies=()):
    both = 2 * width
    for m in range(members):
        base = m * both
        rows = []
        for lat in range(2):
            x = u[base + lat * width : base + (lat + 1) * width]
            rows.append((x * inverse_rms(x) * gain).astype(BF16).astype(F32))
        n[base : base + both] = jnp.concatenate(rows, axis=0).astype(BF16)
        mean[base : base + both] = jnp.concatenate(neighbours(rows), axis=0).astype(BF16)
    for copy in copies[:2]:
        copy.wait()
    pre[...] = dot(n[...], ws[...]) + dot(mean[...], wn[...])
    for m in range(members):
        base = m * both
        p = pre[base : base + both]
        sig = sigmoid(p)
        act[base : base + both] = (p * sig).astype(BF16)
        if d is not None:
            pre[base : base + both] = sig * (1.0 + p * (1.0 - sig))
    if d is not None:
        for m in range(members):
            slim_copy(d, pre, m)
    for copy in copies[2:]:
        copy.wait()
    pre[...] = dot(act[...], wo[...])
    for r in range(2 * members):
        out(r, u[r * width : (r + 1) * width] + pre[r * width : (r + 1) * width])


def slim_edge(wide, r):
    low = wide[r * WIDE + 16 : r * WIDE + 24]
    high = wide[r * WIDE + 32 : r * WIDE + 40]
    return jnp.where(sublane(low.shape) < 4, low, high)


def slim_copy(to, wide, m):
    parts = []
    for r in (2 * m, 2 * m + 1):
        parts += [wide[r * WIDE : r * WIDE + 16], slim_edge(wide, r)]
    both = jnp.concatenate(parts, axis=0)
    to[m * 2 * SLIM : (m + 1) * 2 * SLIM] = both.astype(to.dtype)


def reports(arrays, out_hbm, key, meta, picked, out, sem):
    pack(*arrays, out, key, meta, picked)
    store = pltpu.make_async_copy(out, out_hbm, sem)
    store.start()
    store.wait()


def early():
    return lax.axis_index("tile") < lax.axis_size("tile") // 2


def first_kernel(control_hbm, *refs):
    sources, (held, out_hbm), arrays, (key, meta, picked, out, sems) = refs[:5], refs[5:7], refs[7:12], refs[12:]
    copies = [
        pltpu.make_async_copy(source, to, sems.at[i]) for i, (source, to) in enumerate(zip(sources, arrays))
    ]
    copies.append(pltpu.make_async_copy(control_hbm, held, sems.at[5]))
    for copy in copies:
        copy.start()
    for copy in copies[:5]:
        copy.wait()

    @pl.when(early())
    def _():
        reports(arrays, out_hbm, key, meta, picked, out, sems.at[6])

    copies[5].wait()


def later_kernel(packed_hbm, *refs):
    arrays, out_hbm, (key, meta, picked, out, sem) = refs[:5], refs[6], refs[7:]

    @pl.when(jnp.logical_not(early()))
    def _():
        reports(arrays, out_hbm, key, meta, picked, out, sem)


def pack(owner, stencil, weights, precision, values, out, key, meta, picked):
    steps, _, rows = owner.shape
    tiles = out.shape[0] // CHUNK
    total = steps * rows
    place = lax.axis_index("tile") % SENDERS * SLOTS
    earlier = lax.broadcasted_iota(jnp.int32, (rows, rows), 0) < lax.broadcasted_iota(jnp.int32, (rows, rows), 1)
    earlier = earlier.astype(F32).astype(BF16)
    meta[...] = jnp.zeros_like(meta)
    for k in range(steps):
        at = slice(k * rows, (k + 1) * rows)
        named = lax.broadcasted_iota(jnp.int32, (tiles, rows), 0) == owner[k]
        hits = named.astype(F32)
        before = dot(hits.astype(BF16), earlier)
        rank = jnp.sum(hits * before, axis=0, keepdims=True).astype(jnp.int32)
        key[0:1, at] = owner[k] * (2 * CAP) + k * CAP + rank
        meta[4:8, at] = stencil[k].astype(F32)
        meta[8:12, at] = weights[k].astype(F32)
        meta[12:13, at] = precision[k : k + 1].astype(F32)
    row = lax.broadcasted_iota(jnp.int32, (tiles * CHUNK, total), 0)
    tile = row // CHUNK
    slot = row % CHUNK
    other = jnp.where(tile % 2 == 0, (tile + tiles - 1) % tiles, (tile + 1) % tiles)
    mine = slot < 2 * CAP
    wanted = jnp.where(mine, tile * (2 * CAP) + slot, other * (2 * CAP) + slot - 2 * CAP)
    wanted = jnp.where(slot < SLOTS, wanted, -1)
    placement = (wanted == key[...]).astype(F32).astype(BF16)
    picked[...] = dot(placement, values[...])
    entries = dot_t(meta[...].astype(BF16), placement)
    lane = lax.broadcasted_iota(jnp.int32, (META, LANES), 1)
    used = jnp.logical_and(lane >= place, lane < place + SLOTS)
    per_tile = LANES // CHUNK
    for t in range(tiles):
        block = entries[:, t // per_tile * LANES : (t // per_tile + 1) * LANES]
        shift = (place + LANES - t % per_tile * CHUNK) % LANES
        block = jnp.where(used, pltpu.roll(block, shift, 1), 0.0)
        low = picked[t * CHUNK + 16 : (t + 1) * CHUNK]
        picked[t * CHUNK + 16 : (t + 1) * CHUNK] = jnp.where(sublane((META, 1)) < 4, low, block)
    out[...] = picked[...].astype(BF16)


def tile_kernel(control, mate, out, held):
    even = lax.rem(lax.axis_index("tile"), 2) == 0
    size = control.shape[0]
    out[0:size] = control[...].astype(BF16)
    for r in range(size // 16):
        held[r * 2 : (r + 1) * 2] = jnp.where(
            even, mate[r * 16 : r * 16 + 2], mate[r * 16 + 14 : (r + 1) * 16]
        )
    out[size:] = held[...].astype(BF16)


def relay_kernel(control, mate, oth, tile, out, near4, wide):
    even = lax.rem(lax.axis_index("tile"), 2) == 0
    size = mate.shape[0]
    tile[...] = control[...]
    wide[...] = oth[0:size].astype(F32)
    for r in range(size // 16):
        a, b = r * 16, (r + 1) * 16
        out[r * 2 : (r + 1) * 2] = jnp.where(even, wide[b - 2 : b], wide[a : a + 2])
        near4[r * 4 : (r + 1) * 4] = jnp.where(even, mate[a : a + 4], mate[b - 4 : b])
        start = size // 8 + r * 2
        out[start : start + 2] = jnp.where(even, mate[a : a + 2], mate[b - 2 : b])


def forward_kernel(
    gain_hbm, ws_hbm, wn_hbm, wo_hbm, readout_hbm, control, mate, oth,
    edge0, u1x, d0x, d1x, f2x, field, final, wo, readout,
    ua, ub, n, mean, act, pre, edge, states, gain, ws, wn, sems,
):
    pairs = ((gain_hbm, gain), (ws_hbm, ws), (wn_hbm, wn), (wo_hbm, wo), (readout_hbm, readout))
    copies = [pltpu.make_async_copy(source, to, sems.at[i]) for i, (source, to) in enumerate(pairs)]
    for copy in copies:
        copy.start()
    members = final.shape[0] // 32
    even = lax.rem(lax.axis_index("tile"), 2) == 0
    tile_at = jnp.where(even, 24, 16)
    edge_at = jnp.where(even, 16, 32)
    far = oth[members * 32 :].astype(F32)
    for r in range(2 * members):
        ua[r * WIDE : r * WIDE + 16] = control[r * 16 : (r + 1) * 16]
        ua[pl.ds(pl.multiple_of(r * WIDE + tile_at, 8), 16)] = oth[r * 16 : (r + 1) * 16].astype(F32)
        near4 = mate[r * 4 : (r + 1) * 4]
        far2 = far[r * 2 : (r + 1) * 2]
        edge[...] = jnp.zeros_like(edge)
        edge[0:4] = near4
        edge[6:8] = far2
        edge[8:10] = far2
        edge[12:16] = near4
        ua[pl.ds(pl.multiple_of(r * WIDE + edge_at, 8), 8)] = jnp.where(even, edge[0:8], edge[8:16])
    for r in range(2 * members):
        edge0[r * 8 : (r + 1) * 8] = slim_edge(ua, r)
    copies[0].wait()
    g = gain[...]

    def keep(ref):
        def store(r, value):
            ref[r * WIDE : (r + 1) * WIDE] = value

        return store

    def keep_states(ref, k):
        own = k * members * 32
        away = (2 + k) * members * 32
        for r in range(2 * members):
            states[own + r * 16 : own + (r + 1) * 16] = ref[r * WIDE : r * WIDE + 16].astype(BF16)
            taken = ref[pl.ds(pl.multiple_of(r * WIDE + tile_at, 8), 16)]
            states[away + r * 16 : away + (r + 1) * 16] = taken.astype(BF16)

    forward_step(ua, n, mean, act, pre, d0x, g, ws, wn, wo, WIDE, members, keep(ub), copies[1:])
    for m in range(members):
        slim_copy(u1x, ub, m)
    keep_states(ub, 0)
    forward_step(ub, n, mean, act, pre, d1x, g, ws, wn, wo, WIDE, members, keep(ua))
    for m in range(members):
        slim_copy(f2x, ua, m)
    keep_states(ua, 1)
    final[...] = states[members * 32 : 2 * members * 32]
    read = dot(states[...], readout[...])
    for q in range(4):
        for m in range(members):
            start = (q * members + m) * 32
            field[q * 32 : (q + 1) * 32, m * LANES : (m + 1) * LANES] = read[start : start + 32]


def split(x):
    high = x.astype(BF16)
    return high, (x - high.astype(F32)).astype(BF16)


def observe_kernel(
    tiles,
    error_hbm, control_hbm, background_hbm, arrived, field,
    spread, message, error, control, background,
    th, tl, ph, plo, vals, wide, sems,
):
    pairs = ((error_hbm, error), (control_hbm, control), (background_hbm, background))
    copies = [pltpu.make_async_copy(source, to, sems.at[i]) for i, (source, to) in enumerate(pairs)]
    for copy in copies:
        copy.start()
    steps = 2
    members = field.shape[1] // LANES
    even = lax.rem(lax.axis_index("tile"), 2) == 0
    cells = sublane((32, LANES)).astype(F32)
    lane = lax.broadcasted_iota(jnp.int32, (1, LANES), 1)
    table_of = jnp.where(lane < SENDERS * SLOTS, lane % SLOTS // CAP, -1)
    wide[...] = arrived[...].astype(F32)
    vals[...] = jnp.zeros_like(vals)
    for p in range(th.shape[1] // LANES):
        meta = jnp.zeros((META, LANES), F32)
        for d in range(p * SENDERS, min((p + 1) * SENDERS, tiles)):
            meta += wide[d * CHUNK + 16 : (d + 1) * CHUNK]
            start = p * LANES + d % SENDERS * SLOTS
            vals[start : start + SLOTS] = wide[d * CHUNK : d * CHUNK + SLOTS]
        weight = jnp.zeros((32, LANES), F32)
        for i in range(4):
            weight += jnp.where(cells == meta[4 + i : 5 + i], meta[8 + i : 9 + i], 0.0)
        scaled = weight * meta[12:13]
        wh, wl = split(weight)
        sh, sl = split(scaled)
        parts = ((th, wh.astype(F32)), (tl, wl.astype(F32)), (ph, sh.astype(F32)), (plo, sl.astype(F32)))
        for q in range(2 * steps):
            hit = table_of == q
            for ref, value in parts:
                kept = jnp.where(hit, value, 0.0).astype(BF16)
                ref[q * 32 : (q + 1) * 32, p * LANES : (p + 1) * LANES] = kept
    cross = dot_t(ph[...], th[...]) + dot_t(plo[...], th[...]) + dot_t(ph[...], tl[...])
    taken = vals[...].astype(BF16)
    target = dot(ph[...], taken) + dot(plo[...], taken)
    ch, cl = split(cross)
    fh, fl = split(field[...])
    mixed = dot(ch, fh) + dot(cl, fh) + dot(ch, fl)
    for q in range(2 * steps):
        for m in range(members):
            start = (q * members + m) * 32
            value = mixed[q * 32 : (q + 1) * 32, m * LANES : (m + 1) * LANES] - target[q * 32 : (q + 1) * 32]
            spread[start : start + 32] = value.astype(BF16)
    size = members * 32
    for k in range(steps):
        for m in range(members):
            start = k * size + m * 32
            pair = spread[start : start + 32].astype(F32)
            near = [jnp.where(even, pair[i + 8 : i + 16], pair[i : i + 8]) for i in (0, 16)]
            start = k * size // 2 + m * 16
            message[start : start + 16] = jnp.concatenate(near, axis=0).astype(BF16)
    for copy in copies:
        copy.wait()


def adjoint_step(u, cot, gb, gm, flat, d, add, out, gain, ws, wn, wo, members):
    both = 2 * SLIM
    gb[...] = cot[...].astype(BF16)
    flat[...] = dot_t(gb[...], wo[...])
    gb[...] = (flat[...] * d[...]).astype(BF16)
    gm[...] = dot_t(gb[...], wn[...])
    flat[...] = dot_t(gb[...], ws[...])
    for m in range(members):
        base = m * both
        rows = []
        for lat in range(2):
            start = base + lat * SLIM
            rows.append(gm[start : start + SLIM].astype(BF16).astype(F32))
        around = neighbours(rows)
        for lat in range(2):
            start = base + lat * SLIM
            x = u[start : start + SLIM]
            s = inverse_rms(x)
            scaled = gain * (flat[start : start + SLIM] + around[lat])
            inner = jnp.mean(x * scaled, axis=-1, keepdims=True)
            value = cot[start : start + SLIM] + s * scaled - x * (s * s * s * inner)
            if add is not None:
                value = value + add[start : start + SLIM]
            out[start : start + SLIM] = value


def edges(nxt, edge, r):
    even = lax.rem(lax.axis_index("tile"), 2) == 0
    far = nxt[r * 2 : (r + 1) * 2]
    start = nxt.shape[0] // 2 + r * 2
    near = nxt[start : start + 2]
    edge[...] = jnp.zeros_like(edge)
    edge[0:2] = near
    edge[6:8] = far
    edge[8:10] = far
    edge[14:16] = near
    return jnp.where(even, edge[0:8], edge[8:16])


def pull_kernel(
    wn_hbm, ws_hbm, gain_hbm, spread, readout,
    last, first, wn, ws, gain,
    pulled, sems,
):
    pairs = ((wn_hbm, wn), (ws_hbm, ws), (gain_hbm, gain))
    copies = [pltpu.make_async_copy(source, to, sems.at[i]) for i, (source, to) in enumerate(pairs)]
    for copy in copies:
        copy.start()
    size = pulled.shape[0] // 4
    even = lax.rem(lax.axis_index("tile"), 2) == 0
    row8 = sublane((8, 1))
    pulled[...] = dot_t(spread[...], readout[...])
    for k, out in enumerate((first, last)):
        for r in range(size // 16):
            start = k * size + r * 16
            out[r * SLIM : r * SLIM + 16] = pulled[start : start + 16]
            start += 2 * size
            low = jnp.where(row8 < 4, pulled[start : start + 8], 0.0)
            high = jnp.where(row8 >= 4, pulled[start + 8 : start + 16], 0.0)
            out[r * SLIM + 16 : (r + 1) * SLIM] = jnp.where(even, high, low)
    for copy in copies:
        copy.wait()


def backward_kernel(
    last, early_pull, wn, ws, gain, control, background, edge0, nxt, nxt_edges, f2x, wo, readout, error, message,
    u1x, d0x, d1x, before,
    result,
    cot2, cot1, add, gb, gm, flat, mate_pull, edge, u0x, final,
):
    size = result.shape[0]
    members = size // 32
    even = lax.rem(lax.axis_index("tile"), 2) == 0
    slot = lax.axis_index("slot")
    first = slot == 0
    weight = jnp.where(slot == lax.axis_size("slot") - 1, 0.0, 1.0) * error[...]
    row8 = sublane((8, 1))
    mate_side = jnp.where(even, 1, 0) == jnp.where(row8 < 4, 1, 0)
    mate_pull[...] = dot_t(message[...], readout[...])
    final[...] = f2x[...].astype(F32)
    add[...] = early_pull[...]
    for r in range(2 * members):
        a, b = r * SLIM, r * SLIM + 16
        cot2[a:b] = last[a:b] - weight * (nxt[r * 16 : (r + 1) * 16] - final[a:b])
        u0x[a:b] = control[r * 16 : (r + 1) * 16]
        a, b = b, b + 8
        start = size // 2 + r * 8
        pulled = last[a:b] + jnp.where(mate_side, mate_pull[start : start + 8], 0.0)
        cot2[a:b] = pulled - weight * (edges(nxt_edges, edge, r) - final[a:b])
        add[a:b] = early_pull[a:b] + jnp.where(mate_side, mate_pull[r * 8 : (r + 1) * 8], 0.0)
        u0x[a:b] = edge0[r * 8 : (r + 1) * 8]
    adjoint_step(u1x, cot2, gb, gm, flat, d1x, add, cot1, gain[...], ws, wn, wo, members)
    adjoint_step(u0x, cot1, gb, gm, flat, d0x, None, cot2, gain[...], ws, wn, wo, members)
    taken = jnp.where(first, background[...].astype(F32), before[...].astype(F32))
    for r in range(2 * members):
        a, b, start = r * 16, (r + 1) * 16, r * SLIM
        result[a:b] = cot2[start : start + 16] + error[...] * (u0x[start : start + 16] - taken[a:b])


def kernel_call(body, outs, scratch, flops, moved, hbm=0, out_places=None, aliases={}):
    def call(*operands):
        fixed = [i in range(hbm) and i not in aliases for i in range(len(operands))]
        operands = [
            pltpu.with_memory_space_constraint(x, pltpu.HBM) if fix else x for x, fix in zip(operands, fixed)
        ]
        places = [pltpu.HBM] * hbm + [pltpu.VMEM] * (len(operands) - hbm)
        given = {} if out_places is None else {"out_specs": [pl.BlockSpec(memory_space=p) for p in out_places]}
        return pl.pallas_call(
            body,
            out_shape=outs,
            in_specs=[pl.BlockSpec(memory_space=place) for place in places],
            **given,
            scratch_shapes=scratch,
            input_output_aliases=aliases,
            compiler_params=pltpu.CompilerParams(vmem_limit_bytes=VMEM_LIMIT),
            cost_estimate=pl.CostEstimate(flops=flops, bytes_accessed=moved, transcendentals=0),
        )(*operands)

    return call


def per_device(
    control,
    background,
    self_weight,
    neighbour_weight,
    output_weight,
    norm_gain,
    readout,
    error_weight,
    report_owner,
    report_stencil,
    report_weights,
    report_values,
    report_precision,
):
    tiles = lax.axis_size("tile")
    slots = lax.axis_size("slot")
    members, lats, cols, channels = control.shape[1:]
    groups = members * lats
    size = groups * cols
    steps = report_owner.shape[1]
    rows = report_owner.shape[2]
    gain = norm_gain.reshape(1, channels)
    error = error_weight.reshape(1, channels)
    flat = control.reshape(size, channels)

    def spec(count, dtype=F32, width=channels):
        return jax.ShapeDtypeStruct((count, width), dtype)

    def scratch(count, dtype=F32, width=channels):
        return pltpu.VMEM((count, width), dtype)

    mate_of = [(i, i ^ 1) for i in range(tiles)]
    other_of = [(i, (i - 1) % tiles if i % 2 == 0 else (i + 1) % tiles) for i in range(tiles)]

    def across(block, shift, route):
        pairs = [
            (((s + shift) % slots) * tiles + i, s * tiles + j)
            for s in range(slots)
            for i, j in route
        ]
        return lax.ppermute(block, ("slot", "tile"), pairs)

    straight = [(i, i) for i in range(tiles)]
    mate = lax.ppermute(flat, "tile", mate_of)
    listed = (
        jnp.transpose(report_owner[0], (0, 2, 1)),
        jnp.transpose(report_stencil[0], (0, 2, 1)),
        jnp.transpose(report_weights[0], (0, 2, 1)),
        report_precision[0],
        report_values[0].reshape(steps * rows, LANES),
    )
    work = [
        pltpu.VMEM((1, steps * rows), jnp.int32),
        scratch(META, F32, steps * rows),
        scratch(tiles * CHUNK, F32, LANES),
        scratch(tiles * CHUNK, BF16, LANES),
    ]
    held, packed, *listed = kernel_call(
        first_kernel,
        [spec(size), spec(tiles * CHUNK, BF16, LANES)]
        + [jax.ShapeDtypeStruct(block.shape, block.dtype) for block in listed],
        work + [pltpu.SemaphoreType.DMA((7,))],
        10**7,
        200000,
        hbm=6,
        out_places=[pltpu.VMEM, pltpu.HBM] + [pltpu.VMEM] * 5,
    )(flat, *listed)
    sent = kernel_call(
        tile_kernel, spec(groups * (cols + 2), BF16), [scratch(groups * 2)], 1000, 400000
    )(held, mate)
    oth = lax.ppermute(sent, "tile", other_of)
    (packed,) = kernel_call(
        later_kernel,
        [spec(tiles * CHUNK, BF16, LANES)],
        work + [pltpu.SemaphoreType.DMA],
        10**7,
        200000,
        hbm=1,
        out_places=[pltpu.HBM],
        aliases={0: 0},
    )(packed, *listed, sent)
    arrived = lax.all_to_all(packed, "tile", split_axis=0, concat_axis=0, tiled=True)

    tile, near2, near4 = kernel_call(
        relay_kernel, [spec(size), spec(4 * groups), spec(4 * groups)], [scratch(size)], 1000, 700000
    )(held, mate, oth)
    nxt = across(tile, 1, straight)
    nxt_edges = across(near2, 1, straight)
    wide = groups * WIDE
    slim = groups * SLIM
    edge0, u1x, d0x, d1x, f2x, field, final, wo, readout_held = kernel_call(
        forward_kernel,
        [spec(groups * 8), spec(slim)] + [spec(slim, BF16)] * 3
        + [spec(4 * lats * cols, F32, members * LANES), spec(size, BF16)]
        + [spec(channels, BF16), spec(channels, BF16, LANES)],
        [scratch(wide), scratch(wide), scratch(wide, BF16), scratch(wide, BF16), scratch(wide, BF16)]
        + [scratch(wide), scratch(16), scratch(4 * size, BF16)]
        + [scratch(1), scratch(channels, BF16), scratch(channels, BF16), pltpu.SemaphoreType.DMA((5,))],
        10**11,
        4000000,
        hbm=5,
    )(gain, self_weight, neighbour_weight, output_weight, readout, held, near4, oth)
    before = across(final, -1, straight)
    total = -(-tiles // SENDERS) * LANES
    spread, near_spread, error, held, background = kernel_call(
        functools.partial(observe_kernel, tiles),
        [spec(4 * size, BF16, LANES), spec(size, BF16, LANES), spec(1), spec(size), spec(size, BF16)],
        [scratch(128, BF16, total)] * 4
        + [scratch(total, F32, LANES), scratch(tiles * CHUNK, F32, LANES), pltpu.SemaphoreType.DMA((3,))],
        10**9,
        2000000,
        hbm=3,
    )(error, flat, background.reshape(size, channels), arrived, field)
    from_mate = lax.ppermute(near_spread, "tile", mate_of)
    handed = kernel_call(
        pull_kernel,
        [spec(slim), spec(slim), spec(channels, BF16), spec(channels, BF16), spec(1)],
        [scratch(4 * size), pltpu.SemaphoreType.DMA((3,))],
        10**9,
        3000000,
        hbm=3,
    )(neighbour_weight, self_weight, gain, spread, readout_held)
    result = kernel_call(
        backward_kernel,
        spec(size),
        [scratch(slim), scratch(slim), scratch(slim), scratch(slim, BF16), scratch(slim), scratch(slim)]
        + [scratch(size), scratch(16), scratch(slim), scratch(slim)],
        12 * slim * channels * channels,
        6000000,
    )(
        *handed, held, background, edge0, nxt, nxt_edges, f2x, wo, readout_held, error, from_mate,
        u1x, d0x, d1x, before,
    )
    return result.reshape(control.shape)


def solution(mesh):
    in_specs = (
        P("slot", None, None, "tile", None),
        P(None, None, "tile", None),
        P(),
        P(),
        P(),
        P(),
        P(),
        P(),
        P("slot", None, "tile", None),
        P("slot", None, "tile", None),
        P("slot", None, "tile", None),
        P("slot", None, "tile", None),
        P("slot", None, "tile"),
    )
    out_specs = P("slot", None, None, "tile", None)
    return jax.shard_map(
        per_device, mesh=mesh, in_specs=in_specs, out_specs=out_specs, check_vma=False
    )
```

```python
import functools
import jax
import jax.numpy as jnp
from jax import lax
from jax.experimental import pallas as pl
from jax.experimental.pallas import tpu as pltpu
from jax.sharding import PartitionSpec as P

EPSILON = 1e-06
F32 = jnp.float32
BF16 = jnp.bfloat16
LANES = 128
CAP = 5
SLOTS = 4 * CAP
CHUNK = 32
META = 16
SENDERS = LANES // SLOTS
WIDE = 40
SLIM = 24
VMEM_LIMIT = 28 * 1024 * 1024


def dot(a, b):
    return jnp.dot(a, b, preferred_element_type=F32)


def dot_t(a, b):
    return lax.dot_general(a, b, (((1,), (1,)), ((), ())), preferred_element_type=F32)


def sublane(shape):
    return lax.broadcasted_iota(jnp.int32, shape, 0)


def inverse_rms(x):
    return lax.rsqrt(jnp.mean(x * x, axis=-1, keepdims=True) + EPSILON)


def sigmoid(p):
    return 0.5 * jnp.tanh(0.5 * p) + 0.5


def neighbours(rows):
    width = rows[0].shape[0]
    return [
        0.25 * (rows[1 - i] + pltpu.roll(rows[i], 1, 0) + pltpu.roll(rows[i], width - 1, 0))
        for i in range(2)
    ]


def forward_step(u, n, mean, act, pre, d, gain, ws, wn, wo, width, members, out, copies=()):
    both = 2 * width
    for m in range(members):
        base = m * both
        rows = []
        for lat in range(2):
            x = u[base + lat * width : base + (lat + 1) * width]
            rows.append((x * inverse_rms(x) * gain).astype(BF16).astype(F32))
        n[base : base + both] = jnp.concatenate(rows, axis=0).astype(BF16)
        mean[base : base + both] = jnp.concatenate(neighbours(rows), axis=0).astype(BF16)
    for copy in copies[:2]:
        copy.wait()
    pre[...] = dot(n[...], ws[...]) + dot(mean[...], wn[...])
    for m in range(members):
        base = m * both
        p = pre[base : base + both]
        sig = sigmoid(p)
        act[base : base + both] = (p * sig).astype(BF16)
        if d is not None:
            pre[base : base + both] = sig * (1.0 + p * (1.0 - sig))
    if d is not None:
        for m in range(members):
            slim_copy(d, pre, m)
    for copy in copies[2:]:
        copy.wait()
    pre[...] = dot(act[...], wo[...])
    for r in range(2 * members):
        out(r, u[r * width : (r + 1) * width] + pre[r * width : (r + 1) * width])


def slim_edge(wide, r):
    low = wide[r * WIDE + 16 : r * WIDE + 24]
    high = wide[r * WIDE + 32 : r * WIDE + 40]
    return jnp.where(sublane(low.shape) < 4, low, high)


def slim_copy(to, wide, m):
    parts = []
    for r in (2 * m, 2 * m + 1):
        parts += [wide[r * WIDE : r * WIDE + 16], slim_edge(wide, r)]
    both = jnp.concatenate(parts, axis=0)
    to[m * 2 * SLIM : (m + 1) * 2 * SLIM] = both.astype(to.dtype)


def reports(arrays, out_hbm, key, meta, picked, out, sem):
    pack(*arrays, out, key, meta, picked)
    store = pltpu.make_async_copy(out, out_hbm, sem)
    store.start()
    store.wait()


def early():
    return lax.axis_index("tile") < lax.axis_size("tile") // 2


def first_kernel(control_hbm, *refs):
    sources, (held, out_hbm), arrays, (key, meta, picked, out, sems) = refs[:5], refs[5:7], refs[7:12], refs[12:]
    copies = [
        pltpu.make_async_copy(source, to, sems.at[i]) for i, (source, to) in enumerate(zip(sources, arrays))
    ]
    copies.append(pltpu.make_async_copy(control_hbm, held, sems.at[5]))
    for copy in copies:
        copy.start()
    for copy in copies[:5]:
        copy.wait()

    @pl.when(early())
    def _():
        reports(arrays, out_hbm, key, meta, picked, out, sems.at[6])

    copies[5].wait()


def later_kernel(packed_hbm, *refs):
    arrays, out_hbm, (key, meta, picked, out, sem) = refs[:5], refs[6], refs[7:]

    @pl.when(jnp.logical_not(early()))
    def _():
        reports(arrays, out_hbm, key, meta, picked, out, sem)


def pack(owner, stencil, weights, precision, values, out, key, meta, picked):
    steps, _, rows = owner.shape
    tiles = out.shape[0] // CHUNK
    total = steps * rows
    place = lax.axis_index("tile") % SENDERS * SLOTS
    earlier = lax.broadcasted_iota(jnp.int32, (rows, rows), 0) < lax.broadcasted_iota(jnp.int32, (rows, rows), 1)
    earlier = earlier.astype(F32).astype(BF16)
    meta[...] = jnp.zeros_like(meta)
    for k in range(steps):
        at = slice(k * rows, (k + 1) * rows)
        named = lax.broadcasted_iota(jnp.int32, (tiles, rows), 0) == owner[k]
        hits = named.astype(F32)
        before = dot(hits.astype(BF16), earlier)
        rank = jnp.sum(hits * before, axis=0, keepdims=True).astype(jnp.int32)
        key[0:1, at] = owner[k] * (2 * CAP) + k * CAP + rank
        meta[4:8, at] = stencil[k].astype(F32)
        meta[8:12, at] = weights[k].astype(F32)
        meta[12:13, at] = precision[k : k + 1].astype(F32)
    row = lax.broadcasted_iota(jnp.int32, (tiles * CHUNK, total), 0)
    tile = row // CHUNK
    slot = row % CHUNK
    other = jnp.where(tile % 2 == 0, (tile + tiles - 1) % tiles, (tile + 1) % tiles)
    mine = slot < 2 * CAP
    wanted = jnp.where(mine, tile * (2 * CAP) + slot, other * (2 * CAP) + slot - 2 * CAP)
    wanted = jnp.where(slot < SLOTS, wanted, -1)
    placement = (wanted == key[...]).astype(F32).astype(BF16)
    picked[...] = dot(placement, values[...])
    entries = dot_t(meta[...].astype(BF16), placement)
    lane = lax.broadcasted_iota(jnp.int32, (META, LANES), 1)
    used = jnp.logical_and(lane >= place, lane < place + SLOTS)
    per_tile = LANES // CHUNK
    for t in range(tiles):
        block = entries[:, t // per_tile * LANES : (t // per_tile + 1) * LANES]
        shift = (place + LANES - t % per_tile * CHUNK) % LANES
        block = jnp.where(used, pltpu.roll(block, shift, 1), 0.0)
        low = picked[t * CHUNK + 16 : (t + 1) * CHUNK]
        picked[t * CHUNK + 16 : (t + 1) * CHUNK] = jnp.where(sublane((META, 1)) < 4, low, block)
    out[...] = picked[...].astype(BF16)


def tile_kernel(control, mate, out, held):
    even = lax.rem(lax.axis_index("tile"), 2) == 0
    size = control.shape[0]
    out[0:size] = control[...].astype(BF16)
    for r in range(size // 16):
        held[r * 2 : (r + 1) * 2] = jnp.where(
            even, mate[r * 16 : r * 16 + 2], mate[r * 16 + 14 : (r + 1) * 16]
        )
    out[size:] = held[...].astype(BF16)


def relay_kernel(control, mate, oth, out, near4, wide):
    even = lax.rem(lax.axis_index("tile"), 2) == 0
    size = mate.shape[0]
    out[0:size] = control[...]
    wide[...] = oth[0:size].astype(F32)
    for r in range(size // 16):
        a, b = r * 16, (r + 1) * 16
        out[size + r * 2 : size + (r + 1) * 2] = jnp.where(even, wide[b - 2 : b], wide[a : a + 2])
        near4[r * 4 : (r + 1) * 4] = jnp.where(even, mate[a : a + 4], mate[b - 4 : b])
        start = size + size // 8 + r * 2
        out[start : start + 2] = jnp.where(even, mate[a : a + 2], mate[b - 2 : b])


def forward_kernel(
    gain_hbm, ws_hbm, wn_hbm, wo_hbm, readout_hbm, control, mate, oth,
    edge0, u1x, d0x, d1x, f2x, field, final, wo, readout,
    ua, ub, n, mean, act, pre, edge, states, gain, ws, wn, sems,
):
    pairs = ((gain_hbm, gain), (ws_hbm, ws), (wn_hbm, wn), (wo_hbm, wo), (readout_hbm, readout))
    copies = [pltpu.make_async_copy(source, to, sems.at[i]) for i, (source, to) in enumerate(pairs)]
    for copy in copies:
        copy.start()
    members = final.shape[0] // 32
    even = lax.rem(lax.axis_index("tile"), 2) == 0
    tile_at = jnp.where(even, 24, 16)
    edge_at = jnp.where(even, 16, 32)
    far = oth[members * 32 :].astype(F32)
    for r in range(2 * members):
        ua[r * WIDE : r * WIDE + 16] = control[r * 16 : (r + 1) * 16]
        ua[pl.ds(pl.multiple_of(r * WIDE + tile_at, 8), 16)] = oth[r * 16 : (r + 1) * 16].astype(F32)
        near4 = mate[r * 4 : (r + 1) * 4]
        far2 = far[r * 2 : (r + 1) * 2]
        edge[...] = jnp.zeros_like(edge)
        edge[0:4] = near4
        edge[6:8] = far2
        edge[8:10] = far2
        edge[12:16] = near4
        ua[pl.ds(pl.multiple_of(r * WIDE + edge_at, 8), 8)] = jnp.where(even, edge[0:8], edge[8:16])
    for r in range(2 * members):
        edge0[r * 8 : (r + 1) * 8] = slim_edge(ua, r)
    copies[0].wait()
    g = gain[...]

    def keep(ref):
        def store(r, value):
            ref[r * WIDE : (r + 1) * WIDE] = value

        return store

    def keep_states(ref, k):
        own = k * members * 32
        away = (2 + k) * members * 32
        for r in range(2 * members):
            states[own + r * 16 : own + (r + 1) * 16] = ref[r * WIDE : r * WIDE + 16].astype(BF16)
            taken = ref[pl.ds(pl.multiple_of(r * WIDE + tile_at, 8), 16)]
            states[away + r * 16 : away + (r + 1) * 16] = taken.astype(BF16)

    forward_step(ua, n, mean, act, pre, d0x, g, ws, wn, wo, WIDE, members, keep(ub), copies[1:])
    for m in range(members):
        slim_copy(u1x, ub, m)
    keep_states(ub, 0)
    forward_step(ub, n, mean, act, pre, d1x, g, ws, wn, wo, WIDE, members, keep(ua))
    for m in range(members):
        slim_copy(f2x, ua, m)
    keep_states(ua, 1)
    final[...] = states[members * 32 : 2 * members * 32]
    read = dot(states[...], readout[...])
    for q in range(4):
        for m in range(members):
            start = (q * members + m) * 32
            field[q * 32 : (q + 1) * 32, m * LANES : (m + 1) * LANES] = read[start : start + 32]


def split(x):
    high = x.astype(BF16)
    return high, (x - high.astype(F32)).astype(BF16)


def observe_kernel(
    tiles,
    error_hbm, control_hbm, background_hbm, arrived, field,
    spread, message, error, control, background,
    th, tl, ph, plo, vals, wide, sems,
):
    pairs = ((error_hbm, error), (control_hbm, control), (background_hbm, background))
    copies = [pltpu.make_async_copy(source, to, sems.at[i]) for i, (source, to) in enumerate(pairs)]
    for copy in copies:
        copy.start()
    steps = 2
    members = field.shape[1] // LANES
    even = lax.rem(lax.axis_index("tile"), 2) == 0
    cells = sublane((32, LANES)).astype(F32)
    lane = lax.broadcasted_iota(jnp.int32, (1, LANES), 1)
    table_of = jnp.where(lane < SENDERS * SLOTS, lane % SLOTS // CAP, -1)
    wide[...] = arrived[...].astype(F32)
    vals[...] = jnp.zeros_like(vals)
    for p in range(th.shape[1] // LANES):
        meta = jnp.zeros((META, LANES), F32)
        for d in range(p * SENDERS, min((p + 1) * SENDERS, tiles)):
            meta += wide[d * CHUNK + 16 : (d + 1) * CHUNK]
            start = p * LANES + d % SENDERS * SLOTS
            vals[start : start + SLOTS] = wide[d * CHUNK : d * CHUNK + SLOTS]
        weight = jnp.zeros((32, LANES), F32)
        for i in range(4):
            weight += jnp.where(cells == meta[4 + i : 5 + i], meta[8 + i : 9 + i], 0.0)
        at = slice(p * LANES, (p + 1) * LANES)
        th[:, at], tl[:, at] = split(weight)
        scaled = weight * meta[12:13]
        for q in range(2 * steps):
            kept = jnp.where(table_of == q, scaled, 0.0)
            ph[q * 32 : (q + 1) * 32, at], plo[q * 32 : (q + 1) * 32, at] = split(kept)
    cross = dot_t(ph[...], th[...]) + dot_t(plo[...], th[...]) + dot_t(ph[...], tl[...])
    block = jnp.concatenate([cross] * (2 * steps), axis=1)
    on_block = sublane(block.shape) // 32 == lax.broadcasted_iota(jnp.int32, block.shape, 1) // 32
    cross = jnp.where(on_block, block, 0.0)
    taken = vals[...].astype(BF16)
    target = dot(ph[...], taken) + dot(plo[...], taken)
    ch, cl = split(cross)
    fh, fl = split(field[...])
    mixed = dot(ch, fh) + dot(cl, fh) + dot(ch, fl)
    for q in range(2 * steps):
        for m in range(members):
            start = (q * members + m) * 32
            value = mixed[q * 32 : (q + 1) * 32, m * LANES : (m + 1) * LANES] - target[q * 32 : (q + 1) * 32]
            spread[start : start + 32] = value.astype(BF16)
    size = members * 32
    for k in range(steps):
        for m in range(members):
            start = k * size + m * 32
            pair = spread[start : start + 32].astype(F32)
            near = [jnp.where(even, pair[i + 8 : i + 16], pair[i : i + 8]) for i in (0, 16)]
            start = k * size // 2 + m * 16
            message[start : start + 16] = jnp.concatenate(near, axis=0).astype(BF16)
    for copy in copies:
        copy.wait()


def adjoint_step(u, cot, gb, gm, flat, d, out, gain, ws, wn, wo, members):
    both = 2 * SLIM
    gb[...] = cot[...].astype(BF16)
    flat[...] = dot_t(gb[...], wo[...])
    gb[...] = (flat[...] * d[...]).astype(BF16)
    gm[...] = dot_t(gb[...], wn[...])
    flat[...] = dot_t(gb[...], ws[...])
    for m in range(members):
        base = m * both
        rows = []
        for lat in range(2):
            start = base + lat * SLIM
            rows.append(gm[start : start + SLIM].astype(BF16).astype(F32))
        around = neighbours(rows)
        for lat in range(2):
            start = base + lat * SLIM
            x = u[start : start + SLIM]
            s = inverse_rms(x)
            scaled = gain * (flat[start : start + SLIM] + around[lat])
            inner = jnp.mean(x * scaled, axis=-1, keepdims=True)
            out(2 * m + lat, cot[start : start + SLIM] + s * scaled - x * (s * s * s * inner))


def edges(nxt, size, edge, r):
    even = lax.rem(lax.axis_index("tile"), 2) == 0
    start = size + r * 2
    far = nxt[start : start + 2]
    start = size + size // 8 + r * 2
    near = nxt[start : start + 2]
    edge[...] = jnp.zeros_like(edge)
    edge[0:2] = near
    edge[6:8] = far
    edge[8:10] = far
    edge[14:16] = near
    return jnp.where(even, edge[0:8], edge[8:16])


def pull_kernel(
    wn_hbm, ws_hbm, gain_hbm, spread, readout,
    last, first, wn, ws, gain,
    pulled, sems,
):
    pairs = ((wn_hbm, wn), (ws_hbm, ws), (gain_hbm, gain))
    copies = [pltpu.make_async_copy(source, to, sems.at[i]) for i, (source, to) in enumerate(pairs)]
    for copy in copies:
        copy.start()
    size = pulled.shape[0] // 4
    even = lax.rem(lax.axis_index("tile"), 2) == 0
    row8 = sublane((8, 1))
    pulled[...] = dot_t(spread[...], readout[...])
    for k, out in enumerate((first, last)):
        for r in range(size // 16):
            start = k * size + r * 16
            out[r * SLIM : r * SLIM + 16] = pulled[start : start + 16]
            start += 2 * size
            low = jnp.where(row8 < 4, pulled[start : start + 8], 0.0)
            high = jnp.where(row8 >= 4, pulled[start + 8 : start + 16], 0.0)
            out[r * SLIM + 16 : (r + 1) * SLIM] = jnp.where(even, high, low)
    for copy in copies:
        copy.wait()


def backward_kernel(
    last, early_pull, wn, ws, gain, control, background, edge0, nxt, f2x, wo, readout, error, message,
    u1x, d0x, d1x, before,
    result,
    cot2, cot1, add, gb, gm, flat, mate_pull, edge, u0x, final, held, sems,
):
    size = held.shape[0]
    members = size // 32
    even = lax.rem(lax.axis_index("tile"), 2) == 0
    slot = lax.axis_index("slot")
    first = slot == 0
    weight = jnp.where(slot == lax.axis_size("slot") - 1, 0.0, 1.0) * error[...]
    row8 = sublane((8, 1))
    mate_side = jnp.where(even, 1, 0) == jnp.where(row8 < 4, 1, 0)
    mate_pull[...] = dot_t(message[...], readout[...])
    final[...] = f2x[...].astype(F32)
    add[...] = early_pull[...]
    for r in range(2 * members):
        a, b = r * SLIM, r * SLIM + 16
        cot2[a:b] = last[a:b] - weight * (nxt[r * 16 : (r + 1) * 16] - final[a:b])
        u0x[a:b] = control[r * 16 : (r + 1) * 16]
        a, b = b, b + 8
        start = size // 2 + r * 8
        pulled = last[a:b] + jnp.where(mate_side, mate_pull[start : start + 8], 0.0)
        cot2[a:b] = pulled - weight * (edges(nxt, size, edge, r) - final[a:b])
        add[a:b] = early_pull[a:b] + jnp.where(mate_side, mate_pull[r * 8 : (r + 1) * 8], 0.0)
        u0x[a:b] = edge0[r * 8 : (r + 1) * 8]
    def keep(r, value):
        cot1[r * SLIM : (r + 1) * SLIM] = value + add[r * SLIM : (r + 1) * SLIM]

    copies = []

    def finish(r, value):
        a, b, start = r * 16, (r + 1) * 16, r * SLIM
        taken = jnp.where(first, background[a:b].astype(F32), before[a:b].astype(F32))
        held[a:b] = value[0:16] + error[...] * (u0x[start : start + 16] - taken)
        if r % 2 == 1:
            rows = pl.ds(b - 32, 32)
            copies.append(pltpu.make_async_copy(held.at[rows], result.at[rows], sems.at[r // 2]))
            copies[-1].start()

    adjoint_step(u1x, cot2, gb, gm, flat, d1x, keep, gain[...], ws, wn, wo, members)
    adjoint_step(u0x, cot1, gb, gm, flat, d0x, finish, gain[...], ws, wn, wo, members)
    for copy in copies:
        copy.wait()


def kernel_call(body, outs, scratch, flops, moved, hbm=0, out_places=None, aliases={}):
    def call(*operands):
        fixed = [i in range(hbm) and i not in aliases for i in range(len(operands))]
        operands = [
            pltpu.with_memory_space_constraint(x, pltpu.HBM) if fix else x for x, fix in zip(operands, fixed)
        ]
        places = [pltpu.HBM] * hbm + [pltpu.VMEM] * (len(operands) - hbm)
        given = {} if out_places is None else {"out_specs": [pl.BlockSpec(memory_space=p) for p in out_places]}
        return pl.pallas_call(
            body,
            out_shape=outs,
            in_specs=[pl.BlockSpec(memory_space=place) for place in places],
            **given,
            scratch_shapes=scratch,
            input_output_aliases=aliases,
            compiler_params=pltpu.CompilerParams(vmem_limit_bytes=VMEM_LIMIT),
            cost_estimate=pl.CostEstimate(flops=flops, bytes_accessed=moved, transcendentals=0),
        )(*operands)

    return call


def per_device(
    control,
    background,
    self_weight,
    neighbour_weight,
    output_weight,
    norm_gain,
    readout,
    error_weight,
    report_owner,
    report_stencil,
    report_weights,
    report_values,
    report_precision,
):
    tiles = lax.axis_size("tile")
    slots = lax.axis_size("slot")
    members, lats, cols, channels = control.shape[1:]
    groups = members * lats
    size = groups * cols
    steps = report_owner.shape[1]
    rows = report_owner.shape[2]
    gain = norm_gain.reshape(1, channels)
    error = error_weight.reshape(1, channels)
    flat = control.reshape(size, channels)

    def spec(count, dtype=F32, width=channels):
        return jax.ShapeDtypeStruct((count, width), dtype)

    def scratch(count, dtype=F32, width=channels):
        return pltpu.VMEM((count, width), dtype)

    mate_of = [(i, i ^ 1) for i in range(tiles)]
    other_of = [(i, (i - 1) % tiles if i % 2 == 0 else (i + 1) % tiles) for i in range(tiles)]

    def across(block, shift):
        pairs = [
            ((s + shift) * tiles + i, s * tiles + i)
            for s in range(slots)
            for i in range(tiles)
            if 0 <= s + shift < slots
        ]
        return lax.ppermute(block, ("slot", "tile"), pairs)

    mate = lax.ppermute(flat, "tile", mate_of)
    listed = (
        jnp.transpose(report_owner[0], (0, 2, 1)),
        jnp.transpose(report_stencil[0], (0, 2, 1)),
        jnp.transpose(report_weights[0], (0, 2, 1)),
        report_precision[0],
        report_values[0].reshape(steps * rows, LANES),
    )
    work = [
        pltpu.VMEM((1, steps * rows), jnp.int32),
        scratch(META, F32, steps * rows),
        scratch(tiles * CHUNK, F32, LANES),
        scratch(tiles * CHUNK, BF16, LANES),
    ]
    held, packed, *listed = kernel_call(
        first_kernel,
        [spec(size), spec(tiles * CHUNK, BF16, LANES)]
        + [jax.ShapeDtypeStruct(block.shape, block.dtype) for block in listed],
        work + [pltpu.SemaphoreType.DMA((7,))],
        10**7,
        200000,
        hbm=6,
        out_places=[pltpu.VMEM, pltpu.HBM] + [pltpu.VMEM] * 5,
    )(flat, *listed)
    sent = kernel_call(
        tile_kernel, spec(groups * (cols + 2), BF16), [scratch(groups * 2)], 1000, 400000
    )(held, mate)
    oth = lax.ppermute(sent, "tile", other_of)
    (packed,) = kernel_call(
        later_kernel,
        [spec(tiles * CHUNK, BF16, LANES)],
        work + [pltpu.SemaphoreType.DMA],
        10**7,
        200000,
        hbm=1,
        out_places=[pltpu.HBM],
        aliases={0: 0},
    )(packed, *listed, sent)
    arrived = lax.all_to_all(packed, "tile", split_axis=0, concat_axis=0, tiled=True)

    message, near4 = kernel_call(
        relay_kernel, [spec(size + 4 * groups), spec(4 * groups)], [scratch(size)], 1000, 700000
    )(held, mate, oth)
    nxt = across(message, 1)
    wide = groups * WIDE
    slim = groups * SLIM
    edge0, u1x, d0x, d1x, f2x, field, final, wo, readout_held = kernel_call(
        forward_kernel,
        [spec(groups * 8), spec(slim)] + [spec(slim, BF16)] * 3
        + [spec(4 * lats * cols, F32, members * LANES), spec(size, BF16)]
        + [spec(channels, BF16), spec(channels, BF16, LANES)],
        [scratch(wide), scratch(wide), scratch(wide, BF16), scratch(wide, BF16), scratch(wide, BF16)]
        + [scratch(wide), scratch(16), scratch(4 * size, BF16)]
        + [scratch(1), scratch(channels, BF16), scratch(channels, BF16), pltpu.SemaphoreType.DMA((5,))],
        10**11,
        4000000,
        hbm=5,
    )(gain, self_weight, neighbour_weight, output_weight, readout, held, near4, oth)
    before = across(final, -1)
    total = -(-tiles // SENDERS) * LANES
    spread, near_spread, error, held, background = kernel_call(
        functools.partial(observe_kernel, tiles),
        [spec(4 * size, BF16, LANES), spec(size, BF16, LANES), spec(1), spec(size), spec(size, BF16)],
        [scratch(32, BF16, total)] * 2 + [scratch(128, BF16, total)] * 2
        + [scratch(total, F32, LANES), scratch(tiles * CHUNK, F32, LANES), pltpu.SemaphoreType.DMA((3,))],
        10**9,
        2000000,
        hbm=3,
    )(error, flat, background.reshape(size, channels), arrived, field)
    from_mate = lax.ppermute(near_spread, "tile", mate_of)
    handed = kernel_call(
        pull_kernel,
        [spec(slim), spec(slim), spec(channels, BF16), spec(channels, BF16), spec(1)],
        [scratch(4 * size), pltpu.SemaphoreType.DMA((3,))],
        10**9,
        3000000,
        hbm=3,
    )(neighbour_weight, self_weight, gain, spread, readout_held)
    (result,) = kernel_call(
        backward_kernel,
        [spec(size)],
        [scratch(slim), scratch(slim), scratch(slim), scratch(slim, BF16), scratch(slim), scratch(slim)]
        + [scratch(size), scratch(16), scratch(slim), scratch(slim), scratch(size)]
        + [pltpu.SemaphoreType.DMA((members,))],
        12 * slim * channels * channels,
        6000000,
        out_places=[pltpu.HBM],
    )(
        *handed, held, background, edge0, nxt, f2x, wo, readout_held, error, from_mate,
        u1x, d0x, d1x, before,
    )
    return result.reshape(control.shape)


def solution(mesh):
    in_specs = (
        P("slot", None, None, "tile", None),
        P(None, None, "tile", None),
        P(),
        P(),
        P(),
        P(),
        P(),
        P(),
        P("slot", None, "tile", None),
        P("slot", None, "tile", None),
        P("slot", None, "tile", None),
        P("slot", None, "tile", None),
        P("slot", None, "tile"),
    )
    out_specs = P("slot", None, None, "tile", None)
    return jax.shard_map(
        per_device, mesh=mesh, in_specs=in_specs, out_specs=out_specs, check_vma=False
    )
```

```python
import functools
import jax
import jax.numpy as jnp
from jax import lax
from jax.experimental import pallas as pl
from jax.experimental.pallas import tpu as pltpu
from jax.sharding import PartitionSpec as P

EPSILON = 1e-06
F32 = jnp.float32
BF16 = jnp.bfloat16
LANES = 128
CAP = 5
SLOTS = 4 * CAP
CHUNK = 32
META = 16
SENDERS = LANES // SLOTS
WIDE = 40
SLIM = 24
VMEM_LIMIT = 28 * 1024 * 1024


def dot(a, b):
    return jnp.dot(a, b, preferred_element_type=F32)


def dot_t(a, b):
    return lax.dot_general(a, b, (((1,), (1,)), ((), ())), preferred_element_type=F32)


def sublane(shape):
    return lax.broadcasted_iota(jnp.int32, shape, 0)


def inverse_rms(x):
    return lax.rsqrt(jnp.mean(x * x, axis=-1, keepdims=True) + EPSILON)


def sigmoid(p):
    return 0.5 * jnp.tanh(0.5 * p) + 0.5


def neighbours(rows):
    width = rows[0].shape[0]
    return [
        0.25 * (rows[1 - i] + pltpu.roll(rows[i], 1, 0) + pltpu.roll(rows[i], width - 1, 0))
        for i in range(2)
    ]


def forward_step(u, n, mean, act, pre, d, gain, ws, wn, wo, width, members, out, copies=()):
    both = 2 * width
    for m in range(members):
        base = m * both
        rows = []
        for lat in range(2):
            x = u[base + lat * width : base + (lat + 1) * width]
            rows.append((x * inverse_rms(x) * gain).astype(BF16).astype(F32))
        n[base : base + both] = jnp.concatenate(rows, axis=0).astype(BF16)
        mean[base : base + both] = jnp.concatenate(neighbours(rows), axis=0).astype(BF16)
    for copy in copies[:2]:
        copy.wait()
    pre[...] = dot(n[...], ws[...]) + dot(mean[...], wn[...])
    for m in range(members):
        base = m * both
        p = pre[base : base + both]
        sig = sigmoid(p)
        act[base : base + both] = (p * sig).astype(BF16)
        if d is not None:
            pre[base : base + both] = sig * (1.0 + p * (1.0 - sig))
    if d is not None:
        for m in range(members):
            slim_copy(d, pre, m)
    for copy in copies[2:]:
        copy.wait()
    pre[...] = dot(act[...], wo[...])
    for r in range(2 * members):
        out(r, u[r * width : (r + 1) * width] + pre[r * width : (r + 1) * width])


def slim_edge(wide, r):
    low = wide[r * WIDE + 16 : r * WIDE + 24]
    high = wide[r * WIDE + 32 : r * WIDE + 40]
    return jnp.where(sublane(low.shape) < 4, low, high)


def slim_copy(to, wide, m):
    parts = []
    for r in (2 * m, 2 * m + 1):
        parts += [wide[r * WIDE : r * WIDE + 16], slim_edge(wide, r)]
    both = jnp.concatenate(parts, axis=0)
    to[m * 2 * SLIM : (m + 1) * 2 * SLIM] = both.astype(to.dtype)


def reports(arrays, out_hbm, key, meta, picked, out, sem):
    pack(*arrays, out, key, meta, picked)
    store = pltpu.make_async_copy(out, out_hbm, sem)
    store.start()
    store.wait()


def early():
    return lax.axis_index("tile") < lax.axis_size("tile") // 2


def first_kernel(control_hbm, *refs):
    sources, (held, out_hbm), arrays, (key, meta, picked, out, sems) = refs[:5], refs[5:7], refs[7:12], refs[12:]
    copies = [
        pltpu.make_async_copy(source, to, sems.at[i]) for i, (source, to) in enumerate(zip(sources, arrays))
    ]
    copies.append(pltpu.make_async_copy(control_hbm, held, sems.at[5]))
    for copy in copies:
        copy.start()
    for copy in copies[:5]:
        copy.wait()

    @pl.when(early())
    def _():
        reports(arrays, out_hbm, key, meta, picked, out, sems.at[6])

    copies[5].wait()


def later_kernel(packed_hbm, *refs):
    arrays, out_hbm, (key, meta, picked, out, sem) = refs[:5], refs[6], refs[7:]

    @pl.when(jnp.logical_not(early()))
    def _():
        reports(arrays, out_hbm, key, meta, picked, out, sem)


def pack(owner, stencil, weights, precision, values, out, key, meta, picked):
    steps, _, rows = owner.shape
    tiles = out.shape[0] // CHUNK
    total = steps * rows
    place = lax.axis_index("tile") % SENDERS * SLOTS
    earlier = lax.broadcasted_iota(jnp.int32, (rows, rows), 0) < lax.broadcasted_iota(jnp.int32, (rows, rows), 1)
    earlier = earlier.astype(F32).astype(BF16)
    meta[...] = jnp.zeros_like(meta)
    for k in range(steps):
        at = slice(k * rows, (k + 1) * rows)
        named = lax.broadcasted_iota(jnp.int32, (tiles, rows), 0) == owner[k]
        hits = named.astype(F32)
        before = dot(hits.astype(BF16), earlier)
        rank = jnp.sum(hits * before, axis=0, keepdims=True).astype(jnp.int32)
        key[0:1, at] = owner[k] * (2 * CAP) + k * CAP + rank
        meta[4:8, at] = stencil[k].astype(F32)
        meta[8:12, at] = weights[k].astype(F32)
        meta[12:13, at] = precision[k : k + 1].astype(F32)
    row = lax.broadcasted_iota(jnp.int32, (tiles * CHUNK, total), 0)
    tile = row // CHUNK
    slot = row % CHUNK
    other = jnp.where(tile % 2 == 0, (tile + tiles - 1) % tiles, (tile + 1) % tiles)
    mine = slot < 2 * CAP
    wanted = jnp.where(mine, tile * (2 * CAP) + slot, other * (2 * CAP) + slot - 2 * CAP)
    wanted = jnp.where(slot < SLOTS, wanted, -1)
    placement = (wanted == key[...]).astype(F32).astype(BF16)
    picked[...] = dot(placement, values[...])
    entries = dot_t(meta[...].astype(BF16), placement)
    lane = lax.broadcasted_iota(jnp.int32, (META, LANES), 1)
    used = jnp.logical_and(lane >= place, lane < place + SLOTS)
    per_tile = LANES // CHUNK
    for t in range(tiles):
        block = entries[:, t // per_tile * LANES : (t // per_tile + 1) * LANES]
        shift = (place + LANES - t % per_tile * CHUNK) % LANES
        block = jnp.where(used, pltpu.roll(block, shift, 1), 0.0)
        low = picked[t * CHUNK + 16 : (t + 1) * CHUNK]
        picked[t * CHUNK + 16 : (t + 1) * CHUNK] = jnp.where(sublane((META, 1)) < 4, low, block)
    out[...] = picked[...].astype(BF16)


def tile_kernel(control, mate, out, held):
    even = lax.rem(lax.axis_index("tile"), 2) == 0
    size = control.shape[0]
    out[0:size] = control[...].astype(BF16)
    for r in range(size // 16):
        held[r * 2 : (r + 1) * 2] = jnp.where(
            even, mate[r * 16 : r * 16 + 2], mate[r * 16 + 14 : (r + 1) * 16]
        )
    out[size:] = held[...].astype(BF16)


def relay_kernel(control, mate, oth, out, near4, wide, edge):
    even = lax.rem(lax.axis_index("tile"), 2) == 0
    size = mate.shape[0]
    out[0:size] = control[...].astype(BF16)
    wide[...] = oth[0:size].astype(F32)
    for r in range(size // 16):
        a, b = r * 16, (r + 1) * 16
        edge[r * 2 : (r + 1) * 2] = jnp.where(even, wide[b - 2 : b], wide[a : a + 2])
        near4[r * 4 : (r + 1) * 4] = jnp.where(even, mate[a : a + 4], mate[b - 4 : b])
        start = size // 8 + r * 2
        edge[start : start + 2] = jnp.where(even, mate[a : a + 2], mate[b - 2 : b])
    out[size:] = edge[...].astype(BF16)


def forward_kernel(
    gain_hbm, ws_hbm, wn_hbm, wo_hbm, readout_hbm, error_hbm, background_hbm, control, mate, oth,
    edge0, u1x, d0x, d1x, f2x, field, final, wo, readout, gain, error, background,
    ua, ub, n, mean, act, pre, edge, states, ws, wn, sems,
):
    pairs = (
        (gain_hbm, gain), (ws_hbm, ws), (wn_hbm, wn), (wo_hbm, wo), (readout_hbm, readout),
        (error_hbm, error), (background_hbm, background),
    )
    copies = [pltpu.make_async_copy(source, to, sems.at[i]) for i, (source, to) in enumerate(pairs)]
    for copy in copies:
        copy.start()
    members = final.shape[0] // 32
    even = lax.rem(lax.axis_index("tile"), 2) == 0
    tile_at = jnp.where(even, 24, 16)
    edge_at = jnp.where(even, 16, 32)
    far = oth[members * 32 :].astype(F32)
    for r in range(2 * members):
        ua[r * WIDE : r * WIDE + 16] = control[r * 16 : (r + 1) * 16]
        ua[pl.ds(pl.multiple_of(r * WIDE + tile_at, 8), 16)] = oth[r * 16 : (r + 1) * 16].astype(F32)
        near4 = mate[r * 4 : (r + 1) * 4]
        far2 = far[r * 2 : (r + 1) * 2]
        edge[...] = jnp.zeros_like(edge)
        edge[0:4] = near4
        edge[6:8] = far2
        edge[8:10] = far2
        edge[12:16] = near4
        ua[pl.ds(pl.multiple_of(r * WIDE + edge_at, 8), 8)] = jnp.where(even, edge[0:8], edge[8:16])
    for r in range(2 * members):
        edge0[r * 8 : (r + 1) * 8] = slim_edge(ua, r)
    copies[0].wait()
    g = gain[...]

    def keep(ref):
        def store(r, value):
            ref[r * WIDE : (r + 1) * WIDE] = value

        return store

    def keep_states(ref, k):
        own = k * members * 32
        away = (2 + k) * members * 32
        for r in range(2 * members):
            states[own + r * 16 : own + (r + 1) * 16] = ref[r * WIDE : r * WIDE + 16].astype(BF16)
            taken = ref[pl.ds(pl.multiple_of(r * WIDE + tile_at, 8), 16)]
            states[away + r * 16 : away + (r + 1) * 16] = taken.astype(BF16)

    forward_step(ua, n, mean, act, pre, d0x, g, ws, wn, wo, WIDE, members, keep(ub), copies[1:])
    for m in range(members):
        slim_copy(u1x, ub, m)
    keep_states(ub, 0)
    forward_step(ub, n, mean, act, pre, d1x, g, ws, wn, wo, WIDE, members, keep(ua))
    for m in range(members):
        slim_copy(f2x, ua, m)
    keep_states(ua, 1)
    final[...] = states[members * 32 : 2 * members * 32]
    read = dot(states[...], readout[...])
    for q in range(4):
        for m in range(members):
            start = (q * members + m) * 32
            field[q * 32 : (q + 1) * 32, m * LANES : (m + 1) * LANES] = read[start : start + 32]


def split(x):
    high = x.astype(BF16)
    return high, (x - high.astype(F32)).astype(BF16)


def observe_kernel(
    tiles, arrived, field,
    spread, message,
    th, tl, ph, plo, vals, wide,
):
    steps = 2
    members = field.shape[1] // LANES
    even = lax.rem(lax.axis_index("tile"), 2) == 0
    cells = sublane((32, LANES)).astype(F32)
    lane = lax.broadcasted_iota(jnp.int32, (1, LANES), 1)
    table_of = jnp.where(lane < SENDERS * SLOTS, lane % SLOTS // CAP, -1)
    wide[...] = arrived[...].astype(F32)
    vals[...] = jnp.zeros_like(vals)
    for p in range(th.shape[1] // LANES):
        meta = jnp.zeros((META, LANES), F32)
        for d in range(p * SENDERS, min((p + 1) * SENDERS, tiles)):
            meta += wide[d * CHUNK + 16 : (d + 1) * CHUNK]
            start = p * LANES + d % SENDERS * SLOTS
            vals[start : start + SLOTS] = wide[d * CHUNK : d * CHUNK + SLOTS]
        weight = jnp.zeros((32, LANES), F32)
        for i in range(4):
            weight += jnp.where(cells == meta[4 + i : 5 + i], meta[8 + i : 9 + i], 0.0)
        at = slice(p * LANES, (p + 1) * LANES)
        th[:, at], tl[:, at] = split(weight)
        scaled = weight * meta[12:13]
        for q in range(2 * steps):
            kept = jnp.where(table_of == q, scaled, 0.0)
            ph[q * 32 : (q + 1) * 32, at], plo[q * 32 : (q + 1) * 32, at] = split(kept)
    cross = dot_t(ph[...], th[...]) + dot_t(plo[...], th[...]) + dot_t(ph[...], tl[...])
    block = jnp.concatenate([cross] * (2 * steps), axis=1)
    on_block = sublane(block.shape) // 32 == lax.broadcasted_iota(jnp.int32, block.shape, 1) // 32
    cross = jnp.where(on_block, block, 0.0)
    taken = vals[...].astype(BF16)
    target = dot(ph[...], taken) + dot(plo[...], taken)
    ch, cl = split(cross)
    fh, fl = split(field[...])
    mixed = dot(ch, fh) + dot(cl, fh) + dot(ch, fl)
    for q in range(2 * steps):
        for m in range(members):
            start = (q * members + m) * 32
            value = mixed[q * 32 : (q + 1) * 32, m * LANES : (m + 1) * LANES] - target[q * 32 : (q + 1) * 32]
            spread[start : start + 32] = value.astype(BF16)
    size = members * 32
    for k in range(steps):
        for m in range(members):
            start = k * size + m * 32
            pair = spread[start : start + 32].astype(F32)
            near = [jnp.where(even, pair[i + 8 : i + 16], pair[i : i + 8]) for i in (0, 16)]
            start = k * size // 2 + m * 16
            message[start : start + 16] = jnp.concatenate(near, axis=0).astype(BF16)


def adjoint_step(u, cot, gb, gm, flat, d, out, gain, ws, wn, wo, members):
    both = 2 * SLIM
    gb[...] = cot[...].astype(BF16)
    flat[...] = dot_t(gb[...], wo[...])
    gb[...] = (flat[...] * d[...]).astype(BF16)
    gm[...] = dot_t(gb[...], wn[...])
    flat[...] = dot_t(gb[...], ws[...])
    for m in range(members):
        base = m * both
        rows = []
        for lat in range(2):
            start = base + lat * SLIM
            rows.append(gm[start : start + SLIM].astype(BF16).astype(F32))
        around = neighbours(rows)
        for lat in range(2):
            start = base + lat * SLIM
            x = u[start : start + SLIM]
            s = inverse_rms(x)
            scaled = gain * (flat[start : start + SLIM] + around[lat])
            inner = jnp.mean(x * scaled, axis=-1, keepdims=True)
            out(2 * m + lat, cot[start : start + SLIM] + s * scaled - x * (s * s * s * inner))


def edges(nxt, size, edge, r):
    even = lax.rem(lax.axis_index("tile"), 2) == 0
    start = size + r * 2
    far = nxt[start : start + 2]
    start = size + size // 8 + r * 2
    near = nxt[start : start + 2]
    edge[...] = jnp.zeros_like(edge)
    edge[0:2] = near
    edge[6:8] = far
    edge[8:10] = far
    edge[14:16] = near
    return jnp.where(even, edge[0:8], edge[8:16])


def pull_kernel(
    wn_hbm, ws_hbm, spread, readout,
    last, first, wn, ws,
    pulled, sems,
):
    pairs = ((wn_hbm, wn), (ws_hbm, ws))
    copies = [pltpu.make_async_copy(source, to, sems.at[i]) for i, (source, to) in enumerate(pairs)]
    for copy in copies:
        copy.start()
    size = pulled.shape[0] // 4
    even = lax.rem(lax.axis_index("tile"), 2) == 0
    row8 = sublane((8, 1))
    pulled[...] = dot_t(spread[...], readout[...])
    for k, out in enumerate((first, last)):
        for r in range(size // 16):
            start = k * size + r * 16
            out[r * SLIM : r * SLIM + 16] = pulled[start : start + 16]
            start += 2 * size
            low = jnp.where(row8 < 4, pulled[start : start + 8], 0.0)
            high = jnp.where(row8 >= 4, pulled[start + 8 : start + 16], 0.0)
            out[r * SLIM + 16 : (r + 1) * SLIM] = jnp.where(even, high, low)
    for copy in copies:
        copy.wait()


def backward_kernel(
    last, early_pull, wn, ws, gain, control, edge0, message16, f2x, wo, readout, error, message,
    u1x, d0x, d1x,
    result,
    cot2, cot1, add, gb, gm, flat, mate_pull, edge, u0x, final, nxt,
):
    size = result.shape[0]
    members = size // 32
    even = lax.rem(lax.axis_index("tile"), 2) == 0
    nxt[...] = message16[...].astype(F32)
    weight = jnp.where(lax.axis_index("slot") == lax.axis_size("slot") - 1, 0.0, 1.0) * error[...]
    row8 = sublane((8, 1))
    mate_side = jnp.where(even, 1, 0) == jnp.where(row8 < 4, 1, 0)
    mate_pull[...] = dot_t(message[...], readout[...])
    final[...] = f2x[...].astype(F32)
    add[...] = early_pull[...]
    for r in range(2 * members):
        a, b = r * SLIM, r * SLIM + 16
        cot2[a:b] = last[a:b] - weight * (nxt[r * 16 : (r + 1) * 16] - final[a:b])
        u0x[a:b] = control[r * 16 : (r + 1) * 16]
        a, b = b, b + 8
        start = size // 2 + r * 8
        pulled = last[a:b] + jnp.where(mate_side, mate_pull[start : start + 8], 0.0)
        cot2[a:b] = pulled - weight * (edges(nxt, size, edge, r) - final[a:b])
        add[a:b] = early_pull[a:b] + jnp.where(mate_side, mate_pull[r * 8 : (r + 1) * 8], 0.0)
        u0x[a:b] = edge0[r * 8 : (r + 1) * 8]
    def keep(r, value):
        cot1[r * SLIM : (r + 1) * SLIM] = value + add[r * SLIM : (r + 1) * SLIM]

    def finish(r, value):
        a, b = r * SLIM, r * SLIM + 16
        result[r * 16 : (r + 1) * 16] = value[0:16] + error[...] * u0x[a:b]

    adjoint_step(u1x, cot2, gb, gm, flat, d1x, keep, gain[...], ws, wn, wo, members)
    adjoint_step(u0x, cot1, gb, gm, flat, d0x, finish, gain[...], ws, wn, wo, members)


def last_kernel(base, background, before, error, result):
    first = lax.axis_index("slot") == 0
    taken = jnp.where(first, background[...].astype(F32), before[...].astype(F32))
    result[...] = base[...] - error[...] * taken


def kernel_call(body, outs, scratch, flops, moved, hbm=0, out_places=None, aliases={}):
    def call(*operands):
        fixed = [i in range(hbm) and i not in aliases for i in range(len(operands))]
        operands = [
            pltpu.with_memory_space_constraint(x, pltpu.HBM) if fix else x for x, fix in zip(operands, fixed)
        ]
        places = [pltpu.HBM] * hbm + [pltpu.VMEM] * (len(operands) - hbm)
        given = {} if out_places is None else {"out_specs": [pl.BlockSpec(memory_space=p) for p in out_places]}
        return pl.pallas_call(
            body,
            out_shape=outs,
            in_specs=[pl.BlockSpec(memory_space=place) for place in places],
            **given,
            scratch_shapes=scratch,
            input_output_aliases=aliases,
            compiler_params=pltpu.CompilerParams(vmem_limit_bytes=VMEM_LIMIT),
            cost_estimate=pl.CostEstimate(flops=flops, bytes_accessed=moved, transcendentals=0),
        )(*operands)

    return call


def per_device(
    control,
    background,
    self_weight,
    neighbour_weight,
    output_weight,
    norm_gain,
    readout,
    error_weight,
    report_owner,
    report_stencil,
    report_weights,
    report_values,
    report_precision,
):
    tiles = lax.axis_size("tile")
    slots = lax.axis_size("slot")
    members, lats, cols, channels = control.shape[1:]
    groups = members * lats
    size = groups * cols
    steps = report_owner.shape[1]
    rows = report_owner.shape[2]
    gain = norm_gain.reshape(1, channels)
    error = error_weight.reshape(1, channels)
    flat = control.reshape(size, channels)

    def spec(count, dtype=F32, width=channels):
        return jax.ShapeDtypeStruct((count, width), dtype)

    def scratch(count, dtype=F32, width=channels):
        return pltpu.VMEM((count, width), dtype)

    mate_of = [(i, i ^ 1) for i in range(tiles)]
    other_of = [(i, (i - 1) % tiles if i % 2 == 0 else (i + 1) % tiles) for i in range(tiles)]

    def across(block, shift):
        pairs = [
            ((s + shift) % slots * tiles + i, s * tiles + i) for s in range(slots) for i in range(tiles)
        ]
        return lax.ppermute(block, ("slot", "tile"), pairs)

    mate = lax.ppermute(flat, "tile", mate_of)
    listed = (
        jnp.transpose(report_owner[0], (0, 2, 1)),
        jnp.transpose(report_stencil[0], (0, 2, 1)),
        jnp.transpose(report_weights[0], (0, 2, 1)),
        report_precision[0],
        report_values[0].reshape(steps * rows, LANES),
    )
    work = [
        pltpu.VMEM((1, steps * rows), jnp.int32),
        scratch(META, F32, steps * rows),
        scratch(tiles * CHUNK, F32, LANES),
        scratch(tiles * CHUNK, BF16, LANES),
    ]
    held, packed, *listed = kernel_call(
        first_kernel,
        [spec(size), spec(tiles * CHUNK, BF16, LANES)]
        + [jax.ShapeDtypeStruct(block.shape, block.dtype) for block in listed],
        work + [pltpu.SemaphoreType.DMA((7,))],
        10**7,
        200000,
        hbm=6,
        out_places=[pltpu.VMEM, pltpu.HBM] + [pltpu.VMEM] * 5,
    )(flat, *listed)
    sent = kernel_call(
        tile_kernel, spec(groups * (cols + 2), BF16), [scratch(groups * 2)], 1000, 400000
    )(held, mate)
    oth = lax.ppermute(sent, "tile", other_of)
    (packed,) = kernel_call(
        later_kernel,
        [spec(tiles * CHUNK, BF16, LANES)],
        work + [pltpu.SemaphoreType.DMA],
        10**7,
        200000,
        hbm=1,
        out_places=[pltpu.HBM],
        aliases={0: 0},
    )(packed, *listed, sent)
    arrived = lax.all_to_all(packed, "tile", split_axis=0, concat_axis=0, tiled=True)

    message, near4 = kernel_call(
        relay_kernel,
        [spec(size + 4 * groups, BF16), spec(4 * groups)],
        [scratch(size), scratch(4 * groups)],
        1000,
        700000,
    )(held, mate, oth)
    nxt = across(message, 1)
    wide = groups * WIDE
    slim = groups * SLIM
    (
        edge0, u1x, d0x, d1x, f2x, field, final, wo, readout_held, gain_held, error_held, background_held,
    ) = kernel_call(
        forward_kernel,
        [spec(groups * 8), spec(slim)] + [spec(slim, BF16)] * 3
        + [spec(4 * lats * cols, F32, members * LANES), spec(size, BF16)]
        + [spec(channels, BF16), spec(channels, BF16, LANES), spec(1), spec(1), spec(size, BF16)],
        [scratch(wide), scratch(wide), scratch(wide, BF16), scratch(wide, BF16), scratch(wide, BF16)]
        + [scratch(wide), scratch(16), scratch(4 * size, BF16)]
        + [scratch(channels, BF16), scratch(channels, BF16), pltpu.SemaphoreType.DMA((7,))],
        10**11,
        4000000,
        hbm=7,
    )(
        gain, self_weight, neighbour_weight, output_weight, readout, error, background.reshape(size, channels),
        held, near4, oth,
    )
    before = across(final, -1)
    total = -(-tiles // SENDERS) * LANES
    spread, near_spread = kernel_call(
        functools.partial(observe_kernel, tiles),
        [spec(4 * size, BF16, LANES), spec(size, BF16, LANES)],
        [scratch(32, BF16, total)] * 2 + [scratch(128, BF16, total)] * 2
        + [scratch(total, F32, LANES), scratch(tiles * CHUNK, F32, LANES)],
        10**9,
        2000000,
    )(arrived, field)
    from_mate = lax.ppermute(near_spread, "tile", mate_of)
    handed = kernel_call(
        pull_kernel,
        [spec(slim), spec(slim), spec(channels, BF16), spec(channels, BF16)],
        [scratch(4 * size), pltpu.SemaphoreType.DMA((2,))],
        10**9,
        3000000,
        hbm=2,
    )(neighbour_weight, self_weight, spread, readout_held)
    base = kernel_call(
        backward_kernel,
        spec(size),
        [scratch(slim), scratch(slim), scratch(slim), scratch(slim, BF16), scratch(slim), scratch(slim)]
        + [scratch(size), scratch(16), scratch(slim), scratch(slim), scratch(size + 4 * groups)],
        12 * slim * channels * channels,
        6000000,
    )(
        *handed, gain_held, held, edge0, nxt, f2x, wo, readout_held, error_held, from_mate,
        u1x, d0x, d1x,
    )
    result = kernel_call(last_kernel, spec(size), [], 10**6, 900000)(base, background_held, before, error_held)
    return result.reshape(control.shape)


def solution(mesh):
    in_specs = (
        P("slot", None, None, "tile", None),
        P(None, None, "tile", None),
        P(),
        P(),
        P(),
        P(),
        P(),
        P(),
        P("slot", None, "tile", None),
        P("slot", None, "tile", None),
        P("slot", None, "tile", None),
        P("slot", None, "tile", None),
        P("slot", None, "tile"),
    )
    out_specs = P("slot", None, None, "tile", None)
    return jax.shard_map(
        per_device, mesh=mesh, in_specs=in_specs, out_specs=out_specs, check_vma=False
    )
```

```python
import functools
import jax
import jax.numpy as jnp
from jax import lax
from jax.experimental import pallas as pl
from jax.experimental.pallas import tpu as pltpu
from jax.sharding import PartitionSpec as P

EPSILON = 1e-06
F32 = jnp.float32
BF16 = jnp.bfloat16
LANES = 128
CAP = 5
SLOTS = 4 * CAP
CHUNK = 32
META = 16
SENDERS = LANES // SLOTS
WIDE = 40
SLIM = 24
VMEM_LIMIT = 28 * 1024 * 1024


def dot(a, b):
    return jnp.dot(a, b, preferred_element_type=F32)


def dot_t(a, b):
    return lax.dot_general(a, b, (((1,), (1,)), ((), ())), preferred_element_type=F32)


def sublane(shape):
    return lax.broadcasted_iota(jnp.int32, shape, 0)


def inverse_rms(x):
    return lax.rsqrt(jnp.mean(x * x, axis=-1, keepdims=True) + EPSILON)


def sigmoid(p):
    return 0.5 * jnp.tanh(0.5 * p) + 0.5


def neighbours(rows):
    width = rows[0].shape[0]
    return [
        0.25 * (rows[1 - i] + pltpu.roll(rows[i], 1, 0) + pltpu.roll(rows[i], width - 1, 0))
        for i in range(2)
    ]


def forward_step(u, n, mean, act, pre, d, gain, ws, wn, wo, width, members, out, copies=()):
    both = 2 * width
    for m in range(members):
        base = m * both
        rows = []
        for lat in range(2):
            x = u[base + lat * width : base + (lat + 1) * width]
            rows.append((x * inverse_rms(x) * gain).astype(BF16).astype(F32))
        n[base : base + both] = jnp.concatenate(rows, axis=0).astype(BF16)
        mean[base : base + both] = jnp.concatenate(neighbours(rows), axis=0).astype(BF16)
    for copy in copies[:2]:
        copy.wait()
    pre[...] = dot(n[...], ws[...]) + dot(mean[...], wn[...])
    for m in range(members):
        base = m * both
        p = pre[base : base + both]
        sig = sigmoid(p)
        act[base : base + both] = (p * sig).astype(BF16)
        if d is not None:
            pre[base : base + both] = sig * (1.0 + p * (1.0 - sig))
    if d is not None:
        for m in range(members):
            slim_copy(d, pre, m)
    for copy in copies[2:]:
        copy.wait()
    pre[...] = dot(act[...], wo[...])
    for r in range(2 * members):
        out(r, u[r * width : (r + 1) * width] + pre[r * width : (r + 1) * width])


def slim_edge(wide, r):
    low = wide[r * WIDE + 16 : r * WIDE + 24]
    high = wide[r * WIDE + 32 : r * WIDE + 40]
    return jnp.where(sublane(low.shape) < 4, low, high)


def slim_copy(to, wide, m):
    parts = []
    for r in (2 * m, 2 * m + 1):
        parts += [wide[r * WIDE : r * WIDE + 16], slim_edge(wide, r)]
    both = jnp.concatenate(parts, axis=0)
    to[m * 2 * SLIM : (m + 1) * 2 * SLIM] = both.astype(to.dtype)


def reports(arrays, out_hbm, key, meta, picked, out, sem):
    pack(*arrays, out, key, meta, picked)
    store = pltpu.make_async_copy(out, out_hbm, sem)
    store.start()
    store.wait()


def early():
    return lax.axis_index("tile") < lax.axis_size("tile") // 2


def first_kernel(control_hbm, *refs):
    sources, (held, out_hbm), arrays, (key, meta, picked, out, sems) = refs[:5], refs[5:7], refs[7:12], refs[12:]
    copies = [
        pltpu.make_async_copy(source, to, sems.at[i]) for i, (source, to) in enumerate(zip(sources, arrays))
    ]
    copies.append(pltpu.make_async_copy(control_hbm, held, sems.at[5]))
    for copy in copies:
        copy.start()
    for copy in copies[:5]:
        copy.wait()

    @pl.when(early())
    def _():
        reports(arrays, out_hbm, key, meta, picked, out, sems.at[6])

    copies[5].wait()


def later_kernel(packed_hbm, *refs):
    arrays, out_hbm, (key, meta, picked, out, sem) = refs[:5], refs[6], refs[7:]

    @pl.when(jnp.logical_not(early()))
    def _():
        reports(arrays, out_hbm, key, meta, picked, out, sem)


def pack(owner, stencil, weights, precision, values, out, key, meta, picked):
    steps, _, rows = owner.shape
    tiles = out.shape[0] // CHUNK
    total = steps * rows
    place = lax.axis_index("tile") % SENDERS * SLOTS
    earlier = lax.broadcasted_iota(jnp.int32, (rows, rows), 0) < lax.broadcasted_iota(jnp.int32, (rows, rows), 1)
    earlier = earlier.astype(F32).astype(BF16)
    meta[...] = jnp.zeros_like(meta)
    for k in range(steps):
        at = slice(k * rows, (k + 1) * rows)
        named = lax.broadcasted_iota(jnp.int32, (tiles, rows), 0) == owner[k]
        hits = named.astype(F32)
        before = dot(hits.astype(BF16), earlier)
        rank = jnp.sum(hits * before, axis=0, keepdims=True).astype(jnp.int32)
        key[0:1, at] = owner[k] * (2 * CAP) + k * CAP + rank
        meta[4:8, at] = stencil[k].astype(F32)
        meta[8:12, at] = weights[k].astype(F32)
        meta[12:13, at] = precision[k : k + 1].astype(F32)
    row = lax.broadcasted_iota(jnp.int32, (tiles * CHUNK, total), 0)
    tile = row // CHUNK
    slot = row % CHUNK
    other = jnp.where(tile % 2 == 0, (tile + tiles - 1) % tiles, (tile + 1) % tiles)
    mine = slot < 2 * CAP
    wanted = jnp.where(mine, tile * (2 * CAP) + slot, other * (2 * CAP) + slot - 2 * CAP)
    wanted = jnp.where(slot < SLOTS, wanted, -1)
    placement = (wanted == key[...]).astype(F32).astype(BF16)
    picked[...] = dot(placement, values[...])
    entries = dot_t(meta[...].astype(BF16), placement)
    lane = lax.broadcasted_iota(jnp.int32, (META, LANES), 1)
    used = jnp.logical_and(lane >= place, lane < place + SLOTS)
    per_tile = LANES // CHUNK
    for t in range(tiles):
        block = entries[:, t // per_tile * LANES : (t // per_tile + 1) * LANES]
        shift = (place + LANES - t % per_tile * CHUNK) % LANES
        block = jnp.where(used, pltpu.roll(block, shift, 1), 0.0)
        low = picked[t * CHUNK + 16 : (t + 1) * CHUNK]
        picked[t * CHUNK + 16 : (t + 1) * CHUNK] = jnp.where(sublane((META, 1)) < 4, low, block)
    out[...] = picked[...].astype(BF16)


def tile_kernel(control, mate, out, held):
    even = lax.rem(lax.axis_index("tile"), 2) == 0
    size = control.shape[0]
    out[0:size] = control[...].astype(BF16)
    for r in range(size // 16):
        held[r * 2 : (r + 1) * 2] = jnp.where(
            even, mate[r * 16 : r * 16 + 2], mate[r * 16 + 14 : (r + 1) * 16]
        )
    out[size:] = held[...].astype(BF16)


def relay_kernel(control, mate, oth, out, near4, wide, edge):
    even = lax.rem(lax.axis_index("tile"), 2) == 0
    size = mate.shape[0]
    out[0:size] = control[...].astype(BF16)
    wide[...] = oth[0:size].astype(F32)
    for r in range(size // 16):
        a, b = r * 16, (r + 1) * 16
        edge[r * 2 : (r + 1) * 2] = jnp.where(even, wide[b - 2 : b], wide[a : a + 2])
        near4[r * 4 : (r + 1) * 4] = jnp.where(even, mate[a : a + 4], mate[b - 4 : b])
        start = size // 8 + r * 2
        edge[start : start + 2] = jnp.where(even, mate[a : a + 2], mate[b - 2 : b])
    out[size:] = edge[...].astype(BF16)


def forward_kernel(
    gain_hbm, ws_hbm, wn_hbm, wo_hbm, readout_hbm, error_hbm, background_hbm, control, mate, oth,
    edge0, u1x, d0x, d1x, f2x, field, final, wo, readout, gain, error, background,
    ua, ub, n, mean, act, pre, edge, states, ws, wn, sems,
):
    pairs = (
        (gain_hbm, gain), (ws_hbm, ws), (wn_hbm, wn), (wo_hbm, wo), (readout_hbm, readout),
        (error_hbm, error), (background_hbm, background),
    )
    copies = [pltpu.make_async_copy(source, to, sems.at[i]) for i, (source, to) in enumerate(pairs)]
    for copy in copies:
        copy.start()
    members = final.shape[0] // 32
    even = lax.rem(lax.axis_index("tile"), 2) == 0
    tile_at = jnp.where(even, 24, 16)
    edge_at = jnp.where(even, 16, 32)
    far = oth[members * 32 :].astype(F32)
    for r in range(2 * members):
        ua[r * WIDE : r * WIDE + 16] = control[r * 16 : (r + 1) * 16]
        ua[pl.ds(pl.multiple_of(r * WIDE + tile_at, 8), 16)] = oth[r * 16 : (r + 1) * 16].astype(F32)
        near4 = mate[r * 4 : (r + 1) * 4]
        far2 = far[r * 2 : (r + 1) * 2]
        edge[...] = jnp.zeros_like(edge)
        edge[0:4] = near4
        edge[6:8] = far2
        edge[8:10] = far2
        edge[12:16] = near4
        ua[pl.ds(pl.multiple_of(r * WIDE + edge_at, 8), 8)] = jnp.where(even, edge[0:8], edge[8:16])
    for r in range(2 * members):
        edge0[r * 8 : (r + 1) * 8] = slim_edge(ua, r)
    copies[0].wait()
    g = gain[...]

    def keep(ref):
        def store(r, value):
            ref[r * WIDE : (r + 1) * WIDE] = value

        return store

    def keep_states(ref, k):
        own = k * members * 32
        away = (2 + k) * members * 32
        for r in range(2 * members):
            states[own + r * 16 : own + (r + 1) * 16] = ref[r * WIDE : r * WIDE + 16].astype(BF16)
            taken = ref[pl.ds(pl.multiple_of(r * WIDE + tile_at, 8), 16)]
            states[away + r * 16 : away + (r + 1) * 16] = taken.astype(BF16)

    forward_step(ua, n, mean, act, pre, d0x, g, ws, wn, wo, WIDE, members, keep(ub), copies[1:])
    for m in range(members):
        slim_copy(u1x, ub, m)
    keep_states(ub, 0)
    forward_step(ub, n, mean, act, pre, d1x, g, ws, wn, wo, WIDE, members, keep(ua))
    for m in range(members):
        slim_copy(f2x, ua, m)
    keep_states(ua, 1)
    final[...] = states[members * 32 : 2 * members * 32]
    read = dot(states[...], readout[...])
    for q in range(4):
        for m in range(members):
            start = (q * members + m) * 32
            field[q * 32 : (q + 1) * 32, m * LANES : (m + 1) * LANES] = read[start : start + 32]


def split(x):
    high = x.astype(BF16)
    return high, (x - high.astype(F32)).astype(BF16)


def spread_of(first, th, tl, scaled, taken, field, ph, plo, spread):
    lane = lax.broadcasted_iota(jnp.int32, (1, LANES), 1)
    table_of = jnp.where(lane < SENDERS * SLOTS, lane % SLOTS // CAP, -1)
    members = field.shape[1] // LANES
    for p in range(th.shape[1] // LANES):
        at = slice(p * LANES, (p + 1) * LANES)
        for q in range(2):
            kept = jnp.where(table_of == first + q, scaled[:, at], 0.0)
            ph[q * 32 : (q + 1) * 32, at], plo[q * 32 : (q + 1) * 32, at] = split(kept)
    cross = dot_t(ph[...], th[...]) + dot_t(plo[...], th[...]) + dot_t(ph[...], tl[...])
    block = jnp.concatenate([cross] * 2, axis=1)
    on_block = sublane(block.shape) // 32 == lax.broadcasted_iota(jnp.int32, block.shape, 1) // 32
    target = dot(ph[...], taken[...]) + dot(plo[...], taken[...])
    ch, cl = split(jnp.where(on_block, block, 0.0))
    fh, fl = split(field[first * 32 : (first + 2) * 32])
    mixed = dot(ch, fh) + dot(cl, fh) + dot(ch, fl)
    for q in range(2):
        for m in range(members):
            start = (q * members + m) * 32
            value = mixed[q * 32 : (q + 1) * 32, m * LANES : (m + 1) * LANES] - target[q * 32 : (q + 1) * 32]
            spread[start : start + 32] = value.astype(BF16)


def observe_kernel(
    tiles, arrived, field,
    spread, message, th, tl, scaled, taken,
    ph, plo, vals, wide,
):
    steps = 2
    members = field.shape[1] // LANES
    even = lax.rem(lax.axis_index("tile"), 2) == 0
    cells = sublane((32, LANES)).astype(F32)
    wide[...] = arrived[...].astype(F32)
    vals[...] = jnp.zeros_like(vals)
    for p in range(th.shape[1] // LANES):
        meta = jnp.zeros((META, LANES), F32)
        for d in range(p * SENDERS, min((p + 1) * SENDERS, tiles)):
            meta += wide[d * CHUNK + 16 : (d + 1) * CHUNK]
            start = p * LANES + d % SENDERS * SLOTS
            vals[start : start + SLOTS] = wide[d * CHUNK : d * CHUNK + SLOTS]
        weight = jnp.zeros((32, LANES), F32)
        for i in range(4):
            weight += jnp.where(cells == meta[4 + i : 5 + i], meta[8 + i : 9 + i], 0.0)
        at = slice(p * LANES, (p + 1) * LANES)
        th[:, at], tl[:, at] = split(weight)
        scaled[:, at] = weight * meta[12:13]
    taken[...] = vals[...].astype(BF16)
    spread_of(0, th, tl, scaled, taken, field, ph, plo, spread)
    size = members * 32
    for k in range(steps):
        for m in range(members):
            start = k * size + m * 32
            pair = spread[start : start + 32].astype(F32)
            near = [jnp.where(even, pair[i + 8 : i + 16], pair[i : i + 8]) for i in (0, 16)]
            start = k * size // 2 + m * 16
            message[start : start + 16] = jnp.concatenate(near, axis=0).astype(BF16)


def adjoint_step(u, s, cot, gb, gm, flat, d, out, gain, ws, wn, wo, members):
    both = 2 * SLIM
    for m in range(members):
        gb[m * both : (m + 1) * both] = jnp.concatenate([cot(2 * m), cot(2 * m + 1)], axis=0).astype(BF16)
    flat[...] = dot_t(gb[...], wo[...])
    gb[...] = (flat[...] * d[...]).astype(BF16)
    gm[...] = dot_t(gb[...], wn[...])
    flat[...] = dot_t(gb[...], ws[...])
    for m in range(members):
        base = m * both
        rows = []
        for lat in range(2):
            start = base + lat * SLIM
            rows.append(gm[start : start + SLIM].astype(BF16).astype(F32))
        around = neighbours(rows)
        for lat in range(2):
            at = slice(base + lat * SLIM, base + (lat + 1) * SLIM)
            x = u[at]
            inverse = jnp.concatenate([s[at]] * (x.shape[1] // LANES), axis=1)
            scaled = gain * (flat[at] + around[lat])
            inner = jnp.mean(x * scaled, axis=-1, keepdims=True)
            out(2 * m + lat, cot(2 * m + lat) + inverse * (scaled - x * (inverse * inverse * inner)))


def edges(nxt, size, edge, r):
    even = lax.rem(lax.axis_index("tile"), 2) == 0
    start = size + r * 2
    far = nxt[start : start + 2]
    start = size + size // 8 + r * 2
    near = nxt[start : start + 2]
    edge[...] = jnp.zeros_like(edge)
    edge[0:2] = near
    edge[6:8] = far
    edge[8:10] = far
    edge[14:16] = near
    return jnp.where(even, edge[0:8], edge[8:16])


def pull_kernel(
    wn_hbm, ws_hbm, spread_own, readout, th, tl, scaled, taken, field, control, edge0, message, f2x, error, u1x,
    cot_own, cot_edge, add_own, add_edge, u0x, s0, s1, wn, ws,
    ph, plo, spread, pulled, away, nxt, final, edge, sems,
):
    pairs = ((wn_hbm, wn), (ws_hbm, ws))
    copies = [pltpu.make_async_copy(source, to, sems.at[i]) for i, (source, to) in enumerate(pairs)]
    for copy in copies:
        copy.start()
    size = control.shape[0]
    even = lax.rem(lax.axis_index("tile"), 2) == 0
    weight = jnp.where(lax.axis_index("slot") == lax.axis_size("slot") - 1, 0.0, 1.0) * error[...]
    row8 = sublane((8, 1))
    spread_of(2, th, tl, scaled, taken, field, ph, plo, spread)
    pulled[...] = dot_t(spread_own[...], readout[...])
    away[...] = dot_t(spread[...], readout[...])
    nxt[...] = message[...].astype(F32)
    final[...] = f2x[...].astype(F32)

    def other_edge(k, r):
        start = k * size + r * 16
        low = jnp.where(row8 < 4, away[start : start + 8], 0.0)
        high = jnp.where(row8 >= 4, away[start + 8 : start + 16], 0.0)
        return jnp.where(even, high, low)

    for r in range(size // 16):
        a, b = r * 16, (r + 1) * 16
        c, d, e = r * SLIM, r * SLIM + 16, (r + 1) * SLIM
        cot_own[a:b] = pulled[size + a : size + b] - weight * (nxt[a:b] - final[c:d])
        cot_edge[r * 8 : (r + 1) * 8] = other_edge(1, r) - weight * (edges(nxt, size, edge, r) - final[d:e])
        add_own[a:b] = pulled[a:b]
        add_edge[r * 8 : (r + 1) * 8] = other_edge(0, r)
        u0x[c:d] = control[a:b]
        u0x[d:e] = edge0[r * 8 : (r + 1) * 8]
        for u, s in ((u0x, s0), (u1x, s1)):
            s[c:e] = jnp.broadcast_to(inverse_rms(u[c:e]), (SLIM, LANES))
    for copy in copies:
        copy.wait()


def backward_kernel(
    cot_own, cot_edge, add_own, add_edge, u0x, s0, s1, wn, ws, wo, gain, readout, error, message, u1x, d0x, d1x,
    result,
    cot1, gb, gm, flat, mate_pull, edge2, edge1,
):
    size = result.shape[0]
    members = size // 32
    even = lax.rem(lax.axis_index("tile"), 2) == 0
    row8 = sublane((8, 1))
    mate_side = jnp.where(even, 1, 0) == jnp.where(row8 < 4, 1, 0)
    mate_pull[...] = dot_t(message[...], readout[...])
    for r in range(2 * members):
        a, b, start = r * 8, (r + 1) * 8, size // 2 + r * 8
        edge2[a:b] = cot_edge[a:b] + jnp.where(mate_side, mate_pull[start : start + 8], 0.0)
        edge1[a:b] = add_edge[a:b] + jnp.where(mate_side, mate_pull[a:b], 0.0)

    def joined(own, edge):
        return lambda r: jnp.concatenate([own[r * 16 : (r + 1) * 16], edge[r * 8 : (r + 1) * 8]], axis=0)

    added = joined(add_own, edge1)

    def keep(r, value):
        cot1[r * SLIM : (r + 1) * SLIM] = value + added(r)

    def finish(r, value):
        result[r * 16 : (r + 1) * 16] = value[0:16] + error[...] * u0x[r * SLIM : r * SLIM + 16]

    def kept(r):
        return cot1[r * SLIM : (r + 1) * SLIM]

    adjoint_step(u1x, s1, joined(cot_own, edge2), gb, gm, flat, d1x, keep, gain[...], ws, wn, wo, members)
    adjoint_step(u0x, s0, kept, gb, gm, flat, d0x, finish, gain[...], ws, wn, wo, members)


def last_kernel(base, background, before, error, result):
    first = lax.axis_index("slot") == 0
    taken = jnp.where(first, background[...].astype(F32), before[...].astype(F32))
    result[...] = base[...] - error[...] * taken


def kernel_call(body, outs, scratch, flops, moved, hbm=0, out_places=None, aliases={}):
    def call(*operands):
        fixed = [i in range(hbm) and i not in aliases for i in range(len(operands))]
        operands = [
            pltpu.with_memory_space_constraint(x, pltpu.HBM) if fix else x for x, fix in zip(operands, fixed)
        ]
        places = [pltpu.HBM] * hbm + [pltpu.VMEM] * (len(operands) - hbm)
        given = {} if out_places is None else {"out_specs": [pl.BlockSpec(memory_space=p) for p in out_places]}
        return pl.pallas_call(
            body,
            out_shape=outs,
            in_specs=[pl.BlockSpec(memory_space=place) for place in places],
            **given,
            scratch_shapes=scratch,
            input_output_aliases=aliases,
            compiler_params=pltpu.CompilerParams(vmem_limit_bytes=VMEM_LIMIT),
            cost_estimate=pl.CostEstimate(flops=flops, bytes_accessed=moved, transcendentals=0),
        )(*operands)

    return call


def per_device(
    control,
    background,
    self_weight,
    neighbour_weight,
    output_weight,
    norm_gain,
    readout,
    error_weight,
    report_owner,
    report_stencil,
    report_weights,
    report_values,
    report_precision,
):
    tiles = lax.axis_size("tile")
    slots = lax.axis_size("slot")
    members, lats, cols, channels = control.shape[1:]
    groups = members * lats
    size = groups * cols
    steps = report_owner.shape[1]
    rows = report_owner.shape[2]
    gain = norm_gain.reshape(1, channels)
    error = error_weight.reshape(1, channels)
    flat = control.reshape(size, channels)

    def spec(count, dtype=F32, width=channels):
        return jax.ShapeDtypeStruct((count, width), dtype)

    def scratch(count, dtype=F32, width=channels):
        return pltpu.VMEM((count, width), dtype)

    mate_of = [(i, i ^ 1) for i in range(tiles)]
    other_of = [(i, (i - 1) % tiles if i % 2 == 0 else (i + 1) % tiles) for i in range(tiles)]

    def across(block, shift):
        pairs = [
            ((s + shift) % slots * tiles + i, s * tiles + i) for s in range(slots) for i in range(tiles)
        ]
        return lax.ppermute(block, ("slot", "tile"), pairs)

    mate = lax.ppermute(flat, "tile", mate_of)
    listed = (
        jnp.transpose(report_owner[0], (0, 2, 1)),
        jnp.transpose(report_stencil[0], (0, 2, 1)),
        jnp.transpose(report_weights[0], (0, 2, 1)),
        report_precision[0],
        report_values[0].reshape(steps * rows, LANES),
    )
    work = [
        pltpu.VMEM((1, steps * rows), jnp.int32),
        scratch(META, F32, steps * rows),
        scratch(tiles * CHUNK, F32, LANES),
        scratch(tiles * CHUNK, BF16, LANES),
    ]
    held, packed, *listed = kernel_call(
        first_kernel,
        [spec(size), spec(tiles * CHUNK, BF16, LANES)]
        + [jax.ShapeDtypeStruct(block.shape, block.dtype) for block in listed],
        work + [pltpu.SemaphoreType.DMA((7,))],
        10**7,
        200000,
        hbm=6,
        out_places=[pltpu.VMEM, pltpu.HBM] + [pltpu.VMEM] * 5,
    )(flat, *listed)
    sent = kernel_call(
        tile_kernel, spec(groups * (cols + 2), BF16), [scratch(groups * 2)], 1000, 400000
    )(held, mate)
    oth = lax.ppermute(sent, "tile", other_of)
    (packed,) = kernel_call(
        later_kernel,
        [spec(tiles * CHUNK, BF16, LANES)],
        work + [pltpu.SemaphoreType.DMA],
        10**7,
        200000,
        hbm=1,
        out_places=[pltpu.HBM],
        aliases={0: 0},
    )(packed, *listed, sent)
    arrived = lax.all_to_all(packed, "tile", split_axis=0, concat_axis=0, tiled=True)

    message, near4 = kernel_call(
        relay_kernel,
        [spec(size + 4 * groups, BF16), spec(4 * groups)],
        [scratch(size), scratch(4 * groups)],
        1000,
        700000,
    )(held, mate, oth)
    nxt = across(message, 1)
    wide = groups * WIDE
    slim = groups * SLIM
    (
        edge0, u1x, d0x, d1x, f2x, field, final, wo, readout_held, gain_held, error_held, background_held,
    ) = kernel_call(
        forward_kernel,
        [spec(groups * 8), spec(slim)] + [spec(slim, BF16)] * 3
        + [spec(4 * lats * cols, F32, members * LANES), spec(size, BF16)]
        + [spec(channels, BF16), spec(channels, BF16, LANES), spec(1), spec(1), spec(size, BF16)],
        [scratch(wide), scratch(wide), scratch(wide, BF16), scratch(wide, BF16), scratch(wide, BF16)]
        + [scratch(wide), scratch(16), scratch(4 * size, BF16)]
        + [scratch(channels, BF16), scratch(channels, BF16), pltpu.SemaphoreType.DMA((7,))],
        10**11,
        4000000,
        hbm=7,
    )(
        gain, self_weight, neighbour_weight, output_weight, readout, error, background.reshape(size, channels),
        held, near4, oth,
    )
    before = across(final, -1)
    total = -(-tiles // SENDERS) * LANES
    tables = [scratch(64, BF16, total), scratch(64, BF16, total)]
    spread, near_spread, *reports_held = kernel_call(
        functools.partial(observe_kernel, tiles),
        [spec(2 * size, BF16, LANES), spec(size, BF16, LANES)]
        + [spec(32, BF16, total), spec(32, BF16, total), spec(32, F32, total), spec(total, BF16, LANES)],
        tables + [scratch(total, F32, LANES), scratch(tiles * CHUNK, F32, LANES)],
        10**9,
        2000000,
    )(arrived, field)
    from_mate = lax.ppermute(near_spread, "tile", mate_of)
    handed = kernel_call(
        pull_kernel,
        [spec(size), spec(size // 2), spec(size), spec(size // 2), spec(slim), spec(slim, F32, LANES)]
        + [spec(slim, F32, LANES), spec(channels, BF16), spec(channels, BF16)],
        tables
        + [scratch(2 * size, BF16, LANES), scratch(2 * size), scratch(2 * size), scratch(size + 4 * groups)]
        + [scratch(slim), scratch(16), pltpu.SemaphoreType.DMA((2,))],
        10**9,
        3000000,
        hbm=2,
    )(
        neighbour_weight, self_weight, spread, readout_held, *reports_held, field, held, edge0, nxt, f2x,
        error_held, u1x,
    )
    base = kernel_call(
        backward_kernel,
        spec(size),
        [scratch(slim), scratch(slim, BF16), scratch(slim), scratch(slim), scratch(size)]
        + [scratch(size // 2), scratch(size // 2)],
        12 * slim * channels * channels,
        6000000,
    )(*handed, wo, gain_held, readout_held, error_held, from_mate, u1x, d0x, d1x)
    result = kernel_call(last_kernel, spec(size), [], 10**6, 900000)(base, background_held, before, error_held)
    return result.reshape(control.shape)


def solution(mesh):
    in_specs = (
        P("slot", None, None, "tile", None),
        P(None, None, "tile", None),
        P(),
        P(),
        P(),
        P(),
        P(),
        P(),
        P("slot", None, "tile", None),
        P("slot", None, "tile", None),
        P("slot", None, "tile", None),
        P("slot", None, "tile", None),
        P("slot", None, "tile"),
    )
    out_specs = P("slot", None, None, "tile", None)
    return jax.shard_map(
        per_device, mesh=mesh, in_specs=in_specs, out_specs=out_specs, check_vma=False
    )
```

```python
import functools
import jax
import jax.numpy as jnp
from jax import lax
from jax.experimental import pallas as pl
from jax.experimental.pallas import tpu as pltpu
from jax.sharding import PartitionSpec as P

EPSILON = 1e-06
F32 = jnp.float32
BF16 = jnp.bfloat16
LANES = 128
CAP = 5
SLOTS = 4 * CAP
CHUNK = 24
STRIDE = 32
SENDERS = LANES // SLOTS
WIDE = 40
SLIM = 24
VMEM_LIMIT = 28 * 1024 * 1024


def dot(a, b):
    return jnp.dot(a, b, preferred_element_type=F32)


def dot_t(a, b):
    return lax.dot_general(a, b, (((1,), (1,)), ((), ())), preferred_element_type=F32)


def sublane(shape):
    return lax.broadcasted_iota(jnp.int32, shape, 0)


def inverse_rms(x):
    return lax.rsqrt(jnp.mean(x * x, axis=-1, keepdims=True) + EPSILON)


def sigmoid(p):
    return 0.5 * jnp.tanh(0.5 * p) + 0.5


def neighbours(rows):
    width = rows[0].shape[0]
    return [
        0.25 * (rows[1 - i] + pltpu.roll(rows[i], 1, 0) + pltpu.roll(rows[i], width - 1, 0))
        for i in range(2)
    ]


def forward_step(u, n, mean, act, pre, d, gain, ws, wn, wo, width, members, out, copies=()):
    both = 2 * width
    for m in range(members):
        base = m * both
        rows = []
        for lat in range(2):
            x = u[base + lat * width : base + (lat + 1) * width]
            rows.append((x * inverse_rms(x) * gain).astype(BF16).astype(F32))
        n[base : base + both] = jnp.concatenate(rows, axis=0).astype(BF16)
        mean[base : base + both] = jnp.concatenate(neighbours(rows), axis=0).astype(BF16)
    for copy in copies[:2]:
        copy.wait()
    pre[...] = dot(n[...], ws[...]) + dot(mean[...], wn[...])
    for m in range(members):
        base = m * both
        p = pre[base : base + both]
        sig = sigmoid(p)
        act[base : base + both] = (p * sig).astype(BF16)
        if d is not None:
            pre[base : base + both] = sig * (1.0 + p * (1.0 - sig))
    if d is not None:
        for m in range(members):
            slim_copy(d, pre, m)
    for copy in copies[2:]:
        copy.wait()
    pre[...] = dot(act[...], wo[...])
    for r in range(2 * members):
        out(r, u[r * width : (r + 1) * width] + pre[r * width : (r + 1) * width])


def slim_edge(wide, r):
    low = wide[r * WIDE + 16 : r * WIDE + 24]
    high = wide[r * WIDE + 32 : r * WIDE + 40]
    return jnp.where(sublane(low.shape) < 4, low, high)


def slim_copy(to, wide, m):
    parts = []
    for r in (2 * m, 2 * m + 1):
        parts += [wide[r * WIDE : r * WIDE + 16], slim_edge(wide, r)]
    both = jnp.concatenate(parts, axis=0)
    to[m * 2 * SLIM : (m + 1) * 2 * SLIM] = both.astype(to.dtype)


def reports(arrays, out_hbm, key, meta, picked, out, sem):
    pack(*arrays, out, key, meta, picked)
    store = pltpu.make_async_copy(out, out_hbm, sem)
    store.start()
    store.wait()


def early():
    return lax.axis_index("tile") < lax.axis_size("tile") // 2


def first_kernel(control_hbm, *refs):
    sources, (held, out_hbm), arrays, (key, meta, picked, out, sems) = refs[:5], refs[5:7], refs[7:12], refs[12:]
    copies = [
        pltpu.make_async_copy(source, to, sems.at[i]) for i, (source, to) in enumerate(zip(sources, arrays))
    ]
    copies.append(pltpu.make_async_copy(control_hbm, held, sems.at[5]))
    for copy in copies:
        copy.start()
    for copy in copies[:5]:
        copy.wait()

    @pl.when(early())
    def _():
        reports(arrays, out_hbm, key, meta, picked, out, sems.at[6])

    copies[5].wait()


def later_kernel(packed_hbm, *refs):
    arrays, out_hbm, (key, meta, picked, out, sem) = refs[:5], refs[6], refs[7:]

    @pl.when(jnp.logical_not(early()))
    def _():
        reports(arrays, out_hbm, key, meta, picked, out, sem)


def fan(x, shift):
    if shift % LANES:
        x = pltpu.roll(x, shift % LANES, 1)
    for _ in range(2):
        x = pltpu.roll(x, 0, 1, stride=SLOTS // 2, stride_axis=0)
    return x


def pack(owner, stencil, weights, precision, values, out, key, meta, picked):
    steps, _, rows = owner.shape
    tiles = out.shape[0] // CHUNK
    total = steps * rows
    earlier = lax.broadcasted_iota(jnp.int32, (rows, rows), 0) < lax.broadcasted_iota(jnp.int32, (rows, rows), 1)
    earlier = earlier.astype(F32).astype(BF16)
    meta[...] = jnp.zeros_like(meta)
    for k in range(steps):
        at = slice(k * rows, (k + 1) * rows)
        named = lax.broadcasted_iota(jnp.int32, (tiles, rows), 0) == owner[k]
        hits = named.astype(F32)
        before = dot(hits.astype(BF16), earlier)
        rank = jnp.sum(hits * before, axis=0, keepdims=True).astype(jnp.int32)
        key[0:1, at] = owner[k] * (2 * CAP) + k * CAP + rank
        meta[0:4, at] = stencil[k].astype(F32)
        meta[4:6, at] = weights[k, 0:2].astype(F32)
        meta[8:10, at] = weights[k, 2:4].astype(F32)
        meta[10:11, at] = precision[k : k + 1].astype(F32)
    row = lax.broadcasted_iota(jnp.int32, (tiles * STRIDE, total), 0)
    tile = row // STRIDE
    slot = row % STRIDE
    other = jnp.where(tile % 2 == 0, (tile + tiles - 1) % tiles, (tile + 1) % tiles)
    mine = slot < 2 * CAP
    wanted = jnp.where(mine, tile * (2 * CAP) + slot, other * (2 * CAP) + slot - 2 * CAP)
    wanted = jnp.where(slot < SLOTS, wanted, -1)
    placement = (wanted == key[...]).astype(F32).astype(BF16)
    placed = dot(placement, values[...])
    entries = dot_t(meta[...].astype(BF16), placement)
    lane = lax.broadcasted_iota(jnp.int32, (16, LANES), 1)
    per_tile = LANES // STRIDE
    for t in range(tiles):
        picked[t * CHUNK : (t + 1) * CHUNK] = placed[t * STRIDE : t * STRIDE + CHUNK]
        start = t % per_tile * STRIDE
        used = jnp.logical_and(lane >= start, lane < start + SLOTS)
        block = jnp.where(used, entries[:, t // per_tile * LANES : (t // per_tile + 1) * LANES], 0.0)
        for j in range(2):
            spread = fan(block[j * 8 : (j + 1) * 8], LANES - start)
            row = t * CHUNK + SLOTS + j
            picked[row : row + 1] = jnp.sum(spread, axis=0, keepdims=True)
    out[...] = picked[...].astype(BF16)


def tile_kernel(control, mate, out, held):
    even = lax.rem(lax.axis_index("tile"), 2) == 0
    size = control.shape[0]
    out[0:size] = control[...].astype(BF16)
    for r in range(size // 16):
        held[r * 2 : (r + 1) * 2] = jnp.where(
            even, mate[r * 16 : r * 16 + 2], mate[r * 16 + 14 : (r + 1) * 16]
        )
    out[size:] = held[...].astype(BF16)


def relay_kernel(control, mate, oth, out, near4, wide, edge):
    even = lax.rem(lax.axis_index("tile"), 2) == 0
    size = mate.shape[0]
    out[0:size] = control[...].astype(BF16)
    wide[...] = oth[0:size].astype(F32)
    for r in range(size // 16):
        a, b = r * 16, (r + 1) * 16
        edge[r * 2 : (r + 1) * 2] = jnp.where(even, wide[b - 2 : b], wide[a : a + 2])
        near4[r * 4 : (r + 1) * 4] = jnp.where(even, mate[a : a + 4], mate[b - 4 : b])
        start = size // 8 + r * 2
        edge[start : start + 2] = jnp.where(even, mate[a : a + 2], mate[b - 2 : b])
    out[size:] = edge[...].astype(BF16)


def forward_kernel(
    gain_hbm, ws_hbm, wn_hbm, wo_hbm, readout_hbm, error_hbm, background_hbm, control, mate, oth,
    edge0, u1x, d0x, d1x, f2x, field, final, wo, readout, gain, error, background,
    ua, ub, n, mean, act, pre, edge, states, ws, wn, sems,
):
    pairs = (
        (gain_hbm, gain), (ws_hbm, ws), (wn_hbm, wn), (wo_hbm, wo), (readout_hbm, readout),
        (error_hbm, error), (background_hbm, background),
    )
    copies = [pltpu.make_async_copy(source, to, sems.at[i]) for i, (source, to) in enumerate(pairs)]
    for copy in copies:
        copy.start()
    members = final.shape[0] // 32
    even = lax.rem(lax.axis_index("tile"), 2) == 0
    tile_at = jnp.where(even, 24, 16)
    edge_at = jnp.where(even, 16, 32)
    far = oth[members * 32 :].astype(F32)
    for r in range(2 * members):
        ua[r * WIDE : r * WIDE + 16] = control[r * 16 : (r + 1) * 16]
        ua[pl.ds(pl.multiple_of(r * WIDE + tile_at, 8), 16)] = oth[r * 16 : (r + 1) * 16].astype(F32)
        near4 = mate[r * 4 : (r + 1) * 4]
        far2 = far[r * 2 : (r + 1) * 2]
        edge[...] = jnp.zeros_like(edge)
        edge[0:4] = near4
        edge[6:8] = far2
        edge[8:10] = far2
        edge[12:16] = near4
        ua[pl.ds(pl.multiple_of(r * WIDE + edge_at, 8), 8)] = jnp.where(even, edge[0:8], edge[8:16])
    for r in range(2 * members):
        edge0[r * 8 : (r + 1) * 8] = slim_edge(ua, r)
    copies[0].wait()
    g = gain[...]

    def keep(ref):
        def store(r, value):
            ref[r * WIDE : (r + 1) * WIDE] = value

        return store

    def keep_states(ref, k):
        own = k * members * 32
        away = (2 + k) * members * 32
        for r in range(2 * members):
            states[own + r * 16 : own + (r + 1) * 16] = ref[r * WIDE : r * WIDE + 16].astype(BF16)
            taken = ref[pl.ds(pl.multiple_of(r * WIDE + tile_at, 8), 16)]
            states[away + r * 16 : away + (r + 1) * 16] = taken.astype(BF16)

    forward_step(ua, n, mean, act, pre, d0x, g, ws, wn, wo, WIDE, members, keep(ub), copies[1:])
    for m in range(members):
        slim_copy(u1x, ub, m)
    keep_states(ub, 0)
    forward_step(ub, n, mean, act, pre, d1x, g, ws, wn, wo, WIDE, members, keep(ua))
    for m in range(members):
        slim_copy(f2x, ua, m)
    keep_states(ua, 1)
    final[...] = states[members * 32 : 2 * members * 32]
    read = dot(states[...], readout[...])
    for q in range(4):
        for m in range(members):
            start = (q * members + m) * 32
            field[q * 32 : (q + 1) * 32, m * LANES : (m + 1) * LANES] = read[start : start + 32]


def split(x):
    high = x.astype(BF16)
    return high, (x - high.astype(F32)).astype(BF16)


def spread_of(first, th, tl, scaled, taken, field, ph, plo, spread):
    lane = lax.broadcasted_iota(jnp.int32, (1, LANES), 1)
    table_of = jnp.where(lane < SENDERS * SLOTS, lane % SLOTS // CAP, -1)
    members = field.shape[1] // LANES
    for p in range(th.shape[1] // LANES):
        at = slice(p * LANES, (p + 1) * LANES)
        for q in range(2):
            kept = jnp.where(table_of == first + q, scaled[:, at], 0.0)
            ph[q * 32 : (q + 1) * 32, at], plo[q * 32 : (q + 1) * 32, at] = split(kept)
    cross = dot_t(ph[...], th[...]) + dot_t(plo[...], th[...]) + dot_t(ph[...], tl[...])
    block = jnp.concatenate([cross] * 2, axis=1)
    on_block = sublane(block.shape) // 32 == lax.broadcasted_iota(jnp.int32, block.shape, 1) // 32
    target = dot(ph[...], taken[...]) + dot(plo[...], taken[...])
    ch, cl = split(jnp.where(on_block, block, 0.0))
    fh, fl = split(field[first * 32 : (first + 2) * 32])
    mixed = dot(ch, fh) + dot(cl, fh) + dot(ch, fl)
    for q in range(2):
        for m in range(members):
            start = (q * members + m) * 32
            value = mixed[q * 32 : (q + 1) * 32, m * LANES : (m + 1) * LANES] - target[q * 32 : (q + 1) * 32]
            spread[start : start + 32] = value.astype(BF16)


def observe_kernel(
    tiles, arrived, field,
    spread, message, th, tl, scaled, taken,
    ph, plo, vals, wide,
):
    steps = 2
    members = field.shape[1] // LANES
    even = lax.rem(lax.axis_index("tile"), 2) == 0
    cells = sublane((32, LANES)).astype(F32)
    lane = lax.broadcasted_iota(jnp.int32, (8, LANES), 1)
    wide[...] = arrived[...].astype(F32)
    vals[...] = jnp.zeros_like(vals)
    for p in range(th.shape[1] // LANES):
        meta = [jnp.zeros((8, LANES), F32)] * 2
        for d in range(p * SENDERS, min((p + 1) * SENDERS, tiles)):
            start = d % SENDERS * SLOTS
            used = jnp.logical_and(lane >= start, lane < start + SLOTS)
            for j in range(2):
                row = d * CHUNK + SLOTS + j
                rows = jnp.broadcast_to(wide[row : row + 1], (8, LANES))
                turned = fan(rows, start + LANES - 5 * SLOTS)
                meta[j] = meta[j] + jnp.where(used, turned, 0.0)
            start += p * LANES
            vals[start : start + SLOTS] = wide[d * CHUNK : d * CHUNK + SLOTS]
        entry = [meta[i // 6][5 - i % 6 : 6 - i % 6] for i in range(9)]
        weight = jnp.zeros((32, LANES), F32)
        for i in range(4):
            weight += jnp.where(cells == entry[i], entry[4 + i], 0.0)
        at = slice(p * LANES, (p + 1) * LANES)
        th[:, at], tl[:, at] = split(weight)
        scaled[:, at] = weight * entry[8]
    taken[...] = vals[...].astype(BF16)
    spread_of(0, th, tl, scaled, taken, field, ph, plo, spread)
    size = members * 32
    for k in range(steps):
        for m in range(members):
            start = k * size + m * 32
            pair = spread[start : start + 32].astype(F32)
            near = [jnp.where(even, pair[i + 8 : i + 16], pair[i : i + 8]) for i in (0, 16)]
            start = k * size // 2 + m * 16
            message[start : start + 16] = jnp.concatenate(near, axis=0).astype(BF16)


def adjoint_step(u, cot, gb, gm, flat, d, out, gain, ws, wn, wo, members):
    both = 2 * SLIM
    gb[...] = cot[...].astype(BF16)
    flat[...] = dot_t(gb[...], wo[...])
    gb[...] = (flat[...] * d[...]).astype(BF16)
    gm[...] = dot_t(gb[...], wn[...])
    flat[...] = dot_t(gb[...], ws[...])
    for m in range(members):
        base = m * both
        rows = []
        for lat in range(2):
            start = base + lat * SLIM
            rows.append(gm[start : start + SLIM].astype(BF16).astype(F32))
        around = neighbours(rows)
        for lat in range(2):
            start = base + lat * SLIM
            x = u[start : start + SLIM]
            s = inverse_rms(x)
            scaled = gain * (flat[start : start + SLIM] + around[lat])
            inner = jnp.mean(x * scaled, axis=-1, keepdims=True)
            out(2 * m + lat, cot[start : start + SLIM] + s * scaled - x * (s * s * s * inner))


def edges(nxt, size, edge, r):
    even = lax.rem(lax.axis_index("tile"), 2) == 0
    start = size + r * 2
    far = nxt[start : start + 2]
    start = size + size // 8 + r * 2
    near = nxt[start : start + 2]
    edge[...] = jnp.zeros_like(edge)
    edge[0:2] = near
    edge[6:8] = far
    edge[8:10] = far
    edge[14:16] = near
    return jnp.where(even, edge[0:8], edge[8:16])


def pull_kernel(
    wn_hbm, ws_hbm, spread_own, readout, th, tl, scaled, taken, field,
    last, first, wn, ws,
    ph, plo, spread, pulled, away, sems,
):
    pairs = ((wn_hbm, wn), (ws_hbm, ws))
    copies = [pltpu.make_async_copy(source, to, sems.at[i]) for i, (source, to) in enumerate(pairs)]
    for copy in copies:
        copy.start()
    size = pulled.shape[0] // 2
    even = lax.rem(lax.axis_index("tile"), 2) == 0
    row8 = sublane((8, 1))
    spread_of(2, th, tl, scaled, taken, field, ph, plo, spread)
    pulled[...] = dot_t(spread_own[...], readout[...])
    away[...] = dot_t(spread[...], readout[...])
    for k, out in enumerate((first, last)):
        for r in range(size // 16):
            start = k * size + r * 16
            out[r * SLIM : r * SLIM + 16] = pulled[start : start + 16]
            low = jnp.where(row8 < 4, away[start : start + 8], 0.0)
            high = jnp.where(row8 >= 4, away[start + 8 : start + 16], 0.0)
            out[r * SLIM + 16 : (r + 1) * SLIM] = jnp.where(even, high, low)
    for copy in copies:
        copy.wait()


def backward_kernel(
    last, early_pull, wn, ws, gain, control, edge0, message16, f2x, wo, readout, error, message,
    u1x, d0x, d1x,
    result,
    cot2, cot1, add, gb, gm, flat, mate_pull, edge, u0x, final, nxt,
):
    size = result.shape[0]
    members = size // 32
    even = lax.rem(lax.axis_index("tile"), 2) == 0
    nxt[...] = message16[...].astype(F32)
    weight = jnp.where(lax.axis_index("slot") == lax.axis_size("slot") - 1, 0.0, 1.0) * error[...]
    row8 = sublane((8, 1))
    mate_side = jnp.where(even, 1, 0) == jnp.where(row8 < 4, 1, 0)
    mate_pull[...] = dot_t(message[...], readout[...])
    final[...] = f2x[...].astype(F32)
    add[...] = early_pull[...]
    for r in range(2 * members):
        a, b = r * SLIM, r * SLIM + 16
        cot2[a:b] = last[a:b] - weight * (nxt[r * 16 : (r + 1) * 16] - final[a:b])
        u0x[a:b] = control[r * 16 : (r + 1) * 16]
        a, b = b, b + 8
        start = size // 2 + r * 8
        pulled = last[a:b] + jnp.where(mate_side, mate_pull[start : start + 8], 0.0)
        cot2[a:b] = pulled - weight * (edges(nxt, size, edge, r) - final[a:b])
        add[a:b] = early_pull[a:b] + jnp.where(mate_side, mate_pull[r * 8 : (r + 1) * 8], 0.0)
        u0x[a:b] = edge0[r * 8 : (r + 1) * 8]
    def keep(r, value):
        cot1[r * SLIM : (r + 1) * SLIM] = value + add[r * SLIM : (r + 1) * SLIM]

    def finish(r, value):
        a, b = r * SLIM, r * SLIM + 16
        result[r * 16 : (r + 1) * 16] = value[0:16] + error[...] * u0x[a:b]

    adjoint_step(u1x, cot2, gb, gm, flat, d1x, keep, gain[...], ws, wn, wo, members)
    adjoint_step(u0x, cot1, gb, gm, flat, d0x, finish, gain[...], ws, wn, wo, members)


def last_kernel(base, background, before, error, result):
    first = lax.axis_index("slot") == 0
    taken = jnp.where(first, background[...].astype(F32), before[...].astype(F32))
    result[...] = base[...] - error[...] * taken


def kernel_call(body, outs, scratch, flops, moved, hbm=0, out_places=None, aliases={}):
    def call(*operands):
        fixed = [i in range(hbm) and i not in aliases for i in range(len(operands))]
        operands = [
            pltpu.with_memory_space_constraint(x, pltpu.HBM) if fix else x for x, fix in zip(operands, fixed)
        ]
        places = [pltpu.HBM] * hbm + [pltpu.VMEM] * (len(operands) - hbm)
        given = {} if out_places is None else {"out_specs": [pl.BlockSpec(memory_space=p) for p in out_places]}
        return pl.pallas_call(
            body,
            out_shape=outs,
            in_specs=[pl.BlockSpec(memory_space=place) for place in places],
            **given,
            scratch_shapes=scratch,
            input_output_aliases=aliases,
            compiler_params=pltpu.CompilerParams(vmem_limit_bytes=VMEM_LIMIT),
            cost_estimate=pl.CostEstimate(flops=flops, bytes_accessed=moved, transcendentals=0),
        )(*operands)

    return call


def per_device(
    control,
    background,
    self_weight,
    neighbour_weight,
    output_weight,
    norm_gain,
    readout,
    error_weight,
    report_owner,
    report_stencil,
    report_weights,
    report_values,
    report_precision,
):
    tiles = lax.axis_size("tile")
    slots = lax.axis_size("slot")
    members, lats, cols, channels = control.shape[1:]
    groups = members * lats
    size = groups * cols
    steps = report_owner.shape[1]
    rows = report_owner.shape[2]
    gain = norm_gain.reshape(1, channels)
    error = error_weight.reshape(1, channels)
    flat = control.reshape(size, channels)

    def spec(count, dtype=F32, width=channels):
        return jax.ShapeDtypeStruct((count, width), dtype)

    def scratch(count, dtype=F32, width=channels):
        return pltpu.VMEM((count, width), dtype)

    mate_of = [(i, i ^ 1) for i in range(tiles)]
    other_of = [(i, (i - 1) % tiles if i % 2 == 0 else (i + 1) % tiles) for i in range(tiles)]

    def across(block, shift):
        pairs = [
            ((s + shift) % slots * tiles + i, s * tiles + i) for s in range(slots) for i in range(tiles)
        ]
        return lax.ppermute(block, ("slot", "tile"), pairs)

    mate = lax.ppermute(flat, "tile", mate_of)
    listed = (
        jnp.transpose(report_owner[0], (0, 2, 1)),
        jnp.transpose(report_stencil[0], (0, 2, 1)),
        jnp.transpose(report_weights[0], (0, 2, 1)),
        report_precision[0],
        report_values[0].reshape(steps * rows, LANES),
    )
    work = [
        pltpu.VMEM((1, steps * rows), jnp.int32),
        scratch(16, F32, steps * rows),
        scratch(tiles * CHUNK, F32, LANES),
        scratch(tiles * CHUNK, BF16, LANES),
    ]
    held, packed, *listed = kernel_call(
        first_kernel,
        [spec(size), spec(tiles * CHUNK, BF16, LANES)]
        + [jax.ShapeDtypeStruct(block.shape, block.dtype) for block in listed],
        work + [pltpu.SemaphoreType.DMA((7,))],
        10**7,
        200000,
        hbm=6,
        out_places=[pltpu.VMEM, pltpu.HBM] + [pltpu.VMEM] * 5,
    )(flat, *listed)
    sent = kernel_call(
        tile_kernel, spec(groups * (cols + 2), BF16), [scratch(groups * 2)], 1000, 400000
    )(held, mate)
    oth = lax.ppermute(sent, "tile", other_of)
    (packed,) = kernel_call(
        later_kernel,
        [spec(tiles * CHUNK, BF16, LANES)],
        work + [pltpu.SemaphoreType.DMA],
        10**7,
        200000,
        hbm=1,
        out_places=[pltpu.HBM],
        aliases={0: 0},
    )(packed, *listed, sent)
    arrived = lax.all_to_all(packed, "tile", split_axis=0, concat_axis=0, tiled=True)

    message, near4 = kernel_call(
        relay_kernel,
        [spec(size + 4 * groups, BF16), spec(4 * groups)],
        [scratch(size), scratch(4 * groups)],
        1000,
        700000,
    )(held, mate, oth)
    nxt = across(message, 1)
    wide = groups * WIDE
    slim = groups * SLIM
    (
        edge0, u1x, d0x, d1x, f2x, field, final, wo, readout_held, gain_held, error_held, background_held,
    ) = kernel_call(
        forward_kernel,
        [spec(groups * 8), spec(slim)] + [spec(slim, BF16)] * 3
        + [spec(4 * lats * cols, F32, members * LANES), spec(size, BF16)]
        + [spec(channels, BF16), spec(channels, BF16, LANES), spec(1), spec(1), spec(size, BF16)],
        [scratch(wide), scratch(wide), scratch(wide, BF16), scratch(wide, BF16), scratch(wide, BF16)]
        + [scratch(wide), scratch(16), scratch(4 * size, BF16)]
        + [scratch(channels, BF16), scratch(channels, BF16), pltpu.SemaphoreType.DMA((7,))],
        10**11,
        4000000,
        hbm=7,
    )(
        gain, self_weight, neighbour_weight, output_weight, readout, error, background.reshape(size, channels),
        held, near4, oth,
    )
    before = across(final, -1)
    total = -(-tiles // SENDERS) * LANES
    tables = [scratch(64, BF16, total), scratch(64, BF16, total)]
    spread, near_spread, *reports_held = kernel_call(
        functools.partial(observe_kernel, tiles),
        [spec(2 * size, BF16, LANES), spec(size, BF16, LANES)]
        + [spec(32, BF16, total), spec(32, BF16, total), spec(32, F32, total), spec(total, BF16, LANES)],
        tables + [scratch(total, F32, LANES), scratch(tiles * CHUNK, F32, LANES)],
        10**9,
        2000000,
    )(arrived, field)
    from_mate = lax.ppermute(near_spread, "tile", mate_of)
    handed = kernel_call(
        pull_kernel,
        [spec(slim), spec(slim), spec(channels, BF16), spec(channels, BF16)],
        tables
        + [scratch(2 * size, BF16, LANES), scratch(2 * size), scratch(2 * size), pltpu.SemaphoreType.DMA((2,))],
        10**9,
        3000000,
        hbm=2,
    )(neighbour_weight, self_weight, spread, readout_held, *reports_held, field)
    base = kernel_call(
        backward_kernel,
        spec(size),
        [scratch(slim), scratch(slim), scratch(slim), scratch(slim, BF16), scratch(slim), scratch(slim)]
        + [scratch(size), scratch(16), scratch(slim), scratch(slim), scratch(size + 4 * groups)],
        12 * slim * channels * channels,
        6000000,
    )(
        *handed, gain_held, held, edge0, nxt, f2x, wo, readout_held, error_held, from_mate,
        u1x, d0x, d1x,
    )
    result = kernel_call(last_kernel, spec(size), [], 10**6, 900000)(base, background_held, before, error_held)
    return result.reshape(control.shape)


def solution(mesh):
    in_specs = (
        P("slot", None, None, "tile", None),
        P(None, None, "tile", None),
        P(),
        P(),
        P(),
        P(),
        P(),
        P(),
        P("slot", None, "tile", None),
        P("slot", None, "tile", None),
        P("slot", None, "tile", None),
        P("slot", None, "tile", None),
        P("slot", None, "tile"),
    )
    out_specs = P("slot", None, None, "tile", None)
    return jax.shard_map(
        per_device, mesh=mesh, in_specs=in_specs, out_specs=out_specs, check_vma=False
    )
```

```python
import functools
import jax
import jax.numpy as jnp
from jax import lax
from jax.experimental import pallas as pl
from jax.experimental.pallas import tpu as pltpu
from jax.sharding import PartitionSpec as P

EPSILON = 1e-06
F32 = jnp.float32
BF16 = jnp.bfloat16
LANES = 128
CAP = 5
SLOTS = 4 * CAP
CHUNK = 24
STRIDE = 32
WIDE = 40
SLIM = 24
VMEM_LIMIT = 28 * 1024 * 1024


def dot(a, b):
    return jnp.dot(a, b, preferred_element_type=F32)


def dot_t(a, b):
    return lax.dot_general(a, b, (((1,), (1,)), ((), ())), preferred_element_type=F32)


def sublane(shape):
    return lax.broadcasted_iota(jnp.int32, shape, 0)


def inverse_rms(x):
    return lax.rsqrt(jnp.mean(x * x, axis=-1, keepdims=True) + EPSILON)


def sigmoid(p):
    return 0.5 * jnp.tanh(0.5 * p) + 0.5


def neighbours(rows):
    width = rows[0].shape[0]
    return [
        0.25 * (rows[1 - i] + pltpu.roll(rows[i], 1, 0) + pltpu.roll(rows[i], width - 1, 0))
        for i in range(2)
    ]


def forward_step(u, n, mean, act, pre, d, gain, ws, wn, wo, width, members, out, copies=()):
    both = 2 * width
    for m in range(members):
        base = m * both
        rows = []
        for lat in range(2):
            x = u[base + lat * width : base + (lat + 1) * width]
            rows.append((x * inverse_rms(x) * gain).astype(BF16).astype(F32))
        n[base : base + both] = jnp.concatenate(rows, axis=0).astype(BF16)
        mean[base : base + both] = jnp.concatenate(neighbours(rows), axis=0).astype(BF16)
    for copy in copies[:2]:
        copy.wait()
    pre[...] = dot(n[...], ws[...]) + dot(mean[...], wn[...])
    for m in range(members):
        base = m * both
        p = pre[base : base + both]
        sig = sigmoid(p)
        act[base : base + both] = (p * sig).astype(BF16)
        if d is not None:
            pre[base : base + both] = sig * (1.0 + p * (1.0 - sig))
    if d is not None:
        for m in range(members):
            slim_copy(d, pre, m)
    for copy in copies[2:]:
        copy.wait()
    pre[...] = dot(act[...], wo[...])
    for r in range(2 * members):
        out(r, u[r * width : (r + 1) * width] + pre[r * width : (r + 1) * width])


def slim_edge(wide, r):
    low = wide[r * WIDE + 16 : r * WIDE + 24]
    high = wide[r * WIDE + 32 : r * WIDE + 40]
    return jnp.where(sublane(low.shape) < 4, low, high)


def slim_copy(to, wide, m):
    parts = []
    for r in (2 * m, 2 * m + 1):
        parts += [wide[r * WIDE : r * WIDE + 16], slim_edge(wide, r)]
    both = jnp.concatenate(parts, axis=0)
    to[m * 2 * SLIM : (m + 1) * 2 * SLIM] = both.astype(to.dtype)


def reports(arrays, out_hbm, key, meta, picked, out, sem):
    pack(*arrays, out, key, meta, picked)
    store = pltpu.make_async_copy(out, out_hbm, sem)
    store.start()
    store.wait()


def early():
    return lax.axis_index("tile") < lax.axis_size("tile") // 2


def first_kernel(control_hbm, *refs):
    sources, (held, out_hbm), arrays, (key, meta, picked, out, sems) = refs[:5], refs[5:7], refs[7:12], refs[12:]
    copies = [
        pltpu.make_async_copy(source, to, sems.at[i]) for i, (source, to) in enumerate(zip(sources, arrays))
    ]
    copies.append(pltpu.make_async_copy(control_hbm, held, sems.at[5]))
    for copy in copies:
        copy.start()
    for copy in copies[:5]:
        copy.wait()

    @pl.when(early())
    def _():
        reports(arrays, out_hbm, key, meta, picked, out, sems.at[6])

    copies[5].wait()


def later_kernel(packed_hbm, *refs):
    arrays, out_hbm, (key, meta, picked, out, sem) = refs[:5], refs[6], refs[7:]

    @pl.when(jnp.logical_not(early()))
    def _():
        reports(arrays, out_hbm, key, meta, picked, out, sem)


def fan(x, shift):
    if shift % LANES:
        x = pltpu.roll(x, shift % LANES, 1)
    for _ in range(2):
        x = pltpu.roll(x, 0, 1, stride=SLOTS // 2, stride_axis=0)
    return x


def pack(owner, stencil, weights, precision, values, out, key, meta, picked):
    steps, _, rows = owner.shape
    tiles = out.shape[0] // CHUNK
    total = steps * rows
    earlier = lax.broadcasted_iota(jnp.int32, (rows, rows), 0) < lax.broadcasted_iota(jnp.int32, (rows, rows), 1)
    earlier = earlier.astype(F32).astype(BF16)
    meta[...] = jnp.zeros_like(meta)
    for k in range(steps):
        at = slice(k * rows, (k + 1) * rows)
        named = lax.broadcasted_iota(jnp.int32, (tiles, rows), 0) == owner[k]
        hits = named.astype(F32)
        before = dot(hits.astype(BF16), earlier)
        rank = jnp.sum(hits * before, axis=0, keepdims=True).astype(jnp.int32)
        key[0:1, at] = owner[k] * (2 * CAP) + k * CAP + rank
        meta[0:4, at] = stencil[k].astype(F32)
        meta[4:6, at] = weights[k, 0:2].astype(F32)
        meta[8:10, at] = weights[k, 2:4].astype(F32)
        meta[10:11, at] = precision[k : k + 1].astype(F32)
    row = lax.broadcasted_iota(jnp.int32, (tiles * STRIDE, total), 0)
    tile = row // STRIDE
    slot = row % STRIDE
    other = jnp.where(tile % 2 == 0, (tile + tiles - 1) % tiles, (tile + 1) % tiles)
    mine = slot < 2 * CAP
    wanted = jnp.where(mine, tile * (2 * CAP) + slot, other * (2 * CAP) + slot - 2 * CAP)
    wanted = jnp.where(slot < SLOTS, wanted, -1)
    placement = (wanted == key[...]).astype(F32).astype(BF16)
    placed = dot(placement, values[...])
    entries = dot_t(meta[...].astype(BF16), placement)
    lane = lax.broadcasted_iota(jnp.int32, (16, LANES), 1)
    per_tile = LANES // STRIDE
    for t in range(tiles):
        picked[t * CHUNK : (t + 1) * CHUNK] = placed[t * STRIDE : t * STRIDE + CHUNK]
        start = t % per_tile * STRIDE
        used = jnp.logical_and(lane >= start, lane < start + SLOTS)
        block = jnp.where(used, entries[:, t // per_tile * LANES : (t // per_tile + 1) * LANES], 0.0)
        for j in range(2):
            spread = fan(block[j * 8 : (j + 1) * 8], LANES - start)
            row = t * CHUNK + SLOTS + j
            picked[row : row + 1] = jnp.sum(spread, axis=0, keepdims=True)
    out[...] = picked[...].astype(BF16)


def tile_kernel(control, mate, out, held):
    even = lax.rem(lax.axis_index("tile"), 2) == 0
    size = control.shape[0]
    out[0:size] = control[...].astype(BF16)
    for r in range(size // 16):
        held[r * 2 : (r + 1) * 2] = jnp.where(
            even, mate[r * 16 : r * 16 + 2], mate[r * 16 + 14 : (r + 1) * 16]
        )
    out[size:] = held[...].astype(BF16)


def relay_kernel(control, mate, oth, out, near4, wide, edge):
    even = lax.rem(lax.axis_index("tile"), 2) == 0
    size = mate.shape[0]
    out[0:size] = control[...].astype(BF16)
    wide[...] = oth[0:size].astype(F32)
    for r in range(size // 16):
        a, b = r * 16, (r + 1) * 16
        edge[r * 2 : (r + 1) * 2] = jnp.where(even, wide[b - 2 : b], wide[a : a + 2])
        near4[r * 4 : (r + 1) * 4] = jnp.where(even, mate[a : a + 4], mate[b - 4 : b])
        start = size // 8 + r * 2
        edge[start : start + 2] = jnp.where(even, mate[a : a + 2], mate[b - 2 : b])
    out[size:] = edge[...].astype(BF16)


def forward_kernel(
    gain_hbm, ws_hbm, wn_hbm, wo_hbm, readout_hbm, error_hbm, background_hbm, control, mate, oth,
    edge0, u1x, d0x, d1x, f2x, field, final, wo, readout, gain, error, background,
    ua, ub, n, mean, act, pre, edge, states, ws, wn, sems,
):
    pairs = (
        (gain_hbm, gain), (ws_hbm, ws), (wn_hbm, wn), (wo_hbm, wo), (readout_hbm, readout),
        (error_hbm, error), (background_hbm, background),
    )
    copies = [pltpu.make_async_copy(source, to, sems.at[i]) for i, (source, to) in enumerate(pairs)]
    for copy in copies:
        copy.start()
    members = final.shape[0] // 32
    even = lax.rem(lax.axis_index("tile"), 2) == 0
    tile_at = jnp.where(even, 24, 16)
    edge_at = jnp.where(even, 16, 32)
    far = oth[members * 32 :].astype(F32)
    for r in range(2 * members):
        ua[r * WIDE : r * WIDE + 16] = control[r * 16 : (r + 1) * 16]
        ua[pl.ds(pl.multiple_of(r * WIDE + tile_at, 8), 16)] = oth[r * 16 : (r + 1) * 16].astype(F32)
        near4 = mate[r * 4 : (r + 1) * 4]
        far2 = far[r * 2 : (r + 1) * 2]
        edge[...] = jnp.zeros_like(edge)
        edge[0:4] = near4
        edge[6:8] = far2
        edge[8:10] = far2
        edge[12:16] = near4
        ua[pl.ds(pl.multiple_of(r * WIDE + edge_at, 8), 8)] = jnp.where(even, edge[0:8], edge[8:16])
    for r in range(2 * members):
        edge0[r * 8 : (r + 1) * 8] = slim_edge(ua, r)
    copies[0].wait()
    g = gain[...]

    def keep(ref):
        def store(r, value):
            ref[r * WIDE : (r + 1) * WIDE] = value

        return store

    def keep_states(ref, k):
        own = k * members * 32
        away = (2 + k) * members * 32
        for r in range(2 * members):
            states[own + r * 16 : own + (r + 1) * 16] = ref[r * WIDE : r * WIDE + 16].astype(BF16)
            taken = ref[pl.ds(pl.multiple_of(r * WIDE + tile_at, 8), 16)]
            states[away + r * 16 : away + (r + 1) * 16] = taken.astype(BF16)

    forward_step(ua, n, mean, act, pre, d0x, g, ws, wn, wo, WIDE, members, keep(ub), copies[1:])
    for m in range(members):
        slim_copy(u1x, ub, m)
    keep_states(ub, 0)
    forward_step(ub, n, mean, act, pre, d1x, g, ws, wn, wo, WIDE, members, keep(ua))
    for m in range(members):
        slim_copy(f2x, ua, m)
    keep_states(ua, 1)
    final[...] = states[members * 32 : 2 * members * 32]
    read = dot(states[...], readout[...])
    for q in range(4):
        for m in range(members):
            start = (q * members + m) * 32
            field[q * 32 : (q + 1) * 32, m * LANES : (m + 1) * LANES] = read[start : start + 32]


def split(x):
    high = x.astype(BF16)
    return high, (x - high.astype(F32)).astype(BF16)


def spread_of(first, th, tl, scaled, taken, field, ph, plo, spread):
    lane = lax.broadcasted_iota(jnp.int32, (1, LANES), 1)
    members = field.shape[1] // LANES
    for p in range(th.shape[1] // LANES):
        at = slice(p * LANES, (p + 1) * LANES)
        slot = (lane + p * LANES) % CHUNK
        table_of = jnp.where(slot < SLOTS, slot // CAP, -1)
        for q in range(2):
            kept = jnp.where(table_of == first + q, scaled[:, at], 0.0)
            ph[q * 32 : (q + 1) * 32, at], plo[q * 32 : (q + 1) * 32, at] = split(kept)
    cross = dot_t(ph[...], th[...]) + dot_t(plo[...], th[...]) + dot_t(ph[...], tl[...])
    block = jnp.concatenate([cross] * 2, axis=1)
    on_block = sublane(block.shape) // 32 == lax.broadcasted_iota(jnp.int32, block.shape, 1) // 32
    target = dot(ph[...], taken[...]) + dot(plo[...], taken[...])
    ch, cl = split(jnp.where(on_block, block, 0.0))
    fh, fl = split(field[first * 32 : (first + 2) * 32])
    mixed = dot(ch, fh) + dot(cl, fh) + dot(ch, fl)
    for q in range(2):
        for m in range(members):
            start = (q * members + m) * 32
            value = mixed[q * 32 : (q + 1) * 32, m * LANES : (m + 1) * LANES] - target[q * 32 : (q + 1) * 32]
            spread[start : start + 32] = value.astype(BF16)


def observe_kernel(
    tiles, arrived, field,
    spread, message, th, tl, scaled,
    ph, plo, wide,
):
    steps = 2
    members = field.shape[1] // LANES
    even = lax.rem(lax.axis_index("tile"), 2) == 0
    cells = sublane((32, LANES)).astype(F32)
    lane = lax.broadcasted_iota(jnp.int32, (8, LANES), 1)
    wide[...] = arrived[...].astype(F32)
    packs = th.shape[1] // LANES
    meta = [[jnp.zeros((8, LANES), F32)] * 2 for _ in range(packs)]
    for d in range(tiles):
        p, start = divmod(d * CHUNK, LANES)
        ends = start + SLOTS - LANES
        here = jnp.logical_and(lane >= start, lane < start + SLOTS)
        for j in range(2):
            row = d * CHUNK + SLOTS + j
            turned = fan(jnp.broadcast_to(wide[row : row + 1], (8, LANES)), start + LANES - 5 * SLOTS)
            meta[p][j] = meta[p][j] + jnp.where(here, turned, 0.0)
            if ends > 0:
                meta[p + 1][j] = meta[p + 1][j] + jnp.where(lane < ends, turned, 0.0)
    for p in range(packs):
        entry = [meta[p][i // 6][5 - i % 6 : 6 - i % 6] for i in range(9)]
        weight = jnp.zeros((32, LANES), F32)
        for i in range(4):
            weight += jnp.where(cells == entry[i], entry[4 + i], 0.0)
        at = slice(p * LANES, (p + 1) * LANES)
        th[:, at], tl[:, at] = split(weight)
        scaled[:, at] = weight * entry[8]
    spread_of(0, th, tl, scaled, arrived, field, ph, plo, spread)
    size = members * 32
    for k in range(steps):
        for m in range(members):
            start = k * size + m * 32
            pair = spread[start : start + 32].astype(F32)
            near = [jnp.where(even, pair[i + 8 : i + 16], pair[i : i + 8]) for i in (0, 16)]
            start = k * size // 2 + m * 16
            message[start : start + 16] = jnp.concatenate(near, axis=0).astype(BF16)


def adjoint_step(u, cot, gb, gm, flat, d, out, gain, ws, wn, wo, members):
    both = 2 * SLIM
    gb[...] = cot[...].astype(BF16)
    flat[...] = dot_t(gb[...], wo[...])
    gb[...] = (flat[...] * d[...]).astype(BF16)
    gm[...] = dot_t(gb[...], wn[...])
    flat[...] = dot_t(gb[...], ws[...])
    for m in range(members):
        base = m * both
        rows = []
        for lat in range(2):
            start = base + lat * SLIM
            rows.append(gm[start : start + SLIM].astype(BF16).astype(F32))
        around = neighbours(rows)
        for lat in range(2):
            start = base + lat * SLIM
            x = u[start : start + SLIM]
            s = inverse_rms(x)
            scaled = gain * (flat[start : start + SLIM] + around[lat])
            inner = jnp.mean(x * scaled, axis=-1, keepdims=True)
            out(2 * m + lat, cot[start : start + SLIM] + s * scaled - x * (s * s * s * inner))


def edges(nxt, size, edge, r):
    even = lax.rem(lax.axis_index("tile"), 2) == 0
    start = size + r * 2
    far = nxt[start : start + 2]
    start = size + size // 8 + r * 2
    near = nxt[start : start + 2]
    edge[...] = jnp.zeros_like(edge)
    edge[0:2] = near
    edge[6:8] = far
    edge[8:10] = far
    edge[14:16] = near
    return jnp.where(even, edge[0:8], edge[8:16])


def pull_kernel(
    wn_hbm, ws_hbm, spread_own, readout, th, tl, scaled, arrived, field,
    pulled, away, wn, ws,
    ph, plo, spread, near, sems,
):
    pairs = ((wn_hbm, wn), (ws_hbm, ws))
    copies = [pltpu.make_async_copy(source, to, sems.at[i]) for i, (source, to) in enumerate(pairs)]
    for copy in copies:
        copy.start()
    even = lax.rem(lax.axis_index("tile"), 2) == 0
    pulled[...] = dot_t(spread_own[...], readout[...])
    spread_of(2, th, tl, scaled, arrived, field, ph, plo, spread)
    for start in range(0, spread.shape[0], 32):
        pair = spread[start : start + 32].astype(F32)
        rows = [jnp.where(even, pair[i + 8 : i + 16], pair[i : i + 8]) for i in (0, 16)]
        near[start // 2 : start // 2 + 16] = jnp.concatenate(rows, axis=0).astype(BF16)
    away[...] = dot_t(near[...], readout[...])
    for copy in copies:
        copy.wait()


def backward_kernel(
    pulled, away, wn, ws, gain, control, edge0, message16, f2x, wo, readout, error, message,
    u1x, d0x, d1x,
    result,
    cot2, cot1, gb, gm, flat, mate_pull, edge, u0x, final, nxt,
):
    size = result.shape[0]
    members = size // 32
    even = lax.rem(lax.axis_index("tile"), 2) == 0
    nxt[...] = message16[...].astype(F32)
    weight = jnp.where(lax.axis_index("slot") == lax.axis_size("slot") - 1, 0.0, 1.0) * error[...]
    row8 = sublane((8, 1))
    mate_side = jnp.where(even, 1, 0) == jnp.where(row8 < 4, 1, 0)
    mate_pull[...] = dot_t(message[...], readout[...])
    final[...] = f2x[...].astype(F32)

    def pulls(k, r):
        own = k * size + r * 16
        near = k * size // 2 + r * 8
        group = jnp.where(mate_side, mate_pull[near : near + 8], away[near : near + 8])
        return pulled[own : own + 16], group

    for r in range(2 * members):
        own, group = pulls(1, r)
        a, b = r * SLIM, r * SLIM + 16
        cot2[a:b] = own - weight * (nxt[r * 16 : (r + 1) * 16] - final[a:b])
        u0x[a:b] = control[r * 16 : (r + 1) * 16]
        a, b = b, b + 8
        cot2[a:b] = group - weight * (edges(nxt, size, edge, r) - final[a:b])
        u0x[a:b] = edge0[r * 8 : (r + 1) * 8]

    def keep(r, value):
        cot1[r * SLIM : (r + 1) * SLIM] = value + jnp.concatenate(pulls(0, r), axis=0)

    def finish(r, value):
        a, b = r * SLIM, r * SLIM + 16
        result[r * 16 : (r + 1) * 16] = value[0:16] + error[...] * u0x[a:b]

    adjoint_step(u1x, cot2, gb, gm, flat, d1x, keep, gain[...], ws, wn, wo, members)
    adjoint_step(u0x, cot1, gb, gm, flat, d0x, finish, gain[...], ws, wn, wo, members)


def last_kernel(base, background, before, error, result):
    first = lax.axis_index("slot") == 0
    taken = jnp.where(first, background[...].astype(F32), before[...].astype(F32))
    result[...] = base[...] - error[...] * taken


def kernel_call(body, outs, scratch, flops, moved, hbm=0, out_places=None, aliases={}):
    def call(*operands):
        fixed = [i in range(hbm) and i not in aliases for i in range(len(operands))]
        operands = [
            pltpu.with_memory_space_constraint(x, pltpu.HBM) if fix else x for x, fix in zip(operands, fixed)
        ]
        places = [pltpu.HBM] * hbm + [pltpu.VMEM] * (len(operands) - hbm)
        given = {} if out_places is None else {"out_specs": [pl.BlockSpec(memory_space=p) for p in out_places]}
        return pl.pallas_call(
            body,
            out_shape=outs,
            in_specs=[pl.BlockSpec(memory_space=place) for place in places],
            **given,
            scratch_shapes=scratch,
            input_output_aliases=aliases,
            compiler_params=pltpu.CompilerParams(vmem_limit_bytes=VMEM_LIMIT),
            cost_estimate=pl.CostEstimate(flops=flops, bytes_accessed=moved, transcendentals=0),
        )(*operands)

    return call


def per_device(
    control,
    background,
    self_weight,
    neighbour_weight,
    output_weight,
    norm_gain,
    readout,
    error_weight,
    report_owner,
    report_stencil,
    report_weights,
    report_values,
    report_precision,
):
    tiles = lax.axis_size("tile")
    slots = lax.axis_size("slot")
    members, lats, cols, channels = control.shape[1:]
    groups = members * lats
    size = groups * cols
    steps = report_owner.shape[1]
    rows = report_owner.shape[2]
    gain = norm_gain.reshape(1, channels)
    error = error_weight.reshape(1, channels)
    flat = control.reshape(size, channels)

    def spec(count, dtype=F32, width=channels):
        return jax.ShapeDtypeStruct((count, width), dtype)

    def scratch(count, dtype=F32, width=channels):
        return pltpu.VMEM((count, width), dtype)

    mate_of = [(i, i ^ 1) for i in range(tiles)]
    other_of = [(i, (i - 1) % tiles if i % 2 == 0 else (i + 1) % tiles) for i in range(tiles)]

    def across(block, shift):
        pairs = [
            ((s + shift) % slots * tiles + i, s * tiles + i) for s in range(slots) for i in range(tiles)
        ]
        return lax.ppermute(block, ("slot", "tile"), pairs)

    mate = lax.ppermute(flat, "tile", mate_of)
    listed = (
        jnp.transpose(report_owner[0], (0, 2, 1)),
        jnp.transpose(report_stencil[0], (0, 2, 1)),
        jnp.transpose(report_weights[0], (0, 2, 1)),
        report_precision[0],
        report_values[0].reshape(steps * rows, LANES),
    )
    work = [
        pltpu.VMEM((1, steps * rows), jnp.int32),
        scratch(16, F32, steps * rows),
        scratch(tiles * CHUNK, F32, LANES),
        scratch(tiles * CHUNK, BF16, LANES),
    ]
    held, packed, *listed = kernel_call(
        first_kernel,
        [spec(size), spec(tiles * CHUNK, BF16, LANES)]
        + [jax.ShapeDtypeStruct(block.shape, block.dtype) for block in listed],
        work + [pltpu.SemaphoreType.DMA((7,))],
        10**7,
        200000,
        hbm=6,
        out_places=[pltpu.VMEM, pltpu.HBM] + [pltpu.VMEM] * 5,
    )(flat, *listed)
    sent = kernel_call(
        tile_kernel, spec(groups * (cols + 2), BF16), [scratch(groups * 2)], 1000, 400000
    )(held, mate)
    oth = lax.ppermute(sent, "tile", other_of)
    (packed,) = kernel_call(
        later_kernel,
        [spec(tiles * CHUNK, BF16, LANES)],
        work + [pltpu.SemaphoreType.DMA],
        10**7,
        200000,
        hbm=1,
        out_places=[pltpu.HBM],
        aliases={0: 0},
    )(packed, *listed, sent)
    arrived = lax.all_to_all(packed, "tile", split_axis=0, concat_axis=0, tiled=True)

    message, near4 = kernel_call(
        relay_kernel,
        [spec(size + 4 * groups, BF16), spec(4 * groups)],
        [scratch(size), scratch(4 * groups)],
        1000,
        700000,
    )(held, mate, oth)
    nxt = across(message, 1)
    wide = groups * WIDE
    slim = groups * SLIM
    (
        edge0, u1x, d0x, d1x, f2x, field, final, wo, readout_held, gain_held, error_held, background_held,
    ) = kernel_call(
        forward_kernel,
        [spec(groups * 8), spec(slim)] + [spec(slim, BF16)] * 3
        + [spec(4 * lats * cols, F32, members * LANES), spec(size, BF16)]
        + [spec(channels, BF16), spec(channels, BF16, LANES), spec(1), spec(1), spec(size, BF16)],
        [scratch(wide), scratch(wide), scratch(wide, BF16), scratch(wide, BF16), scratch(wide, BF16)]
        + [scratch(wide), scratch(16), scratch(4 * size, BF16)]
        + [scratch(channels, BF16), scratch(channels, BF16), pltpu.SemaphoreType.DMA((7,))],
        10**11,
        4000000,
        hbm=7,
    )(
        gain, self_weight, neighbour_weight, output_weight, readout, error, background.reshape(size, channels),
        held, near4, oth,
    )
    before = across(final, -1)
    total = tiles * CHUNK
    tables = [scratch(64, BF16, total), scratch(64, BF16, total)]
    spread, near_spread, *reports_held = kernel_call(
        functools.partial(observe_kernel, tiles),
        [spec(2 * size, BF16, LANES), spec(size, BF16, LANES)]
        + [spec(32, BF16, total), spec(32, BF16, total), spec(32, F32, total)],
        tables + [scratch(total, F32, LANES)],
        10**9,
        2000000,
    )(arrived, field)
    from_mate = lax.ppermute(near_spread, "tile", mate_of)
    handed = kernel_call(
        pull_kernel,
        [spec(2 * size), spec(size), spec(channels, BF16), spec(channels, BF16)],
        tables + [scratch(2 * size, BF16, LANES), scratch(size, BF16, LANES), pltpu.SemaphoreType.DMA((2,))],
        10**9,
        3000000,
        hbm=2,
    )(neighbour_weight, self_weight, spread, readout_held, *reports_held, arrived, field)
    base = kernel_call(
        backward_kernel,
        spec(size),
        [scratch(slim), scratch(slim), scratch(slim, BF16), scratch(slim), scratch(slim)]
        + [scratch(size), scratch(16), scratch(slim), scratch(slim), scratch(size + 4 * groups)],
        12 * slim * channels * channels,
        6000000,
    )(
        *handed, gain_held, held, edge0, nxt, f2x, wo, readout_held, error_held, from_mate,
        u1x, d0x, d1x,
    )
    result = kernel_call(last_kernel, spec(size), [], 10**6, 900000)(base, background_held, before, error_held)
    return result.reshape(control.shape)


def solution(mesh):
    in_specs = (
        P("slot", None, None, "tile", None),
        P(None, None, "tile", None),
        P(),
        P(),
        P(),
        P(),
        P(),
        P(),
        P("slot", None, "tile", None),
        P("slot", None, "tile", None),
        P("slot", None, "tile", None),
        P("slot", None, "tile", None),
        P("slot", None, "tile"),
    )
    out_specs = P("slot", None, None, "tile", None)
    return jax.shard_map(
        per_device, mesh=mesh, in_specs=in_specs, out_specs=out_specs, check_vma=False
    )
```

```python
import functools
import jax
import jax.numpy as jnp
from jax import lax
from jax.experimental import pallas as pl
from jax.experimental.pallas import tpu as pltpu
from jax.sharding import PartitionSpec as P

EPSILON = 1e-06
F32 = jnp.float32
BF16 = jnp.bfloat16
LANES = 128
CAP = 5
SLOTS = 4 * CAP
CHUNK = 24
APART = 36
STRIDE = 32
WIDE = 40
SLIM = 24
VMEM_LIMIT = 28 * 1024 * 1024


def dot(a, b):
    return jnp.dot(a, b, preferred_element_type=F32)


def dot_t(a, b):
    return lax.dot_general(a, b, (((1,), (1,)), ((), ())), preferred_element_type=F32)


def sublane(shape):
    return lax.broadcasted_iota(jnp.int32, shape, 0)


def inverse_rms(x):
    return lax.rsqrt(jnp.mean(x * x, axis=-1, keepdims=True) + EPSILON)


def sigmoid(p):
    return 0.5 * jnp.tanh(0.5 * p) + 0.5


def neighbours(rows):
    width = rows[0].shape[0]
    return [
        0.25 * (rows[1 - i] + pltpu.roll(rows[i], 1, 0) + pltpu.roll(rows[i], width - 1, 0))
        for i in range(2)
    ]


def forward_step(u, n, act, pre, d, gain, weights, wo, width, members, out, copies=()):
    both = 2 * width
    for m in range(members):
        base = m * both
        rows = []
        for lat in range(2):
            x = u[base + lat * width : base + (lat + 1) * width]
            rows.append((x * inverse_rms(x) * gain).astype(BF16).astype(F32))
        channels = rows[0].shape[1]
        n[base : base + both, :channels] = jnp.concatenate(rows, axis=0).astype(BF16)
        n[base : base + both, channels:] = jnp.concatenate(neighbours(rows), axis=0).astype(BF16)
    for copy in copies[:2]:
        copy.wait()
    pre[...] = dot(n[...], weights[...])
    for m in range(members):
        base = m * both
        p = pre[base : base + both]
        sig = sigmoid(p)
        act[base : base + both] = (p * sig).astype(BF16)
        if d is not None:
            pre[base : base + both] = sig * (1.0 + p * (1.0 - sig))
    if d is not None:
        for m in range(members):
            slim_copy(d, pre, m)
    for copy in copies[2:]:
        copy.wait()
    pre[...] = dot(act[...], wo[...])
    for r in range(2 * members):
        out(r, u[r * width : (r + 1) * width] + pre[r * width : (r + 1) * width])


def slim_edge(wide, r):
    low = wide[r * WIDE + 16 : r * WIDE + 24]
    high = wide[r * WIDE + 32 : r * WIDE + 40]
    return jnp.where(sublane(low.shape) < 4, low, high)


def slim_copy(to, wide, m):
    parts = []
    for r in (2 * m, 2 * m + 1):
        parts += [wide[r * WIDE : r * WIDE + 16], slim_edge(wide, r)]
    both = jnp.concatenate(parts, axis=0)
    to[m * 2 * SLIM : (m + 1) * 2 * SLIM] = both.astype(to.dtype)


def reports(arrays, out_hbm, key, meta, picked, out, sem):
    pack(*arrays, out, key, meta, picked)
    store = pltpu.make_async_copy(out, out_hbm, sem)
    store.start()
    store.wait()


def early():
    return lax.axis_index("tile") < lax.axis_size("tile") // 2


def first_kernel(control_hbm, *refs):
    sources, (held, out_hbm), arrays, (key, meta, picked, out, sems) = refs[:5], refs[5:7], refs[7:12], refs[12:]
    copies = [
        pltpu.make_async_copy(source, to, sems.at[i]) for i, (source, to) in enumerate(zip(sources, arrays))
    ]
    copies.append(pltpu.make_async_copy(control_hbm, held, sems.at[5]))
    for copy in copies:
        copy.start()
    for copy in copies[:5]:
        copy.wait()

    @pl.when(early())
    def _():
        reports(arrays, out_hbm, key, meta, picked, out, sems.at[6])

    copies[5].wait()


def later_kernel(packed_hbm, *refs):
    arrays, out_hbm, (key, meta, picked, out, sem) = refs[:5], refs[6], refs[7:]

    @pl.when(jnp.logical_not(early()))
    def _():
        reports(arrays, out_hbm, key, meta, picked, out, sem)


def fan(x, shift):
    if shift % LANES:
        x = pltpu.roll(x, shift % LANES, 1)
    for _ in range(2):
        x = pltpu.roll(x, 0, 1, stride=APART // 2, stride_axis=0)
    return x


def pack(owner, stencil, weights, precision, values, out, key, meta, picked):
    steps, _, rows = owner.shape
    tiles = out.shape[0] // CHUNK
    total = steps * rows
    earlier = lax.broadcasted_iota(jnp.int32, (rows, rows), 0) < lax.broadcasted_iota(jnp.int32, (rows, rows), 1)
    earlier = earlier.astype(F32).astype(BF16)
    meta[...] = jnp.zeros_like(meta)
    for k in range(steps):
        at = slice(k * rows, (k + 1) * rows)
        named = lax.broadcasted_iota(jnp.int32, (tiles, rows), 0) == owner[k]
        hits = named.astype(F32)
        before = dot(hits.astype(BF16), earlier)
        rank = jnp.sum(hits * before, axis=0, keepdims=True).astype(jnp.int32)
        key[0:1, at] = owner[k] * (2 * CAP) + k * CAP + rank
        for i in range(4):
            meta[i // 3 * 8 + i % 3 : i // 3 * 8 + i % 3 + 1, at] = stencil[k, i : i + 1].astype(F32)
            j = 4 + i
            meta[j // 3 * 8 + j % 3 : j // 3 * 8 + j % 3 + 1, at] = weights[k, i : i + 1].astype(F32)
        meta[18:19, at] = precision[k : k + 1].astype(F32)
    row = lax.broadcasted_iota(jnp.int32, (tiles * STRIDE, total), 0)
    tile = row // STRIDE
    slot = row % STRIDE
    other = jnp.where(tile % 2 == 0, (tile + tiles - 1) % tiles, (tile + 1) % tiles)
    mine = slot < 2 * CAP
    wanted = jnp.where(mine, tile * (2 * CAP) + slot, other * (2 * CAP) + slot - 2 * CAP)
    wanted = jnp.where(slot < SLOTS, wanted, -1)
    placement = (wanted == key[...]).astype(F32).astype(BF16)
    placed = dot(placement, values[...])
    entries = dot_t(meta[...].astype(BF16), placement)
    lane = lax.broadcasted_iota(jnp.int32, (24, LANES), 1)
    turn = lax.axis_index("tile") * CHUNK % LANES
    per_tile = LANES // STRIDE
    for t in range(tiles):
        picked[t * CHUNK : (t + 1) * CHUNK] = placed[t * STRIDE : t * STRIDE + CHUNK]
        start = t % per_tile * STRIDE
        used = jnp.logical_and(lane >= start, lane < start + SLOTS)
        block = jnp.where(used, entries[:, t // per_tile * LANES : (t // per_tile + 1) * LANES], 0.0)
        for j in range(3):
            laid = fan(block[j * 8 : (j + 1) * 8], LANES - start)
            row = t * CHUNK + SLOTS + j
            picked[row : row + 1] = jnp.sum(laid, axis=0, keepdims=True)
        group = picked[t * CHUNK + 16 : (t + 1) * CHUNK]
        picked[t * CHUNK + 16 : (t + 1) * CHUNK] = jnp.where(sublane((8, 1)) < 4, group, pltpu.roll(group, turn, 1))
    out[...] = picked[...].astype(BF16)


def tile_kernel(control, mate, out, held):
    even = lax.rem(lax.axis_index("tile"), 2) == 0
    size = control.shape[0]
    out[0:size] = control[...].astype(BF16)
    for r in range(size // 16):
        held[r * 2 : (r + 1) * 2] = jnp.where(
            even, mate[r * 16 : r * 16 + 2], mate[r * 16 + 14 : (r + 1) * 16]
        )
    out[size:] = held[...].astype(BF16)


def relay_kernel(control, mate, oth, out, near4, wide, edge):
    even = lax.rem(lax.axis_index("tile"), 2) == 0
    size = mate.shape[0]
    out[0:size] = control[...].astype(BF16)
    wide[...] = oth[0:size].astype(F32)
    for r in range(size // 16):
        a, b = r * 16, (r + 1) * 16
        edge[r * 2 : (r + 1) * 2] = jnp.where(even, wide[b - 2 : b], wide[a : a + 2])
        near4[r * 4 : (r + 1) * 4] = jnp.where(even, mate[a : a + 4], mate[b - 4 : b])
        start = size // 8 + r * 2
        edge[start : start + 2] = jnp.where(even, mate[a : a + 2], mate[b - 2 : b])
    out[size:] = edge[...].astype(BF16)


def forward_kernel(
    gain_hbm, ws_hbm, wn_hbm, wo_hbm, readout_hbm, error_hbm, background_hbm, control, mate, oth,
    edge0, u1x, d0x, d1x, f2x, field, final, wo, readout, gain, error, background,
    ua, ub, n, act, pre, edge, states, weights, sems,
):
    channels = wo.shape[0]
    halves = weights.at[pl.ds(0, channels)], weights.at[pl.ds(channels, channels)]
    pairs = (
        (gain_hbm, gain), (ws_hbm, halves[0]), (wn_hbm, halves[1]), (wo_hbm, wo), (readout_hbm, readout),
        (error_hbm, error), (background_hbm, background),
    )
    copies = [pltpu.make_async_copy(source, to, sems.at[i]) for i, (source, to) in enumerate(pairs)]
    for copy in copies:
        copy.start()
    members = final.shape[0] // 32
    even = lax.rem(lax.axis_index("tile"), 2) == 0
    tile_at = jnp.where(even, 24, 16)
    edge_at = jnp.where(even, 16, 32)
    far = oth[members * 32 :].astype(F32)
    for r in range(2 * members):
        ua[r * WIDE : r * WIDE + 16] = control[r * 16 : (r + 1) * 16]
        ua[pl.ds(pl.multiple_of(r * WIDE + tile_at, 8), 16)] = oth[r * 16 : (r + 1) * 16].astype(F32)
        near4 = mate[r * 4 : (r + 1) * 4]
        far2 = far[r * 2 : (r + 1) * 2]
        edge[...] = jnp.zeros_like(edge)
        edge[0:4] = near4
        edge[6:8] = far2
        edge[8:10] = far2
        edge[12:16] = near4
        ua[pl.ds(pl.multiple_of(r * WIDE + edge_at, 8), 8)] = jnp.where(even, edge[0:8], edge[8:16])
    for r in range(2 * members):
        edge0[r * 8 : (r + 1) * 8] = slim_edge(ua, r)
    copies[0].wait()
    g = gain[...]

    def keep(ref):
        def store(r, value):
            ref[r * WIDE : (r + 1) * WIDE] = value

        return store

    def keep_states(ref, k):
        own = k * members * 32
        away = (2 + k) * members * 32
        for r in range(2 * members):
            states[own + r * 16 : own + (r + 1) * 16] = ref[r * WIDE : r * WIDE + 16].astype(BF16)
            taken = ref[pl.ds(pl.multiple_of(r * WIDE + tile_at, 8), 16)]
            states[away + r * 16 : away + (r + 1) * 16] = taken.astype(BF16)

    forward_step(ua, n, act, pre, d0x, g, weights, wo, WIDE, members, keep(ub), copies[1:])
    for m in range(members):
        slim_copy(u1x, ub, m)
    keep_states(ub, 0)
    forward_step(ub, n, act, pre, d1x, g, weights, wo, WIDE, members, keep(ua))
    for m in range(members):
        slim_copy(f2x, ua, m)
    keep_states(ua, 1)
    final[...] = states[members * 32 : 2 * members * 32]
    read = dot(states[...], readout[...])
    for q in range(4):
        for m in range(members):
            start = (q * members + m) * 32
            field[q * 32 : (q + 1) * 32, m * LANES : (m + 1) * LANES] = read[start : start + 32]


def split(x):
    high = x.astype(BF16)
    return high, (x - high.astype(F32)).astype(BF16)


def spread_of(first, th, tl, scaled, taken, field, ph, plo, spread):
    lane = lax.broadcasted_iota(jnp.int32, (1, LANES), 1)
    members = field.shape[1] // LANES
    for p in range(th.shape[1] // LANES):
        at = slice(p * LANES, (p + 1) * LANES)
        slot = (lane + p * LANES) % CHUNK
        table_of = jnp.where(slot < SLOTS, slot // CAP, -1)
        for q in range(2):
            kept = jnp.where(table_of == first + q, scaled[:, at], 0.0)
            ph[q * 32 : (q + 1) * 32, at], plo[q * 32 : (q + 1) * 32, at] = split(kept)
    cross = dot_t(ph[...], th[...]) + dot_t(plo[...], th[...]) + dot_t(ph[...], tl[...])
    block = jnp.concatenate([cross] * 2, axis=1)
    on_block = sublane(block.shape) // 32 == lax.broadcasted_iota(jnp.int32, block.shape, 1) // 32
    target = dot(ph[...], taken[...]) + dot(plo[...], taken[...])
    ch, cl = split(jnp.where(on_block, block, 0.0))
    fh, fl = split(field[first * 32 : (first + 2) * 32])
    mixed = dot(ch, fh) + dot(cl, fh) + dot(ch, fl)
    for q in range(2):
        for m in range(members):
            start = (q * members + m) * 32
            value = mixed[q * 32 : (q + 1) * 32, m * LANES : (m + 1) * LANES] - target[q * 32 : (q + 1) * 32]
            spread[start : start + 32] = value.astype(BF16)


def observe_kernel(
    tiles, arrived, field,
    spread, message, th, tl, scaled,
    ph, plo, wide,
):
    steps = 2
    members = field.shape[1] // LANES
    even = lax.rem(lax.axis_index("tile"), 2) == 0
    cells = sublane((32, LANES)).astype(F32)
    lane = lax.broadcasted_iota(jnp.int32, (8, LANES), 1)
    wide[...] = arrived[...].astype(F32)
    packs = th.shape[1] // LANES
    sums = [[jnp.zeros((8, LANES), F32)] * 3 for _ in range(packs)]
    for d in range(tiles):
        p, start = divmod(d * CHUNK, LANES)
        group = wide[d * CHUNK + 16 : (d + 1) * CHUNK]
        for b in range(3):
            first = start + b * APART
            place = lane - first % LANES
            place = jnp.where(place < 0, place + LANES, place)
            ends = min(LANES - start, SLOTS)
            sums[p][b] = sums[p][b] + jnp.where(place < ends, group, 0.0)
            if ends < SLOTS:
                rest = jnp.logical_and(place >= ends, place < SLOTS)
                sums[p + 1][b] = sums[p + 1][b] + jnp.where(rest, group, 0.0)
    for p in range(packs):
        kinds = [pltpu.roll(sums[p][b], (LANES - b * APART) % LANES, 1) if b else sums[p][b] for b in range(3)]
        entry = [kinds[i % 3][4 + i // 3 : 5 + i // 3] for i in range(9)]
        weight = jnp.zeros((32, LANES), F32)
        for i in range(4):
            weight += jnp.where(cells == entry[i], entry[4 + i], 0.0)
        at = slice(p * LANES, (p + 1) * LANES)
        th[:, at], tl[:, at] = split(weight)
        scaled[:, at] = weight * entry[8]
    spread_of(0, th, tl, scaled, arrived, field, ph, plo, spread)
    size = members * 32
    for k in range(steps):
        for m in range(members):
            start = k * size + m * 32
            pair = spread[start : start + 32].astype(F32)
            near = [jnp.where(even, pair[i + 8 : i + 16], pair[i : i + 8]) for i in (0, 16)]
            start = k * size // 2 + m * 16
            message[start : start + 16] = jnp.concatenate(near, axis=0).astype(BF16)


def adjoint_step(u, cot, gb, flat, products, d, out, gain, weights, wo, members):
    both = 2 * SLIM
    channels = flat.shape[1]
    gb[...] = cot[...].astype(BF16)
    flat[...] = dot_t(gb[...], wo[...])
    gb[...] = (flat[...] * d[...]).astype(BF16)
    products[...] = dot_t(gb[...], weights[...])
    for m in range(members):
        base = m * both
        rows = []
        for lat in range(2):
            start = base + lat * SLIM
            rows.append(products[start : start + SLIM, :channels].astype(BF16).astype(F32))
        around = neighbours(rows)
        for lat in range(2):
            start = base + lat * SLIM
            x = u[start : start + SLIM]
            s = inverse_rms(x)
            scaled = gain * (products[start : start + SLIM, channels:] + around[lat])
            inner = jnp.mean(x * scaled, axis=-1, keepdims=True)
            out(2 * m + lat, cot[start : start + SLIM] + s * scaled - x * (s * s * s * inner))


def edges(nxt, size, edge, r):
    even = lax.rem(lax.axis_index("tile"), 2) == 0
    start = size + r * 2
    far = nxt[start : start + 2]
    start = size + size // 8 + r * 2
    near = nxt[start : start + 2]
    edge[...] = jnp.zeros_like(edge)
    edge[0:2] = near
    edge[6:8] = far
    edge[8:10] = far
    edge[14:16] = near
    return jnp.where(even, edge[0:8], edge[8:16])


def pull_kernel(
    wn_hbm, ws_hbm, spread_own, readout, th, tl, scaled, arrived, field,
    pulled, away, weights,
    ph, plo, spread, near, sems,
):
    channels = wn_hbm.shape[0]
    pairs = ((wn_hbm, weights.at[pl.ds(0, channels)]), (ws_hbm, weights.at[pl.ds(channels, channels)]))
    copies = [pltpu.make_async_copy(source, to, sems.at[i]) for i, (source, to) in enumerate(pairs)]
    for copy in copies:
        copy.start()
    even = lax.rem(lax.axis_index("tile"), 2) == 0
    pulled[...] = dot_t(spread_own[...], readout[...])
    spread_of(2, th, tl, scaled, arrived, field, ph, plo, spread)
    for start in range(0, spread.shape[0], 32):
        pair = spread[start : start + 32].astype(F32)
        rows = [jnp.where(even, pair[i + 8 : i + 16], pair[i : i + 8]) for i in (0, 16)]
        near[start // 2 : start // 2 + 16] = jnp.concatenate(rows, axis=0).astype(BF16)
    away[...] = dot_t(near[...], readout[...])
    for copy in copies:
        copy.wait()


def backward_kernel(
    pulled, away, weights, gain, control, edge0, message16, f2x, wo, readout, error, message,
    u1x, d0x, d1x,
    result,
    cot2, cot1, gb, flat, both, mate_pull, edge, u0x, final, nxt,
):
    size = result.shape[0]
    members = size // 32
    even = lax.rem(lax.axis_index("tile"), 2) == 0
    nxt[...] = message16[...].astype(F32)
    weight = jnp.where(lax.axis_index("slot") == lax.axis_size("slot") - 1, 0.0, 1.0) * error[...]
    row8 = sublane((8, 1))
    mate_side = jnp.where(even, 1, 0) == jnp.where(row8 < 4, 1, 0)
    mate_pull[...] = dot_t(message[...], readout[...])
    final[...] = f2x[...].astype(F32)

    def pulls(k, r):
        own = k * size + r * 16
        near = k * size // 2 + r * 8
        group = jnp.where(mate_side, mate_pull[near : near + 8], away[near : near + 8])
        return pulled[own : own + 16], group

    for r in range(2 * members):
        own, group = pulls(1, r)
        a, b = r * SLIM, r * SLIM + 16
        cot2[a:b] = own - weight * (nxt[r * 16 : (r + 1) * 16] - final[a:b])
        u0x[a:b] = control[r * 16 : (r + 1) * 16]
        a, b = b, b + 8
        cot2[a:b] = group - weight * (edges(nxt, size, edge, r) - final[a:b])
        u0x[a:b] = edge0[r * 8 : (r + 1) * 8]

    def keep(r, value):
        cot1[r * SLIM : (r + 1) * SLIM] = value + jnp.concatenate(pulls(0, r), axis=0)

    def finish(r, value):
        a, b = r * SLIM, r * SLIM + 16
        result[r * 16 : (r + 1) * 16] = value[0:16] + error[...] * u0x[a:b]

    adjoint_step(u1x, cot2, gb, flat, both, d1x, keep, gain[...], weights, wo, members)
    adjoint_step(u0x, cot1, gb, flat, both, d0x, finish, gain[...], weights, wo, members)


def last_kernel(base, background, before, error, result):
    first = lax.axis_index("slot") == 0
    taken = jnp.where(first, background[...].astype(F32), before[...].astype(F32))
    result[...] = base[...] - error[...] * taken


def kernel_call(body, outs, scratch, flops, moved, hbm=0, out_places=None, aliases={}):
    def call(*operands):
        fixed = [i in range(hbm) and i not in aliases for i in range(len(operands))]
        operands = [
            pltpu.with_memory_space_constraint(x, pltpu.HBM) if fix else x for x, fix in zip(operands, fixed)
        ]
        places = [pltpu.HBM] * hbm + [pltpu.VMEM] * (len(operands) - hbm)
        given = {} if out_places is None else {"out_specs": [pl.BlockSpec(memory_space=p) for p in out_places]}
        return pl.pallas_call(
            body,
            out_shape=outs,
            in_specs=[pl.BlockSpec(memory_space=place) for place in places],
            **given,
            scratch_shapes=scratch,
            input_output_aliases=aliases,
            compiler_params=pltpu.CompilerParams(vmem_limit_bytes=VMEM_LIMIT),
            cost_estimate=pl.CostEstimate(flops=flops, bytes_accessed=moved, transcendentals=0),
        )(*operands)

    return call


def per_device(
    control,
    background,
    self_weight,
    neighbour_weight,
    output_weight,
    norm_gain,
    readout,
    error_weight,
    report_owner,
    report_stencil,
    report_weights,
    report_values,
    report_precision,
):
    tiles = lax.axis_size("tile")
    slots = lax.axis_size("slot")
    members, lats, cols, channels = control.shape[1:]
    groups = members * lats
    size = groups * cols
    steps = report_owner.shape[1]
    rows = report_owner.shape[2]
    gain = norm_gain.reshape(1, channels)
    error = error_weight.reshape(1, channels)
    flat = control.reshape(size, channels)

    def spec(count, dtype=F32, width=channels):
        return jax.ShapeDtypeStruct((count, width), dtype)

    def scratch(count, dtype=F32, width=channels):
        return pltpu.VMEM((count, width), dtype)

    mate_of = [(i, i ^ 1) for i in range(tiles)]
    other_of = [(i, (i - 1) % tiles if i % 2 == 0 else (i + 1) % tiles) for i in range(tiles)]

    def across(block, shift):
        pairs = [
            ((s + shift) % slots * tiles + i, s * tiles + i) for s in range(slots) for i in range(tiles)
        ]
        return lax.ppermute(block, ("slot", "tile"), pairs)

    mate = lax.ppermute(flat, "tile", mate_of)
    listed = (
        jnp.transpose(report_owner[0], (0, 2, 1)),
        jnp.transpose(report_stencil[0], (0, 2, 1)),
        jnp.transpose(report_weights[0], (0, 2, 1)),
        report_precision[0],
        report_values[0].reshape(steps * rows, LANES),
    )
    work = [
        pltpu.VMEM((1, steps * rows), jnp.int32),
        scratch(24, F32, steps * rows),
        scratch(tiles * CHUNK, F32, LANES),
        scratch(tiles * CHUNK, BF16, LANES),
    ]
    held, packed, *listed = kernel_call(
        first_kernel,
        [spec(size), spec(tiles * CHUNK, BF16, LANES)]
        + [jax.ShapeDtypeStruct(block.shape, block.dtype) for block in listed],
        work + [pltpu.SemaphoreType.DMA((7,))],
        10**7,
        200000,
        hbm=6,
        out_places=[pltpu.VMEM, pltpu.HBM] + [pltpu.VMEM] * 5,
    )(flat, *listed)
    sent = kernel_call(
        tile_kernel, spec(groups * (cols + 2), BF16), [scratch(groups * 2)], 1000, 400000
    )(held, mate)
    oth = lax.ppermute(sent, "tile", other_of)
    (packed,) = kernel_call(
        later_kernel,
        [spec(tiles * CHUNK, BF16, LANES)],
        work + [pltpu.SemaphoreType.DMA],
        10**7,
        200000,
        hbm=1,
        out_places=[pltpu.HBM],
        aliases={0: 0},
    )(packed, *listed, sent)
    arrived = lax.all_to_all(packed, "tile", split_axis=0, concat_axis=0, tiled=True)

    message, near4 = kernel_call(
        relay_kernel,
        [spec(size + 4 * groups, BF16), spec(4 * groups)],
        [scratch(size), scratch(4 * groups)],
        1000,
        700000,
    )(held, mate, oth)
    nxt = across(message, 1)
    wide = groups * WIDE
    slim = groups * SLIM
    (
        edge0, u1x, d0x, d1x, f2x, field, final, wo, readout_held, gain_held, error_held, background_held,
    ) = kernel_call(
        forward_kernel,
        [spec(groups * 8), spec(slim)] + [spec(slim, BF16)] * 3
        + [spec(4 * lats * cols, F32, members * LANES), spec(size, BF16)]
        + [spec(channels, BF16), spec(channels, BF16, LANES), spec(1), spec(1), spec(size, BF16)],
        [scratch(wide), scratch(wide), scratch(wide, BF16, 2 * channels), scratch(wide, BF16)]
        + [scratch(wide), scratch(16), scratch(4 * size, BF16)]
        + [scratch(2 * channels, BF16), pltpu.SemaphoreType.DMA((7,))],
        10**11,
        4000000,
        hbm=7,
    )(
        gain, self_weight, neighbour_weight, output_weight, readout, error, background.reshape(size, channels),
        held, near4, oth,
    )
    before = across(final, -1)
    total = tiles * CHUNK
    tables = [scratch(64, BF16, total), scratch(64, BF16, total)]
    spread, near_spread, *reports_held = kernel_call(
        functools.partial(observe_kernel, tiles),
        [spec(2 * size, BF16, LANES), spec(size, BF16, LANES)]
        + [spec(32, BF16, total), spec(32, BF16, total), spec(32, F32, total)],
        tables + [scratch(total, F32, LANES)],
        10**9,
        2000000,
    )(arrived, field)
    from_mate = lax.ppermute(near_spread, "tile", mate_of)
    handed = kernel_call(
        pull_kernel,
        [spec(2 * size), spec(size), spec(2 * channels, BF16)],
        tables + [scratch(2 * size, BF16, LANES), scratch(size, BF16, LANES), pltpu.SemaphoreType.DMA((2,))],
        10**9,
        3000000,
        hbm=2,
    )(neighbour_weight, self_weight, spread, readout_held, *reports_held, arrived, field)
    base = kernel_call(
        backward_kernel,
        spec(size),
        [scratch(slim), scratch(slim), scratch(slim, BF16), scratch(slim), scratch(slim, F32, 2 * channels)]
        + [scratch(size), scratch(16), scratch(slim), scratch(slim), scratch(size + 4 * groups)],
        12 * slim * channels * channels,
        6000000,
    )(
        *handed, gain_held, held, edge0, nxt, f2x, wo, readout_held, error_held, from_mate,
        u1x, d0x, d1x,
    )
    result = kernel_call(last_kernel, spec(size), [], 10**6, 900000)(base, background_held, before, error_held)
    return result.reshape(control.shape)


def solution(mesh):
    in_specs = (
        P("slot", None, None, "tile", None),
        P(None, None, "tile", None),
        P(),
        P(),
        P(),
        P(),
        P(),
        P(),
        P("slot", None, "tile", None),
        P("slot", None, "tile", None),
        P("slot", None, "tile", None),
        P("slot", None, "tile", None),
        P("slot", None, "tile"),
    )
    out_specs = P("slot", None, None, "tile", None)
    return jax.shard_map(
        per_device, mesh=mesh, in_specs=in_specs, out_specs=out_specs, check_vma=False
    )
```

```python
import functools
import jax
import jax.numpy as jnp
from jax import lax
from jax.experimental import pallas as pl
from jax.experimental.pallas import tpu as pltpu
from jax.sharding import PartitionSpec as P

EPSILON = 1e-06
F32 = jnp.float32
BF16 = jnp.bfloat16
LANES = 128
CAP = 5
SLOTS = 4 * CAP
CHUNK = 24
APART = 36
STRIDE = 32
WIDE = 40
SLIM = 24
VMEM_LIMIT = 28 * 1024 * 1024


def dot(a, b):
    return jnp.dot(a, b, preferred_element_type=F32)


def dot_t(a, b):
    return lax.dot_general(a, b, (((1,), (1,)), ((), ())), preferred_element_type=F32)


def sublane(shape):
    return lax.broadcasted_iota(jnp.int32, shape, 0)


def inverse_rms(x):
    return lax.rsqrt(jnp.mean(x * x, axis=-1, keepdims=True) + EPSILON)


def sigmoid(p):
    return 0.5 * jnp.tanh(0.5 * p) + 0.5


def neighbours(rows):
    width = rows[0].shape[0]
    return [
        0.25 * (rows[1 - i] + pltpu.roll(rows[i], 1, 0) + pltpu.roll(rows[i], width - 1, 0))
        for i in range(2)
    ]


def forward_step(u, n, act, pre, d, gain, weights, wo, width, members, out, copies=()):
    both = 2 * width
    for m in range(members):
        base = m * both
        rows = []
        for lat in range(2):
            x = u[base + lat * width : base + (lat + 1) * width]
            rows.append((x * inverse_rms(x) * gain).astype(BF16).astype(F32))
        channels = rows[0].shape[1]
        n[base : base + both, :channels] = jnp.concatenate(rows, axis=0).astype(BF16)
        n[base : base + both, channels:] = jnp.concatenate(neighbours(rows), axis=0).astype(BF16)
    for copy in copies[:2]:
        copy.wait()
    pre[...] = dot(n[...], weights[...])
    for m in range(members):
        base = m * both
        p = pre[base : base + both]
        sig = sigmoid(p)
        act[base : base + both] = (p * sig).astype(BF16)
        if d is not None:
            pre[base : base + both] = sig * (1.0 + p * (1.0 - sig))
    if d is not None:
        for m in range(members):
            slim_copy(d, pre, m)
    for copy in copies[2:]:
        copy.wait()
    pre[...] = dot(act[...], wo[...])
    for r in range(2 * members):
        out(r, u[r * width : (r + 1) * width] + pre[r * width : (r + 1) * width])


def slim_edge(wide, r):
    low = wide[r * WIDE + 16 : r * WIDE + 24]
    high = wide[r * WIDE + 32 : r * WIDE + 40]
    return jnp.where(sublane(low.shape) < 4, low, high)


def slim_copy(to, wide, m):
    parts = []
    for r in (2 * m, 2 * m + 1):
        parts += [wide[r * WIDE : r * WIDE + 16], slim_edge(wide, r)]
    both = jnp.concatenate(parts, axis=0)
    to[m * 2 * SLIM : (m + 1) * 2 * SLIM] = both.astype(to.dtype)


def reports(arrays, out_hbm, key, meta, picked, out, sem):
    pack(*arrays, out, key, meta, picked)
    store = pltpu.make_async_copy(out, out_hbm, sem)
    store.start()
    store.wait()


def early():
    return lax.axis_index("tile") < lax.axis_size("tile") // 2


def first_kernel(control_hbm, *refs):
    sources, (held, out_hbm), arrays, (key, meta, picked, out, sems) = refs[:5], refs[5:7], refs[7:12], refs[12:]
    copies = [
        pltpu.make_async_copy(source, to, sems.at[i]) for i, (source, to) in enumerate(zip(sources, arrays))
    ]
    copies.append(pltpu.make_async_copy(control_hbm, held, sems.at[5]))
    for copy in copies:
        copy.start()
    for copy in copies[:5]:
        copy.wait()

    @pl.when(early())
    def _():
        reports(arrays, out_hbm, key, meta, picked, out, sems.at[6])

    copies[5].wait()


def later_kernel(packed_hbm, *refs):
    arrays, out_hbm, (key, meta, picked, out, sem) = refs[:5], refs[6], refs[7:]

    @pl.when(jnp.logical_not(early()))
    def _():
        reports(arrays, out_hbm, key, meta, picked, out, sem)


def fan(x, shift):
    if shift % LANES:
        x = pltpu.roll(x, shift % LANES, 1)
    for _ in range(2):
        x = pltpu.roll(x, 0, 1, stride=APART // 2, stride_axis=0)
    return x


def pack(owner, stencil, weights, precision, values, out, key, meta, picked):
    steps, _, rows = owner.shape
    tiles = out.shape[0] // CHUNK
    total = steps * rows
    earlier = lax.broadcasted_iota(jnp.int32, (rows, rows), 0) < lax.broadcasted_iota(jnp.int32, (rows, rows), 1)
    earlier = earlier.astype(F32).astype(BF16)
    meta[...] = jnp.zeros_like(meta)
    for k in range(steps):
        at = slice(k * rows, (k + 1) * rows)
        named = lax.broadcasted_iota(jnp.int32, (tiles, rows), 0) == owner[k]
        hits = named.astype(F32)
        before = dot(hits.astype(BF16), earlier)
        rank = jnp.sum(hits * before, axis=0, keepdims=True).astype(jnp.int32)
        key[0:1, at] = owner[k] * (2 * CAP) + k * CAP + rank
        for i in range(4):
            meta[i // 3 * 8 + i % 3 : i // 3 * 8 + i % 3 + 1, at] = stencil[k, i : i + 1].astype(F32)
            j = 4 + i
            meta[j // 3 * 8 + j % 3 : j // 3 * 8 + j % 3 + 1, at] = weights[k, i : i + 1].astype(F32)
        meta[18:19, at] = precision[k : k + 1].astype(F32)
    row = lax.broadcasted_iota(jnp.int32, (tiles * STRIDE, total), 0)
    tile = row // STRIDE
    slot = row % STRIDE
    other = jnp.where(tile % 2 == 0, (tile + tiles - 1) % tiles, (tile + 1) % tiles)
    mine = slot < 2 * CAP
    wanted = jnp.where(mine, tile * (2 * CAP) + slot, other * (2 * CAP) + slot - 2 * CAP)
    wanted = jnp.where(slot < SLOTS, wanted, -1)
    placement = (wanted == key[...]).astype(F32).astype(BF16)
    placed = dot(placement, values[...])
    entries = dot_t(meta[...].astype(BF16), placement)
    lane = lax.broadcasted_iota(jnp.int32, (24, LANES), 1)
    turn = lax.axis_index("tile") * CHUNK % LANES
    per_tile = LANES // STRIDE
    for t in range(tiles):
        picked[t * CHUNK : (t + 1) * CHUNK] = placed[t * STRIDE : t * STRIDE + CHUNK]
        start = t % per_tile * STRIDE
        used = jnp.logical_and(lane >= start, lane < start + SLOTS)
        block = jnp.where(used, entries[:, t // per_tile * LANES : (t // per_tile + 1) * LANES], 0.0)
        for j in range(3):
            laid = fan(block[j * 8 : (j + 1) * 8], LANES - start)
            row = t * CHUNK + SLOTS + j
            picked[row : row + 1] = jnp.sum(laid, axis=0, keepdims=True)
        group = picked[t * CHUNK + 16 : (t + 1) * CHUNK]
        picked[t * CHUNK + 16 : (t + 1) * CHUNK] = jnp.where(sublane((8, 1)) < 4, group, pltpu.roll(group, turn, 1))
    out[...] = picked[...].astype(BF16)


def tile_kernel(control, mate, out, held):
    even = lax.rem(lax.axis_index("tile"), 2) == 0
    size = control.shape[0]
    out[0:size] = control[...].astype(BF16)
    for r in range(size // 16):
        held[r * 2 : (r + 1) * 2] = jnp.where(
            even, mate[r * 16 : r * 16 + 2], mate[r * 16 + 14 : (r + 1) * 16]
        )
    out[size:] = held[...].astype(BF16)


def relay_kernel(control, mate, oth, out, near4, wide, edge):
    even = lax.rem(lax.axis_index("tile"), 2) == 0
    size = mate.shape[0]
    out[0:size] = control[...].astype(BF16)
    wide[...] = oth[0:size].astype(F32)
    for r in range(size // 16):
        a, b = r * 16, (r + 1) * 16
        edge[r * 2 : (r + 1) * 2] = jnp.where(even, wide[b - 2 : b], wide[a : a + 2])
        near4[r * 4 : (r + 1) * 4] = jnp.where(even, mate[a : a + 4], mate[b - 4 : b])
        start = size // 8 + r * 2
        edge[start : start + 2] = jnp.where(even, mate[a : a + 2], mate[b - 2 : b])
    out[size:] = edge[...].astype(BF16)


def forward_kernel(
    gain_hbm, ws_hbm, wn_hbm, wo_hbm, readout_hbm, error_hbm, background_hbm, control, mate, oth,
    edge0, u1x, d0x, d1x, f2x, field, final, wo, readout, gain, error, background,
    ua, ub, n, act, pre, edge, states, weights, sems,
):
    channels = wo.shape[0]
    halves = weights.at[pl.ds(0, channels)], weights.at[pl.ds(channels, channels)]
    pairs = (
        (gain_hbm, gain), (ws_hbm, halves[0]), (wn_hbm, halves[1]), (wo_hbm, wo), (readout_hbm, readout),
        (error_hbm, error), (background_hbm, background),
    )
    copies = [pltpu.make_async_copy(source, to, sems.at[i]) for i, (source, to) in enumerate(pairs)]
    for copy in copies:
        copy.start()
    members = final.shape[0] // 32
    even = lax.rem(lax.axis_index("tile"), 2) == 0
    tile_at = jnp.where(even, 24, 16)
    edge_at = jnp.where(even, 16, 32)
    far = oth[members * 32 :].astype(F32)
    for r in range(2 * members):
        ua[r * WIDE : r * WIDE + 16] = control[r * 16 : (r + 1) * 16]
        ua[pl.ds(pl.multiple_of(r * WIDE + tile_at, 8), 16)] = oth[r * 16 : (r + 1) * 16].astype(F32)
        near4 = mate[r * 4 : (r + 1) * 4]
        far2 = far[r * 2 : (r + 1) * 2]
        edge[...] = jnp.zeros_like(edge)
        edge[0:4] = near4
        edge[6:8] = far2
        edge[8:10] = far2
        edge[12:16] = near4
        ua[pl.ds(pl.multiple_of(r * WIDE + edge_at, 8), 8)] = jnp.where(even, edge[0:8], edge[8:16])
    for r in range(2 * members):
        edge0[r * 8 : (r + 1) * 8] = slim_edge(ua, r)
    copies[0].wait()
    g = gain[...]

    def keep(ref):
        def store(r, value):
            ref[r * WIDE : (r + 1) * WIDE] = value

        return store

    def keep_states(ref, k):
        own = k * members * 32
        away = (2 + k) * members * 32
        for r in range(2 * members):
            states[own + r * 16 : own + (r + 1) * 16] = ref[r * WIDE : r * WIDE + 16].astype(BF16)
            taken = ref[pl.ds(pl.multiple_of(r * WIDE + tile_at, 8), 16)]
            states[away + r * 16 : away + (r + 1) * 16] = taken.astype(BF16)

    forward_step(ua, n, act, pre, d0x, g, weights, wo, WIDE, members, keep(ub), copies[1:])
    for m in range(members):
        slim_copy(u1x, ub, m)
    keep_states(ub, 0)
    forward_step(ub, n, act, pre, d1x, g, weights, wo, WIDE, members, keep(ua))
    for m in range(members):
        slim_copy(f2x, ua, m)
    keep_states(ua, 1)
    final[...] = states[members * 32 : 2 * members * 32]
    read = dot(states[...], readout[...])
    for q in range(4):
        for m in range(members):
            start = (q * members + m) * 32
            field[q * 32 : (q + 1) * 32, m * LANES : (m + 1) * LANES] = read[start : start + 32]


def split(x):
    high = x.astype(BF16)
    return high, (x - high.astype(F32)).astype(BF16)


def spread_of(first, th, tl, scaled, taken, field, ph, plo, spread):
    lane = lax.broadcasted_iota(jnp.int32, (1, LANES), 1)
    members = field.shape[1] // LANES
    for p in range(th.shape[1] // LANES):
        at = slice(p * LANES, (p + 1) * LANES)
        slot = (lane + p * LANES) % CHUNK
        table_of = jnp.where(slot < SLOTS, slot // CAP, -1)
        for q in range(2):
            kept = jnp.where(table_of == first + q, scaled[:, at], 0.0)
            ph[q * 32 : (q + 1) * 32, at], plo[q * 32 : (q + 1) * 32, at] = split(kept)
    cross = dot_t(ph[...], th[...]) + dot_t(plo[...], th[...]) + dot_t(ph[...], tl[...])
    block = jnp.concatenate([cross] * 2, axis=1)
    on_block = sublane(block.shape) // 32 == lax.broadcasted_iota(jnp.int32, block.shape, 1) // 32
    target = dot(ph[...], taken[...]) + dot(plo[...], taken[...])
    ch, cl = split(jnp.where(on_block, block, 0.0))
    fh, fl = split(field[first * 32 : (first + 2) * 32])
    mixed = dot(ch, fh) + dot(cl, fh) + dot(ch, fl)
    for q in range(2):
        for m in range(members):
            start = (q * members + m) * 32
            value = mixed[q * 32 : (q + 1) * 32, m * LANES : (m + 1) * LANES] - target[q * 32 : (q + 1) * 32]
            spread[start : start + 32] = value.astype(BF16)


def observe_kernel(
    tiles, arrived, field,
    spread, message, th, tl, scaled,
    ph, plo, wide,
):
    steps = 2
    members = field.shape[1] // LANES
    even = lax.rem(lax.axis_index("tile"), 2) == 0
    cells = sublane((32, LANES)).astype(F32)
    lane = lax.broadcasted_iota(jnp.int32, (8, LANES), 1)
    wide[...] = arrived[...].astype(F32)
    packs = th.shape[1] // LANES
    sums = [[jnp.zeros((8, LANES), F32)] * 3 for _ in range(packs)]
    for d in range(tiles):
        p, start = divmod(d * CHUNK, LANES)
        group = wide[d * CHUNK + 16 : (d + 1) * CHUNK]
        for b in range(3):
            first = start + b * APART
            place = lane - first % LANES
            place = jnp.where(place < 0, place + LANES, place)
            ends = min(LANES - start, SLOTS)
            sums[p][b] = sums[p][b] + jnp.where(place < ends, group, 0.0)
            if ends < SLOTS:
                rest = jnp.logical_and(place >= ends, place < SLOTS)
                sums[p + 1][b] = sums[p + 1][b] + jnp.where(rest, group, 0.0)
    for p in range(packs):
        kinds = [pltpu.roll(sums[p][b], (LANES - b * APART) % LANES, 1) if b else sums[p][b] for b in range(3)]
        entry = [kinds[i % 3][4 + i // 3 : 5 + i // 3] for i in range(9)]
        weight = jnp.zeros((32, LANES), F32)
        for i in range(4):
            weight += jnp.where(cells == entry[i], entry[4 + i], 0.0)
        at = slice(p * LANES, (p + 1) * LANES)
        th[:, at], tl[:, at] = split(weight)
        scaled[:, at] = weight * entry[8]
    spread_of(0, th, tl, scaled, arrived, field, ph, plo, spread)
    size = members * 32
    for k in range(steps):
        for m in range(members):
            start = k * size + m * 32
            pair = spread[start : start + 32].astype(F32)
            near = [jnp.where(even, pair[i + 8 : i + 16], pair[i : i + 8]) for i in (0, 16)]
            start = k * size // 2 + m * 16
            message[start : start + 16] = jnp.concatenate(near, axis=0).astype(BF16)


def adjoint_step(u, cot, gb, gm, flat, d, out, gain, ws, wn, wo, members):
    both = 2 * SLIM
    gb[...] = cot[...].astype(BF16)
    flat[...] = dot_t(gb[...], wo[...])
    gb[...] = (flat[...] * d[...]).astype(BF16)
    gm[...] = dot_t(gb[...], wn[...])
    flat[...] = dot_t(gb[...], ws[...])
    for m in range(members):
        base = m * both
        rows = []
        for lat in range(2):
            start = base + lat * SLIM
            rows.append(gm[start : start + SLIM].astype(BF16).astype(F32))
        around = neighbours(rows)
        for lat in range(2):
            start = base + lat * SLIM
            x = u[start : start + SLIM]
            s = inverse_rms(x)
            scaled = gain * (flat[start : start + SLIM] + around[lat])
            inner = jnp.mean(x * scaled, axis=-1, keepdims=True)
            out(2 * m + lat, cot[start : start + SLIM] + s * scaled - x * (s * s * s * inner))


def edges(nxt, size, edge, r):
    even = lax.rem(lax.axis_index("tile"), 2) == 0
    start = size + r * 2
    far = nxt[start : start + 2]
    start = size + size // 8 + r * 2
    near = nxt[start : start + 2]
    edge[...] = jnp.zeros_like(edge)
    edge[0:2] = near
    edge[6:8] = far
    edge[8:10] = far
    edge[14:16] = near
    return jnp.where(even, edge[0:8], edge[8:16])


def pull_kernel(
    wn_hbm, ws_hbm, spread_own, readout, th, tl, scaled, arrived, field,
    pulled, away, wn, ws,
    ph, plo, spread, near, sems,
):
    pairs = ((wn_hbm, wn), (ws_hbm, ws))
    copies = [pltpu.make_async_copy(source, to, sems.at[i]) for i, (source, to) in enumerate(pairs)]
    for copy in copies:
        copy.start()
    even = lax.rem(lax.axis_index("tile"), 2) == 0
    pulled[...] = dot_t(spread_own[...], readout[...])
    spread_of(2, th, tl, scaled, arrived, field, ph, plo, spread)
    for start in range(0, spread.shape[0], 32):
        pair = spread[start : start + 32].astype(F32)
        rows = [jnp.where(even, pair[i + 8 : i + 16], pair[i : i + 8]) for i in (0, 16)]
        near[start // 2 : start // 2 + 16] = jnp.concatenate(rows, axis=0).astype(BF16)
    away[...] = dot_t(near[...], readout[...])
    for copy in copies:
        copy.wait()


def backward_kernel(
    pulled, away, wn, ws, gain, control, edge0, message16, f2x, wo, readout, error, message,
    u1x, d0x, d1x,
    result,
    cot2, cot1, gb, gm, flat, mate_pull, edge, u0x, final, nxt,
):
    size = result.shape[0]
    members = size // 32
    even = lax.rem(lax.axis_index("tile"), 2) == 0
    nxt[...] = message16[...].astype(F32)
    weight = jnp.where(lax.axis_index("slot") == lax.axis_size("slot") - 1, 0.0, 1.0) * error[...]
    row8 = sublane((8, 1))
    mate_side = jnp.where(even, 1, 0) == jnp.where(row8 < 4, 1, 0)
    mate_pull[...] = dot_t(message[...], readout[...])
    final[...] = f2x[...].astype(F32)

    def pulls(k, r):
        own = k * size + r * 16
        near = k * size // 2 + r * 8
        group = jnp.where(mate_side, mate_pull[near : near + 8], away[near : near + 8])
        return pulled[own : own + 16], group

    for r in range(2 * members):
        own, group = pulls(1, r)
        a, b = r * SLIM, r * SLIM + 16
        cot2[a:b] = own - weight * (nxt[r * 16 : (r + 1) * 16] - final[a:b])
        u0x[a:b] = control[r * 16 : (r + 1) * 16]
        a, b = b, b + 8
        cot2[a:b] = group - weight * (edges(nxt, size, edge, r) - final[a:b])
        u0x[a:b] = edge0[r * 8 : (r + 1) * 8]

    def keep(r, value):
        cot1[r * SLIM : (r + 1) * SLIM] = value + jnp.concatenate(pulls(0, r), axis=0)

    def finish(r, value):
        a, b = r * SLIM, r * SLIM + 16
        result[r * 16 : (r + 1) * 16] = value[0:16] + error[...] * u0x[a:b]

    adjoint_step(u1x, cot2, gb, gm, flat, d1x, keep, gain[...], ws, wn, wo, members)
    adjoint_step(u0x, cot1, gb, gm, flat, d0x, finish, gain[...], ws, wn, wo, members)


def last_kernel(base, background, before, error, result):
    first = lax.axis_index("slot") == 0
    taken = jnp.where(first, background[...].astype(F32), before[...].astype(F32))
    result[...] = base[...] - error[...] * taken


def kernel_call(body, outs, scratch, flops, moved, hbm=0, out_places=None, aliases={}):
    def call(*operands):
        fixed = [i in range(hbm) and i not in aliases for i in range(len(operands))]
        operands = [
            pltpu.with_memory_space_constraint(x, pltpu.HBM) if fix else x for x, fix in zip(operands, fixed)
        ]
        places = [pltpu.HBM] * hbm + [pltpu.VMEM] * (len(operands) - hbm)
        given = {} if out_places is None else {"out_specs": [pl.BlockSpec(memory_space=p) for p in out_places]}
        return pl.pallas_call(
            body,
            out_shape=outs,
            in_specs=[pl.BlockSpec(memory_space=place) for place in places],
            **given,
            scratch_shapes=scratch,
            input_output_aliases=aliases,
            compiler_params=pltpu.CompilerParams(vmem_limit_bytes=VMEM_LIMIT),
            cost_estimate=pl.CostEstimate(flops=flops, bytes_accessed=moved, transcendentals=0),
        )(*operands)

    return call


def per_device(
    control,
    background,
    self_weight,
    neighbour_weight,
    output_weight,
    norm_gain,
    readout,
    error_weight,
    report_owner,
    report_stencil,
    report_weights,
    report_values,
    report_precision,
):
    tiles = lax.axis_size("tile")
    slots = lax.axis_size("slot")
    members, lats, cols, channels = control.shape[1:]
    groups = members * lats
    size = groups * cols
    steps = report_owner.shape[1]
    rows = report_owner.shape[2]
    gain = norm_gain.reshape(1, channels)
    error = error_weight.reshape(1, channels)
    flat = control.reshape(size, channels)

    def spec(count, dtype=F32, width=channels):
        return jax.ShapeDtypeStruct((count, width), dtype)

    def scratch(count, dtype=F32, width=channels):
        return pltpu.VMEM((count, width), dtype)

    mate_of = [(i, i ^ 1) for i in range(tiles)]
    other_of = [(i, (i - 1) % tiles if i % 2 == 0 else (i + 1) % tiles) for i in range(tiles)]

    def across(block, shift):
        pairs = [
            ((s + shift) % slots * tiles + i, s * tiles + i) for s in range(slots) for i in range(tiles)
        ]
        return lax.ppermute(block, ("slot", "tile"), pairs)

    mate = lax.ppermute(flat, "tile", mate_of)
    listed = (
        jnp.transpose(report_owner[0], (0, 2, 1)),
        jnp.transpose(report_stencil[0], (0, 2, 1)),
        jnp.transpose(report_weights[0], (0, 2, 1)),
        report_precision[0],
        report_values[0].reshape(steps * rows, LANES),
    )
    work = [
        pltpu.VMEM((1, steps * rows), jnp.int32),
        scratch(24, F32, steps * rows),
        scratch(tiles * CHUNK, F32, LANES),
        scratch(tiles * CHUNK, BF16, LANES),
    ]
    held, packed, *listed = kernel_call(
        first_kernel,
        [spec(size), spec(tiles * CHUNK, BF16, LANES)]
        + [jax.ShapeDtypeStruct(block.shape, block.dtype) for block in listed],
        work + [pltpu.SemaphoreType.DMA((7,))],
        10**7,
        200000,
        hbm=6,
        out_places=[pltpu.VMEM, pltpu.HBM] + [pltpu.VMEM] * 5,
    )(flat, *listed)
    sent = kernel_call(
        tile_kernel, spec(groups * (cols + 2), BF16), [scratch(groups * 2)], 1000, 400000
    )(held, mate)
    oth = lax.ppermute(sent, "tile", other_of)
    (packed,) = kernel_call(
        later_kernel,
        [spec(tiles * CHUNK, BF16, LANES)],
        work + [pltpu.SemaphoreType.DMA],
        10**7,
        200000,
        hbm=1,
        out_places=[pltpu.HBM],
        aliases={0: 0},
    )(packed, *listed, sent)
    arrived = lax.all_to_all(packed, "tile", split_axis=0, concat_axis=0, tiled=True)

    message, near4 = kernel_call(
        relay_kernel,
        [spec(size + 4 * groups, BF16), spec(4 * groups)],
        [scratch(size), scratch(4 * groups)],
        1000,
        700000,
    )(held, mate, oth)
    nxt = across(message, 1)
    wide = groups * WIDE
    slim = groups * SLIM
    (
        edge0, u1x, d0x, d1x, f2x, field, final, wo, readout_held, gain_held, error_held, background_held,
    ) = kernel_call(
        forward_kernel,
        [spec(groups * 8), spec(slim)] + [spec(slim, BF16)] * 3
        + [spec(4 * lats * cols, F32, members * LANES), spec(size, BF16)]
        + [spec(channels, BF16), spec(channels, BF16, LANES), spec(1), spec(1), spec(size, BF16)],
        [scratch(wide), scratch(wide), scratch(wide, BF16, 2 * channels), scratch(wide, BF16)]
        + [scratch(wide), scratch(16), scratch(4 * size, BF16)]
        + [scratch(2 * channels, BF16), pltpu.SemaphoreType.DMA((7,))],
        10**11,
        4000000,
        hbm=7,
    )(
        gain, self_weight, neighbour_weight, output_weight, readout, error, background.reshape(size, channels),
        held, near4, oth,
    )
    before = across(final, -1)
    total = tiles * CHUNK
    tables = [scratch(64, BF16, total), scratch(64, BF16, total)]
    spread, near_spread, *reports_held = kernel_call(
        functools.partial(observe_kernel, tiles),
        [spec(2 * size, BF16, LANES), spec(size, BF16, LANES)]
        + [spec(32, BF16, total), spec(32, BF16, total), spec(32, F32, total)],
        tables + [scratch(total, F32, LANES)],
        10**9,
        2000000,
    )(arrived, field)
    from_mate = lax.ppermute(near_spread, "tile", mate_of)
    handed = kernel_call(
        pull_kernel,
        [spec(2 * size), spec(size), spec(channels, BF16), spec(channels, BF16)],
        tables + [scratch(2 * size, BF16, LANES), scratch(size, BF16, LANES), pltpu.SemaphoreType.DMA((2,))],
        10**9,
        3000000,
        hbm=2,
    )(neighbour_weight, self_weight, spread, readout_held, *reports_held, arrived, field)
    base = kernel_call(
        backward_kernel,
        spec(size),
        [scratch(slim), scratch(slim), scratch(slim, BF16), scratch(slim), scratch(slim)]
        + [scratch(size), scratch(16), scratch(slim), scratch(slim), scratch(size + 4 * groups)],
        12 * slim * channels * channels,
        6000000,
    )(
        *handed, gain_held, held, edge0, nxt, f2x, wo, readout_held, error_held, from_mate,
        u1x, d0x, d1x,
    )
    result = kernel_call(last_kernel, spec(size), [], 10**6, 900000)(base, background_held, before, error_held)
    return result.reshape(control.shape)


def solution(mesh):
    in_specs = (
        P("slot", None, None, "tile", None),
        P(None, None, "tile", None),
        P(),
        P(),
        P(),
        P(),
        P(),
        P(),
        P("slot", None, "tile", None),
        P("slot", None, "tile", None),
        P("slot", None, "tile", None),
        P("slot", None, "tile", None),
        P("slot", None, "tile"),
    )
    out_specs = P("slot", None, None, "tile", None)
    return jax.shard_map(
        per_device, mesh=mesh, in_specs=in_specs, out_specs=out_specs, check_vma=False
    )
```

```python
import functools
import jax
import jax.numpy as jnp
from jax import lax
from jax.experimental import pallas as pl
from jax.experimental.pallas import tpu as pltpu
from jax.sharding import PartitionSpec as P

EPSILON = 1e-06
F32 = jnp.float32
BF16 = jnp.bfloat16
LANES = 128
CAP = 5
SLOTS = 4 * CAP
CHUNK = 24
APART = 36
STRIDE = 32
WIDE = 40
SLIM = 24
VMEM_LIMIT = 28 * 1024 * 1024


def dot(a, b):
    return jnp.dot(a, b, preferred_element_type=F32)


def dot_t(a, b):
    return lax.dot_general(a, b, (((1,), (1,)), ((), ())), preferred_element_type=F32)


def sublane(shape):
    return lax.broadcasted_iota(jnp.int32, shape, 0)


def inverse_rms(x):
    return lax.rsqrt(jnp.mean(x * x, axis=-1, keepdims=True) + EPSILON)


def sigmoid(p):
    return 0.5 * jnp.tanh(0.5 * p) + 0.5


def neighbours(rows):
    width = rows[0].shape[0]
    return [
        0.25 * (rows[1 - i] + pltpu.roll(rows[i], 1, 0) + pltpu.roll(rows[i], width - 1, 0))
        for i in range(2)
    ]


def forward_step(u, n, act, pre, d, gain, weights, wo, width, members, out, copies=()):
    both = 2 * width
    for m in range(members):
        base = m * both
        rows = []
        for lat in range(2):
            x = u[base + lat * width : base + (lat + 1) * width]
            rows.append((x * inverse_rms(x) * gain).astype(BF16).astype(F32))
        channels = rows[0].shape[1]
        n[base : base + both, :channels] = jnp.concatenate(rows, axis=0).astype(BF16)
        n[base : base + both, channels:] = jnp.concatenate(neighbours(rows), axis=0).astype(BF16)
    for copy in copies[:2]:
        copy.wait()
    pre[...] = dot(n[...], weights[...])
    for m in range(members):
        base = m * both
        p = pre[base : base + both]
        sig = sigmoid(p)
        act[base : base + both] = (p * sig).astype(BF16)
        if d is not None:
            pre[base : base + both] = sig * (1.0 + p * (1.0 - sig))
    if d is not None:
        for m in range(members):
            slim_copy(d, pre, m)
    for copy in copies[2:]:
        copy.wait()
    pre[...] = dot(act[...], wo[...])
    for r in range(2 * members):
        out(r, u[r * width : (r + 1) * width] + pre[r * width : (r + 1) * width])


def slim_edge(wide, r):
    low = wide[r * WIDE + 16 : r * WIDE + 24]
    high = wide[r * WIDE + 32 : r * WIDE + 40]
    return jnp.where(sublane(low.shape) < 4, low, high)


def slim_copy(to, wide, m):
    parts = []
    for r in (2 * m, 2 * m + 1):
        parts += [wide[r * WIDE : r * WIDE + 16], slim_edge(wide, r)]
    both = jnp.concatenate(parts, axis=0)
    to[m * 2 * SLIM : (m + 1) * 2 * SLIM] = both.astype(to.dtype)


def reports(arrays, out_hbm, key, meta, picked, out, sem):
    pack(*arrays, out, key, meta, picked)
    store = pltpu.make_async_copy(out, out_hbm, sem)
    store.start()
    store.wait()


def early():
    return lax.axis_index("tile") < lax.axis_size("tile") // 2


def first_kernel(control_hbm, *refs):
    sources, (held, out_hbm), arrays, (key, meta, picked, out, sems) = refs[:5], refs[5:7], refs[7:12], refs[12:]
    copies = [
        pltpu.make_async_copy(source, to, sems.at[i]) for i, (source, to) in enumerate(zip(sources, arrays))
    ]
    copies.append(pltpu.make_async_copy(control_hbm, held, sems.at[5]))
    for copy in copies:
        copy.start()
    for copy in copies[:5]:
        copy.wait()

    @pl.when(early())
    def _():
        reports(arrays, out_hbm, key, meta, picked, out, sems.at[6])

    copies[5].wait()


def later_kernel(packed_hbm, *refs):
    arrays, out_hbm, (key, meta, picked, out, sem) = refs[:5], refs[6], refs[7:]

    @pl.when(jnp.logical_not(early()))
    def _():
        reports(arrays, out_hbm, key, meta, picked, out, sem)


def fan(x, shift):
    if shift % LANES:
        x = pltpu.roll(x, shift % LANES, 1)
    for _ in range(2):
        x = pltpu.roll(x, 0, 1, stride=APART // 2, stride_axis=0)
    return x


def pack(owner, stencil, weights, precision, values, out, key, meta, picked):
    steps, _, rows = owner.shape
    tiles = out.shape[0] // CHUNK
    total = steps * rows
    earlier = lax.broadcasted_iota(jnp.int32, (rows, rows), 0) < lax.broadcasted_iota(jnp.int32, (rows, rows), 1)
    earlier = earlier.astype(F32).astype(BF16)
    meta[...] = jnp.zeros_like(meta)
    for k in range(steps):
        at = slice(k * rows, (k + 1) * rows)
        named = lax.broadcasted_iota(jnp.int32, (tiles, rows), 0) == owner[k]
        hits = named.astype(F32)
        before = dot(hits.astype(BF16), earlier)
        rank = jnp.sum(hits * before, axis=0, keepdims=True).astype(jnp.int32)
        key[0:1, at] = owner[k] * (2 * CAP) + k * CAP + rank
        for i in range(4):
            meta[i // 3 * 8 + i % 3 : i // 3 * 8 + i % 3 + 1, at] = stencil[k, i : i + 1].astype(F32)
            j = 4 + i
            meta[j // 3 * 8 + j % 3 : j // 3 * 8 + j % 3 + 1, at] = weights[k, i : i + 1].astype(F32)
        meta[18:19, at] = precision[k : k + 1].astype(F32)
    row = lax.broadcasted_iota(jnp.int32, (tiles * STRIDE, total), 0)
    tile = row // STRIDE
    slot = row % STRIDE
    other = jnp.where(tile % 2 == 0, (tile + tiles - 1) % tiles, (tile + 1) % tiles)
    mine = slot < 2 * CAP
    wanted = jnp.where(mine, tile * (2 * CAP) + slot, other * (2 * CAP) + slot - 2 * CAP)
    wanted = jnp.where(slot < SLOTS, wanted, -1)
    placement = (wanted == key[...]).astype(F32).astype(BF16)
    placed = dot(placement, values[...])
    entries = dot_t(meta[...].astype(BF16), placement)
    lane = lax.broadcasted_iota(jnp.int32, (24, LANES), 1)
    turn = lax.axis_index("tile") * CHUNK % LANES
    per_tile = LANES // STRIDE
    for t in range(tiles):
        picked[t * CHUNK : (t + 1) * CHUNK] = placed[t * STRIDE : t * STRIDE + CHUNK]
        start = t % per_tile * STRIDE
        used = jnp.logical_and(lane >= start, lane < start + SLOTS)
        block = jnp.where(used, entries[:, t // per_tile * LANES : (t // per_tile + 1) * LANES], 0.0)
        for j in range(3):
            laid = fan(block[j * 8 : (j + 1) * 8], LANES - start)
            row = t * CHUNK + SLOTS + j
            picked[row : row + 1] = jnp.sum(laid, axis=0, keepdims=True)
        group = picked[t * CHUNK + 16 : (t + 1) * CHUNK]
        picked[t * CHUNK + 16 : (t + 1) * CHUNK] = jnp.where(sublane((8, 1)) < 4, group, pltpu.roll(group, turn, 1))
    out[...] = picked[...].astype(BF16)


def tile_kernel(control, mate, out, held):
    even = lax.rem(lax.axis_index("tile"), 2) == 0
    size = control.shape[0]
    out[0:size] = control[...].astype(BF16)
    for r in range(size // 16):
        held[r * 2 : (r + 1) * 2] = jnp.where(
            even, mate[r * 16 : r * 16 + 2], mate[r * 16 + 14 : (r + 1) * 16]
        )
    out[size:] = held[...].astype(BF16)


def relay_kernel(control, mate, oth, out, near4, wide, edge):
    even = lax.rem(lax.axis_index("tile"), 2) == 0
    size = mate.shape[0]
    out[0:size] = control[...].astype(BF16)
    wide[...] = oth[0:size].astype(F32)
    for r in range(size // 16):
        a, b = r * 16, (r + 1) * 16
        edge[r * 2 : (r + 1) * 2] = jnp.where(even, wide[b - 2 : b], wide[a : a + 2])
        near4[r * 4 : (r + 1) * 4] = jnp.where(even, mate[a : a + 4], mate[b - 4 : b])
        start = size // 8 + r * 2
        edge[start : start + 2] = jnp.where(even, mate[a : a + 2], mate[b - 2 : b])
    out[size:] = edge[...].astype(BF16)


def forward_kernel(
    gain_hbm, ws_hbm, wn_hbm, wo_hbm, readout_hbm, error_hbm, background_hbm, control, mate, oth,
    edge0, u1x, d0x, d1x, f2x, field, final, wo_turned, readout, gain, error, background, ws_hbm_turned, wn_hbm_turned,
    ua, ub, n, act, pre, edge, states, weights, wo, turned, sems,
):
    channels = wo.shape[0]
    halves = weights.at[pl.ds(0, channels)], weights.at[pl.ds(channels, channels)]
    pairs = (
        (gain_hbm, gain), (ws_hbm, halves[0]), (wn_hbm, halves[1]), (wo_hbm, wo), (readout_hbm, readout),
        (error_hbm, error), (background_hbm, background),
    )
    copies = [pltpu.make_async_copy(source, to, sems.at[i]) for i, (source, to) in enumerate(pairs)]
    for copy in copies:
        copy.start()
    members = final.shape[0] // 32
    even = lax.rem(lax.axis_index("tile"), 2) == 0
    tile_at = jnp.where(even, 24, 16)
    edge_at = jnp.where(even, 16, 32)
    far = oth[members * 32 :].astype(F32)
    for r in range(2 * members):
        ua[r * WIDE : r * WIDE + 16] = control[r * 16 : (r + 1) * 16]
        ua[pl.ds(pl.multiple_of(r * WIDE + tile_at, 8), 16)] = oth[r * 16 : (r + 1) * 16].astype(F32)
        near4 = mate[r * 4 : (r + 1) * 4]
        far2 = far[r * 2 : (r + 1) * 2]
        edge[...] = jnp.zeros_like(edge)
        edge[0:4] = near4
        edge[6:8] = far2
        edge[8:10] = far2
        edge[12:16] = near4
        ua[pl.ds(pl.multiple_of(r * WIDE + edge_at, 8), 8)] = jnp.where(even, edge[0:8], edge[8:16])
    for r in range(2 * members):
        edge0[r * 8 : (r + 1) * 8] = slim_edge(ua, r)
    copies[0].wait()
    g = gain[...]

    def keep(ref):
        def store(r, value):
            ref[r * WIDE : (r + 1) * WIDE] = value

        return store

    def keep_states(ref, k):
        own = k * members * 32
        away = (2 + k) * members * 32
        for r in range(2 * members):
            states[own + r * 16 : own + (r + 1) * 16] = ref[r * WIDE : r * WIDE + 16].astype(BF16)
            taken = ref[pl.ds(pl.multiple_of(r * WIDE + tile_at, 8), 16)]
            states[away + r * 16 : away + (r + 1) * 16] = taken.astype(BF16)

    forward_step(ua, n, act, pre, d0x, g, weights, wo, WIDE, members, keep(ub), copies[1:])
    stores = []
    for i, place in enumerate((ws_hbm_turned, wn_hbm_turned)):
        turned[i] = jnp.transpose(halves[i][...])
        stores.append(pltpu.make_async_copy(turned.at[i], place, sems.at[7 + i]))
        stores[-1].start()
    wo_turned[...] = jnp.transpose(wo[...])
    for m in range(members):
        slim_copy(u1x, ub, m)
    keep_states(ub, 0)
    forward_step(ub, n, act, pre, d1x, g, weights, wo, WIDE, members, keep(ua))
    for m in range(members):
        slim_copy(f2x, ua, m)
    keep_states(ua, 1)
    final[...] = states[members * 32 : 2 * members * 32]
    read = dot(states[...], readout[...])
    for q in range(4):
        for m in range(members):
            start = (q * members + m) * 32
            field[q * 32 : (q + 1) * 32, m * LANES : (m + 1) * LANES] = read[start : start + 32]
    for store in stores:
        store.wait()


def split(x):
    high = x.astype(BF16)
    return high, (x - high.astype(F32)).astype(BF16)


def spread_of(first, th, tl, scaled, taken, field, pp, spread):
    lane = lax.broadcasted_iota(jnp.int32, (1, LANES), 1)
    members = field.shape[1] // LANES
    for p in range(th.shape[1] // LANES):
        at = slice(p * LANES, (p + 1) * LANES)
        slot = (lane + p * LANES) % CHUNK
        table_of = jnp.where(slot < SLOTS, slot // CAP, -1)
        for q in range(2):
            kept = jnp.where(table_of == first + q, scaled[:, at], 0.0)
            pp[q * 32 : (q + 1) * 32, at], pp[64 + q * 32 : 96 + q * 32, at] = split(kept)
    cross = dot_t(pp[...], th[...])
    cross = cross[:64] + cross[64:] + dot_t(pp[0:64], tl[...])
    block = jnp.concatenate([cross] * 2, axis=1)
    on_block = sublane(block.shape) // 32 == lax.broadcasted_iota(jnp.int32, block.shape, 1) // 32
    target = dot(pp[...], taken[...])
    target = target[:64] + target[64:]
    ch, cl = split(jnp.where(on_block, block, 0.0))
    fh, fl = split(field[first * 32 : (first + 2) * 32])
    mixed = dot(jnp.concatenate([ch, cl], axis=0), fh)
    mixed = mixed[:64] + mixed[64:] + dot(ch, fl)
    for q in range(2):
        for m in range(members):
            start = (q * members + m) * 32
            value = mixed[q * 32 : (q + 1) * 32, m * LANES : (m + 1) * LANES] - target[q * 32 : (q + 1) * 32]
            spread[start : start + 32] = value.astype(BF16)


def observe_kernel(
    tiles, arrived, field,
    spread, message, th, tl, scaled,
    pp, wide,
):
    steps = 2
    members = field.shape[1] // LANES
    even = lax.rem(lax.axis_index("tile"), 2) == 0
    cells = sublane((32, LANES)).astype(F32)
    lane = lax.broadcasted_iota(jnp.int32, (8, LANES), 1)
    wide[...] = arrived[...].astype(F32)
    packs = th.shape[1] // LANES
    sums = [[jnp.zeros((8, LANES), F32)] * 3 for _ in range(packs)]
    for d in range(tiles):
        p, start = divmod(d * CHUNK, LANES)
        group = wide[d * CHUNK + 16 : (d + 1) * CHUNK]
        for b in range(3):
            first = start + b * APART
            place = lane - first % LANES
            place = jnp.where(place < 0, place + LANES, place)
            ends = min(LANES - start, SLOTS)
            sums[p][b] = sums[p][b] + jnp.where(place < ends, group, 0.0)
            if ends < SLOTS:
                rest = jnp.logical_and(place >= ends, place < SLOTS)
                sums[p + 1][b] = sums[p + 1][b] + jnp.where(rest, group, 0.0)
    for p in range(packs):
        kinds = [pltpu.roll(sums[p][b], (LANES - b * APART) % LANES, 1) if b else sums[p][b] for b in range(3)]
        entry = [kinds[i % 3][4 + i // 3 : 5 + i // 3] for i in range(9)]
        weight = jnp.zeros((32, LANES), F32)
        for i in range(4):
            weight += jnp.where(cells == entry[i], entry[4 + i], 0.0)
        at = slice(p * LANES, (p + 1) * LANES)
        th[:, at], tl[:, at] = split(weight)
        scaled[:, at] = weight * entry[8]
    spread_of(0, th, tl, scaled, arrived, field, pp, spread)
    size = members * 32
    for k in range(steps):
        for m in range(members):
            start = k * size + m * 32
            pair = spread[start : start + 32].astype(F32)
            near = [jnp.where(even, pair[i + 8 : i + 16], pair[i : i + 8]) for i in (0, 16)]
            start = k * size // 2 + m * 16
            message[start : start + 16] = jnp.concatenate(near, axis=0).astype(BF16)


def adjoint_step(u, cot, gb, gm, flat, d, out, gain, ws, wn, wo, members):
    both = 2 * SLIM
    gb[...] = cot[...].astype(BF16)
    flat[...] = dot(gb[...], wo[...])
    gb[...] = (flat[...] * d[...]).astype(BF16)
    gm[...] = dot(gb[...], wn[...])
    flat[...] = dot(gb[...], ws[...])
    for m in range(members):
        base = m * both
        rows = []
        for lat in range(2):
            start = base + lat * SLIM
            rows.append(gm[start : start + SLIM].astype(BF16).astype(F32))
        around = neighbours(rows)
        for lat in range(2):
            start = base + lat * SLIM
            x = u[start : start + SLIM]
            s = inverse_rms(x)
            scaled = gain * (flat[start : start + SLIM] + around[lat])
            inner = jnp.mean(x * scaled, axis=-1, keepdims=True)
            out(2 * m + lat, cot[start : start + SLIM] + s * scaled - x * (s * s * s * inner))


def edges(nxt, size, edge, r):
    even = lax.rem(lax.axis_index("tile"), 2) == 0
    start = size + r * 2
    far = nxt[start : start + 2]
    start = size + size // 8 + r * 2
    near = nxt[start : start + 2]
    edge[...] = jnp.zeros_like(edge)
    edge[0:2] = near
    edge[6:8] = far
    edge[8:10] = far
    edge[14:16] = near
    return jnp.where(even, edge[0:8], edge[8:16])


def pull_kernel(
    wn_hbm, ws_hbm, spread_own, readout, th, tl, scaled, arrived, field,
    pulled, away, wn, ws,
    pp, spread, near, sems,
):
    pairs = ((wn_hbm, wn), (ws_hbm, ws))
    copies = [pltpu.make_async_copy(source, to, sems.at[i]) for i, (source, to) in enumerate(pairs)]
    for copy in copies:
        copy.start()
    even = lax.rem(lax.axis_index("tile"), 2) == 0
    pulled[...] = dot_t(spread_own[...], readout[...])
    spread_of(2, th, tl, scaled, arrived, field, pp, spread)
    for start in range(0, spread.shape[0], 32):
        pair = spread[start : start + 32].astype(F32)
        rows = [jnp.where(even, pair[i + 8 : i + 16], pair[i : i + 8]) for i in (0, 16)]
        near[start // 2 : start // 2 + 16] = jnp.concatenate(rows, axis=0).astype(BF16)
    away[...] = dot_t(near[...], readout[...])
    for copy in copies:
        copy.wait()


def backward_kernel(
    pulled, away, wn, ws, gain, control, edge0, message16, f2x, wo, readout, error, message,
    u1x, d0x, d1x,
    result,
    cot2, cot1, gb, gm, flat, mate_pull, edge, u0x, final, nxt,
):
    size = result.shape[0]
    members = size // 32
    even = lax.rem(lax.axis_index("tile"), 2) == 0
    nxt[...] = message16[...].astype(F32)
    weight = jnp.where(lax.axis_index("slot") == lax.axis_size("slot") - 1, 0.0, 1.0) * error[...]
    row8 = sublane((8, 1))
    mate_side = jnp.where(even, 1, 0) == jnp.where(row8 < 4, 1, 0)
    mate_pull[...] = dot_t(message[...], readout[...])
    final[...] = f2x[...].astype(F32)

    def pulls(k, r):
        own = k * size + r * 16
        near = k * size // 2 + r * 8
        group = jnp.where(mate_side, mate_pull[near : near + 8], away[near : near + 8])
        return pulled[own : own + 16], group

    for r in range(2 * members):
        own, group = pulls(1, r)
        a, b = r * SLIM, r * SLIM + 16
        cot2[a:b] = own - weight * (nxt[r * 16 : (r + 1) * 16] - final[a:b])
        u0x[a:b] = control[r * 16 : (r + 1) * 16]
        a, b = b, b + 8
        cot2[a:b] = group - weight * (edges(nxt, size, edge, r) - final[a:b])
        u0x[a:b] = edge0[r * 8 : (r + 1) * 8]

    def keep(r, value):
        cot1[r * SLIM : (r + 1) * SLIM] = value + jnp.concatenate(pulls(0, r), axis=0)

    def finish(r, value):
        a, b = r * SLIM, r * SLIM + 16
        result[r * 16 : (r + 1) * 16] = value[0:16] + error[...] * u0x[a:b]

    adjoint_step(u1x, cot2, gb, gm, flat, d1x, keep, gain[...], ws, wn, wo, members)
    adjoint_step(u0x, cot1, gb, gm, flat, d0x, finish, gain[...], ws, wn, wo, members)


def last_kernel(base, background, before, error, result):
    first = lax.axis_index("slot") == 0
    taken = jnp.where(first, background[...].astype(F32), before[...].astype(F32))
    result[...] = base[...] - error[...] * taken


def kernel_call(body, outs, scratch, flops, moved, hbm=0, out_places=None, aliases={}):
    def call(*operands):
        fixed = [i in range(hbm) and i not in aliases for i in range(len(operands))]
        operands = [
            pltpu.with_memory_space_constraint(x, pltpu.HBM) if fix else x for x, fix in zip(operands, fixed)
        ]
        places = [pltpu.HBM] * hbm + [pltpu.VMEM] * (len(operands) - hbm)
        given = {} if out_places is None else {"out_specs": [pl.BlockSpec(memory_space=p) for p in out_places]}
        return pl.pallas_call(
            body,
            out_shape=outs,
            in_specs=[pl.BlockSpec(memory_space=place) for place in places],
            **given,
            scratch_shapes=scratch,
            input_output_aliases=aliases,
            compiler_params=pltpu.CompilerParams(vmem_limit_bytes=VMEM_LIMIT),
            cost_estimate=pl.CostEstimate(flops=flops, bytes_accessed=moved, transcendentals=0),
        )(*operands)

    return call


def per_device(
    control,
    background,
    self_weight,
    neighbour_weight,
    output_weight,
    norm_gain,
    readout,
    error_weight,
    report_owner,
    report_stencil,
    report_weights,
    report_values,
    report_precision,
):
    tiles = lax.axis_size("tile")
    slots = lax.axis_size("slot")
    members, lats, cols, channels = control.shape[1:]
    groups = members * lats
    size = groups * cols
    steps = report_owner.shape[1]
    rows = report_owner.shape[2]
    gain = norm_gain.reshape(1, channels)
    error = error_weight.reshape(1, channels)
    flat = control.reshape(size, channels)

    def spec(count, dtype=F32, width=channels):
        return jax.ShapeDtypeStruct((count, width), dtype)

    def scratch(count, dtype=F32, width=channels):
        return pltpu.VMEM((count, width), dtype)

    mate_of = [(i, i ^ 1) for i in range(tiles)]
    other_of = [(i, (i - 1) % tiles if i % 2 == 0 else (i + 1) % tiles) for i in range(tiles)]

    def across(block, shift):
        pairs = [
            ((s + shift) % slots * tiles + i, s * tiles + i) for s in range(slots) for i in range(tiles)
        ]
        return lax.ppermute(block, ("slot", "tile"), pairs)

    mate = lax.ppermute(flat, "tile", mate_of)
    listed = (
        jnp.transpose(report_owner[0], (0, 2, 1)),
        jnp.transpose(report_stencil[0], (0, 2, 1)),
        jnp.transpose(report_weights[0], (0, 2, 1)),
        report_precision[0],
        report_values[0].reshape(steps * rows, LANES),
    )
    work = [
        pltpu.VMEM((1, steps * rows), jnp.int32),
        scratch(24, F32, steps * rows),
        scratch(tiles * CHUNK, F32, LANES),
        scratch(tiles * CHUNK, BF16, LANES),
    ]
    held, packed, *listed = kernel_call(
        first_kernel,
        [spec(size), spec(tiles * CHUNK, BF16, LANES)]
        + [jax.ShapeDtypeStruct(block.shape, block.dtype) for block in listed],
        work + [pltpu.SemaphoreType.DMA((7,))],
        10**7,
        200000,
        hbm=6,
        out_places=[pltpu.VMEM, pltpu.HBM] + [pltpu.VMEM] * 5,
    )(flat, *listed)
    sent = kernel_call(
        tile_kernel, spec(groups * (cols + 2), BF16), [scratch(groups * 2)], 1000, 400000
    )(held, mate)
    oth = lax.ppermute(sent, "tile", other_of)
    (packed,) = kernel_call(
        later_kernel,
        [spec(tiles * CHUNK, BF16, LANES)],
        work + [pltpu.SemaphoreType.DMA],
        10**7,
        200000,
        hbm=1,
        out_places=[pltpu.HBM],
        aliases={0: 0},
    )(packed, *listed, sent)
    arrived = lax.all_to_all(packed, "tile", split_axis=0, concat_axis=0, tiled=True)

    message, near4 = kernel_call(
        relay_kernel,
        [spec(size + 4 * groups, BF16), spec(4 * groups)],
        [scratch(size), scratch(4 * groups)],
        1000,
        700000,
    )(held, mate, oth)
    nxt = across(message, 1)
    wide = groups * WIDE
    slim = groups * SLIM
    (
        edge0, u1x, d0x, d1x, f2x, field, final, wo, readout_held, gain_held, error_held, background_held,
        ws_turned, wn_turned,
    ) = kernel_call(
        forward_kernel,
        [spec(groups * 8), spec(slim)] + [spec(slim, BF16)] * 3
        + [spec(4 * lats * cols, F32, members * LANES), spec(size, BF16)]
        + [spec(channels, BF16), spec(channels, BF16, LANES), spec(1), spec(1), spec(size, BF16)]
        + [spec(channels, BF16), spec(channels, BF16)],
        [scratch(wide), scratch(wide), scratch(wide, BF16, 2 * channels), scratch(wide, BF16)]
        + [scratch(wide), scratch(16), scratch(4 * size, BF16)]
        + [scratch(2 * channels, BF16), scratch(channels, BF16), pltpu.VMEM((2, channels, channels), BF16)]
        + [pltpu.SemaphoreType.DMA((9,))],
        10**11,
        4000000,
        hbm=7,
        out_places=[pltpu.VMEM] * 12 + [pltpu.HBM] * 2,
    )(
        gain, self_weight, neighbour_weight, output_weight, readout, error, background.reshape(size, channels),
        held, near4, oth,
    )
    before = across(final, -1)
    total = tiles * CHUNK
    tables = [scratch(128, BF16, total)]
    spread, near_spread, *reports_held = kernel_call(
        functools.partial(observe_kernel, tiles),
        [spec(2 * size, BF16, LANES), spec(size, BF16, LANES)]
        + [spec(32, BF16, total), spec(32, BF16, total), spec(32, F32, total)],
        tables + [scratch(total, F32, LANES)],
        10**9,
        2000000,
    )(arrived, field)
    from_mate = lax.ppermute(near_spread, "tile", mate_of)
    handed = kernel_call(
        pull_kernel,
        [spec(2 * size), spec(size), spec(channels, BF16), spec(channels, BF16)],
        tables + [scratch(2 * size, BF16, LANES), scratch(size, BF16, LANES), pltpu.SemaphoreType.DMA((2,))],
        10**9,
        3000000,
        hbm=2,
    )(wn_turned, ws_turned, spread, readout_held, *reports_held, arrived, field)
    base = kernel_call(
        backward_kernel,
        spec(size),
        [scratch(slim), scratch(slim), scratch(slim, BF16), scratch(slim), scratch(slim)]
        + [scratch(size), scratch(16), scratch(slim), scratch(slim), scratch(size + 4 * groups)],
        12 * slim * channels * channels,
        6000000,
    )(
        *handed, gain_held, held, edge0, nxt, f2x, wo, readout_held, error_held, from_mate,
        u1x, d0x, d1x,
    )
    result = kernel_call(last_kernel, spec(size), [], 10**6, 900000)(base, background_held, before, error_held)
    return result.reshape(control.shape)


def solution(mesh):
    in_specs = (
        P("slot", None, None, "tile", None),
        P(None, None, "tile", None),
        P(),
        P(),
        P(),
        P(),
        P(),
        P(),
        P("slot", None, "tile", None),
        P("slot", None, "tile", None),
        P("slot", None, "tile", None),
        P("slot", None, "tile", None),
        P("slot", None, "tile"),
    )
    out_specs = P("slot", None, None, "tile", None)
    return jax.shard_map(
        per_device, mesh=mesh, in_specs=in_specs, out_specs=out_specs, check_vma=False
    )
```

```python
import functools
import jax
import jax.numpy as jnp
from jax import lax
from jax.experimental import pallas as pl
from jax.experimental.pallas import tpu as pltpu
from jax.sharding import PartitionSpec as P

EPSILON = 1e-06
F32 = jnp.float32
BF16 = jnp.bfloat16
LANES = 128
CAP = 5
SLOTS = 4 * CAP
CHUNK = 24
APART = 36
STRIDE = 32
WIDE = 40
SLIM = 24
VMEM_LIMIT = 28 * 1024 * 1024


def dot(a, b):
    return jnp.dot(a, b, preferred_element_type=F32)


def dot_t(a, b):
    return lax.dot_general(a, b, (((1,), (1,)), ((), ())), preferred_element_type=F32)


def sublane(shape):
    return lax.broadcasted_iota(jnp.int32, shape, 0)


def inverse_rms(x):
    return lax.rsqrt(jnp.mean(x * x, axis=-1, keepdims=True) + EPSILON)


def sigmoid(p):
    return 0.5 * jnp.tanh(0.5 * p) + 0.5


def neighbours(rows):
    width = rows[0].shape[0]
    return [
        0.25 * (rows[1 - i] + pltpu.roll(rows[i], 1, 0) + pltpu.roll(rows[i], width - 1, 0))
        for i in range(2)
    ]


def forward_step(u, n, act, pre, d, gain, weights, wo, width, members, out, copies=()):
    both = 2 * width
    for m in range(members):
        base = m * both
        rows = []
        for lat in range(2):
            x = u[base + lat * width : base + (lat + 1) * width]
            rows.append((x * inverse_rms(x) * gain).astype(BF16).astype(F32))
        channels = rows[0].shape[1]
        n[base : base + both, :channels] = jnp.concatenate(rows, axis=0).astype(BF16)
        n[base : base + both, channels:] = jnp.concatenate(neighbours(rows), axis=0).astype(BF16)
    for copy in copies[:2]:
        copy.wait()
    pre[...] = dot(n[...], weights[...])
    for m in range(members):
        base = m * both
        p = pre[base : base + both]
        sig = sigmoid(p)
        act[base : base + both] = (p * sig).astype(BF16)
        if d is not None:
            pre[base : base + both] = sig * (1.0 + p * (1.0 - sig))
    if d is not None:
        for m in range(members):
            slim_copy(d, pre, m)
    for copy in copies[2:]:
        copy.wait()
    pre[...] = dot(act[...], wo[...])
    for r in range(2 * members):
        out(r, u[r * width : (r + 1) * width] + pre[r * width : (r + 1) * width])


def slim_edge(wide, r):
    low = wide[r * WIDE + 16 : r * WIDE + 24]
    high = wide[r * WIDE + 32 : r * WIDE + 40]
    return jnp.where(sublane(low.shape) < 4, low, high)


def slim_copy(to, wide, m):
    parts = []
    for r in (2 * m, 2 * m + 1):
        parts += [wide[r * WIDE : r * WIDE + 16], slim_edge(wide, r)]
    both = jnp.concatenate(parts, axis=0)
    to[m * 2 * SLIM : (m + 1) * 2 * SLIM] = both.astype(to.dtype)


def reports(arrays, out_hbm, key, meta, picked, out, sem):
    pack(*arrays, out, key, meta, picked)
    store = pltpu.make_async_copy(out, out_hbm, sem)
    store.start()
    store.wait()


def early():
    return lax.axis_index("tile") < lax.axis_size("tile") // 2


def first_kernel(control_hbm, *refs):
    sources, (held, out_hbm), arrays, (key, meta, picked, out, sems) = refs[:5], refs[5:7], refs[7:12], refs[12:]
    copies = [
        pltpu.make_async_copy(source, to, sems.at[i]) for i, (source, to) in enumerate(zip(sources, arrays))
    ]
    copies.append(pltpu.make_async_copy(control_hbm, held, sems.at[5]))
    for copy in copies:
        copy.start()
    for copy in copies[:5]:
        copy.wait()

    @pl.when(early())
    def _():
        reports(arrays, out_hbm, key, meta, picked, out, sems.at[6])

    copies[5].wait()


def later_kernel(packed_hbm, *refs):
    arrays, out_hbm, (key, meta, picked, out, sem) = refs[:5], refs[6], refs[7:]

    @pl.when(jnp.logical_not(early()))
    def _():
        reports(arrays, out_hbm, key, meta, picked, out, sem)


def fan(x, shift):
    if shift % LANES:
        x = pltpu.roll(x, shift % LANES, 1)
    for _ in range(2):
        x = pltpu.roll(x, 0, 1, stride=APART // 2, stride_axis=0)
    return x


def pack(owner, stencil, weights, precision, values, out, key, meta, picked):
    steps, _, rows = owner.shape
    tiles = out.shape[0] // CHUNK
    total = steps * rows
    earlier = lax.broadcasted_iota(jnp.int32, (rows, rows), 0) < lax.broadcasted_iota(jnp.int32, (rows, rows), 1)
    earlier = earlier.astype(F32).astype(BF16)
    meta[...] = jnp.zeros_like(meta)
    for k in range(steps):
        at = slice(k * rows, (k + 1) * rows)
        named = lax.broadcasted_iota(jnp.int32, (tiles, rows), 0) == owner[k]
        hits = named.astype(F32)
        before = dot(hits.astype(BF16), earlier)
        rank = jnp.sum(hits * before, axis=0, keepdims=True).astype(jnp.int32)
        key[0:1, at] = owner[k] * (2 * CAP) + k * CAP + rank
        for i in range(4):
            meta[i // 3 * 8 + i % 3 : i // 3 * 8 + i % 3 + 1, at] = stencil[k, i : i + 1].astype(F32)
            j = 4 + i
            meta[j // 3 * 8 + j % 3 : j // 3 * 8 + j % 3 + 1, at] = weights[k, i : i + 1].astype(F32)
        meta[18:19, at] = precision[k : k + 1].astype(F32)
    row = lax.broadcasted_iota(jnp.int32, (tiles * STRIDE, total), 0)
    tile = row // STRIDE
    slot = row % STRIDE
    other = jnp.where(tile % 2 == 0, (tile + tiles - 1) % tiles, (tile + 1) % tiles)
    mine = slot < 2 * CAP
    wanted = jnp.where(mine, tile * (2 * CAP) + slot, other * (2 * CAP) + slot - 2 * CAP)
    wanted = jnp.where(slot < SLOTS, wanted, -1)
    placement = (wanted == key[...]).astype(F32).astype(BF16)
    placed = dot(placement, values[...])
    entries = dot_t(meta[...].astype(BF16), placement)
    lane = lax.broadcasted_iota(jnp.int32, (24, LANES), 1)
    turn = lax.axis_index("tile") * CHUNK % LANES
    per_tile = LANES // STRIDE
    for t in range(tiles):
        picked[t * CHUNK : (t + 1) * CHUNK] = placed[t * STRIDE : t * STRIDE + CHUNK]
        start = t % per_tile * STRIDE
        used = jnp.logical_and(lane >= start, lane < start + SLOTS)
        block = jnp.where(used, entries[:, t // per_tile * LANES : (t // per_tile + 1) * LANES], 0.0)
        for j in range(3):
            laid = fan(block[j * 8 : (j + 1) * 8], LANES - start)
            row = t * CHUNK + SLOTS + j
            picked[row : row + 1] = jnp.sum(laid, axis=0, keepdims=True)
        group = picked[t * CHUNK + 16 : (t + 1) * CHUNK]
        picked[t * CHUNK + 16 : (t + 1) * CHUNK] = jnp.where(sublane((8, 1)) < 4, group, pltpu.roll(group, turn, 1))
    out[...] = picked[...].astype(BF16)


def tile_kernel(control, mate, out, held):
    even = lax.rem(lax.axis_index("tile"), 2) == 0
    size = control.shape[0]
    out[0:size] = control[...].astype(BF16)
    for r in range(size // 16):
        held[r * 2 : (r + 1) * 2] = jnp.where(
            even, mate[r * 16 : r * 16 + 2], mate[r * 16 + 14 : (r + 1) * 16]
        )
    out[size:] = held[...].astype(BF16)


def relay_kernel(control, mate, oth, out, near4, wide, edge):
    even = lax.rem(lax.axis_index("tile"), 2) == 0
    size = mate.shape[0]
    out[0:size] = control[...].astype(BF16)
    wide[...] = oth[0:size].astype(F32)
    for r in range(size // 16):
        a, b = r * 16, (r + 1) * 16
        edge[r * 2 : (r + 1) * 2] = jnp.where(even, wide[b - 2 : b], wide[a : a + 2])
        near4[r * 4 : (r + 1) * 4] = jnp.where(even, mate[a : a + 4], mate[b - 4 : b])
        start = size // 8 + r * 2
        edge[start : start + 2] = jnp.where(even, mate[a : a + 2], mate[b - 2 : b])
    out[size:] = edge[...].astype(BF16)


def forward_kernel(
    gain_hbm, ws_hbm, wn_hbm, wo_hbm, readout_hbm, error_hbm, background_hbm, control, mate, oth,
    edge0, u1x, d0x, d1x, f2x, field, final, wo_turned, readout, gain, error, background, both_hbm,
    ua, ub, n, act, pre, edge, states, weights, wo, turned, sems,
):
    channels = wo.shape[0]
    halves = weights.at[pl.ds(0, channels)], weights.at[pl.ds(channels, channels)]
    pairs = (
        (gain_hbm, gain), (ws_hbm, halves[0]), (wn_hbm, halves[1]), (wo_hbm, wo), (readout_hbm, readout),
        (error_hbm, error), (background_hbm, background),
    )
    copies = [pltpu.make_async_copy(source, to, sems.at[i]) for i, (source, to) in enumerate(pairs)]
    for copy in copies:
        copy.start()
    members = final.shape[0] // 32
    even = lax.rem(lax.axis_index("tile"), 2) == 0
    tile_at = jnp.where(even, 24, 16)
    edge_at = jnp.where(even, 16, 32)
    far = oth[members * 32 :].astype(F32)
    for r in range(2 * members):
        ua[r * WIDE : r * WIDE + 16] = control[r * 16 : (r + 1) * 16]
        ua[pl.ds(pl.multiple_of(r * WIDE + tile_at, 8), 16)] = oth[r * 16 : (r + 1) * 16].astype(F32)
        near4 = mate[r * 4 : (r + 1) * 4]
        far2 = far[r * 2 : (r + 1) * 2]
        edge[...] = jnp.zeros_like(edge)
        edge[0:4] = near4
        edge[6:8] = far2
        edge[8:10] = far2
        edge[12:16] = near4
        ua[pl.ds(pl.multiple_of(r * WIDE + edge_at, 8), 8)] = jnp.where(even, edge[0:8], edge[8:16])
    for r in range(2 * members):
        edge0[r * 8 : (r + 1) * 8] = slim_edge(ua, r)
    copies[0].wait()
    g = gain[...]

    def keep(ref):
        def store(r, value):
            ref[r * WIDE : (r + 1) * WIDE] = value

        return store

    def keep_states(ref, k):
        own = k * members * 32
        away = (2 + k) * members * 32
        for r in range(2 * members):
            states[own + r * 16 : own + (r + 1) * 16] = ref[r * WIDE : r * WIDE + 16].astype(BF16)
            taken = ref[pl.ds(pl.multiple_of(r * WIDE + tile_at, 8), 16)]
            states[away + r * 16 : away + (r + 1) * 16] = taken.astype(BF16)

    forward_step(ua, n, act, pre, d0x, g, weights, wo, WIDE, members, keep(ub), copies[1:])
    for i in range(2):
        turned[i * channels : (i + 1) * channels] = jnp.transpose(halves[i][...])
    store = pltpu.make_async_copy(turned, both_hbm, sems.at[7])
    store.start()
    wo_turned[...] = jnp.transpose(wo[...])
    for m in range(members):
        slim_copy(u1x, ub, m)
    keep_states(ub, 0)
    forward_step(ub, n, act, pre, d1x, g, weights, wo, WIDE, members, keep(ua))
    for m in range(members):
        slim_copy(f2x, ua, m)
    keep_states(ua, 1)
    final[...] = states[members * 32 : 2 * members * 32]
    read = dot(states[...], readout[...])
    for q in range(4):
        for m in range(members):
            start = (q * members + m) * 32
            field[q * 32 : (q + 1) * 32, m * LANES : (m + 1) * LANES] = read[start : start + 32]
    store.wait()


def split(x):
    high = x.astype(BF16)
    return high, (x - high.astype(F32)).astype(BF16)


def spread_of(first, th, tl, scaled, taken, field, pp, spread):
    lane = lax.broadcasted_iota(jnp.int32, (1, LANES), 1)
    members = field.shape[1] // LANES
    for p in range(th.shape[1] // LANES):
        at = slice(p * LANES, (p + 1) * LANES)
        slot = (lane + p * LANES) % CHUNK
        table_of = jnp.where(slot < SLOTS, slot // CAP, -1)
        for q in range(2):
            kept = jnp.where(table_of == first + q, scaled[:, at], 0.0)
            pp[q * 32 : (q + 1) * 32, at], pp[64 + q * 32 : 96 + q * 32, at] = split(kept)
    cross = dot_t(pp[...], th[...])
    cross = cross[:64] + cross[64:] + dot_t(pp[0:64], tl[...])
    block = jnp.concatenate([cross] * 2, axis=1)
    on_block = sublane(block.shape) // 32 == lax.broadcasted_iota(jnp.int32, block.shape, 1) // 32
    target = dot(pp[...], taken[...])
    target = target[:64] + target[64:]
    ch, cl = split(jnp.where(on_block, block, 0.0))
    fh, fl = split(field[first * 32 : (first + 2) * 32])
    mixed = dot(jnp.concatenate([ch, cl], axis=0), fh)
    mixed = mixed[:64] + mixed[64:] + dot(ch, fl)
    for q in range(2):
        for m in range(members):
            start = (q * members + m) * 32
            value = mixed[q * 32 : (q + 1) * 32, m * LANES : (m + 1) * LANES] - target[q * 32 : (q + 1) * 32]
            spread[start : start + 32] = value.astype(BF16)


def observe_kernel(
    tiles, arrived, field,
    spread, message, th, tl, scaled,
    pp, wide,
):
    steps = 2
    members = field.shape[1] // LANES
    even = lax.rem(lax.axis_index("tile"), 2) == 0
    cells = sublane((32, LANES)).astype(F32)
    lane = lax.broadcasted_iota(jnp.int32, (8, LANES), 1)
    wide[...] = arrived[...].astype(F32)
    packs = th.shape[1] // LANES
    sums = [[jnp.zeros((8, LANES), F32)] * 3 for _ in range(packs)]
    for d in range(tiles):
        p, start = divmod(d * CHUNK, LANES)
        group = wide[d * CHUNK + 16 : (d + 1) * CHUNK]
        for b in range(3):
            first = start + b * APART
            place = lane - first % LANES
            place = jnp.where(place < 0, place + LANES, place)
            ends = min(LANES - start, SLOTS)
            sums[p][b] = sums[p][b] + jnp.where(place < ends, group, 0.0)
            if ends < SLOTS:
                rest = jnp.logical_and(place >= ends, place < SLOTS)
                sums[p + 1][b] = sums[p + 1][b] + jnp.where(rest, group, 0.0)
    for p in range(packs):
        kinds = [pltpu.roll(sums[p][b], (LANES - b * APART) % LANES, 1) if b else sums[p][b] for b in range(3)]
        entry = [kinds[i % 3][4 + i // 3 : 5 + i // 3] for i in range(9)]
        weight = jnp.zeros((32, LANES), F32)
        for i in range(4):
            weight += jnp.where(cells == entry[i], entry[4 + i], 0.0)
        at = slice(p * LANES, (p + 1) * LANES)
        th[:, at], tl[:, at] = split(weight)
        scaled[:, at] = weight * entry[8]
    spread_of(0, th, tl, scaled, arrived, field, pp, spread)
    size = members * 32
    for k in range(steps):
        for m in range(members):
            start = k * size + m * 32
            pair = spread[start : start + 32].astype(F32)
            near = [jnp.where(even, pair[i + 8 : i + 16], pair[i : i + 8]) for i in (0, 16)]
            start = k * size // 2 + m * 16
            message[start : start + 16] = jnp.concatenate(near, axis=0).astype(BF16)


def adjoint_step(u, cot, gb, gm, flat, d, out, gain, ws, wn, wo, members):
    both = 2 * SLIM
    gb[...] = cot[...].astype(BF16)
    flat[...] = dot(gb[...], wo[...])
    gb[...] = (flat[...] * d[...]).astype(BF16)
    gm[...] = dot(gb[...], wn[...])
    flat[...] = dot(gb[...], ws[...])
    for m in range(members):
        base = m * both
        rows = []
        for lat in range(2):
            start = base + lat * SLIM
            rows.append(gm[start : start + SLIM].astype(BF16).astype(F32))
        around = neighbours(rows)
        for lat in range(2):
            start = base + lat * SLIM
            x = u[start : start + SLIM]
            s = inverse_rms(x)
            scaled = gain * (flat[start : start + SLIM] + around[lat])
            inner = jnp.mean(x * scaled, axis=-1, keepdims=True)
            out(2 * m + lat, cot[start : start + SLIM] + s * scaled - x * (s * s * s * inner))


def edges(nxt, size, edge, r):
    even = lax.rem(lax.axis_index("tile"), 2) == 0
    start = size + r * 2
    far = nxt[start : start + 2]
    start = size + size // 8 + r * 2
    near = nxt[start : start + 2]
    edge[...] = jnp.zeros_like(edge)
    edge[0:2] = near
    edge[6:8] = far
    edge[8:10] = far
    edge[14:16] = near
    return jnp.where(even, edge[0:8], edge[8:16])


def pull_kernel(
    both_hbm, spread_own, readout, th, tl, scaled, arrived, field,
    pulled, away, wn, ws,
    pp, spread, near, sems,
):
    channels = wn.shape[0]
    pairs = ((both_hbm.at[pl.ds(channels, channels)], wn), (both_hbm.at[pl.ds(0, channels)], ws))
    copies = [pltpu.make_async_copy(source, to, sems.at[i]) for i, (source, to) in enumerate(pairs)]
    for copy in copies:
        copy.start()
    even = lax.rem(lax.axis_index("tile"), 2) == 0
    pulled[...] = dot_t(spread_own[...], readout[...])
    spread_of(2, th, tl, scaled, arrived, field, pp, spread)
    for start in range(0, spread.shape[0], 32):
        pair = spread[start : start + 32].astype(F32)
        rows = [jnp.where(even, pair[i + 8 : i + 16], pair[i : i + 8]) for i in (0, 16)]
        near[start // 2 : start // 2 + 16] = jnp.concatenate(rows, axis=0).astype(BF16)
    away[...] = dot_t(near[...], readout[...])
    for copy in copies:
        copy.wait()


def backward_kernel(
    pulled, away, wn, ws, gain, control, edge0, message16, f2x, wo, readout, error, message,
    u1x, d0x, d1x,
    result,
    cot2, cot1, gb, gm, flat, mate_pull, edge, u0x, final, nxt,
):
    size = result.shape[0]
    members = size // 32
    even = lax.rem(lax.axis_index("tile"), 2) == 0
    nxt[...] = message16[...].astype(F32)
    weight = jnp.where(lax.axis_index("slot") == lax.axis_size("slot") - 1, 0.0, 1.0) * error[...]
    row8 = sublane((8, 1))
    mate_side = jnp.where(even, 1, 0) == jnp.where(row8 < 4, 1, 0)
    mate_pull[...] = dot_t(message[...], readout[...])
    final[...] = f2x[...].astype(F32)

    def pulls(k, r):
        own = k * size + r * 16
        near = k * size // 2 + r * 8
        group = jnp.where(mate_side, mate_pull[near : near + 8], away[near : near + 8])
        return pulled[own : own + 16], group

    for r in range(2 * members):
        own, group = pulls(1, r)
        a, b = r * SLIM, r * SLIM + 16
        cot2[a:b] = own - weight * (nxt[r * 16 : (r + 1) * 16] - final[a:b])
        u0x[a:b] = control[r * 16 : (r + 1) * 16]
        a, b = b, b + 8
        cot2[a:b] = group - weight * (edges(nxt, size, edge, r) - final[a:b])
        u0x[a:b] = edge0[r * 8 : (r + 1) * 8]

    def keep(r, value):
        cot1[r * SLIM : (r + 1) * SLIM] = value + jnp.concatenate(pulls(0, r), axis=0)

    def finish(r, value):
        a, b = r * SLIM, r * SLIM + 16
        result[r * 16 : (r + 1) * 16] = value[0:16] + error[...] * u0x[a:b]

    adjoint_step(u1x, cot2, gb, gm, flat, d1x, keep, gain[...], ws, wn, wo, members)
    adjoint_step(u0x, cot1, gb, gm, flat, d0x, finish, gain[...], ws, wn, wo, members)


def last_kernel(base, background, before, error, result):
    first = lax.axis_index("slot") == 0
    taken = jnp.where(first, background[...].astype(F32), before[...].astype(F32))
    result[...] = base[...] - error[...] * taken


def kernel_call(body, outs, scratch, flops, moved, hbm=0, out_places=None, aliases={}, fixed=True):
    def call(*operands):
        there = [fixed and i < hbm and i not in aliases for i in range(len(operands))]
        operands = [
            pltpu.with_memory_space_constraint(x, pltpu.HBM) if fix else x for x, fix in zip(operands, there)
        ]
        places = [pltpu.HBM] * hbm + [pltpu.VMEM] * (len(operands) - hbm)
        given = {} if out_places is None else {"out_specs": [pl.BlockSpec(memory_space=p) for p in out_places]}
        return pl.pallas_call(
            body,
            out_shape=outs,
            in_specs=[pl.BlockSpec(memory_space=place) for place in places],
            **given,
            scratch_shapes=scratch,
            input_output_aliases=aliases,
            compiler_params=pltpu.CompilerParams(vmem_limit_bytes=VMEM_LIMIT),
            cost_estimate=pl.CostEstimate(flops=flops, bytes_accessed=moved, transcendentals=0),
        )(*operands)

    return call


def per_device(
    control,
    background,
    self_weight,
    neighbour_weight,
    output_weight,
    norm_gain,
    readout,
    error_weight,
    report_owner,
    report_stencil,
    report_weights,
    report_values,
    report_precision,
):
    tiles = lax.axis_size("tile")
    slots = lax.axis_size("slot")
    members, lats, cols, channels = control.shape[1:]
    groups = members * lats
    size = groups * cols
    steps = report_owner.shape[1]
    rows = report_owner.shape[2]
    gain = norm_gain.reshape(1, channels)
    error = error_weight.reshape(1, channels)
    flat = control.reshape(size, channels)

    def spec(count, dtype=F32, width=channels):
        return jax.ShapeDtypeStruct((count, width), dtype)

    def scratch(count, dtype=F32, width=channels):
        return pltpu.VMEM((count, width), dtype)

    mate_of = [(i, i ^ 1) for i in range(tiles)]
    other_of = [(i, (i - 1) % tiles if i % 2 == 0 else (i + 1) % tiles) for i in range(tiles)]

    def across(block, shift):
        pairs = [
            ((s + shift) % slots * tiles + i, s * tiles + i) for s in range(slots) for i in range(tiles)
        ]
        return lax.ppermute(block, ("slot", "tile"), pairs)

    mate = lax.ppermute(flat, "tile", mate_of)
    listed = (
        jnp.transpose(report_owner[0], (0, 2, 1)),
        jnp.transpose(report_stencil[0], (0, 2, 1)),
        jnp.transpose(report_weights[0], (0, 2, 1)),
        report_precision[0],
        report_values[0].reshape(steps * rows, LANES),
    )
    work = [
        pltpu.VMEM((1, steps * rows), jnp.int32),
        scratch(24, F32, steps * rows),
        scratch(tiles * CHUNK, F32, LANES),
        scratch(tiles * CHUNK, BF16, LANES),
    ]
    held, packed, *listed = kernel_call(
        first_kernel,
        [spec(size), spec(tiles * CHUNK, BF16, LANES)]
        + [jax.ShapeDtypeStruct(block.shape, block.dtype) for block in listed],
        work + [pltpu.SemaphoreType.DMA((7,))],
        10**7,
        200000,
        hbm=6,
        out_places=[pltpu.VMEM, pltpu.HBM] + [pltpu.VMEM] * 5,
    )(flat, *listed)
    sent = kernel_call(
        tile_kernel, spec(groups * (cols + 2), BF16), [scratch(groups * 2)], 1000, 400000
    )(held, mate)
    oth = lax.ppermute(sent, "tile", other_of)
    (packed,) = kernel_call(
        later_kernel,
        [spec(tiles * CHUNK, BF16, LANES)],
        work + [pltpu.SemaphoreType.DMA],
        10**7,
        200000,
        hbm=1,
        out_places=[pltpu.HBM],
        aliases={0: 0},
    )(packed, *listed, sent)
    arrived = lax.all_to_all(packed, "tile", split_axis=0, concat_axis=0, tiled=True)

    message, near4 = kernel_call(
        relay_kernel,
        [spec(size + 4 * groups, BF16), spec(4 * groups)],
        [scratch(size), scratch(4 * groups)],
        1000,
        700000,
    )(held, mate, oth)
    nxt = across(message, 1)
    wide = groups * WIDE
    slim = groups * SLIM
    (
        edge0, u1x, d0x, d1x, f2x, field, final, wo, readout_held, gain_held, error_held, background_held,
        both_turned,
    ) = kernel_call(
        forward_kernel,
        [spec(groups * 8), spec(slim)] + [spec(slim, BF16)] * 3
        + [spec(4 * lats * cols, F32, members * LANES), spec(size, BF16)]
        + [spec(channels, BF16), spec(channels, BF16, LANES), spec(1), spec(1), spec(size, BF16)]
        + [spec(2 * channels, BF16)],
        [scratch(wide), scratch(wide), scratch(wide, BF16, 2 * channels), scratch(wide, BF16)]
        + [scratch(wide), scratch(16), scratch(4 * size, BF16)]
        + [scratch(2 * channels, BF16), scratch(channels, BF16), scratch(2 * channels, BF16)]
        + [pltpu.SemaphoreType.DMA((8,))],
        10**11,
        4000000,
        hbm=7,
        out_places=[pltpu.VMEM] * 12 + [pltpu.HBM],
    )(
        gain, self_weight, neighbour_weight, output_weight, readout, error, background.reshape(size, channels),
        held, near4, oth,
    )
    before = across(final, -1)
    total = tiles * CHUNK
    tables = [scratch(128, BF16, total)]
    spread, near_spread, *reports_held = kernel_call(
        functools.partial(observe_kernel, tiles),
        [spec(2 * size, BF16, LANES), spec(size, BF16, LANES)]
        + [spec(32, BF16, total), spec(32, BF16, total), spec(32, F32, total)],
        tables + [scratch(total, F32, LANES)],
        10**9,
        2000000,
    )(arrived, field)
    from_mate = lax.ppermute(near_spread, "tile", mate_of)
    handed = kernel_call(
        pull_kernel,
        [spec(2 * size), spec(size), spec(channels, BF16), spec(channels, BF16)],
        tables + [scratch(2 * size, BF16, LANES), scratch(size, BF16, LANES), pltpu.SemaphoreType.DMA((2,))],
        10**9,
        3000000,
        hbm=1,
        fixed=False,
    )(both_turned, spread, readout_held, *reports_held, arrived, field)
    base = kernel_call(
        backward_kernel,
        spec(size),
        [scratch(slim), scratch(slim), scratch(slim, BF16), scratch(slim), scratch(slim)]
        + [scratch(size), scratch(16), scratch(slim), scratch(slim), scratch(size + 4 * groups)],
        12 * slim * channels * channels,
        6000000,
    )(
        *handed, gain_held, held, edge0, nxt, f2x, wo, readout_held, error_held, from_mate,
        u1x, d0x, d1x,
    )
    result = kernel_call(last_kernel, spec(size), [], 10**6, 900000)(base, background_held, before, error_held)
    return result.reshape(control.shape)


def solution(mesh):
    in_specs = (
        P("slot", None, None, "tile", None),
        P(None, None, "tile", None),
        P(),
        P(),
        P(),
        P(),
        P(),
        P(),
        P("slot", None, "tile", None),
        P("slot", None, "tile", None),
        P("slot", None, "tile", None),
        P("slot", None, "tile", None),
        P("slot", None, "tile"),
    )
    out_specs = P("slot", None, None, "tile", None)
    return jax.shard_map(
        per_device, mesh=mesh, in_specs=in_specs, out_specs=out_specs, check_vma=False
    )
```

```python
import functools
import jax
import jax.numpy as jnp
from jax import lax
from jax.experimental import pallas as pl
from jax.experimental.pallas import tpu as pltpu
from jax.sharding import PartitionSpec as P

EPSILON = 1e-06
F32 = jnp.float32
BF16 = jnp.bfloat16
LANES = 128
CAP = 5
SLOTS = 4 * CAP
CHUNK = 24
APART = 36
STRIDE = 32
WIDE = 40
SLIM = 24
VMEM_LIMIT = 28 * 1024 * 1024


def dot(a, b):
    return jnp.dot(a, b, preferred_element_type=F32)


def dot_t(a, b):
    return lax.dot_general(a, b, (((1,), (1,)), ((), ())), preferred_element_type=F32)


def sublane(shape):
    return lax.broadcasted_iota(jnp.int32, shape, 0)


def inverse_rms(x):
    return lax.rsqrt(jnp.mean(x * x, axis=-1, keepdims=True) + EPSILON)


def sigmoid(p):
    return 0.5 * jnp.tanh(0.5 * p) + 0.5


def neighbours(rows):
    width = rows[0].shape[0]
    return [
        0.25 * (rows[1 - i] + pltpu.roll(rows[i], 1, 0) + pltpu.roll(rows[i], width - 1, 0))
        for i in range(2)
    ]


def forward_step(u, n, act, pre, d, gain, weights, wo, width, members, out, copies=()):
    both = 2 * width
    for m in range(members):
        base = m * both
        rows = []
        for lat in range(2):
            x = u[base + lat * width : base + (lat + 1) * width]
            rows.append((x * inverse_rms(x) * gain).astype(BF16).astype(F32))
        channels = rows[0].shape[1]
        n[base : base + both, :channels] = jnp.concatenate(rows, axis=0).astype(BF16)
        n[base : base + both, channels:] = jnp.concatenate(neighbours(rows), axis=0).astype(BF16)
    for copy in copies[:2]:
        copy.wait()
    pre[...] = dot(n[...], weights[...])
    for m in range(members):
        base = m * both
        p = pre[base : base + both]
        sig = sigmoid(p)
        act[base : base + both] = (p * sig).astype(BF16)
        if d is not None:
            pre[base : base + both] = sig * (1.0 + p * (1.0 - sig))
    if d is not None:
        for m in range(members):
            slim_copy(d, pre, m)
    for copy in copies[2:]:
        copy.wait()
    pre[...] = dot(act[...], wo[...])
    for r in range(2 * members):
        out(r, u[r * width : (r + 1) * width] + pre[r * width : (r + 1) * width])


def slim_edge(wide, r):
    low = wide[r * WIDE + 16 : r * WIDE + 24]
    high = wide[r * WIDE + 32 : r * WIDE + 40]
    return jnp.where(sublane(low.shape) < 4, low, high)


def slim_copy(to, wide, m):
    parts = []
    for r in (2 * m, 2 * m + 1):
        parts += [wide[r * WIDE : r * WIDE + 16], slim_edge(wide, r)]
    both = jnp.concatenate(parts, axis=0)
    to[m * 2 * SLIM : (m + 1) * 2 * SLIM] = both.astype(to.dtype)


def reports(arrays, out_hbm, key, meta, picked, out, sem):
    pack(*arrays, out, key, meta, picked)
    store = pltpu.make_async_copy(out, out_hbm, sem)
    store.start()
    store.wait()


def early():
    return lax.axis_index("tile") < lax.axis_size("tile") // 2


def first_kernel(control_hbm, *refs):
    sources, (held, out_hbm), arrays, (key, meta, picked, out, sems) = refs[:5], refs[5:7], refs[7:12], refs[12:]
    copies = [
        pltpu.make_async_copy(source, to, sems.at[i]) for i, (source, to) in enumerate(zip(sources, arrays))
    ]
    copies.append(pltpu.make_async_copy(control_hbm, held, sems.at[5]))
    for copy in copies:
        copy.start()
    for copy in copies[:5]:
        copy.wait()

    @pl.when(early())
    def _():
        reports(arrays, out_hbm, key, meta, picked, out, sems.at[6])

    copies[5].wait()


def later_kernel(packed_hbm, *refs):
    arrays, out_hbm, (key, meta, picked, out, sem) = refs[:5], refs[6], refs[7:]

    @pl.when(jnp.logical_not(early()))
    def _():
        reports(arrays, out_hbm, key, meta, picked, out, sem)


def fan(x, shift):
    if shift % LANES:
        x = pltpu.roll(x, shift % LANES, 1)
    for _ in range(2):
        x = pltpu.roll(x, 0, 1, stride=APART // 2, stride_axis=0)
    return x


def pack(owner, stencil, weights, precision, values, out, key, meta, picked):
    steps, _, rows = owner.shape
    tiles = out.shape[0] // CHUNK
    total = steps * rows
    earlier = lax.broadcasted_iota(jnp.int32, (rows, rows), 0) < lax.broadcasted_iota(jnp.int32, (rows, rows), 1)
    earlier = earlier.astype(F32).astype(BF16)
    meta[...] = jnp.zeros_like(meta)
    for k in range(steps):
        at = slice(k * rows, (k + 1) * rows)
        named = lax.broadcasted_iota(jnp.int32, (tiles, rows), 0) == owner[k]
        hits = named.astype(F32)
        before = dot(hits.astype(BF16), earlier)
        rank = jnp.sum(hits * before, axis=0, keepdims=True).astype(jnp.int32)
        key[0:1, at] = owner[k] * (2 * CAP) + k * CAP + rank
        for i in range(4):
            meta[i // 3 * 8 + i % 3 : i // 3 * 8 + i % 3 + 1, at] = stencil[k, i : i + 1].astype(F32)
            j = 4 + i
            meta[j // 3 * 8 + j % 3 : j // 3 * 8 + j % 3 + 1, at] = weights[k, i : i + 1].astype(F32)
        meta[18:19, at] = precision[k : k + 1].astype(F32)
    row = lax.broadcasted_iota(jnp.int32, (tiles * STRIDE, total), 0)
    tile = row // STRIDE
    slot = row % STRIDE
    other = jnp.where(tile % 2 == 0, (tile + tiles - 1) % tiles, (tile + 1) % tiles)
    mine = slot < 2 * CAP
    wanted = jnp.where(mine, tile * (2 * CAP) + slot, other * (2 * CAP) + slot - 2 * CAP)
    wanted = jnp.where(slot < SLOTS, wanted, -1)
    placement = (wanted == key[...]).astype(F32).astype(BF16)
    placed = dot(placement, values[...])
    entries = dot_t(meta[...].astype(BF16), placement)
    lane = lax.broadcasted_iota(jnp.int32, (24, LANES), 1)
    turn = lax.axis_index("tile") * CHUNK % LANES
    per_tile = LANES // STRIDE
    for t in range(tiles):
        picked[t * CHUNK : (t + 1) * CHUNK] = placed[t * STRIDE : t * STRIDE + CHUNK]
        start = t % per_tile * STRIDE
        used = jnp.logical_and(lane >= start, lane < start + SLOTS)
        block = jnp.where(used, entries[:, t // per_tile * LANES : (t // per_tile + 1) * LANES], 0.0)
        for j in range(3):
            laid = fan(block[j * 8 : (j + 1) * 8], LANES - start)
            row = t * CHUNK + SLOTS + j
            picked[row : row + 1] = jnp.sum(laid, axis=0, keepdims=True)
        group = picked[t * CHUNK + 16 : (t + 1) * CHUNK]
        picked[t * CHUNK + 16 : (t + 1) * CHUNK] = jnp.where(sublane((8, 1)) < 4, group, pltpu.roll(group, turn, 1))
    out[...] = picked[...].astype(BF16)


def tile_kernel(control, mate, out, held):
    even = lax.rem(lax.axis_index("tile"), 2) == 0
    size = control.shape[0]
    out[0:size] = control[...].astype(BF16)
    for r in range(size // 16):
        held[r * 2 : (r + 1) * 2] = jnp.where(
            even, mate[r * 16 : r * 16 + 2], mate[r * 16 + 14 : (r + 1) * 16]
        )
    out[size:] = held[...].astype(BF16)


def relay_kernel(control, mate, oth, out, near4, wide, edge):
    even = lax.rem(lax.axis_index("tile"), 2) == 0
    size = mate.shape[0]
    out[0:size] = control[...].astype(BF16)
    wide[...] = oth[0:size].astype(F32)
    for r in range(size // 16):
        a, b = r * 16, (r + 1) * 16
        edge[r * 2 : (r + 1) * 2] = jnp.where(even, wide[b - 2 : b], wide[a : a + 2])
        near4[r * 4 : (r + 1) * 4] = jnp.where(even, mate[a : a + 4], mate[b - 4 : b])
        start = size // 8 + r * 2
        edge[start : start + 2] = jnp.where(even, mate[a : a + 2], mate[b - 2 : b])
    out[size:] = edge[...].astype(BF16)


def forward_kernel(
    gain_hbm, ws_hbm, wn_hbm, wo_hbm, readout_hbm, error_hbm, background_hbm, control, mate, oth,
    edge0, u1x, d0x, d1x, f2x, field, final, wo_turned, readout, gain, error, background,
    ua, ub, n, act, pre, edge, states, weights, wo, sems,
):
    channels = wo.shape[0]
    halves = weights.at[pl.ds(0, channels)], weights.at[pl.ds(channels, channels)]
    pairs = (
        (gain_hbm, gain), (ws_hbm, halves[0]), (wn_hbm, halves[1]), (wo_hbm, wo), (readout_hbm, readout),
        (error_hbm, error), (background_hbm, background),
    )
    copies = [pltpu.make_async_copy(source, to, sems.at[i]) for i, (source, to) in enumerate(pairs)]
    for copy in copies:
        copy.start()
    members = final.shape[0] // 32
    even = lax.rem(lax.axis_index("tile"), 2) == 0
    tile_at = jnp.where(even, 24, 16)
    edge_at = jnp.where(even, 16, 32)
    far = oth[members * 32 :].astype(F32)
    for r in range(2 * members):
        ua[r * WIDE : r * WIDE + 16] = control[r * 16 : (r + 1) * 16]
        ua[pl.ds(pl.multiple_of(r * WIDE + tile_at, 8), 16)] = oth[r * 16 : (r + 1) * 16].astype(F32)
        near4 = mate[r * 4 : (r + 1) * 4]
        far2 = far[r * 2 : (r + 1) * 2]
        edge[...] = jnp.zeros_like(edge)
        edge[0:4] = near4
        edge[6:8] = far2
        edge[8:10] = far2
        edge[12:16] = near4
        ua[pl.ds(pl.multiple_of(r * WIDE + edge_at, 8), 8)] = jnp.where(even, edge[0:8], edge[8:16])
    for r in range(2 * members):
        edge0[r * 8 : (r + 1) * 8] = slim_edge(ua, r)
    copies[0].wait()
    g = gain[...]

    def keep(ref):
        def store(r, value):
            ref[r * WIDE : (r + 1) * WIDE] = value

        return store

    def keep_states(ref, k):
        own = k * members * 32
        away = (2 + k) * members * 32
        for r in range(2 * members):
            states[own + r * 16 : own + (r + 1) * 16] = ref[r * WIDE : r * WIDE + 16].astype(BF16)
            taken = ref[pl.ds(pl.multiple_of(r * WIDE + tile_at, 8), 16)]
            states[away + r * 16 : away + (r + 1) * 16] = taken.astype(BF16)

    forward_step(ua, n, act, pre, d0x, g, weights, wo, WIDE, members, keep(ub), copies[1:])
    wo_turned[...] = jnp.transpose(wo[...])
    for m in range(members):
        slim_copy(u1x, ub, m)
    keep_states(ub, 0)
    forward_step(ub, n, act, pre, d1x, g, weights, wo, WIDE, members, keep(ua))
    for m in range(members):
        slim_copy(f2x, ua, m)
    keep_states(ua, 1)
    final[...] = states[members * 32 : 2 * members * 32]
    read = dot(states[...], readout[...])
    for q in range(4):
        for m in range(members):
            start = (q * members + m) * 32
            field[q * 32 : (q + 1) * 32, m * LANES : (m + 1) * LANES] = read[start : start + 32]


def split(x):
    high = x.astype(BF16)
    return high, (x - high.astype(F32)).astype(BF16)


def near_rows(x):
    even = lax.rem(lax.axis_index("tile"), 2) == 0
    return jnp.where(
        even, jnp.concatenate([x[8:16], x[24:32]], axis=0), jnp.concatenate([x[0:8], x[16:24]], axis=0)
    )


def spread_of(first, near, th, tl, scaled, taken, field, pp, out):
    count = 16 if near else 32
    half = 2 * count
    lane = lax.broadcasted_iota(jnp.int32, (1, LANES), 1)
    members = field.shape[1] // LANES
    for p in range(th.shape[1] // LANES):
        at = slice(p * LANES, (p + 1) * LANES)
        slot = (lane + p * LANES) % CHUNK
        table_of = jnp.where(slot < SLOTS, slot // CAP, -1)
        rows = scaled[:, at]
        rows = near_rows(rows) if near else rows
        for q in range(2):
            a, b = q * count, (q + 1) * count
            pp[a:b, at], pp[half + a : half + b, at] = split(jnp.where(table_of == first + q, rows, 0.0))
    both = pp[0 : 2 * half]
    cross = dot_t(both, th[...])
    cross = cross[:half] + cross[half:] + dot_t(pp[0:half], tl[...])
    block = jnp.concatenate([cross] * 2, axis=1)
    on_block = sublane(block.shape) // count == lax.broadcasted_iota(jnp.int32, block.shape, 1) // 32
    target = dot(both, taken[...])
    target = target[:half] + target[half:]
    ch, cl = split(jnp.where(on_block, block, 0.0))
    fh, fl = split(field[first * 32 : (first + 2) * 32])
    mixed = dot(jnp.concatenate([ch, cl], axis=0), fh)
    mixed = mixed[:half] + mixed[half:] + dot(ch, fl)
    for q in range(2):
        for m in range(members):
            start = (q * members + m) * count
            a, b = q * count, (q + 1) * count
            value = mixed[a:b, m * LANES : (m + 1) * LANES] - target[a:b]
            out[start : start + count] = value.astype(BF16)


def observe_kernel(
    tiles, arrived, field,
    message, th, tl, scaled,
    pp, wide,
):
    cells = sublane((32, LANES)).astype(F32)
    lane = lax.broadcasted_iota(jnp.int32, (8, LANES), 1)
    wide[...] = arrived[...].astype(F32)
    packs = th.shape[1] // LANES
    sums = [[jnp.zeros((8, LANES), F32)] * 3 for _ in range(packs)]
    for d in range(tiles):
        p, start = divmod(d * CHUNK, LANES)
        group = wide[d * CHUNK + 16 : (d + 1) * CHUNK]
        for b in range(3):
            first = start + b * APART
            place = lane - first % LANES
            place = jnp.where(place < 0, place + LANES, place)
            ends = min(LANES - start, SLOTS)
            sums[p][b] = sums[p][b] + jnp.where(place < ends, group, 0.0)
            if ends < SLOTS:
                rest = jnp.logical_and(place >= ends, place < SLOTS)
                sums[p + 1][b] = sums[p + 1][b] + jnp.where(rest, group, 0.0)
    for p in range(packs):
        kinds = [pltpu.roll(sums[p][b], (LANES - b * APART) % LANES, 1) if b else sums[p][b] for b in range(3)]
        entry = [kinds[i % 3][4 + i // 3 : 5 + i // 3] for i in range(9)]
        weight = jnp.zeros((32, LANES), F32)
        for i in range(4):
            weight += jnp.where(cells == entry[i], entry[4 + i], 0.0)
        at = slice(p * LANES, (p + 1) * LANES)
        th[:, at], tl[:, at] = split(weight)
        scaled[:, at] = weight * entry[8]
    spread_of(0, True, th, tl, scaled, arrived, field, pp, message)


def adjoint_step(u, cot, gb, gm, flat, d, out, gain, ws, wn, wo, members):
    both = 2 * SLIM
    gb[...] = cot[...].astype(BF16)
    flat[...] = dot(gb[...], wo[...])
    gb[...] = (flat[...] * d[...]).astype(BF16)
    gm[...] = dot_t(gb[...], wn[...])
    flat[...] = dot_t(gb[...], ws[...])
    for m in range(members):
        base = m * both
        rows = []
        for lat in range(2):
            start = base + lat * SLIM
            rows.append(gm[start : start + SLIM].astype(BF16).astype(F32))
        around = neighbours(rows)
        for lat in range(2):
            start = base + lat * SLIM
            x = u[start : start + SLIM]
            s = inverse_rms(x)
            scaled = gain * (flat[start : start + SLIM] + around[lat])
            inner = jnp.mean(x * scaled, axis=-1, keepdims=True)
            out(2 * m + lat, cot[start : start + SLIM] + s * scaled - x * (s * s * s * inner))


def edges(nxt, size, edge, r):
    even = lax.rem(lax.axis_index("tile"), 2) == 0
    start = size + r * 2
    far = nxt[start : start + 2]
    start = size + size // 8 + r * 2
    near = nxt[start : start + 2]
    edge[...] = jnp.zeros_like(edge)
    edge[0:2] = near
    edge[6:8] = far
    edge[8:10] = far
    edge[14:16] = near
    return jnp.where(even, edge[0:8], edge[8:16])


def pull_kernel(
    wn_hbm, ws_hbm, readout, th, tl, scaled, arrived, field,
    pulled, away, wn, ws,
    pp, spread, near, sems,
):
    pairs = ((wn_hbm, wn), (ws_hbm, ws))
    copies = [pltpu.make_async_copy(source, to, sems.at[i]) for i, (source, to) in enumerate(pairs)]
    for copy in copies:
        copy.start()
    spread_of(0, False, th, tl, scaled, arrived, field, pp, spread)
    pulled[...] = dot_t(spread[...], readout[...])
    spread_of(2, True, th, tl, scaled, arrived, field, pp, near)
    away[...] = dot_t(near[...], readout[...])
    for copy in copies:
        copy.wait()


def backward_kernel(
    pulled, away, wn, ws, gain, control, edge0, message16, f2x, wo, readout, error, message,
    u1x, d0x, d1x,
    result,
    cot2, cot1, gb, gm, flat, mate_pull, edge, u0x, final, nxt,
):
    size = result.shape[0]
    members = size // 32
    even = lax.rem(lax.axis_index("tile"), 2) == 0
    nxt[...] = message16[...].astype(F32)
    weight = jnp.where(lax.axis_index("slot") == lax.axis_size("slot") - 1, 0.0, 1.0) * error[...]
    row8 = sublane((8, 1))
    mate_side = jnp.where(even, 1, 0) == jnp.where(row8 < 4, 1, 0)
    mate_pull[...] = dot_t(message[...], readout[...])
    final[...] = f2x[...].astype(F32)

    def pulls(k, r):
        own = k * size + r * 16
        near = k * size // 2 + r * 8
        group = jnp.where(mate_side, mate_pull[near : near + 8], away[near : near + 8])
        return pulled[own : own + 16], group

    for r in range(2 * members):
        own, group = pulls(1, r)
        a, b = r * SLIM, r * SLIM + 16
        cot2[a:b] = own - weight * (nxt[r * 16 : (r + 1) * 16] - final[a:b])
        u0x[a:b] = control[r * 16 : (r + 1) * 16]
        a, b = b, b + 8
        cot2[a:b] = group - weight * (edges(nxt, size, edge, r) - final[a:b])
        u0x[a:b] = edge0[r * 8 : (r + 1) * 8]

    def keep(r, value):
        cot1[r * SLIM : (r + 1) * SLIM] = value + jnp.concatenate(pulls(0, r), axis=0)

    def finish(r, value):
        a, b = r * SLIM, r * SLIM + 16
        result[r * 16 : (r + 1) * 16] = value[0:16] + error[...] * u0x[a:b]

    adjoint_step(u1x, cot2, gb, gm, flat, d1x, keep, gain[...], ws, wn, wo, members)
    adjoint_step(u0x, cot1, gb, gm, flat, d0x, finish, gain[...], ws, wn, wo, members)


def last_kernel(base, background, before, error, result):
    first = lax.axis_index("slot") == 0
    taken = jnp.where(first, background[...].astype(F32), before[...].astype(F32))
    result[...] = base[...] - error[...] * taken


def kernel_call(body, outs, scratch, flops, moved, hbm=0, out_places=None, aliases={}):
    def call(*operands):
        fixed = [i in range(hbm) and i not in aliases for i in range(len(operands))]
        operands = [
            pltpu.with_memory_space_constraint(x, pltpu.HBM) if fix else x for x, fix in zip(operands, fixed)
        ]
        places = [pltpu.HBM] * hbm + [pltpu.VMEM] * (len(operands) - hbm)
        given = {} if out_places is None else {"out_specs": [pl.BlockSpec(memory_space=p) for p in out_places]}
        return pl.pallas_call(
            body,
            out_shape=outs,
            in_specs=[pl.BlockSpec(memory_space=place) for place in places],
            **given,
            scratch_shapes=scratch,
            input_output_aliases=aliases,
            compiler_params=pltpu.CompilerParams(vmem_limit_bytes=VMEM_LIMIT),
            cost_estimate=pl.CostEstimate(flops=flops, bytes_accessed=moved, transcendentals=0),
        )(*operands)

    return call


def per_device(
    control,
    background,
    self_weight,
    neighbour_weight,
    output_weight,
    norm_gain,
    readout,
    error_weight,
    report_owner,
    report_stencil,
    report_weights,
    report_values,
    report_precision,
):
    tiles = lax.axis_size("tile")
    slots = lax.axis_size("slot")
    members, lats, cols, channels = control.shape[1:]
    groups = members * lats
    size = groups * cols
    steps = report_owner.shape[1]
    rows = report_owner.shape[2]
    gain = norm_gain.reshape(1, channels)
    error = error_weight.reshape(1, channels)
    flat = control.reshape(size, channels)

    def spec(count, dtype=F32, width=channels):
        return jax.ShapeDtypeStruct((count, width), dtype)

    def scratch(count, dtype=F32, width=channels):
        return pltpu.VMEM((count, width), dtype)

    mate_of = [(i, i ^ 1) for i in range(tiles)]
    other_of = [(i, (i - 1) % tiles if i % 2 == 0 else (i + 1) % tiles) for i in range(tiles)]

    def across(block, shift):
        pairs = [
            ((s + shift) % slots * tiles + i, s * tiles + i) for s in range(slots) for i in range(tiles)
        ]
        return lax.ppermute(block, ("slot", "tile"), pairs)

    mate = lax.ppermute(flat, "tile", mate_of)
    listed = (
        jnp.transpose(report_owner[0], (0, 2, 1)),
        jnp.transpose(report_stencil[0], (0, 2, 1)),
        jnp.transpose(report_weights[0], (0, 2, 1)),
        report_precision[0],
        report_values[0].reshape(steps * rows, LANES),
    )
    work = [
        pltpu.VMEM((1, steps * rows), jnp.int32),
        scratch(24, F32, steps * rows),
        scratch(tiles * CHUNK, F32, LANES),
        scratch(tiles * CHUNK, BF16, LANES),
    ]
    held, packed, *listed = kernel_call(
        first_kernel,
        [spec(size), spec(tiles * CHUNK, BF16, LANES)]
        + [jax.ShapeDtypeStruct(block.shape, block.dtype) for block in listed],
        work + [pltpu.SemaphoreType.DMA((7,))],
        10**7,
        200000,
        hbm=6,
        out_places=[pltpu.VMEM, pltpu.HBM] + [pltpu.VMEM] * 5,
    )(flat, *listed)
    sent = kernel_call(
        tile_kernel, spec(groups * (cols + 2), BF16), [scratch(groups * 2)], 1000, 400000
    )(held, mate)
    oth = lax.ppermute(sent, "tile", other_of)
    (packed,) = kernel_call(
        later_kernel,
        [spec(tiles * CHUNK, BF16, LANES)],
        work + [pltpu.SemaphoreType.DMA],
        10**7,
        200000,
        hbm=1,
        out_places=[pltpu.HBM],
        aliases={0: 0},
    )(packed, *listed, sent)
    arrived = lax.all_to_all(packed, "tile", split_axis=0, concat_axis=0, tiled=True)

    message, near4 = kernel_call(
        relay_kernel,
        [spec(size + 4 * groups, BF16), spec(4 * groups)],
        [scratch(size), scratch(4 * groups)],
        1000,
        700000,
    )(held, mate, oth)
    nxt = across(message, 1)
    wide = groups * WIDE
    slim = groups * SLIM
    (
        edge0, u1x, d0x, d1x, f2x, field, final, wo, readout_held, gain_held, error_held, background_held,
    ) = kernel_call(
        forward_kernel,
        [spec(groups * 8), spec(slim)] + [spec(slim, BF16)] * 3
        + [spec(4 * lats * cols, F32, members * LANES), spec(size, BF16)]
        + [spec(channels, BF16), spec(channels, BF16, LANES), spec(1), spec(1), spec(size, BF16)],
        [scratch(wide), scratch(wide), scratch(wide, BF16, 2 * channels), scratch(wide, BF16)]
        + [scratch(wide), scratch(16), scratch(4 * size, BF16)]
        + [scratch(2 * channels, BF16), scratch(channels, BF16), pltpu.SemaphoreType.DMA((7,))],
        10**11,
        4000000,
        hbm=7,
    )(
        gain, self_weight, neighbour_weight, output_weight, readout, error, background.reshape(size, channels),
        held, near4, oth,
    )
    before = across(final, -1)
    total = tiles * CHUNK
    near_spread, *reports_held = kernel_call(
        functools.partial(observe_kernel, tiles),
        [spec(size, BF16, LANES), spec(32, BF16, total), spec(32, BF16, total), spec(32, F32, total)],
        [scratch(64, BF16, total), scratch(total, F32, LANES)],
        10**9,
        2000000,
    )(arrived, field)
    from_mate = lax.ppermute(near_spread, "tile", mate_of)
    handed = kernel_call(
        pull_kernel,
        [spec(2 * size), spec(size), spec(channels, BF16), spec(channels, BF16)],
        [scratch(128, BF16, total), scratch(2 * size, BF16, LANES), scratch(size, BF16, LANES)]
        + [pltpu.SemaphoreType.DMA((2,))],
        10**9,
        3000000,
        hbm=2,
    )(neighbour_weight, self_weight, readout_held, *reports_held, arrived, field)
    base = kernel_call(
        backward_kernel,
        spec(size),
        [scratch(slim), scratch(slim), scratch(slim, BF16), scratch(slim), scratch(slim)]
        + [scratch(size), scratch(16), scratch(slim), scratch(slim), scratch(size + 4 * groups)],
        12 * slim * channels * channels,
        6000000,
    )(
        *handed, gain_held, held, edge0, nxt, f2x, wo, readout_held, error_held, from_mate,
        u1x, d0x, d1x,
    )
    result = kernel_call(last_kernel, spec(size), [], 10**6, 900000)(base, background_held, before, error_held)
    return result.reshape(control.shape)


def solution(mesh):
    in_specs = (
        P("slot", None, None, "tile", None),
        P(None, None, "tile", None),
        P(),
        P(),
        P(),
        P(),
        P(),
        P(),
        P("slot", None, "tile", None),
        P("slot", None, "tile", None),
        P("slot", None, "tile", None),
        P("slot", None, "tile", None),
        P("slot", None, "tile"),
    )
    out_specs = P("slot", None, None, "tile", None)
    return jax.shard_map(
        per_device, mesh=mesh, in_specs=in_specs, out_specs=out_specs, check_vma=False
    )
```

```python
import functools
import jax
import jax.numpy as jnp
from jax import lax
from jax.experimental import pallas as pl
from jax.experimental.pallas import tpu as pltpu
from jax.sharding import PartitionSpec as P

EPSILON = 1e-06
F32 = jnp.float32
BF16 = jnp.bfloat16
LANES = 128
CAP = 5
SLOTS = 4 * CAP
CHUNK = 24
APART = 36
STRIDE = 32
WIDE = 40
SLIM = 24
VMEM_LIMIT = 28 * 1024 * 1024


def dot(a, b):
    return jnp.dot(a, b, preferred_element_type=F32)


def dot_t(a, b):
    return lax.dot_general(a, b, (((1,), (1,)), ((), ())), preferred_element_type=F32)


def sublane(shape):
    return lax.broadcasted_iota(jnp.int32, shape, 0)


def inverse_rms(x):
    return lax.rsqrt(jnp.mean(x * x, axis=-1, keepdims=True) + EPSILON)


def sigmoid(p):
    return 0.5 * jnp.tanh(0.5 * p) + 0.5


def neighbours(rows):
    width = rows[0].shape[0]
    return [
        0.25 * (rows[1 - i] + pltpu.roll(rows[i], 1, 0) + pltpu.roll(rows[i], width - 1, 0))
        for i in range(2)
    ]


def forward_step(u, n, act, pre, d, gain, weights, wo, width, members, out, copies=()):
    both = 2 * width
    for m in range(members):
        base = m * both
        rows = []
        for lat in range(2):
            x = u[base + lat * width : base + (lat + 1) * width]
            rows.append((x * inverse_rms(x) * gain).astype(BF16).astype(F32))
        channels = rows[0].shape[1]
        n[base : base + both, :channels] = jnp.concatenate(rows, axis=0).astype(BF16)
        n[base : base + both, channels:] = jnp.concatenate(neighbours(rows), axis=0).astype(BF16)
    for copy in copies[:2]:
        copy.wait()
    pre[...] = dot(n[...], weights[...])
    for m in range(members):
        base = m * both
        p = pre[base : base + both]
        sig = sigmoid(p)
        act[base : base + both] = (p * sig).astype(BF16)
        if d is not None:
            pre[base : base + both] = sig * (1.0 + p * (1.0 - sig))
    if d is not None:
        for m in range(members):
            slim_copy(d, pre, m)
    for copy in copies[2:]:
        copy.wait()
    pre[...] = dot(act[...], wo[...])
    for r in range(2 * members):
        out(r, u[r * width : (r + 1) * width] + pre[r * width : (r + 1) * width])


def slim_edge(wide, r):
    low = wide[r * WIDE + 16 : r * WIDE + 24]
    high = wide[r * WIDE + 32 : r * WIDE + 40]
    return jnp.where(sublane(low.shape) < 4, low, high)


def slim_copy(to, wide, m):
    parts = []
    for r in (2 * m, 2 * m + 1):
        parts += [wide[r * WIDE : r * WIDE + 16], slim_edge(wide, r)]
    both = jnp.concatenate(parts, axis=0)
    to[m * 2 * SLIM : (m + 1) * 2 * SLIM] = both.astype(to.dtype)


def reports(arrays, out_hbm, key, meta, picked, out, sem):
    pack(*arrays, out, key, meta, picked)
    store = pltpu.make_async_copy(out, out_hbm, sem)
    store.start()
    store.wait()


def early():
    return lax.axis_index("tile") < lax.axis_size("tile") // 2


def first_kernel(control_hbm, *refs):
    sources, (held, out_hbm), arrays, (key, meta, picked, out, sems) = refs[:5], refs[5:7], refs[7:12], refs[12:]
    copies = [
        pltpu.make_async_copy(source, to, sems.at[i]) for i, (source, to) in enumerate(zip(sources, arrays))
    ]
    copies.append(pltpu.make_async_copy(control_hbm, held, sems.at[5]))
    for copy in copies:
        copy.start()
    for copy in copies[:5]:
        copy.wait()

    @pl.when(early())
    def _():
        reports(arrays, out_hbm, key, meta, picked, out, sems.at[6])

    copies[5].wait()


def later_kernel(packed_hbm, *refs):
    arrays, out_hbm, (key, meta, picked, out, sem) = refs[:5], refs[6], refs[7:]

    @pl.when(jnp.logical_not(early()))
    def _():
        reports(arrays, out_hbm, key, meta, picked, out, sem)


def fan(x, shift):
    if shift % LANES:
        x = pltpu.roll(x, shift % LANES, 1)
    for _ in range(2):
        x = pltpu.roll(x, 0, 1, stride=APART // 2, stride_axis=0)
    return x


def pack(owner, stencil, weights, precision, values, out, key, meta, picked):
    steps, _, rows = owner.shape
    tiles = out.shape[0] // CHUNK
    total = steps * rows
    earlier = lax.broadcasted_iota(jnp.int32, (rows, rows), 0) < lax.broadcasted_iota(jnp.int32, (rows, rows), 1)
    earlier = earlier.astype(F32).astype(BF16)
    meta[...] = jnp.zeros_like(meta)
    for k in range(steps):
        at = slice(k * rows, (k + 1) * rows)
        named = lax.broadcasted_iota(jnp.int32, (tiles, rows), 0) == owner[k]
        hits = named.astype(F32)
        before = dot(hits.astype(BF16), earlier)
        rank = jnp.sum(hits * before, axis=0, keepdims=True).astype(jnp.int32)
        key[0:1, at] = owner[k] * (2 * CAP) + k * CAP + rank
        for i in range(4):
            meta[i // 3 * 8 + i % 3 : i // 3 * 8 + i % 3 + 1, at] = stencil[k, i : i + 1].astype(F32)
            j = 4 + i
            meta[j // 3 * 8 + j % 3 : j // 3 * 8 + j % 3 + 1, at] = weights[k, i : i + 1].astype(F32)
        meta[18:19, at] = precision[k : k + 1].astype(F32)
    row = lax.broadcasted_iota(jnp.int32, (tiles * STRIDE, total), 0)
    tile = row // STRIDE
    slot = row % STRIDE
    other = jnp.where(tile % 2 == 0, (tile + tiles - 1) % tiles, (tile + 1) % tiles)
    mine = slot < 2 * CAP
    wanted = jnp.where(mine, tile * (2 * CAP) + slot, other * (2 * CAP) + slot - 2 * CAP)
    wanted = jnp.where(slot < SLOTS, wanted, -1)
    placement = (wanted == key[...]).astype(F32).astype(BF16)
    placed = dot(placement, values[...])
    entries = dot_t(meta[...].astype(BF16), placement)
    lane = lax.broadcasted_iota(jnp.int32, (24, LANES), 1)
    turn = lax.axis_index("tile") * CHUNK % LANES
    per_tile = LANES // STRIDE
    for t in range(tiles):
        picked[t * CHUNK : (t + 1) * CHUNK] = placed[t * STRIDE : t * STRIDE + CHUNK]
        start = t % per_tile * STRIDE
        used = jnp.logical_and(lane >= start, lane < start + SLOTS)
        block = jnp.where(used, entries[:, t // per_tile * LANES : (t // per_tile + 1) * LANES], 0.0)
        for j in range(3):
            laid = fan(block[j * 8 : (j + 1) * 8], LANES - start)
            row = t * CHUNK + SLOTS + j
            picked[row : row + 1] = jnp.sum(laid, axis=0, keepdims=True)
        group = picked[t * CHUNK + 16 : (t + 1) * CHUNK]
        picked[t * CHUNK + 16 : (t + 1) * CHUNK] = jnp.where(sublane((8, 1)) < 4, group, pltpu.roll(group, turn, 1))
    out[...] = picked[...].astype(BF16)


def tile_kernel(control, mate, out, held):
    even = lax.rem(lax.axis_index("tile"), 2) == 0
    size = control.shape[0]
    out[0:size] = control[...].astype(BF16)
    for r in range(size // 16):
        held[r * 2 : (r + 1) * 2] = jnp.where(
            even, mate[r * 16 : r * 16 + 2], mate[r * 16 + 14 : (r + 1) * 16]
        )
    out[size:] = held[...].astype(BF16)


def relay_kernel(control, mate, oth, out, near4, wide, edge):
    even = lax.rem(lax.axis_index("tile"), 2) == 0
    size = mate.shape[0]
    out[0:size] = control[...].astype(BF16)
    wide[...] = oth[0:size].astype(F32)
    for r in range(size // 16):
        a, b = r * 16, (r + 1) * 16
        edge[r * 2 : (r + 1) * 2] = jnp.where(even, wide[b - 2 : b], wide[a : a + 2])
        near4[r * 4 : (r + 1) * 4] = jnp.where(even, mate[a : a + 4], mate[b - 4 : b])
        start = size // 8 + r * 2
        edge[start : start + 2] = jnp.where(even, mate[a : a + 2], mate[b - 2 : b])
    out[size:] = edge[...].astype(BF16)


def forward_kernel(
    gain_hbm, ws_hbm, wn_hbm, wo_hbm, readout_hbm, error_hbm, background_hbm, control, mate, oth,
    edge0, u1x, d0x, d1x, f2x, field, final, wo, readout, gain, error, background,
    ua, ub, n, act, pre, edge, states, weights, sems,
):
    channels = wo.shape[0]
    halves = weights.at[pl.ds(0, channels)], weights.at[pl.ds(channels, channels)]
    pairs = (
        (gain_hbm, gain), (ws_hbm, halves[0]), (wn_hbm, halves[1]), (wo_hbm, wo), (readout_hbm, readout),
        (error_hbm, error), (background_hbm, background),
    )
    copies = [pltpu.make_async_copy(source, to, sems.at[i]) for i, (source, to) in enumerate(pairs)]
    for copy in copies:
        copy.start()
    members = final.shape[0] // 32
    even = lax.rem(lax.axis_index("tile"), 2) == 0
    tile_at = jnp.where(even, 24, 16)
    edge_at = jnp.where(even, 16, 32)
    far = oth[members * 32 :].astype(F32)
    for r in range(2 * members):
        ua[r * WIDE : r * WIDE + 16] = control[r * 16 : (r + 1) * 16]
        ua[pl.ds(pl.multiple_of(r * WIDE + tile_at, 8), 16)] = oth[r * 16 : (r + 1) * 16].astype(F32)
        near4 = mate[r * 4 : (r + 1) * 4]
        far2 = far[r * 2 : (r + 1) * 2]
        edge[...] = jnp.zeros_like(edge)
        edge[0:4] = near4
        edge[6:8] = far2
        edge[8:10] = far2
        edge[12:16] = near4
        ua[pl.ds(pl.multiple_of(r * WIDE + edge_at, 8), 8)] = jnp.where(even, edge[0:8], edge[8:16])
    for r in range(2 * members):
        edge0[r * 8 : (r + 1) * 8] = slim_edge(ua, r)
    copies[0].wait()
    g = gain[...]

    def keep(ref):
        def store(r, value):
            ref[r * WIDE : (r + 1) * WIDE] = value

        return store

    def keep_states(ref, k):
        own = k * members * 32
        away = (2 + k) * members * 32
        for r in range(2 * members):
            states[own + r * 16 : own + (r + 1) * 16] = ref[r * WIDE : r * WIDE + 16].astype(BF16)
            taken = ref[pl.ds(pl.multiple_of(r * WIDE + tile_at, 8), 16)]
            states[away + r * 16 : away + (r + 1) * 16] = taken.astype(BF16)

    forward_step(ua, n, act, pre, d0x, g, weights, wo, WIDE, members, keep(ub), copies[1:])
    for m in range(members):
        slim_copy(u1x, ub, m)
    keep_states(ub, 0)
    forward_step(ub, n, act, pre, d1x, g, weights, wo, WIDE, members, keep(ua))
    for m in range(members):
        slim_copy(f2x, ua, m)
    keep_states(ua, 1)
    final[...] = states[members * 32 : 2 * members * 32]
    read = dot(states[...], readout[...])
    for q in range(4):
        for m in range(members):
            start = (q * members + m) * 32
            at = slice(m * LANES, (m + 1) * LANES)
            field[q * 32 : (q + 1) * 32, at], field[LANES + q * 32 : LANES + (q + 1) * 32, at] = split(
                read[start : start + 32]
            )


def split(x):
    high = x.astype(BF16)
    return high, (x - high.astype(F32)).astype(BF16)


def spread_of(first, th, tl, scaled, taken, field, pp, spread):
    lane = lax.broadcasted_iota(jnp.int32, (1, LANES), 1)
    members = field.shape[1] // LANES
    for p in range(th.shape[1] // LANES):
        at = slice(p * LANES, (p + 1) * LANES)
        slot = (lane + p * LANES) % CHUNK
        table_of = jnp.where(slot < SLOTS, slot // CAP, -1)
        for q in range(2):
            kept = jnp.where(table_of == first + q, scaled[:, at], 0.0)
            pp[q * 32 : (q + 1) * 32, at], pp[64 + q * 32 : 96 + q * 32, at] = split(kept)
    cross = dot_t(pp[...], th[...])
    cross = cross[:64] + cross[64:] + dot_t(pp[0:64], tl[...])
    block = jnp.concatenate([cross] * 2, axis=1)
    on_block = sublane(block.shape) // 32 == lax.broadcasted_iota(jnp.int32, block.shape, 1) // 32
    target = dot(pp[...], taken[...])
    target = target[:64] + target[64:]
    ch, cl = split(jnp.where(on_block, block, 0.0))
    high = field[first * 32 : (first + 2) * 32]
    low = field[LANES + first * 32 : LANES + (first + 2) * 32]
    mixed = dot(jnp.concatenate([ch, cl], axis=0), high)
    mixed = mixed[:64] + mixed[64:] + dot(ch, low)
    for q in range(2):
        for m in range(members):
            start = (q * members + m) * 32
            value = mixed[q * 32 : (q + 1) * 32, m * LANES : (m + 1) * LANES] - target[q * 32 : (q + 1) * 32]
            spread[start : start + 32] = value.astype(BF16)


def observe_kernel(
    tiles, arrived, field,
    spread, message, th, tl, scaled,
    pp,
):
    steps = 2
    members = field.shape[1] // LANES
    even = lax.rem(lax.axis_index("tile"), 2) == 0
    cells = sublane((32, LANES)).astype(F32)
    lane = lax.broadcasted_iota(jnp.int32, (8, LANES), 1)
    packs = th.shape[1] // LANES
    sums = [[jnp.zeros((8, LANES), F32)] * 3 for _ in range(packs)]
    for d in range(tiles):
        p, start = divmod(d * CHUNK, LANES)
        window = (d * CHUNK + 16) // 16 * 16
        group = arrived[window : window + 16].astype(F32)
        group = group[8:] if d % 2 else group[:8]
        for b in range(3):
            first = start + b * APART
            place = lane - first % LANES
            place = jnp.where(place < 0, place + LANES, place)
            ends = min(LANES - start, SLOTS)
            sums[p][b] = sums[p][b] + jnp.where(place < ends, group, 0.0)
            if ends < SLOTS:
                rest = jnp.logical_and(place >= ends, place < SLOTS)
                sums[p + 1][b] = sums[p + 1][b] + jnp.where(rest, group, 0.0)
    for p in range(packs):
        kinds = [pltpu.roll(sums[p][b], (LANES - b * APART) % LANES, 1) if b else sums[p][b] for b in range(3)]
        entry = [kinds[i % 3][4 + i // 3 : 5 + i // 3] for i in range(9)]
        weight = jnp.zeros((32, LANES), F32)
        for i in range(4):
            weight += jnp.where(cells == entry[i], entry[4 + i], 0.0)
        at = slice(p * LANES, (p + 1) * LANES)
        th[:, at], tl[:, at] = split(weight)
        scaled[:, at] = weight * entry[8]
    spread_of(0, th, tl, scaled, arrived, field, pp, spread)
    size = members * 32
    for k in range(steps):
        for m in range(members):
            start = k * size + m * 32
            pair = spread[start : start + 32].astype(F32)
            near = [jnp.where(even, pair[i + 8 : i + 16], pair[i : i + 8]) for i in (0, 16)]
            start = k * size // 2 + m * 16
            message[start : start + 16] = jnp.concatenate(near, axis=0).astype(BF16)


def adjoint_step(u, cot, gb, gm, flat, d, out, gain, ws, wn, wo, members):
    both = 2 * SLIM
    gb[...] = cot[...].astype(BF16)
    flat[...] = dot_t(gb[...], wo[...])
    gb[...] = (flat[...] * d[...]).astype(BF16)
    gm[...] = dot_t(gb[...], wn[...])
    flat[...] = dot_t(gb[...], ws[...])
    for m in range(members):
        base = m * both
        rows = []
        for lat in range(2):
            start = base + lat * SLIM
            rows.append(gm[start : start + SLIM].astype(BF16).astype(F32))
        around = neighbours(rows)
        for lat in range(2):
            start = base + lat * SLIM
            x = u[start : start + SLIM]
            s = inverse_rms(x)
            scaled = gain * (flat[start : start + SLIM] + around[lat])
            inner = jnp.mean(x * scaled, axis=-1, keepdims=True)
            out(2 * m + lat, cot[start : start + SLIM] + s * scaled - x * (s * s * s * inner))


def edges(nxt, size, edge, r):
    even = lax.rem(lax.axis_index("tile"), 2) == 0
    start = size + r * 2
    far = nxt[start : start + 2]
    start = size + size // 8 + r * 2
    near = nxt[start : start + 2]
    edge[...] = jnp.zeros_like(edge)
    edge[0:2] = near
    edge[6:8] = far
    edge[8:10] = far
    edge[14:16] = near
    return jnp.where(even, edge[0:8], edge[8:16])


def pull_kernel(
    wn_hbm, ws_hbm, spread_own, readout, th, tl, scaled, arrived, field,
    pulled, away, wn, ws,
    pp, spread, near, sems,
):
    pairs = ((wn_hbm, wn), (ws_hbm, ws))
    copies = [pltpu.make_async_copy(source, to, sems.at[i]) for i, (source, to) in enumerate(pairs)]
    for copy in copies:
        copy.start()
    even = lax.rem(lax.axis_index("tile"), 2) == 0
    pulled[...] = dot_t(spread_own[...], readout[...])
    spread_of(2, th, tl, scaled, arrived, field, pp, spread)
    for start in range(0, spread.shape[0], 32):
        pair = spread[start : start + 32].astype(F32)
        rows = [jnp.where(even, pair[i + 8 : i + 16], pair[i : i + 8]) for i in (0, 16)]
        near[start // 2 : start // 2 + 16] = jnp.concatenate(rows, axis=0).astype(BF16)
    away[...] = dot_t(near[...], readout[...])
    for copy in copies:
        copy.wait()


def backward_kernel(
    pulled, away, wn, ws, gain, control, edge0, message16, f2x, wo, readout, error, message,
    u1x, d0x, d1x,
    result,
    cot2, cot1, gb, gm, flat, mate_pull, edge, u0x, final, nxt,
):
    size = result.shape[0]
    members = size // 32
    even = lax.rem(lax.axis_index("tile"), 2) == 0
    nxt[...] = message16[...].astype(F32)
    weight = jnp.where(lax.axis_index("slot") == lax.axis_size("slot") - 1, 0.0, 1.0) * error[...]
    row8 = sublane((8, 1))
    mate_side = jnp.where(even, 1, 0) == jnp.where(row8 < 4, 1, 0)
    mate_pull[...] = dot_t(message[...], readout[...])
    final[...] = f2x[...].astype(F32)

    def pulls(k, r):
        own = k * size + r * 16
        near = k * size // 2 + r * 8
        group = jnp.where(mate_side, mate_pull[near : near + 8], away[near : near + 8])
        return pulled[own : own + 16], group

    for r in range(2 * members):
        own, group = pulls(1, r)
        a, b = r * SLIM, r * SLIM + 16
        cot2[a:b] = own - weight * (nxt[r * 16 : (r + 1) * 16] - final[a:b])
        u0x[a:b] = control[r * 16 : (r + 1) * 16]
        a, b = b, b + 8
        cot2[a:b] = group - weight * (edges(nxt, size, edge, r) - final[a:b])
        u0x[a:b] = edge0[r * 8 : (r + 1) * 8]

    def keep(r, value):
        cot1[r * SLIM : (r + 1) * SLIM] = value + jnp.concatenate(pulls(0, r), axis=0)

    def finish(r, value):
        a, b = r * SLIM, r * SLIM + 16
        result[r * 16 : (r + 1) * 16] = value[0:16] + error[...] * u0x[a:b]

    adjoint_step(u1x, cot2, gb, gm, flat, d1x, keep, gain[...], ws, wn, wo, members)
    adjoint_step(u0x, cot1, gb, gm, flat, d0x, finish, gain[...], ws, wn, wo, members)


def last_kernel(base, background, before, error, result):
    first = lax.axis_index("slot") == 0
    taken = jnp.where(first, background[...].astype(F32), before[...].astype(F32))
    result[...] = base[...] - error[...] * taken


def kernel_call(body, outs, scratch, flops, moved, hbm=0, out_places=None, aliases={}):
    def call(*operands):
        fixed = [i in range(hbm) and i not in aliases for i in range(len(operands))]
        operands = [
            pltpu.with_memory_space_constraint(x, pltpu.HBM) if fix else x for x, fix in zip(operands, fixed)
        ]
        places = [pltpu.HBM] * hbm + [pltpu.VMEM] * (len(operands) - hbm)
        given = {} if out_places is None else {"out_specs": [pl.BlockSpec(memory_space=p) for p in out_places]}
        return pl.pallas_call(
            body,
            out_shape=outs,
            in_specs=[pl.BlockSpec(memory_space=place) for place in places],
            **given,
            scratch_shapes=scratch,
            input_output_aliases=aliases,
            compiler_params=pltpu.CompilerParams(vmem_limit_bytes=VMEM_LIMIT),
            cost_estimate=pl.CostEstimate(flops=flops, bytes_accessed=moved, transcendentals=0),
        )(*operands)

    return call


def per_device(
    control,
    background,
    self_weight,
    neighbour_weight,
    output_weight,
    norm_gain,
    readout,
    error_weight,
    report_owner,
    report_stencil,
    report_weights,
    report_values,
    report_precision,
):
    tiles = lax.axis_size("tile")
    slots = lax.axis_size("slot")
    members, lats, cols, channels = control.shape[1:]
    groups = members * lats
    size = groups * cols
    steps = report_owner.shape[1]
    rows = report_owner.shape[2]
    gain = norm_gain.reshape(1, channels)
    error = error_weight.reshape(1, channels)
    flat = control.reshape(size, channels)

    def spec(count, dtype=F32, width=channels):
        return jax.ShapeDtypeStruct((count, width), dtype)

    def scratch(count, dtype=F32, width=channels):
        return pltpu.VMEM((count, width), dtype)

    mate_of = [(i, i ^ 1) for i in range(tiles)]
    other_of = [(i, (i - 1) % tiles if i % 2 == 0 else (i + 1) % tiles) for i in range(tiles)]

    def across(block, shift):
        pairs = [
            ((s + shift) % slots * tiles + i, s * tiles + i) for s in range(slots) for i in range(tiles)
        ]
        return lax.ppermute(block, ("slot", "tile"), pairs)

    mate = lax.ppermute(flat, "tile", mate_of)
    listed = (
        jnp.transpose(report_owner[0], (0, 2, 1)),
        jnp.transpose(report_stencil[0], (0, 2, 1)),
        jnp.transpose(report_weights[0], (0, 2, 1)),
        report_precision[0],
        report_values[0].reshape(steps * rows, LANES),
    )
    work = [
        pltpu.VMEM((1, steps * rows), jnp.int32),
        scratch(24, F32, steps * rows),
        scratch(tiles * CHUNK, F32, LANES),
        scratch(tiles * CHUNK, BF16, LANES),
    ]
    held, packed, *listed = kernel_call(
        first_kernel,
        [spec(size), spec(tiles * CHUNK, BF16, LANES)]
        + [jax.ShapeDtypeStruct(block.shape, block.dtype) for block in listed],
        work + [pltpu.SemaphoreType.DMA((7,))],
        10**7,
        200000,
        hbm=6,
        out_places=[pltpu.VMEM, pltpu.HBM] + [pltpu.VMEM] * 5,
    )(flat, *listed)
    sent = kernel_call(
        tile_kernel, spec(groups * (cols + 2), BF16), [scratch(groups * 2)], 1000, 400000
    )(held, mate)
    oth = lax.ppermute(sent, "tile", other_of)
    (packed,) = kernel_call(
        later_kernel,
        [spec(tiles * CHUNK, BF16, LANES)],
        work + [pltpu.SemaphoreType.DMA],
        10**7,
        200000,
        hbm=1,
        out_places=[pltpu.HBM],
        aliases={0: 0},
    )(packed, *listed, sent)
    arrived = lax.all_to_all(packed, "tile", split_axis=0, concat_axis=0, tiled=True)

    message, near4 = kernel_call(
        relay_kernel,
        [spec(size + 4 * groups, BF16), spec(4 * groups)],
        [scratch(size), scratch(4 * groups)],
        1000,
        700000,
    )(held, mate, oth)
    nxt = across(message, 1)
    wide = groups * WIDE
    slim = groups * SLIM
    (
        edge0, u1x, d0x, d1x, f2x, field, final, wo, readout_held, gain_held, error_held, background_held,
    ) = kernel_call(
        forward_kernel,
        [spec(groups * 8), spec(slim)] + [spec(slim, BF16)] * 3
        + [spec(8 * lats * cols, BF16, members * LANES), spec(size, BF16)]
        + [spec(channels, BF16), spec(channels, BF16, LANES), spec(1), spec(1), spec(size, BF16)],
        [scratch(wide), scratch(wide), scratch(wide, BF16, 2 * channels), scratch(wide, BF16)]
        + [scratch(wide), scratch(16), scratch(4 * size, BF16)]
        + [scratch(2 * channels, BF16), pltpu.SemaphoreType.DMA((7,))],
        10**11,
        4000000,
        hbm=7,
    )(
        gain, self_weight, neighbour_weight, output_weight, readout, error, background.reshape(size, channels),
        held, near4, oth,
    )
    before = across(final, -1)
    total = tiles * CHUNK
    tables = [scratch(128, BF16, total)]
    spread, near_spread, *reports_held = kernel_call(
        functools.partial(observe_kernel, tiles),
        [spec(2 * size, BF16, LANES), spec(size, BF16, LANES)]
        + [spec(32, BF16, total), spec(32, BF16, total), spec(32, F32, total)],
        tables,
        10**9,
        2000000,
    )(arrived, field)
    from_mate = lax.ppermute(near_spread, "tile", mate_of)
    handed = kernel_call(
        pull_kernel,
        [spec(2 * size), spec(size), spec(channels, BF16), spec(channels, BF16)],
        tables + [scratch(2 * size, BF16, LANES), scratch(size, BF16, LANES), pltpu.SemaphoreType.DMA((2,))],
        10**9,
        3000000,
        hbm=2,
    )(neighbour_weight, self_weight, spread, readout_held, *reports_held, arrived, field)
    base = kernel_call(
        backward_kernel,
        spec(size),
        [scratch(slim), scratch(slim), scratch(slim, BF16), scratch(slim), scratch(slim)]
        + [scratch(size), scratch(16), scratch(slim), scratch(slim), scratch(size + 4 * groups)],
        12 * slim * channels * channels,
        6000000,
    )(
        *handed, gain_held, held, edge0, nxt, f2x, wo, readout_held, error_held, from_mate,
        u1x, d0x, d1x,
    )
    result = kernel_call(last_kernel, spec(size), [], 10**6, 900000)(base, background_held, before, error_held)
    return result.reshape(control.shape)


def solution(mesh):
    in_specs = (
        P("slot", None, None, "tile", None),
        P(None, None, "tile", None),
        P(),
        P(),
        P(),
        P(),
        P(),
        P(),
        P("slot", None, "tile", None),
        P("slot", None, "tile", None),
        P("slot", None, "tile", None),
        P("slot", None, "tile", None),
        P("slot", None, "tile"),
    )
    out_specs = P("slot", None, None, "tile", None)
    return jax.shard_map(
        per_device, mesh=mesh, in_specs=in_specs, out_specs=out_specs, check_vma=False
    )
```

```python
import functools
import jax
import jax.numpy as jnp
from jax import lax
from jax.experimental import pallas as pl
from jax.experimental.pallas import tpu as pltpu
from jax.sharding import PartitionSpec as P

EPSILON = 1e-06
F32 = jnp.float32
BF16 = jnp.bfloat16
LANES = 128
CAP = 5
SLOTS = 4 * CAP
CHUNK = 24
APART = 36
STRIDE = 32
WIDE = 40
SLIM = 24
VMEM_LIMIT = 28 * 1024 * 1024


def dot(a, b):
    return jnp.dot(a, b, preferred_element_type=F32)


def dot_t(a, b):
    return lax.dot_general(a, b, (((1,), (1,)), ((), ())), preferred_element_type=F32)


def sublane(shape):
    return lax.broadcasted_iota(jnp.int32, shape, 0)


def inverse_rms(x):
    return lax.rsqrt(jnp.mean(x * x, axis=-1, keepdims=True) + EPSILON)


def sigmoid(p):
    return 0.5 * jnp.tanh(0.5 * p) + 0.5


def neighbours(rows):
    width = rows[0].shape[0]
    return [
        0.25 * (rows[1 - i] + pltpu.roll(rows[i], 1, 0) + pltpu.roll(rows[i], width - 1, 0))
        for i in range(2)
    ]


def forward_step(u, n, act, pre, d, gain, weights, wo, width, members, out, copies=()):
    both = 2 * width
    for m in range(members):
        base = m * both
        rows = []
        for lat in range(2):
            x = u[base + lat * width : base + (lat + 1) * width]
            rows.append((x * inverse_rms(x) * gain).astype(BF16).astype(F32))
        channels = rows[0].shape[1]
        n[base : base + both, :channels] = jnp.concatenate(rows, axis=0).astype(BF16)
        n[base : base + both, channels:] = jnp.concatenate(neighbours(rows), axis=0).astype(BF16)
    for copy in copies[:2]:
        copy.wait()
    pre[...] = dot(n[...], weights[...])
    for m in range(members):
        base = m * both
        p = pre[base : base + both]
        sig = sigmoid(p)
        act[base : base + both] = (p * sig).astype(BF16)
        if d is not None:
            pre[base : base + both] = sig * (1.0 + p * (1.0 - sig))
    if d is not None:
        for m in range(members):
            slim_copy(d, pre, m)
    for copy in copies[2:]:
        copy.wait()
    pre[...] = dot(act[...], wo[...])
    for r in range(2 * members):
        out(r, u[r * width : (r + 1) * width] + pre[r * width : (r + 1) * width])


def slim_edge(wide, r):
    low = wide[r * WIDE + 16 : r * WIDE + 24]
    high = wide[r * WIDE + 32 : r * WIDE + 40]
    return jnp.where(sublane(low.shape) < 4, low, high)


def slim_copy(to, wide, m):
    parts = []
    for r in (2 * m, 2 * m + 1):
        parts += [wide[r * WIDE : r * WIDE + 16], slim_edge(wide, r)]
    both = jnp.concatenate(parts, axis=0)
    to[m * 2 * SLIM : (m + 1) * 2 * SLIM] = both.astype(to.dtype)


def reports(arrays, out_hbm, key, meta, picked, out, sem):
    pack(*arrays, out, key, meta, picked)
    store = pltpu.make_async_copy(out, out_hbm, sem)
    store.start()
    store.wait()


def early():
    return lax.axis_index("tile") < lax.axis_size("tile") // 2


def first_kernel(control_hbm, *refs):
    sources, (held, out_hbm), arrays, (key, meta, picked, out, sems) = refs[:5], refs[5:7], refs[7:12], refs[12:]
    copies = [
        pltpu.make_async_copy(source, to, sems.at[i]) for i, (source, to) in enumerate(zip(sources, arrays))
    ]
    copies.append(pltpu.make_async_copy(control_hbm, held, sems.at[5]))
    for copy in copies:
        copy.start()
    for copy in copies[:5]:
        copy.wait()

    @pl.when(early())
    def _():
        reports(arrays, out_hbm, key, meta, picked, out, sems.at[6])

    copies[5].wait()


def later_kernel(packed_hbm, *refs):
    arrays, out_hbm, (key, meta, picked, out, sem) = refs[:5], refs[6], refs[7:]

    @pl.when(jnp.logical_not(early()))
    def _():
        reports(arrays, out_hbm, key, meta, picked, out, sem)


def fan(x, shift):
    if shift % LANES:
        x = pltpu.roll(x, shift % LANES, 1)
    for _ in range(2):
        x = pltpu.roll(x, 0, 1, stride=APART // 2, stride_axis=0)
    return x


def pack(owner, stencil, weights, precision, values, out, key, meta, picked):
    steps, _, rows = owner.shape
    tiles = out.shape[0] // CHUNK
    total = steps * rows
    earlier = lax.broadcasted_iota(jnp.int32, (rows, rows), 0) < lax.broadcasted_iota(jnp.int32, (rows, rows), 1)
    earlier = earlier.astype(F32).astype(BF16)
    meta[...] = jnp.zeros_like(meta)
    for k in range(steps):
        at = slice(k * rows, (k + 1) * rows)
        named = lax.broadcasted_iota(jnp.int32, (tiles, rows), 0) == owner[k]
        hits = named.astype(F32)
        before = dot(hits.astype(BF16), earlier)
        rank = jnp.sum(hits * before, axis=0, keepdims=True).astype(jnp.int32)
        key[0:1, at] = owner[k] * (2 * CAP) + k * CAP + rank
        for i in range(4):
            meta[i // 3 * 8 + i % 3 : i // 3 * 8 + i % 3 + 1, at] = stencil[k, i : i + 1].astype(F32)
            j = 4 + i
            meta[j // 3 * 8 + j % 3 : j // 3 * 8 + j % 3 + 1, at] = weights[k, i : i + 1].astype(F32)
        meta[18:19, at] = precision[k : k + 1].astype(F32)
    row = lax.broadcasted_iota(jnp.int32, (tiles * STRIDE, total), 0)
    tile = row // STRIDE
    slot = row % STRIDE
    other = jnp.where(tile % 2 == 0, (tile + tiles - 1) % tiles, (tile + 1) % tiles)
    mine = slot < 2 * CAP
    wanted = jnp.where(mine, tile * (2 * CAP) + slot, other * (2 * CAP) + slot - 2 * CAP)
    wanted = jnp.where(slot < SLOTS, wanted, -1)
    placement = (wanted == key[...]).astype(F32).astype(BF16)
    placed = dot(placement, values[...])
    entries = dot_t(meta[...].astype(BF16), placement)
    lane = lax.broadcasted_iota(jnp.int32, (24, LANES), 1)
    turn = lax.axis_index("tile") * CHUNK % LANES
    per_tile = LANES // STRIDE
    for t in range(tiles):
        picked[t * CHUNK : (t + 1) * CHUNK] = placed[t * STRIDE : t * STRIDE + CHUNK]
        start = t % per_tile * STRIDE
        used = jnp.logical_and(lane >= start, lane < start + SLOTS)
        block = jnp.where(used, entries[:, t // per_tile * LANES : (t // per_tile + 1) * LANES], 0.0)
        for j in range(3):
            laid = fan(block[j * 8 : (j + 1) * 8], LANES - start)
            row = t * CHUNK + SLOTS + j
            picked[row : row + 1] = jnp.sum(laid, axis=0, keepdims=True)
        group = picked[t * CHUNK + 16 : (t + 1) * CHUNK]
        picked[t * CHUNK + 16 : (t + 1) * CHUNK] = jnp.where(sublane((8, 1)) < 4, group, pltpu.roll(group, turn, 1))
    out[...] = picked[...].astype(BF16)


def tile_kernel(control, mate, out, held):
    even = lax.rem(lax.axis_index("tile"), 2) == 0
    size = control.shape[0]
    out[0:size] = control[...].astype(BF16)
    for r in range(size // 16):
        held[r * 2 : (r + 1) * 2] = jnp.where(
            even, mate[r * 16 : r * 16 + 2], mate[r * 16 + 14 : (r + 1) * 16]
        )
    out[size:] = held[...].astype(BF16)


def relay_kernel(control, mate, oth, out, near4, wide, edge):
    even = lax.rem(lax.axis_index("tile"), 2) == 0
    size = mate.shape[0]
    out[0:size] = control[...].astype(BF16)
    wide[...] = oth[0:size].astype(F32)
    for r in range(size // 16):
        a, b = r * 16, (r + 1) * 16
        edge[r * 2 : (r + 1) * 2] = jnp.where(even, wide[b - 2 : b], wide[a : a + 2])
        near4[r * 4 : (r + 1) * 4] = jnp.where(even, mate[a : a + 4], mate[b - 4 : b])
        start = size // 8 + r * 2
        edge[start : start + 2] = jnp.where(even, mate[a : a + 2], mate[b - 2 : b])
    out[size:] = edge[...].astype(BF16)


def forward_kernel(
    gain_hbm, ws_hbm, wn_hbm, wo_hbm, readout_hbm, error_hbm, background_hbm, control, mate, oth,
    edge0, u1x, d0x, d1x, f2x, field, final, wo, readout, gain, error, background,
    ua, ub, n, act, pre, edge, states, weights, sems,
):
    channels = wo.shape[0]
    halves = weights.at[pl.ds(0, channels)], weights.at[pl.ds(channels, channels)]
    pairs = (
        (gain_hbm, gain), (ws_hbm, halves[0]), (wn_hbm, halves[1]), (wo_hbm, wo), (readout_hbm, readout),
        (error_hbm, error), (background_hbm, background),
    )
    copies = [pltpu.make_async_copy(source, to, sems.at[i]) for i, (source, to) in enumerate(pairs)]
    for copy in copies:
        copy.start()
    members = final.shape[0] // 32
    even = lax.rem(lax.axis_index("tile"), 2) == 0
    tile_at = jnp.where(even, 24, 16)
    edge_at = jnp.where(even, 16, 32)
    far = oth[members * 32 :].astype(F32)
    for r in range(2 * members):
        ua[r * WIDE : r * WIDE + 16] = control[r * 16 : (r + 1) * 16]
        ua[pl.ds(pl.multiple_of(r * WIDE + tile_at, 8), 16)] = oth[r * 16 : (r + 1) * 16].astype(F32)
        near4 = mate[r * 4 : (r + 1) * 4]
        far2 = far[r * 2 : (r + 1) * 2]
        edge[...] = jnp.zeros_like(edge)
        edge[0:4] = near4
        edge[6:8] = far2
        edge[8:10] = far2
        edge[12:16] = near4
        ua[pl.ds(pl.multiple_of(r * WIDE + edge_at, 8), 8)] = jnp.where(even, edge[0:8], edge[8:16])
    for r in range(2 * members):
        edge0[r * 8 : (r + 1) * 8] = slim_edge(ua, r)
    copies[0].wait()
    g = gain[...]

    def keep(ref):
        def store(r, value):
            ref[r * WIDE : (r + 1) * WIDE] = value

        return store

    def keep_states(ref, k):
        own = k * members * 32
        away = (2 + k) * members * 32
        for r in range(2 * members):
            states[own + r * 16 : own + (r + 1) * 16] = ref[r * WIDE : r * WIDE + 16].astype(BF16)
            taken = ref[pl.ds(pl.multiple_of(r * WIDE + tile_at, 8), 16)]
            states[away + r * 16 : away + (r + 1) * 16] = taken.astype(BF16)

    forward_step(ua, n, act, pre, d0x, g, weights, wo, WIDE, members, keep(ub), copies[1:])
    for m in range(members):
        slim_copy(u1x, ub, m)
    keep_states(ub, 0)
    forward_step(ub, n, act, pre, d1x, g, weights, wo, WIDE, members, keep(ua))
    for m in range(members):
        slim_copy(f2x, ua, m)
    keep_states(ua, 1)
    final[...] = states[members * 32 : 2 * members * 32]
    read = dot(states[...], readout[...])
    for q in range(4):
        for m in range(members):
            start = (q * members + m) * 32
            at = slice(m * LANES, (m + 1) * LANES)
            field[q * 32 : (q + 1) * 32, at], field[LANES + q * 32 : LANES + (q + 1) * 32, at] = split(
                read[start : start + 32]
            )


def split(x):
    high = x.astype(BF16)
    return high, (x - high.astype(F32)).astype(BF16)


def spread_of(first, th, tl, scaled, taken, field, pp, spread):
    lane = lax.broadcasted_iota(jnp.int32, (1, LANES), 1)
    members = field.shape[1] // LANES
    for p in range(th.shape[1] // LANES):
        at = slice(p * LANES, (p + 1) * LANES)
        slot = (lane + p * LANES) % CHUNK
        table_of = jnp.where(slot < SLOTS, slot // CAP, -1)
        for q in range(2):
            kept = jnp.where(table_of == first + q, scaled[:, at], 0.0)
            pp[q * 32 : (q + 1) * 32, at], pp[64 + q * 32 : 96 + q * 32, at] = split(kept)
    cross = dot_t(pp[...], th[...])
    cross = cross[:64] + cross[64:] + dot_t(pp[0:64], tl[...])
    block = jnp.concatenate([cross] * 2, axis=1)
    on_block = sublane(block.shape) // 32 == lax.broadcasted_iota(jnp.int32, block.shape, 1) // 32
    target = dot(pp[...], taken[...])
    target = target[:64] + target[64:]
    ch, cl = split(jnp.where(on_block, block, 0.0))
    high = field[first * 32 : (first + 2) * 32]
    low = field[LANES + first * 32 : LANES + (first + 2) * 32]
    mixed = dot(jnp.concatenate([ch, cl], axis=0), high)
    mixed = mixed[:64] + mixed[64:] + dot(ch, low)
    for q in range(2):
        for m in range(members):
            start = (q * members + m) * 32
            value = mixed[q * 32 : (q + 1) * 32, m * LANES : (m + 1) * LANES] - target[q * 32 : (q + 1) * 32]
            spread[start : start + 32] = value.astype(BF16)


def observe_kernel(
    tiles, arrived, field,
    spread, message, th, tl, scaled,
    pp,
):
    steps = 2
    members = field.shape[1] // LANES
    even = lax.rem(lax.axis_index("tile"), 2) == 0
    cells = sublane((32, LANES)).astype(F32)
    lane = lax.broadcasted_iota(jnp.int32, (8, LANES), 1)
    packs = th.shape[1] // LANES
    sums = [[jnp.zeros((8, LANES), F32)] * 3 for _ in range(packs)]
    for d in range(tiles):
        p, start = divmod(d * CHUNK, LANES)
        window = (d * CHUNK + 16) // 16 * 16
        group = arrived[window : window + 16].astype(F32)
        group = group[8:] if d % 2 else group[:8]
        for b in range(3):
            first = start + b * APART
            place = lane - first % LANES
            place = jnp.where(place < 0, place + LANES, place)
            ends = min(LANES - start, SLOTS)
            sums[p][b] = sums[p][b] + jnp.where(place < ends, group, 0.0)
            if ends < SLOTS:
                rest = jnp.logical_and(place >= ends, place < SLOTS)
                sums[p + 1][b] = sums[p + 1][b] + jnp.where(rest, group, 0.0)
    for p in range(packs):
        kinds = [pltpu.roll(sums[p][b], (LANES - b * APART) % LANES, 1) if b else sums[p][b] for b in range(3)]
        entry = [kinds[i % 3][4 + i // 3 : 5 + i // 3] for i in range(9)]
        weight = jnp.zeros((32, LANES), F32)
        for i in range(4):
            weight += jnp.where(cells == entry[i], entry[4 + i], 0.0)
        at = slice(p * LANES, (p + 1) * LANES)
        th[:, at], tl[:, at] = split(weight)
        scaled[:, at] = weight * entry[8]
    spread_of(0, th, tl, scaled, arrived, field, pp, spread)
    size = members * 32
    for k in range(steps):
        for m in range(members):
            start = k * size + m * 32
            pair = spread[start : start + 32].astype(F32)
            near = [jnp.where(even, pair[i + 8 : i + 16], pair[i : i + 8]) for i in (0, 16)]
            start = k * size // 2 + m * 16
            message[start : start + 16] = jnp.concatenate(near, axis=0).astype(BF16)


def adjoint_step(u, cot, gb, gm, flat, d, out, gain, ws, wn, wo, members):
    both = 2 * SLIM
    gb[...] = (dot_t(gb[...], wo[...]) * d[...]).astype(BF16)
    gm[...] = dot_t(gb[...], wn[...]).astype(BF16)
    flat[...] = dot_t(gb[...], ws[...])
    for m in range(members):
        base = m * both
        pair = gm[base : base + both].astype(F32)
        around = neighbours([pair[:SLIM], pair[SLIM:]])
        values = []
        for lat in range(2):
            start = base + lat * SLIM
            x = u[start : start + SLIM]
            s = inverse_rms(x)
            scaled = gain * (flat[start : start + SLIM] + around[lat])
            inner = jnp.mean(x * scaled, axis=-1, keepdims=True)
            values.append(cot[start : start + SLIM] + s * scaled - x * (s * s * s * inner))
        out(m, values)


def edges(nxt, size, edge, r):
    even = lax.rem(lax.axis_index("tile"), 2) == 0
    start = size + r * 2
    far = nxt[start : start + 2]
    start = size + size // 8 + r * 2
    near = nxt[start : start + 2]
    edge[...] = jnp.zeros_like(edge)
    edge[0:2] = near
    edge[6:8] = far
    edge[8:10] = far
    edge[14:16] = near
    return jnp.where(even, edge[0:8], edge[8:16])


def pull_kernel(
    wn_hbm, ws_hbm, spread_own, readout, th, tl, scaled, arrived, field,
    pulled, away, wn, ws,
    pp, spread, near, sems,
):
    pairs = ((wn_hbm, wn), (ws_hbm, ws))
    copies = [pltpu.make_async_copy(source, to, sems.at[i]) for i, (source, to) in enumerate(pairs)]
    for copy in copies:
        copy.start()
    even = lax.rem(lax.axis_index("tile"), 2) == 0
    pulled[...] = dot_t(spread_own[...], readout[...])
    spread_of(2, th, tl, scaled, arrived, field, pp, spread)
    for start in range(0, spread.shape[0], 32):
        pair = spread[start : start + 32].astype(F32)
        rows = [jnp.where(even, pair[i + 8 : i + 16], pair[i : i + 8]) for i in (0, 16)]
        near[start // 2 : start // 2 + 16] = jnp.concatenate(rows, axis=0).astype(BF16)
    away[...] = dot_t(near[...], readout[...])
    for copy in copies:
        copy.wait()


def backward_kernel(
    pulled, away, wn, ws, gain, control, edge0, message16, f2x, wo, readout, error, message,
    u1x, d0x, d1x,
    result,
    cot2, cot1, gb, gb2, gm, flat, mate_pull, edge, u0x, final, nxt,
):
    size = result.shape[0]
    members = size // 32
    even = lax.rem(lax.axis_index("tile"), 2) == 0
    nxt[...] = message16[...].astype(F32)
    weight = jnp.where(lax.axis_index("slot") == lax.axis_size("slot") - 1, 0.0, 1.0) * error[...]
    row8 = sublane((8, 1))
    mate_side = jnp.where(even, 1, 0) == jnp.where(row8 < 4, 1, 0)
    mate_pull[...] = dot_t(message[...], readout[...])
    final[...] = f2x[...].astype(F32)

    def pulls(k, r):
        own = k * size + r * 16
        near = k * size // 2 + r * 8
        group = jnp.where(mate_side, mate_pull[near : near + 8], away[near : near + 8])
        return pulled[own : own + 16], group

    for m in range(members):
        pair = []
        for r in (2 * m, 2 * m + 1):
            own, group = pulls(1, r)
            a, b, c = r * SLIM, r * SLIM + 16, (r + 1) * SLIM
            u0x[a:b] = control[r * 16 : (r + 1) * 16]
            u0x[b:c] = edge0[r * 8 : (r + 1) * 8]
            pair.append(own - weight * (nxt[r * 16 : (r + 1) * 16] - final[a:b]))
            pair.append(group - weight * (edges(nxt, size, edge, r) - final[b:c]))
        at = slice(2 * m * SLIM, (2 * m + 2) * SLIM)
        cot2[at] = jnp.concatenate(pair, axis=0)
        gb[at] = jnp.concatenate(pair, axis=0).astype(BF16)

    def keep(m, values):
        pair = [value + jnp.concatenate(pulls(0, 2 * m + i), axis=0) for i, value in enumerate(values)]
        at = slice(2 * m * SLIM, (2 * m + 2) * SLIM)
        cot1[at] = jnp.concatenate(pair, axis=0)
        gb2[at] = jnp.concatenate(pair, axis=0).astype(BF16)

    def finish(m, values):
        for r, value in zip((2 * m, 2 * m + 1), values):
            a, b = r * SLIM, r * SLIM + 16
            result[r * 16 : (r + 1) * 16] = value[0:16] + error[...] * u0x[a:b]

    adjoint_step(u1x, cot2, gb, gm, flat, d1x, keep, gain[...], ws, wn, wo, members)
    adjoint_step(u0x, cot1, gb2, gm, flat, d0x, finish, gain[...], ws, wn, wo, members)


def last_kernel(base, background, before, error, result):
    first = lax.axis_index("slot") == 0
    taken = jnp.where(first, background[...].astype(F32), before[...].astype(F32))
    result[...] = base[...] - error[...] * taken


def kernel_call(body, outs, scratch, flops, moved, hbm=0, out_places=None, aliases={}):
    def call(*operands):
        fixed = [i in range(hbm) and i not in aliases for i in range(len(operands))]
        operands = [
            pltpu.with_memory_space_constraint(x, pltpu.HBM) if fix else x for x, fix in zip(operands, fixed)
        ]
        places = [pltpu.HBM] * hbm + [pltpu.VMEM] * (len(operands) - hbm)
        given = {} if out_places is None else {"out_specs": [pl.BlockSpec(memory_space=p) for p in out_places]}
        return pl.pallas_call(
            body,
            out_shape=outs,
            in_specs=[pl.BlockSpec(memory_space=place) for place in places],
            **given,
            scratch_shapes=scratch,
            input_output_aliases=aliases,
            compiler_params=pltpu.CompilerParams(vmem_limit_bytes=VMEM_LIMIT),
            cost_estimate=pl.CostEstimate(flops=flops, bytes_accessed=moved, transcendentals=0),
        )(*operands)

    return call


def per_device(
    control,
    background,
    self_weight,
    neighbour_weight,
    output_weight,
    norm_gain,
    readout,
    error_weight,
    report_owner,
    report_stencil,
    report_weights,
    report_values,
    report_precision,
):
    tiles = lax.axis_size("tile")
    slots = lax.axis_size("slot")
    members, lats, cols, channels = control.shape[1:]
    groups = members * lats
    size = groups * cols
    steps = report_owner.shape[1]
    rows = report_owner.shape[2]
    gain = norm_gain.reshape(1, channels)
    error = error_weight.reshape(1, channels)
    flat = control.reshape(size, channels)

    def spec(count, dtype=F32, width=channels):
        return jax.ShapeDtypeStruct((count, width), dtype)

    def scratch(count, dtype=F32, width=channels):
        return pltpu.VMEM((count, width), dtype)

    mate_of = [(i, i ^ 1) for i in range(tiles)]
    other_of = [(i, (i - 1) % tiles if i % 2 == 0 else (i + 1) % tiles) for i in range(tiles)]

    def across(block, shift):
        pairs = [
            ((s + shift) % slots * tiles + i, s * tiles + i) for s in range(slots) for i in range(tiles)
        ]
        return lax.ppermute(block, ("slot", "tile"), pairs)

    mate = lax.ppermute(flat, "tile", mate_of)
    listed = (
        jnp.transpose(report_owner[0], (0, 2, 1)),
        jnp.transpose(report_stencil[0], (0, 2, 1)),
        jnp.transpose(report_weights[0], (0, 2, 1)),
        report_precision[0],
        report_values[0].reshape(steps * rows, LANES),
    )
    work = [
        pltpu.VMEM((1, steps * rows), jnp.int32),
        scratch(24, F32, steps * rows),
        scratch(tiles * CHUNK, F32, LANES),
        scratch(tiles * CHUNK, BF16, LANES),
    ]
    held, packed, *listed = kernel_call(
        first_kernel,
        [spec(size), spec(tiles * CHUNK, BF16, LANES)]
        + [jax.ShapeDtypeStruct(block.shape, block.dtype) for block in listed],
        work + [pltpu.SemaphoreType.DMA((7,))],
        10**7,
        200000,
        hbm=6,
        out_places=[pltpu.VMEM, pltpu.HBM] + [pltpu.VMEM] * 5,
    )(flat, *listed)
    sent = kernel_call(
        tile_kernel, spec(groups * (cols + 2), BF16), [scratch(groups * 2)], 1000, 400000
    )(held, mate)
    oth = lax.ppermute(sent, "tile", other_of)
    (packed,) = kernel_call(
        later_kernel,
        [spec(tiles * CHUNK, BF16, LANES)],
        work + [pltpu.SemaphoreType.DMA],
        10**7,
        200000,
        hbm=1,
        out_places=[pltpu.HBM],
        aliases={0: 0},
    )(packed, *listed, sent)
    arrived = lax.all_to_all(packed, "tile", split_axis=0, concat_axis=0, tiled=True)

    message, near4 = kernel_call(
        relay_kernel,
        [spec(size + 4 * groups, BF16), spec(4 * groups)],
        [scratch(size), scratch(4 * groups)],
        1000,
        700000,
    )(held, mate, oth)
    nxt = across(message, 1)
    wide = groups * WIDE
    slim = groups * SLIM
    (
        edge0, u1x, d0x, d1x, f2x, field, final, wo, readout_held, gain_held, error_held, background_held,
    ) = kernel_call(
        forward_kernel,
        [spec(groups * 8), spec(slim)] + [spec(slim, BF16)] * 3
        + [spec(8 * lats * cols, BF16, members * LANES), spec(size, BF16)]
        + [spec(channels, BF16), spec(channels, BF16, LANES), spec(1), spec(1), spec(size, BF16)],
        [scratch(wide), scratch(wide), scratch(wide, BF16, 2 * channels), scratch(wide, BF16)]
        + [scratch(wide), scratch(16), scratch(4 * size, BF16)]
        + [scratch(2 * channels, BF16), pltpu.SemaphoreType.DMA((7,))],
        10**11,
        4000000,
        hbm=7,
    )(
        gain, self_weight, neighbour_weight, output_weight, readout, error, background.reshape(size, channels),
        held, near4, oth,
    )
    before = across(final, -1)
    total = tiles * CHUNK
    tables = [scratch(128, BF16, total)]
    spread, near_spread, *reports_held = kernel_call(
        functools.partial(observe_kernel, tiles),
        [spec(2 * size, BF16, LANES), spec(size, BF16, LANES)]
        + [spec(32, BF16, total), spec(32, BF16, total), spec(32, F32, total)],
        tables,
        10**9,
        2000000,
    )(arrived, field)
    from_mate = lax.ppermute(near_spread, "tile", mate_of)
    handed = kernel_call(
        pull_kernel,
        [spec(2 * size), spec(size), spec(channels, BF16), spec(channels, BF16)],
        tables + [scratch(2 * size, BF16, LANES), scratch(size, BF16, LANES), pltpu.SemaphoreType.DMA((2,))],
        10**9,
        3000000,
        hbm=2,
    )(neighbour_weight, self_weight, spread, readout_held, *reports_held, arrived, field)
    base = kernel_call(
        backward_kernel,
        spec(size),
        [scratch(slim), scratch(slim), scratch(slim, BF16), scratch(slim, BF16), scratch(slim, BF16), scratch(slim)]
        + [scratch(size), scratch(16), scratch(slim), scratch(slim), scratch(size + 4 * groups)],
        12 * slim * channels * channels,
        6000000,
    )(
        *handed, gain_held, held, edge0, nxt, f2x, wo, readout_held, error_held, from_mate,
        u1x, d0x, d1x,
    )
    result = kernel_call(last_kernel, spec(size), [], 10**6, 900000)(base, background_held, before, error_held)
    return result.reshape(control.shape)


def solution(mesh):
    in_specs = (
        P("slot", None, None, "tile", None),
        P(None, None, "tile", None),
        P(),
        P(),
        P(),
        P(),
        P(),
        P(),
        P("slot", None, "tile", None),
        P("slot", None, "tile", None),
        P("slot", None, "tile", None),
        P("slot", None, "tile", None),
        P("slot", None, "tile"),
    )
    out_specs = P("slot", None, None, "tile", None)
    return jax.shard_map(
        per_device, mesh=mesh, in_specs=in_specs, out_specs=out_specs, check_vma=False
    )
```

```python
import functools
import jax
import jax.numpy as jnp
from jax import lax
from jax.experimental import pallas as pl
from jax.experimental.pallas import tpu as pltpu
from jax.sharding import PartitionSpec as P

EPSILON = 1e-06
F32 = jnp.float32
BF16 = jnp.bfloat16
LANES = 128
CAP = 5
SLOTS = 4 * CAP
CHUNK = 24
APART = 36
STRIDE = 32
WIDE = 40
SLIM = 24
VMEM_LIMIT = 28 * 1024 * 1024


def dot(a, b):
    return jnp.dot(a, b, preferred_element_type=F32)


def dot_t(a, b):
    return lax.dot_general(a, b, (((1,), (1,)), ((), ())), preferred_element_type=F32)


def sublane(shape):
    return lax.broadcasted_iota(jnp.int32, shape, 0)


def inverse_rms(x):
    return lax.rsqrt(jnp.mean(x * x, axis=-1, keepdims=True) + EPSILON)


def sigmoid(p):
    return 0.5 * jnp.tanh(0.5 * p) + 0.5


def neighbours(rows):
    width = rows[0].shape[0]
    return [
        0.25 * (rows[1 - i] + pltpu.roll(rows[i], 1, 0) + pltpu.roll(rows[i], width - 1, 0))
        for i in range(2)
    ]


def forward_step(u, n, act, pre, d, gain, weights, wo, width, members, out, copies=()):
    both = 2 * width
    for m in range(members):
        base = m * both
        rows = []
        for lat in range(2):
            x = u[base + lat * width : base + (lat + 1) * width]
            rows.append((x * inverse_rms(x) * gain).astype(BF16).astype(F32))
        channels = rows[0].shape[1]
        n[base : base + both, :channels] = jnp.concatenate(rows, axis=0).astype(BF16)
        n[base : base + both, channels:] = jnp.concatenate(neighbours(rows), axis=0).astype(BF16)
    for copy in copies[:2]:
        copy.wait()
    pre[...] = dot(n[...], weights[...])
    for m in range(members):
        base = m * both
        p = pre[base : base + both]
        sig = sigmoid(p)
        act[base : base + both] = (p * sig).astype(BF16)
        if d is not None:
            pre[base : base + both] = sig * (1.0 + p * (1.0 - sig))
    if d is not None:
        for m in range(members):
            slim_copy(d, pre, m)
    for copy in copies[2:]:
        copy.wait()
    pre[...] = dot(act[...], wo[...])
    for r in range(2 * members):
        out(r, u[r * width : (r + 1) * width] + pre[r * width : (r + 1) * width])


def slim_edge(wide, r):
    low = wide[r * WIDE + 16 : r * WIDE + 24]
    high = wide[r * WIDE + 32 : r * WIDE + 40]
    return jnp.where(sublane(low.shape) < 4, low, high)


def slim_copy(to, wide, m):
    parts = []
    for r in (2 * m, 2 * m + 1):
        parts += [wide[r * WIDE : r * WIDE + 16], slim_edge(wide, r)]
    both = jnp.concatenate(parts, axis=0)
    to[m * 2 * SLIM : (m + 1) * 2 * SLIM] = both.astype(to.dtype)


def reports(arrays, out_hbm, key, meta, picked, out, sem):
    pack(*arrays, out, key, meta, picked)
    store = pltpu.make_async_copy(out, out_hbm, sem)
    store.start()
    store.wait()


def early():
    return lax.axis_index("tile") < lax.axis_size("tile") * 3 // 4


def first_kernel(control_hbm, *refs):
    sources, (held, out_hbm), arrays, (key, meta, picked, out, sems) = refs[:5], refs[5:7], refs[7:12], refs[12:]
    copies = [
        pltpu.make_async_copy(source, to, sems.at[i]) for i, (source, to) in enumerate(zip(sources, arrays))
    ]
    copies.append(pltpu.make_async_copy(control_hbm, held, sems.at[5]))
    for copy in copies:
        copy.start()
    for copy in copies[:5]:
        copy.wait()

    @pl.when(early())
    def _():
        reports(arrays, out_hbm, key, meta, picked, out, sems.at[6])

    copies[5].wait()


def later_kernel(packed_hbm, *refs):
    arrays, out_hbm, (key, meta, picked, out, sem) = refs[:5], refs[6], refs[7:]

    @pl.when(jnp.logical_not(early()))
    def _():
        reports(arrays, out_hbm, key, meta, picked, out, sem)


def fan(x, shift):
    if shift % LANES:
        x = pltpu.roll(x, shift % LANES, 1)
    for _ in range(2):
        x = pltpu.roll(x, 0, 1, stride=APART // 2, stride_axis=0)
    return x


def pack(owner, stencil, weights, precision, values, out, key, meta, picked):
    steps, _, rows = owner.shape
    tiles = out.shape[0] // CHUNK
    total = steps * rows
    earlier = lax.broadcasted_iota(jnp.int32, (rows, rows), 0) < lax.broadcasted_iota(jnp.int32, (rows, rows), 1)
    earlier = earlier.astype(F32).astype(BF16)
    meta[...] = jnp.zeros_like(meta)
    for k in range(steps):
        at = slice(k * rows, (k + 1) * rows)
        named = lax.broadcasted_iota(jnp.int32, (tiles, rows), 0) == owner[k]
        hits = named.astype(F32)
        before = dot(hits.astype(BF16), earlier)
        rank = jnp.sum(hits * before, axis=0, keepdims=True).astype(jnp.int32)
        key[0:1, at] = owner[k] * (2 * CAP) + k * CAP + rank
        for i in range(4):
            meta[i // 3 * 8 + i % 3 : i // 3 * 8 + i % 3 + 1, at] = stencil[k, i : i + 1].astype(F32)
            j = 4 + i
            meta[j // 3 * 8 + j % 3 : j // 3 * 8 + j % 3 + 1, at] = weights[k, i : i + 1].astype(F32)
        meta[18:19, at] = precision[k : k + 1].astype(F32)
    row = lax.broadcasted_iota(jnp.int32, (tiles * STRIDE, total), 0)
    tile = row // STRIDE
    slot = row % STRIDE
    other = jnp.where(tile % 2 == 0, (tile + tiles - 1) % tiles, (tile + 1) % tiles)
    mine = slot < 2 * CAP
    wanted = jnp.where(mine, tile * (2 * CAP) + slot, other * (2 * CAP) + slot - 2 * CAP)
    wanted = jnp.where(slot < SLOTS, wanted, -1)
    placement = (wanted == key[...]).astype(F32).astype(BF16)
    placed = dot(placement, values[...])
    entries = dot_t(meta[...].astype(BF16), placement)
    lane = lax.broadcasted_iota(jnp.int32, (24, LANES), 1)
    turn = lax.axis_index("tile") * CHUNK % LANES
    per_tile = LANES // STRIDE
    for t in range(tiles):
        picked[t * CHUNK : (t + 1) * CHUNK] = placed[t * STRIDE : t * STRIDE + CHUNK]
        start = t % per_tile * STRIDE
        used = jnp.logical_and(lane >= start, lane < start + SLOTS)
        block = jnp.where(used, entries[:, t // per_tile * LANES : (t // per_tile + 1) * LANES], 0.0)
        for j in range(3):
            laid = fan(block[j * 8 : (j + 1) * 8], LANES - start)
            row = t * CHUNK + SLOTS + j
            picked[row : row + 1] = jnp.sum(laid, axis=0, keepdims=True)
        group = picked[t * CHUNK + 16 : (t + 1) * CHUNK]
        picked[t * CHUNK + 16 : (t + 1) * CHUNK] = jnp.where(sublane((8, 1)) < 4, group, pltpu.roll(group, turn, 1))
    out[...] = picked[...].astype(BF16)


def tile_kernel(control, mate, out, held):
    even = lax.rem(lax.axis_index("tile"), 2) == 0
    size = control.shape[0]
    out[0:size] = control[...].astype(BF16)
    for r in range(size // 16):
        held[r * 2 : (r + 1) * 2] = jnp.where(
            even, mate[r * 16 : r * 16 + 2], mate[r * 16 + 14 : (r + 1) * 16]
        )
    out[size:] = held[...].astype(BF16)


def relay_kernel(control, mate, oth, out, near4, wide, edge):
    even = lax.rem(lax.axis_index("tile"), 2) == 0
    size = mate.shape[0]
    out[0:size] = control[...].astype(BF16)
    wide[...] = oth[0:size].astype(F32)
    for r in range(size // 16):
        a, b = r * 16, (r + 1) * 16
        edge[r * 2 : (r + 1) * 2] = jnp.where(even, wide[b - 2 : b], wide[a : a + 2])
        near4[r * 4 : (r + 1) * 4] = jnp.where(even, mate[a : a + 4], mate[b - 4 : b])
        start = size // 8 + r * 2
        edge[start : start + 2] = jnp.where(even, mate[a : a + 2], mate[b - 2 : b])
    out[size:] = edge[...].astype(BF16)


def forward_kernel(
    gain_hbm, ws_hbm, wn_hbm, wo_hbm, readout_hbm, error_hbm, background_hbm, control, mate, oth,
    edge0, u1x, d0x, d1x, f2x, field, final, wo, readout, gain, error, background,
    ua, ub, n, act, pre, edge, states, weights, sems,
):
    channels = wo.shape[0]
    halves = weights.at[pl.ds(0, channels)], weights.at[pl.ds(channels, channels)]
    pairs = (
        (gain_hbm, gain), (ws_hbm, halves[0]), (wn_hbm, halves[1]), (wo_hbm, wo), (readout_hbm, readout),
        (error_hbm, error), (background_hbm, background),
    )
    copies = [pltpu.make_async_copy(source, to, sems.at[i]) for i, (source, to) in enumerate(pairs)]
    for copy in copies:
        copy.start()
    members = final.shape[0] // 32
    even = lax.rem(lax.axis_index("tile"), 2) == 0
    tile_at = jnp.where(even, 24, 16)
    edge_at = jnp.where(even, 16, 32)
    far = oth[members * 32 :].astype(F32)
    for r in range(2 * members):
        ua[r * WIDE : r * WIDE + 16] = control[r * 16 : (r + 1) * 16]
        ua[pl.ds(pl.multiple_of(r * WIDE + tile_at, 8), 16)] = oth[r * 16 : (r + 1) * 16].astype(F32)
        near4 = mate[r * 4 : (r + 1) * 4]
        far2 = far[r * 2 : (r + 1) * 2]
        edge[...] = jnp.zeros_like(edge)
        edge[0:4] = near4
        edge[6:8] = far2
        edge[8:10] = far2
        edge[12:16] = near4
        ua[pl.ds(pl.multiple_of(r * WIDE + edge_at, 8), 8)] = jnp.where(even, edge[0:8], edge[8:16])
    for r in range(2 * members):
        edge0[r * 8 : (r + 1) * 8] = slim_edge(ua, r)
    copies[0].wait()
    g = gain[...]

    def keep(ref):
        def store(r, value):
            ref[r * WIDE : (r + 1) * WIDE] = value

        return store

    def keep_states(ref, k):
        own = k * members * 32
        away = (2 + k) * members * 32
        for r in range(2 * members):
            states[own + r * 16 : own + (r + 1) * 16] = ref[r * WIDE : r * WIDE + 16].astype(BF16)
            taken = ref[pl.ds(pl.multiple_of(r * WIDE + tile_at, 8), 16)]
            states[away + r * 16 : away + (r + 1) * 16] = taken.astype(BF16)

    forward_step(ua, n, act, pre, d0x, g, weights, wo, WIDE, members, keep(ub), copies[1:])
    for m in range(members):
        slim_copy(u1x, ub, m)
    keep_states(ub, 0)
    forward_step(ub, n, act, pre, d1x, g, weights, wo, WIDE, members, keep(ua))
    for m in range(members):
        slim_copy(f2x, ua, m)
    keep_states(ua, 1)
    final[...] = states[members * 32 : 2 * members * 32]
    read = dot(states[...], readout[...])
    for q in range(4):
        for m in range(members):
            start = (q * members + m) * 32
            at = slice(m * LANES, (m + 1) * LANES)
            field[q * 32 : (q + 1) * 32, at], field[LANES + q * 32 : LANES + (q + 1) * 32, at] = split(
                read[start : start + 32]
            )


def split(x):
    high = x.astype(BF16)
    return high, (x - high.astype(F32)).astype(BF16)


def spread_of(first, th, tl, scaled, taken, field, pp, spread):
    lane = lax.broadcasted_iota(jnp.int32, (1, LANES), 1)
    members = field.shape[1] // LANES
    for p in range(th.shape[1] // LANES):
        at = slice(p * LANES, (p + 1) * LANES)
        slot = (lane + p * LANES) % CHUNK
        table_of = jnp.where(slot < SLOTS, slot // CAP, -1)
        for q in range(2):
            kept = jnp.where(table_of == first + q, scaled[:, at], 0.0)
            pp[q * 32 : (q + 1) * 32, at], pp[64 + q * 32 : 96 + q * 32, at] = split(kept)
    cross = dot_t(pp[...], th[...])
    cross = cross[:64] + cross[64:] + dot_t(pp[0:64], tl[...])
    block = jnp.concatenate([cross] * 2, axis=1)
    on_block = sublane(block.shape) // 32 == lax.broadcasted_iota(jnp.int32, block.shape, 1) // 32
    target = dot(pp[...], taken[...])
    target = target[:64] + target[64:]
    ch, cl = split(jnp.where(on_block, block, 0.0))
    high = field[first * 32 : (first + 2) * 32]
    low = field[LANES + first * 32 : LANES + (first + 2) * 32]
    mixed = dot(jnp.concatenate([ch, cl], axis=0), high)
    mixed = mixed[:64] + mixed[64:] + dot(ch, low)
    for q in range(2):
        for m in range(members):
            start = (q * members + m) * 32
            value = mixed[q * 32 : (q + 1) * 32, m * LANES : (m + 1) * LANES] - target[q * 32 : (q + 1) * 32]
            spread[start : start + 32] = value.astype(BF16)


def observe_kernel(
    tiles, arrived, field,
    spread, message, th, tl, scaled,
    pp,
):
    steps = 2
    members = field.shape[1] // LANES
    even = lax.rem(lax.axis_index("tile"), 2) == 0
    cells = sublane((32, LANES)).astype(F32)
    lane = lax.broadcasted_iota(jnp.int32, (8, LANES), 1)
    packs = th.shape[1] // LANES
    sums = [[jnp.zeros((8, LANES), F32)] * 3 for _ in range(packs)]
    for d in range(tiles):
        p, start = divmod(d * CHUNK, LANES)
        window = (d * CHUNK + 16) // 16 * 16
        group = arrived[window : window + 16].astype(F32)
        group = group[8:] if d % 2 else group[:8]
        for b in range(3):
            first = start + b * APART
            place = lane - first % LANES
            place = jnp.where(place < 0, place + LANES, place)
            ends = min(LANES - start, SLOTS)
            sums[p][b] = sums[p][b] + jnp.where(place < ends, group, 0.0)
            if ends < SLOTS:
                rest = jnp.logical_and(place >= ends, place < SLOTS)
                sums[p + 1][b] = sums[p + 1][b] + jnp.where(rest, group, 0.0)
    for p in range(packs):
        kinds = [pltpu.roll(sums[p][b], (LANES - b * APART) % LANES, 1) if b else sums[p][b] for b in range(3)]
        entry = [kinds[i % 3][4 + i // 3 : 5 + i // 3] for i in range(9)]
        weight = jnp.zeros((32, LANES), F32)
        for i in range(4):
            weight += jnp.where(cells == entry[i], entry[4 + i], 0.0)
        at = slice(p * LANES, (p + 1) * LANES)
        th[:, at], tl[:, at] = split(weight)
        scaled[:, at] = weight * entry[8]
    spread_of(0, th, tl, scaled, arrived, field, pp, spread)
    size = members * 32
    for k in range(steps):
        for m in range(members):
            start = k * size + m * 32
            pair = spread[start : start + 32].astype(F32)
            near = [jnp.where(even, pair[i + 8 : i + 16], pair[i : i + 8]) for i in (0, 16)]
            start = k * size // 2 + m * 16
            message[start : start + 16] = jnp.concatenate(near, axis=0).astype(BF16)


def adjoint_step(u, cot, gb, gm, flat, d, out, gain, ws, wn, wo, members):
    both = 2 * SLIM
    gb[...] = cot[...].astype(BF16)
    flat[...] = dot_t(gb[...], wo[...])
    gb[...] = (flat[...] * d[...]).astype(BF16)
    gm[...] = dot_t(gb[...], wn[...])
    flat[...] = dot_t(gb[...], ws[...])
    for m in range(members):
        base = m * both
        rows = []
        for lat in range(2):
            start = base + lat * SLIM
            rows.append(gm[start : start + SLIM].astype(BF16).astype(F32))
        around = neighbours(rows)
        for lat in range(2):
            start = base + lat * SLIM
            x = u[start : start + SLIM]
            s = inverse_rms(x)
            scaled = gain * (flat[start : start + SLIM] + around[lat])
            inner = jnp.mean(x * scaled, axis=-1, keepdims=True)
            out(2 * m + lat, cot[start : start + SLIM] + s * scaled - x * (s * s * s * inner))


def edges(nxt, size, edge, r):
    even = lax.rem(lax.axis_index("tile"), 2) == 0
    start = size + r * 2
    far = nxt[start : start + 2]
    start = size + size // 8 + r * 2
    near = nxt[start : start + 2]
    edge[...] = jnp.zeros_like(edge)
    edge[0:2] = near
    edge[6:8] = far
    edge[8:10] = far
    edge[14:16] = near
    return jnp.where(even, edge[0:8], edge[8:16])


def pull_kernel(
    wn_hbm, ws_hbm, spread_own, readout, th, tl, scaled, arrived, field,
    pulled, away, wn, ws,
    pp, spread, near, sems,
):
    pairs = ((wn_hbm, wn), (ws_hbm, ws))
    copies = [pltpu.make_async_copy(source, to, sems.at[i]) for i, (source, to) in enumerate(pairs)]
    for copy in copies:
        copy.start()
    even = lax.rem(lax.axis_index("tile"), 2) == 0
    pulled[...] = dot_t(spread_own[...], readout[...])
    spread_of(2, th, tl, scaled, arrived, field, pp, spread)
    for start in range(0, spread.shape[0], 32):
        pair = spread[start : start + 32].astype(F32)
        rows = [jnp.where(even, pair[i + 8 : i + 16], pair[i : i + 8]) for i in (0, 16)]
        near[start // 2 : start // 2 + 16] = jnp.concatenate(rows, axis=0).astype(BF16)
    away[...] = dot_t(near[...], readout[...])
    for copy in copies:
        copy.wait()


def backward_kernel(
    pulled, away, wn, ws, gain, control, edge0, message16, f2x, wo, readout, error, message,
    u1x, d0x, d1x,
    result,
    cot2, cot1, gb, gm, flat, mate_pull, edge, u0x, final, nxt,
):
    size = result.shape[0]
    members = size // 32
    even = lax.rem(lax.axis_index("tile"), 2) == 0
    nxt[...] = message16[...].astype(F32)
    weight = jnp.where(lax.axis_index("slot") == lax.axis_size("slot") - 1, 0.0, 1.0) * error[...]
    row8 = sublane((8, 1))
    mate_side = jnp.where(even, 1, 0) == jnp.where(row8 < 4, 1, 0)
    mate_pull[...] = dot_t(message[...], readout[...])
    final[...] = f2x[...].astype(F32)

    def pulls(k, r):
        own = k * size + r * 16
        near = k * size // 2 + r * 8
        group = jnp.where(mate_side, mate_pull[near : near + 8], away[near : near + 8])
        return pulled[own : own + 16], group

    for r in range(2 * members):
        own, group = pulls(1, r)
        a, b = r * SLIM, r * SLIM + 16
        cot2[a:b] = own - weight * (nxt[r * 16 : (r + 1) * 16] - final[a:b])
        u0x[a:b] = control[r * 16 : (r + 1) * 16]
        a, b = b, b + 8
        cot2[a:b] = group - weight * (edges(nxt, size, edge, r) - final[a:b])
        u0x[a:b] = edge0[r * 8 : (r + 1) * 8]

    def keep(r, value):
        cot1[r * SLIM : (r + 1) * SLIM] = value + jnp.concatenate(pulls(0, r), axis=0)

    def finish(r, value):
        a, b = r * SLIM, r * SLIM + 16
        result[r * 16 : (r + 1) * 16] = value[0:16] + error[...] * u0x[a:b]

    adjoint_step(u1x, cot2, gb, gm, flat, d1x, keep, gain[...], ws, wn, wo, members)
    adjoint_step(u0x, cot1, gb, gm, flat, d0x, finish, gain[...], ws, wn, wo, members)


def last_kernel(base, background, before, error, result):
    first = lax.axis_index("slot") == 0
    taken = jnp.where(first, background[...].astype(F32), before[...].astype(F32))
    result[...] = base[...] - error[...] * taken


def kernel_call(body, outs, scratch, flops, moved, hbm=0, out_places=None, aliases={}):
    def call(*operands):
        fixed = [i in range(hbm) and i not in aliases for i in range(len(operands))]
        operands = [
            pltpu.with_memory_space_constraint(x, pltpu.HBM) if fix else x for x, fix in zip(operands, fixed)
        ]
        places = [pltpu.HBM] * hbm + [pltpu.VMEM] * (len(operands) - hbm)
        given = {} if out_places is None else {"out_specs": [pl.BlockSpec(memory_space=p) for p in out_places]}
        return pl.pallas_call(
            body,
            out_shape=outs,
            in_specs=[pl.BlockSpec(memory_space=place) for place in places],
            **given,
            scratch_shapes=scratch,
            input_output_aliases=aliases,
            compiler_params=pltpu.CompilerParams(vmem_limit_bytes=VMEM_LIMIT),
            cost_estimate=pl.CostEstimate(flops=flops, bytes_accessed=moved, transcendentals=0),
        )(*operands)

    return call


def per_device(
    control,
    background,
    self_weight,
    neighbour_weight,
    output_weight,
    norm_gain,
    readout,
    error_weight,
    report_owner,
    report_stencil,
    report_weights,
    report_values,
    report_precision,
):
    tiles = lax.axis_size("tile")
    slots = lax.axis_size("slot")
    members, lats, cols, channels = control.shape[1:]
    groups = members * lats
    size = groups * cols
    steps = report_owner.shape[1]
    rows = report_owner.shape[2]
    gain = norm_gain.reshape(1, channels)
    error = error_weight.reshape(1, channels)
    flat = control.reshape(size, channels)

    def spec(count, dtype=F32, width=channels):
        return jax.ShapeDtypeStruct((count, width), dtype)

    def scratch(count, dtype=F32, width=channels):
        return pltpu.VMEM((count, width), dtype)

    mate_of = [(i, i ^ 1) for i in range(tiles)]
    other_of = [(i, (i - 1) % tiles if i % 2 == 0 else (i + 1) % tiles) for i in range(tiles)]

    def across(block, shift):
        pairs = [
            ((s + shift) % slots * tiles + i, s * tiles + i) for s in range(slots) for i in range(tiles)
        ]
        return lax.ppermute(block, ("slot", "tile"), pairs)

    mate = lax.ppermute(flat, "tile", mate_of)
    listed = (
        jnp.transpose(report_owner[0], (0, 2, 1)),
        jnp.transpose(report_stencil[0], (0, 2, 1)),
        jnp.transpose(report_weights[0], (0, 2, 1)),
        report_precision[0],
        report_values[0].reshape(steps * rows, LANES),
    )
    work = [
        pltpu.VMEM((1, steps * rows), jnp.int32),
        scratch(24, F32, steps * rows),
        scratch(tiles * CHUNK, F32, LANES),
        scratch(tiles * CHUNK, BF16, LANES),
    ]
    held, packed, *listed = kernel_call(
        first_kernel,
        [spec(size), spec(tiles * CHUNK, BF16, LANES)]
        + [jax.ShapeDtypeStruct(block.shape, block.dtype) for block in listed],
        work + [pltpu.SemaphoreType.DMA((7,))],
        10**7,
        200000,
        hbm=6,
        out_places=[pltpu.VMEM, pltpu.HBM] + [pltpu.VMEM] * 5,
    )(flat, *listed)
    sent = kernel_call(
        tile_kernel, spec(groups * (cols + 2), BF16), [scratch(groups * 2)], 1000, 400000
    )(held, mate)
    oth = lax.ppermute(sent, "tile", other_of)
    (packed,) = kernel_call(
        later_kernel,
        [spec(tiles * CHUNK, BF16, LANES)],
        work + [pltpu.SemaphoreType.DMA],
        10**7,
        200000,
        hbm=1,
        out_places=[pltpu.HBM],
        aliases={0: 0},
    )(packed, *listed, sent)
    arrived = lax.all_to_all(packed, "tile", split_axis=0, concat_axis=0, tiled=True)

    message, near4 = kernel_call(
        relay_kernel,
        [spec(size + 4 * groups, BF16), spec(4 * groups)],
        [scratch(size), scratch(4 * groups)],
        1000,
        700000,
    )(held, mate, oth)
    nxt = across(message, 1)
    wide = groups * WIDE
    slim = groups * SLIM
    (
        edge0, u1x, d0x, d1x, f2x, field, final, wo, readout_held, gain_held, error_held, background_held,
    ) = kernel_call(
        forward_kernel,
        [spec(groups * 8), spec(slim)] + [spec(slim, BF16)] * 3
        + [spec(8 * lats * cols, BF16, members * LANES), spec(size, BF16)]
        + [spec(channels, BF16), spec(channels, BF16, LANES), spec(1), spec(1), spec(size, BF16)],
        [scratch(wide), scratch(wide), scratch(wide, BF16, 2 * channels), scratch(wide, BF16)]
        + [scratch(wide), scratch(16), scratch(4 * size, BF16)]
        + [scratch(2 * channels, BF16), pltpu.SemaphoreType.DMA((7,))],
        10**11,
        4000000,
        hbm=7,
    )(
        gain, self_weight, neighbour_weight, output_weight, readout, error, background.reshape(size, channels),
        held, near4, oth,
    )
    before = across(final, -1)
    total = tiles * CHUNK
    tables = [scratch(128, BF16, total)]
    spread, near_spread, *reports_held = kernel_call(
        functools.partial(observe_kernel, tiles),
        [spec(2 * size, BF16, LANES), spec(size, BF16, LANES)]
        + [spec(32, BF16, total), spec(32, BF16, total), spec(32, F32, total)],
        tables,
        10**9,
        2000000,
    )(arrived, field)
    from_mate = lax.ppermute(near_spread, "tile", mate_of)
    handed = kernel_call(
        pull_kernel,
        [spec(2 * size), spec(size), spec(channels, BF16), spec(channels, BF16)],
        tables + [scratch(2 * size, BF16, LANES), scratch(size, BF16, LANES), pltpu.SemaphoreType.DMA((2,))],
        10**9,
        3000000,
        hbm=2,
    )(neighbour_weight, self_weight, spread, readout_held, *reports_held, arrived, field)
    base = kernel_call(
        backward_kernel,
        spec(size),
        [scratch(slim), scratch(slim), scratch(slim, BF16), scratch(slim), scratch(slim)]
        + [scratch(size), scratch(16), scratch(slim), scratch(slim), scratch(size + 4 * groups)],
        12 * slim * channels * channels,
        6000000,
    )(
        *handed, gain_held, held, edge0, nxt, f2x, wo, readout_held, error_held, from_mate,
        u1x, d0x, d1x,
    )
    result = kernel_call(last_kernel, spec(size), [], 10**6, 900000)(base, background_held, before, error_held)
    return result.reshape(control.shape)


def solution(mesh):
    in_specs = (
        P("slot", None, None, "tile", None),
        P(None, None, "tile", None),
        P(),
        P(),
        P(),
        P(),
        P(),
        P(),
        P("slot", None, "tile", None),
        P("slot", None, "tile", None),
        P("slot", None, "tile", None),
        P("slot", None, "tile", None),
        P("slot", None, "tile"),
    )
    out_specs = P("slot", None, None, "tile", None)
    return jax.shard_map(
        per_device, mesh=mesh, in_specs=in_specs, out_specs=out_specs, check_vma=False
    )
```

```python
import functools
import jax
import jax.numpy as jnp
from jax import lax
from jax.experimental import pallas as pl
from jax.experimental.pallas import tpu as pltpu
from jax.sharding import PartitionSpec as P

EPSILON = 1e-06
F32 = jnp.float32
BF16 = jnp.bfloat16
LANES = 128
CAP = 5
SLOTS = 4 * CAP
CHUNK = 24
APART = 36
STRIDE = 32
WIDE = 40
SLIM = 24
VMEM_LIMIT = 28 * 1024 * 1024


def dot(a, b):
    return jnp.dot(a, b, preferred_element_type=F32)


def dot_t(a, b):
    return lax.dot_general(a, b, (((1,), (1,)), ((), ())), preferred_element_type=F32)


def sublane(shape):
    return lax.broadcasted_iota(jnp.int32, shape, 0)


def inverse_rms(x):
    return lax.rsqrt(jnp.mean(x * x, axis=-1, keepdims=True) + EPSILON)


def sigmoid(p):
    return 0.5 * jnp.tanh(0.5 * p) + 0.5


def neighbours(rows):
    width = rows[0].shape[0]
    return [
        0.25 * (rows[1 - i] + pltpu.roll(rows[i], 1, 0) + pltpu.roll(rows[i], width - 1, 0))
        for i in range(2)
    ]


def forward_step(u, n, act, pre, d, gain, weights, wo, width, members, out, copies=()):
    both = 2 * width
    for m in range(members):
        base = m * both
        rows = []
        for lat in range(2):
            x = u[base + lat * width : base + (lat + 1) * width]
            rows.append((x * inverse_rms(x) * gain).astype(BF16).astype(F32))
        channels = rows[0].shape[1]
        n[base : base + both, :channels] = jnp.concatenate(rows, axis=0).astype(BF16)
        n[base : base + both, channels:] = jnp.concatenate(neighbours(rows), axis=0).astype(BF16)
    for copy in copies[:2]:
        copy.wait()
    pre[...] = dot(n[...], weights[...])
    for m in range(members):
        base = m * both
        p = pre[base : base + both]
        sig = sigmoid(p)
        act[base : base + both] = (p * sig).astype(BF16)
        if d is not None:
            pre[base : base + both] = sig * (1.0 + p * (1.0 - sig))
    if d is not None:
        for m in range(members):
            slim_copy(d, pre, m)
    for copy in copies[2:]:
        copy.wait()
    pre[...] = dot(act[...], wo[...])
    for r in range(2 * members):
        out(r, u[r * width : (r + 1) * width] + pre[r * width : (r + 1) * width])


def slim_edge(wide, r):
    low = wide[r * WIDE + 16 : r * WIDE + 24]
    high = wide[r * WIDE + 32 : r * WIDE + 40]
    return jnp.where(sublane(low.shape) < 4, low, high)


def slim_copy(to, wide, m):
    parts = []
    for r in (2 * m, 2 * m + 1):
        parts += [wide[r * WIDE : r * WIDE + 16], slim_edge(wide, r)]
    both = jnp.concatenate(parts, axis=0)
    to[m * 2 * SLIM : (m + 1) * 2 * SLIM] = both.astype(to.dtype)


def reports(arrays, out_hbm, key, meta, picked, out, sem):
    pack(*arrays, out, key, meta, picked)
    store = pltpu.make_async_copy(out, out_hbm, sem)
    store.start()
    store.wait()


def early():
    return lax.axis_index("tile") < lax.axis_size("tile") // 4


def first_kernel(control_hbm, *refs):
    sources, (held, out_hbm), arrays, (key, meta, picked, out, sems) = refs[:5], refs[5:7], refs[7:12], refs[12:]
    copies = [
        pltpu.make_async_copy(source, to, sems.at[i]) for i, (source, to) in enumerate(zip(sources, arrays))
    ]
    copies.append(pltpu.make_async_copy(control_hbm, held, sems.at[5]))
    for copy in copies:
        copy.start()
    for copy in copies[:5]:
        copy.wait()

    @pl.when(early())
    def _():
        reports(arrays, out_hbm, key, meta, picked, out, sems.at[6])

    copies[5].wait()


def later_kernel(packed_hbm, *refs):
    arrays, out_hbm, (key, meta, picked, out, sem) = refs[:5], refs[6], refs[7:]

    @pl.when(jnp.logical_not(early()))
    def _():
        reports(arrays, out_hbm, key, meta, picked, out, sem)


def fan(x, shift):
    if shift % LANES:
        x = pltpu.roll(x, shift % LANES, 1)
    for _ in range(2):
        x = pltpu.roll(x, 0, 1, stride=APART // 2, stride_axis=0)
    return x


def pack(owner, stencil, weights, precision, values, out, key, meta, picked):
    steps, _, rows = owner.shape
    tiles = out.shape[0] // CHUNK
    total = steps * rows
    earlier = lax.broadcasted_iota(jnp.int32, (rows, rows), 0) < lax.broadcasted_iota(jnp.int32, (rows, rows), 1)
    earlier = earlier.astype(F32).astype(BF16)
    meta[...] = jnp.zeros_like(meta)
    for k in range(steps):
        at = slice(k * rows, (k + 1) * rows)
        named = lax.broadcasted_iota(jnp.int32, (tiles, rows), 0) == owner[k]
        hits = named.astype(F32)
        before = dot(hits.astype(BF16), earlier)
        rank = jnp.sum(hits * before, axis=0, keepdims=True).astype(jnp.int32)
        key[0:1, at] = owner[k] * (2 * CAP) + k * CAP + rank
        for i in range(4):
            meta[i // 3 * 8 + i % 3 : i // 3 * 8 + i % 3 + 1, at] = stencil[k, i : i + 1].astype(F32)
            j = 4 + i
            meta[j // 3 * 8 + j % 3 : j // 3 * 8 + j % 3 + 1, at] = weights[k, i : i + 1].astype(F32)
        meta[18:19, at] = precision[k : k + 1].astype(F32)
    row = lax.broadcasted_iota(jnp.int32, (tiles * STRIDE, total), 0)
    tile = row // STRIDE
    slot = row % STRIDE
    other = jnp.where(tile % 2 == 0, (tile + tiles - 1) % tiles, (tile + 1) % tiles)
    mine = slot < 2 * CAP
    wanted = jnp.where(mine, tile * (2 * CAP) + slot, other * (2 * CAP) + slot - 2 * CAP)
    wanted = jnp.where(slot < SLOTS, wanted, -1)
    placement = (wanted == key[...]).astype(F32).astype(BF16)
    placed = dot(placement, values[...])
    entries = dot_t(meta[...].astype(BF16), placement)
    lane = lax.broadcasted_iota(jnp.int32, (24, LANES), 1)
    turn = lax.axis_index("tile") * CHUNK % LANES
    per_tile = LANES // STRIDE
    for t in range(tiles):
        picked[t * CHUNK : (t + 1) * CHUNK] = placed[t * STRIDE : t * STRIDE + CHUNK]
        start = t % per_tile * STRIDE
        used = jnp.logical_and(lane >= start, lane < start + SLOTS)
        block = jnp.where(used, entries[:, t // per_tile * LANES : (t // per_tile + 1) * LANES], 0.0)
        for j in range(3):
            laid = fan(block[j * 8 : (j + 1) * 8], LANES - start)
            row = t * CHUNK + SLOTS + j
            picked[row : row + 1] = jnp.sum(laid, axis=0, keepdims=True)
        group = picked[t * CHUNK + 16 : (t + 1) * CHUNK]
        picked[t * CHUNK + 16 : (t + 1) * CHUNK] = jnp.where(sublane((8, 1)) < 4, group, pltpu.roll(group, turn, 1))
    out[...] = picked[...].astype(BF16)


def tile_kernel(control, mate, out, held):
    even = lax.rem(lax.axis_index("tile"), 2) == 0
    size = control.shape[0]
    out[0:size] = control[...].astype(BF16)
    for r in range(size // 16):
        held[r * 2 : (r + 1) * 2] = jnp.where(
            even, mate[r * 16 : r * 16 + 2], mate[r * 16 + 14 : (r + 1) * 16]
        )
    out[size:] = held[...].astype(BF16)


def relay_kernel(control, mate, oth, out, near4, wide, edge):
    even = lax.rem(lax.axis_index("tile"), 2) == 0
    size = mate.shape[0]
    out[0:size] = control[...].astype(BF16)
    wide[...] = oth[0:size].astype(F32)
    for r in range(size // 16):
        a, b = r * 16, (r + 1) * 16
        edge[r * 2 : (r + 1) * 2] = jnp.where(even, wide[b - 2 : b], wide[a : a + 2])
        near4[r * 4 : (r + 1) * 4] = jnp.where(even, mate[a : a + 4], mate[b - 4 : b])
        start = size // 8 + r * 2
        edge[start : start + 2] = jnp.where(even, mate[a : a + 2], mate[b - 2 : b])
    out[size:] = edge[...].astype(BF16)


def forward_kernel(
    gain_hbm, ws_hbm, wn_hbm, wo_hbm, readout_hbm, error_hbm, background_hbm, control, mate, oth,
    edge0, u1x, d0x, d1x, f2x, field, final, wo, readout, gain, error, background,
    ua, ub, n, act, pre, edge, states, weights, sems,
):
    channels = wo.shape[0]
    halves = weights.at[pl.ds(0, channels)], weights.at[pl.ds(channels, channels)]
    pairs = (
        (gain_hbm, gain), (ws_hbm, halves[0]), (wn_hbm, halves[1]), (wo_hbm, wo), (readout_hbm, readout),
        (error_hbm, error), (background_hbm, background),
    )
    copies = [pltpu.make_async_copy(source, to, sems.at[i]) for i, (source, to) in enumerate(pairs)]
    for copy in copies:
        copy.start()
    members = final.shape[0] // 32
    even = lax.rem(lax.axis_index("tile"), 2) == 0
    tile_at = jnp.where(even, 24, 16)
    edge_at = jnp.where(even, 16, 32)
    far = oth[members * 32 :].astype(F32)
    for r in range(2 * members):
        ua[r * WIDE : r * WIDE + 16] = control[r * 16 : (r + 1) * 16]
        ua[pl.ds(pl.multiple_of(r * WIDE + tile_at, 8), 16)] = oth[r * 16 : (r + 1) * 16].astype(F32)
        near4 = mate[r * 4 : (r + 1) * 4]
        far2 = far[r * 2 : (r + 1) * 2]
        edge[...] = jnp.zeros_like(edge)
        edge[0:4] = near4
        edge[6:8] = far2
        edge[8:10] = far2
        edge[12:16] = near4
        ua[pl.ds(pl.multiple_of(r * WIDE + edge_at, 8), 8)] = jnp.where(even, edge[0:8], edge[8:16])
    for r in range(2 * members):
        edge0[r * 8 : (r + 1) * 8] = slim_edge(ua, r)
    copies[0].wait()
    g = gain[...]

    def keep(ref):
        def store(r, value):
            ref[r * WIDE : (r + 1) * WIDE] = value

        return store

    def keep_states(ref, k):
        own = k * members * 32
        away = (2 + k) * members * 32
        for r in range(2 * members):
            states[own + r * 16 : own + (r + 1) * 16] = ref[r * WIDE : r * WIDE + 16].astype(BF16)
            taken = ref[pl.ds(pl.multiple_of(r * WIDE + tile_at, 8), 16)]
            states[away + r * 16 : away + (r + 1) * 16] = taken.astype(BF16)

    forward_step(ua, n, act, pre, d0x, g, weights, wo, WIDE, members, keep(ub), copies[1:])
    for m in range(members):
        slim_copy(u1x, ub, m)
    keep_states(ub, 0)
    forward_step(ub, n, act, pre, d1x, g, weights, wo, WIDE, members, keep(ua))
    for m in range(members):
        slim_copy(f2x, ua, m)
    keep_states(ua, 1)
    final[...] = states[members * 32 : 2 * members * 32]
    read = dot(states[...], readout[...])
    for q in range(4):
        for m in range(members):
            start = (q * members + m) * 32
            at = slice(m * LANES, (m + 1) * LANES)
            field[q * 32 : (q + 1) * 32, at], field[LANES + q * 32 : LANES + (q + 1) * 32, at] = split(
                read[start : start + 32]
            )


def split(x):
    high = x.astype(BF16)
    return high, (x - high.astype(F32)).astype(BF16)


def spread_of(first, th, tl, scaled, taken, field, pp, spread):
    lane = lax.broadcasted_iota(jnp.int32, (1, LANES), 1)
    members = field.shape[1] // LANES
    for p in range(th.shape[1] // LANES):
        at = slice(p * LANES, (p + 1) * LANES)
        slot = (lane + p * LANES) % CHUNK
        table_of = jnp.where(slot < SLOTS, slot // CAP, -1)
        for q in range(2):
            kept = jnp.where(table_of == first + q, scaled[:, at], 0.0)
            pp[q * 32 : (q + 1) * 32, at], pp[64 + q * 32 : 96 + q * 32, at] = split(kept)
    cross = dot_t(pp[...], th[...])
    cross = cross[:64] + cross[64:] + dot_t(pp[0:64], tl[...])
    block = jnp.concatenate([cross] * 2, axis=1)
    on_block = sublane(block.shape) // 32 == lax.broadcasted_iota(jnp.int32, block.shape, 1) // 32
    target = dot(pp[...], taken[...])
    target = target[:64] + target[64:]
    ch, cl = split(jnp.where(on_block, block, 0.0))
    high = field[first * 32 : (first + 2) * 32]
    low = field[LANES + first * 32 : LANES + (first + 2) * 32]
    mixed = dot(jnp.concatenate([ch, cl], axis=0), high)
    mixed = mixed[:64] + mixed[64:] + dot(ch, low)
    for q in range(2):
        for m in range(members):
            start = (q * members + m) * 32
            value = mixed[q * 32 : (q + 1) * 32, m * LANES : (m + 1) * LANES] - target[q * 32 : (q + 1) * 32]
            spread[start : start + 32] = value.astype(BF16)


def observe_kernel(
    tiles, arrived, field,
    spread, message, th, tl, scaled,
    pp,
):
    steps = 2
    members = field.shape[1] // LANES
    even = lax.rem(lax.axis_index("tile"), 2) == 0
    cells = sublane((32, LANES)).astype(F32)
    lane = lax.broadcasted_iota(jnp.int32, (8, LANES), 1)
    packs = th.shape[1] // LANES
    sums = [[jnp.zeros((8, LANES), F32)] * 3 for _ in range(packs)]
    for d in range(tiles):
        p, start = divmod(d * CHUNK, LANES)
        window = (d * CHUNK + 16) // 16 * 16
        group = arrived[window : window + 16].astype(F32)
        group = group[8:] if d % 2 else group[:8]
        for b in range(3):
            first = start + b * APART
            place = lane - first % LANES
            place = jnp.where(place < 0, place + LANES, place)
            ends = min(LANES - start, SLOTS)
            sums[p][b] = sums[p][b] + jnp.where(place < ends, group, 0.0)
            if ends < SLOTS:
                rest = jnp.logical_and(place >= ends, place < SLOTS)
                sums[p + 1][b] = sums[p + 1][b] + jnp.where(rest, group, 0.0)
    for p in range(packs):
        kinds = [pltpu.roll(sums[p][b], (LANES - b * APART) % LANES, 1) if b else sums[p][b] for b in range(3)]
        entry = [kinds[i % 3][4 + i // 3 : 5 + i // 3] for i in range(9)]
        weight = jnp.zeros((32, LANES), F32)
        for i in range(4):
            weight += jnp.where(cells == entry[i], entry[4 + i], 0.0)
        at = slice(p * LANES, (p + 1) * LANES)
        th[:, at], tl[:, at] = split(weight)
        scaled[:, at] = weight * entry[8]
    spread_of(0, th, tl, scaled, arrived, field, pp, spread)
    size = members * 32
    for k in range(steps):
        for m in range(members):
            start = k * size + m * 32
            pair = spread[start : start + 32].astype(F32)
            near = [jnp.where(even, pair[i + 8 : i + 16], pair[i : i + 8]) for i in (0, 16)]
            start = k * size // 2 + m * 16
            message[start : start + 16] = jnp.concatenate(near, axis=0).astype(BF16)


def adjoint_step(u, cot, gb, gm, flat, d, out, gain, ws, wn, wo, members):
    both = 2 * SLIM
    gb[...] = cot[...].astype(BF16)
    flat[...] = dot_t(gb[...], wo[...])
    gb[...] = (flat[...] * d[...]).astype(BF16)
    gm[...] = dot_t(gb[...], wn[...])
    flat[...] = dot_t(gb[...], ws[...])
    for m in range(members):
        base = m * both
        rows = []
        for lat in range(2):
            start = base + lat * SLIM
            rows.append(gm[start : start + SLIM].astype(BF16).astype(F32))
        around = neighbours(rows)
        for lat in range(2):
            start = base + lat * SLIM
            x = u[start : start + SLIM]
            s = inverse_rms(x)
            scaled = gain * (flat[start : start + SLIM] + around[lat])
            inner = jnp.mean(x * scaled, axis=-1, keepdims=True)
            out(2 * m + lat, cot[start : start + SLIM] + s * scaled - x * (s * s * s * inner))


def edges(nxt, size, edge, r):
    even = lax.rem(lax.axis_index("tile"), 2) == 0
    start = size + r * 2
    far = nxt[start : start + 2]
    start = size + size // 8 + r * 2
    near = nxt[start : start + 2]
    edge[...] = jnp.zeros_like(edge)
    edge[0:2] = near
    edge[6:8] = far
    edge[8:10] = far
    edge[14:16] = near
    return jnp.where(even, edge[0:8], edge[8:16])


def pull_kernel(
    wn_hbm, ws_hbm, spread_own, readout, th, tl, scaled, arrived, field,
    pulled, away, wn, ws,
    pp, spread, near, sems,
):
    pairs = ((wn_hbm, wn), (ws_hbm, ws))
    copies = [pltpu.make_async_copy(source, to, sems.at[i]) for i, (source, to) in enumerate(pairs)]
    for copy in copies:
        copy.start()
    even = lax.rem(lax.axis_index("tile"), 2) == 0
    pulled[...] = dot_t(spread_own[...], readout[...])
    spread_of(2, th, tl, scaled, arrived, field, pp, spread)
    for start in range(0, spread.shape[0], 32):
        pair = spread[start : start + 32].astype(F32)
        rows = [jnp.where(even, pair[i + 8 : i + 16], pair[i : i + 8]) for i in (0, 16)]
        near[start // 2 : start // 2 + 16] = jnp.concatenate(rows, axis=0).astype(BF16)
    away[...] = dot_t(near[...], readout[...])
    for copy in copies:
        copy.wait()


def backward_kernel(
    pulled, away, wn, ws, gain, control, edge0, message16, f2x, wo, readout, error, message,
    u1x, d0x, d1x,
    result,
    cot2, cot1, gb, gm, flat, mate_pull, edge, u0x, final, nxt,
):
    size = result.shape[0]
    members = size // 32
    even = lax.rem(lax.axis_index("tile"), 2) == 0
    nxt[...] = message16[...].astype(F32)
    weight = jnp.where(lax.axis_index("slot") == lax.axis_size("slot") - 1, 0.0, 1.0) * error[...]
    row8 = sublane((8, 1))
    mate_side = jnp.where(even, 1, 0) == jnp.where(row8 < 4, 1, 0)
    mate_pull[...] = dot_t(message[...], readout[...])
    final[...] = f2x[...].astype(F32)

    def pulls(k, r):
        own = k * size + r * 16
        near = k * size // 2 + r * 8
        group = jnp.where(mate_side, mate_pull[near : near + 8], away[near : near + 8])
        return pulled[own : own + 16], group

    for r in range(2 * members):
        own, group = pulls(1, r)
        a, b = r * SLIM, r * SLIM + 16
        cot2[a:b] = own - weight * (nxt[r * 16 : (r + 1) * 16] - final[a:b])
        u0x[a:b] = control[r * 16 : (r + 1) * 16]
        a, b = b, b + 8
        cot2[a:b] = group - weight * (edges(nxt, size, edge, r) - final[a:b])
        u0x[a:b] = edge0[r * 8 : (r + 1) * 8]

    def keep(r, value):
        cot1[r * SLIM : (r + 1) * SLIM] = value + jnp.concatenate(pulls(0, r), axis=0)

    def finish(r, value):
        a, b = r * SLIM, r * SLIM + 16
        result[r * 16 : (r + 1) * 16] = value[0:16] + error[...] * u0x[a:b]

    adjoint_step(u1x, cot2, gb, gm, flat, d1x, keep, gain[...], ws, wn, wo, members)
    adjoint_step(u0x, cot1, gb, gm, flat, d0x, finish, gain[...], ws, wn, wo, members)


def last_kernel(base, background, before, error, result):
    first = lax.axis_index("slot") == 0
    taken = jnp.where(first, background[...].astype(F32), before[...].astype(F32))
    result[...] = base[...] - error[...] * taken


def kernel_call(body, outs, scratch, flops, moved, hbm=0, out_places=None, aliases={}):
    def call(*operands):
        fixed = [i in range(hbm) and i not in aliases for i in range(len(operands))]
        operands = [
            pltpu.with_memory_space_constraint(x, pltpu.HBM) if fix else x for x, fix in zip(operands, fixed)
        ]
        places = [pltpu.HBM] * hbm + [pltpu.VMEM] * (len(operands) - hbm)
        given = {} if out_places is None else {"out_specs": [pl.BlockSpec(memory_space=p) for p in out_places]}
        return pl.pallas_call(
            body,
            out_shape=outs,
            in_specs=[pl.BlockSpec(memory_space=place) for place in places],
            **given,
            scratch_shapes=scratch,
            input_output_aliases=aliases,
            compiler_params=pltpu.CompilerParams(vmem_limit_bytes=VMEM_LIMIT),
            cost_estimate=pl.CostEstimate(flops=flops, bytes_accessed=moved, transcendentals=0),
        )(*operands)

    return call


def per_device(
    control,
    background,
    self_weight,
    neighbour_weight,
    output_weight,
    norm_gain,
    readout,
    error_weight,
    report_owner,
    report_stencil,
    report_weights,
    report_values,
    report_precision,
):
    tiles = lax.axis_size("tile")
    slots = lax.axis_size("slot")
    members, lats, cols, channels = control.shape[1:]
    groups = members * lats
    size = groups * cols
    steps = report_owner.shape[1]
    rows = report_owner.shape[2]
    gain = norm_gain.reshape(1, channels)
    error = error_weight.reshape(1, channels)
    flat = control.reshape(size, channels)

    def spec(count, dtype=F32, width=channels):
        return jax.ShapeDtypeStruct((count, width), dtype)

    def scratch(count, dtype=F32, width=channels):
        return pltpu.VMEM((count, width), dtype)

    mate_of = [(i, i ^ 1) for i in range(tiles)]
    other_of = [(i, (i - 1) % tiles if i % 2 == 0 else (i + 1) % tiles) for i in range(tiles)]

    def across(block, shift):
        pairs = [
            ((s + shift) % slots * tiles + i, s * tiles + i) for s in range(slots) for i in range(tiles)
        ]
        return lax.ppermute(block, ("slot", "tile"), pairs)

    mate = lax.ppermute(flat, "tile", mate_of)
    listed = (
        jnp.transpose(report_owner[0], (0, 2, 1)),
        jnp.transpose(report_stencil[0], (0, 2, 1)),
        jnp.transpose(report_weights[0], (0, 2, 1)),
        report_precision[0],
        report_values[0].reshape(steps * rows, LANES),
    )
    work = [
        pltpu.VMEM((1, steps * rows), jnp.int32),
        scratch(24, F32, steps * rows),
        scratch(tiles * CHUNK, F32, LANES),
        scratch(tiles * CHUNK, BF16, LANES),
    ]
    held, packed, *listed = kernel_call(
        first_kernel,
        [spec(size), spec(tiles * CHUNK, BF16, LANES)]
        + [jax.ShapeDtypeStruct(block.shape, block.dtype) for block in listed],
        work + [pltpu.SemaphoreType.DMA((7,))],
        10**7,
        200000,
        hbm=6,
        out_places=[pltpu.VMEM, pltpu.HBM] + [pltpu.VMEM] * 5,
    )(flat, *listed)
    sent = kernel_call(
        tile_kernel, spec(groups * (cols + 2), BF16), [scratch(groups * 2)], 1000, 400000
    )(held, mate)
    oth = lax.ppermute(sent, "tile", other_of)
    (packed,) = kernel_call(
        later_kernel,
        [spec(tiles * CHUNK, BF16, LANES)],
        work + [pltpu.SemaphoreType.DMA],
        10**7,
        200000,
        hbm=1,
        out_places=[pltpu.HBM],
        aliases={0: 0},
    )(packed, *listed, sent)
    arrived = lax.all_to_all(packed, "tile", split_axis=0, concat_axis=0, tiled=True)

    message, near4 = kernel_call(
        relay_kernel,
        [spec(size + 4 * groups, BF16), spec(4 * groups)],
        [scratch(size), scratch(4 * groups)],
        1000,
        700000,
    )(held, mate, oth)
    nxt = across(message, 1)
    wide = groups * WIDE
    slim = groups * SLIM
    (
        edge0, u1x, d0x, d1x, f2x, field, final, wo, readout_held, gain_held, error_held, background_held,
    ) = kernel_call(
        forward_kernel,
        [spec(groups * 8), spec(slim)] + [spec(slim, BF16)] * 3
        + [spec(8 * lats * cols, BF16, members * LANES), spec(size, BF16)]
        + [spec(channels, BF16), spec(channels, BF16, LANES), spec(1), spec(1), spec(size, BF16)],
        [scratch(wide), scratch(wide), scratch(wide, BF16, 2 * channels), scratch(wide, BF16)]
        + [scratch(wide), scratch(16), scratch(4 * size, BF16)]
        + [scratch(2 * channels, BF16), pltpu.SemaphoreType.DMA((7,))],
        10**11,
        4000000,
        hbm=7,
    )(
        gain, self_weight, neighbour_weight, output_weight, readout, error, background.reshape(size, channels),
        held, near4, oth,
    )
    before = across(final, -1)
    total = tiles * CHUNK
    tables = [scratch(128, BF16, total)]
    spread, near_spread, *reports_held = kernel_call(
        functools.partial(observe_kernel, tiles),
        [spec(2 * size, BF16, LANES), spec(size, BF16, LANES)]
        + [spec(32, BF16, total), spec(32, BF16, total), spec(32, F32, total)],
        tables,
        10**9,
        2000000,
    )(arrived, field)
    from_mate = lax.ppermute(near_spread, "tile", mate_of)
    handed = kernel_call(
        pull_kernel,
        [spec(2 * size), spec(size), spec(channels, BF16), spec(channels, BF16)],
        tables + [scratch(2 * size, BF16, LANES), scratch(size, BF16, LANES), pltpu.SemaphoreType.DMA((2,))],
        10**9,
        3000000,
        hbm=2,
    )(neighbour_weight, self_weight, spread, readout_held, *reports_held, arrived, field)
    base = kernel_call(
        backward_kernel,
        spec(size),
        [scratch(slim), scratch(slim), scratch(slim, BF16), scratch(slim), scratch(slim)]
        + [scratch(size), scratch(16), scratch(slim), scratch(slim), scratch(size + 4 * groups)],
        12 * slim * channels * channels,
        6000000,
    )(
        *handed, gain_held, held, edge0, nxt, f2x, wo, readout_held, error_held, from_mate,
        u1x, d0x, d1x,
    )
    result = kernel_call(last_kernel, spec(size), [], 10**6, 900000)(base, background_held, before, error_held)
    return result.reshape(control.shape)


def solution(mesh):
    in_specs = (
        P("slot", None, None, "tile", None),
        P(None, None, "tile", None),
        P(),
        P(),
        P(),
        P(),
        P(),
        P(),
        P("slot", None, "tile", None),
        P("slot", None, "tile", None),
        P("slot", None, "tile", None),
        P("slot", None, "tile", None),
        P("slot", None, "tile"),
    )
    out_specs = P("slot", None, None, "tile", None)
    return jax.shard_map(
        per_device, mesh=mesh, in_specs=in_specs, out_specs=out_specs, check_vma=False
    )
```

```python
import functools
import jax
import jax.numpy as jnp
from jax import lax
from jax.experimental import pallas as pl
from jax.experimental.pallas import tpu as pltpu
from jax.sharding import PartitionSpec as P

EPSILON = 1e-06
F32 = jnp.float32
BF16 = jnp.bfloat16
LANES = 128
CAP = 5
SLOTS = 4 * CAP
CHUNK = 24
APART = 36
STRIDE = 32
WIDE = 40
SLIM = 24
VMEM_LIMIT = 28 * 1024 * 1024


def dot(a, b):
    return jnp.dot(a, b, preferred_element_type=F32)


def dot_t(a, b):
    return lax.dot_general(a, b, (((1,), (1,)), ((), ())), preferred_element_type=F32)


def sublane(shape):
    return lax.broadcasted_iota(jnp.int32, shape, 0)


def inverse_rms(x):
    return lax.rsqrt(jnp.mean(x * x, axis=-1, keepdims=True) + EPSILON)


def sigmoid(p):
    return 0.5 * jnp.tanh(0.5 * p) + 0.5


def neighbours(rows):
    width = rows[0].shape[0]
    return [
        0.25 * (rows[1 - i] + pltpu.roll(rows[i], 1, 0) + pltpu.roll(rows[i], width - 1, 0))
        for i in range(2)
    ]


def forward_step(u, n, act, pre, d, gain, weights, wo, width, members, out, copies=()):
    both = 2 * width
    for m in range(members):
        base = m * both
        rows = []
        for lat in range(2):
            x = u[base + lat * width : base + (lat + 1) * width]
            rows.append((x * inverse_rms(x) * gain).astype(BF16).astype(F32))
        channels = rows[0].shape[1]
        n[base : base + both, :channels] = jnp.concatenate(rows, axis=0).astype(BF16)
        n[base : base + both, channels:] = jnp.concatenate(neighbours(rows), axis=0).astype(BF16)
    for copy in copies[:2]:
        copy.wait()
    pre[...] = dot(n[...], weights[...])
    for m in range(members):
        base = m * both
        p = pre[base : base + both]
        sig = sigmoid(p)
        act[base : base + both] = (p * sig).astype(BF16)
        if d is not None:
            pre[base : base + both] = sig * (1.0 + p * (1.0 - sig))
    if d is not None:
        for m in range(members):
            slim_copy(d, pre, m)
    for copy in copies[2:]:
        copy.wait()
    pre[...] = dot(act[...], wo[...])
    for r in range(2 * members):
        out(r, u[r * width : (r + 1) * width] + pre[r * width : (r + 1) * width])


def slim_edge(wide, r):
    low = wide[r * WIDE + 16 : r * WIDE + 24]
    high = wide[r * WIDE + 32 : r * WIDE + 40]
    return jnp.where(sublane(low.shape) < 4, low, high)


def slim_copy(to, wide, m):
    parts = []
    for r in (2 * m, 2 * m + 1):
        parts += [wide[r * WIDE : r * WIDE + 16], slim_edge(wide, r)]
    both = jnp.concatenate(parts, axis=0)
    to[m * 2 * SLIM : (m + 1) * 2 * SLIM] = both.astype(to.dtype)


def reports(arrays, out_hbm, key, meta, picked, out, sem):
    pack(*arrays, out, key, meta, picked)
    store = pltpu.make_async_copy(out, out_hbm, sem)
    store.start()
    store.wait()


def early():
    return lax.axis_index("tile") < lax.axis_size("tile") // 2


def first_kernel(control_hbm, *refs):
    sources, (held, out_hbm), arrays, (key, meta, picked, out, sems) = refs[:5], refs[5:7], refs[7:12], refs[12:]
    copies = [
        pltpu.make_async_copy(source, to, sems.at[i]) for i, (source, to) in enumerate(zip(sources, arrays))
    ]
    copies.append(pltpu.make_async_copy(control_hbm, held, sems.at[5]))
    for copy in copies:
        copy.start()
    for copy in copies[:5]:
        copy.wait()

    @pl.when(early())
    def _():
        reports(arrays, out_hbm, key, meta, picked, out, sems.at[6])

    copies[5].wait()


def later_kernel(packed_hbm, *refs):
    arrays, out_hbm, (key, meta, picked, out, sem) = refs[:5], refs[6], refs[7:]

    @pl.when(jnp.logical_not(early()))
    def _():
        reports(arrays, out_hbm, key, meta, picked, out, sem)


def fan(x, shift):
    if shift % LANES:
        x = pltpu.roll(x, shift % LANES, 1)
    for _ in range(2):
        x = pltpu.roll(x, 0, 1, stride=APART // 2, stride_axis=0)
    return x


def pack(owner, stencil, weights, precision, values, out, key, meta, picked):
    steps, _, rows = owner.shape
    tiles = out.shape[0] // CHUNK
    total = steps * rows
    earlier = lax.broadcasted_iota(jnp.int32, (rows, rows), 0) < lax.broadcasted_iota(jnp.int32, (rows, rows), 1)
    earlier = earlier.astype(F32).astype(BF16)
    meta[...] = jnp.zeros_like(meta)
    for k in range(steps):
        at = slice(k * rows, (k + 1) * rows)
        named = lax.broadcasted_iota(jnp.int32, (tiles, rows), 0) == owner[k]
        hits = named.astype(F32)
        before = dot(hits.astype(BF16), earlier)
        rank = jnp.sum(hits * before, axis=0, keepdims=True).astype(jnp.int32)
        key[0:1, at] = owner[k] * (2 * CAP) + k * CAP + rank
        for i in range(4):
            meta[i // 3 * 8 + i % 3 : i // 3 * 8 + i % 3 + 1, at] = stencil[k, i : i + 1].astype(F32)
            j = 4 + i
            meta[j // 3 * 8 + j % 3 : j // 3 * 8 + j % 3 + 1, at] = weights[k, i : i + 1].astype(F32)
        meta[18:19, at] = precision[k : k + 1].astype(F32)
    row = lax.broadcasted_iota(jnp.int32, (tiles * STRIDE, total), 0)
    tile = row // STRIDE
    slot = row % STRIDE
    other = jnp.where(tile % 2 == 0, (tile + tiles - 1) % tiles, (tile + 1) % tiles)
    mine = slot < 2 * CAP
    wanted = jnp.where(mine, tile * (2 * CAP) + slot, other * (2 * CAP) + slot - 2 * CAP)
    wanted = jnp.where(slot < SLOTS, wanted, -1)
    placement = (wanted == key[...]).astype(F32).astype(BF16)
    placed = dot(placement, values[...])
    entries = dot_t(meta[...].astype(BF16), placement)
    lane = lax.broadcasted_iota(jnp.int32, (24, LANES), 1)
    turn = lax.axis_index("tile") * CHUNK % LANES
    per_tile = LANES // STRIDE
    for t in range(tiles):
        picked[t * CHUNK : (t + 1) * CHUNK] = placed[t * STRIDE : t * STRIDE + CHUNK]
        start = t % per_tile * STRIDE
        used = jnp.logical_and(lane >= start, lane < start + SLOTS)
        block = jnp.where(used, entries[:, t // per_tile * LANES : (t // per_tile + 1) * LANES], 0.0)
        for j in range(3):
            laid = fan(block[j * 8 : (j + 1) * 8], LANES - start)
            row = t * CHUNK + SLOTS + j
            picked[row : row + 1] = jnp.sum(laid, axis=0, keepdims=True)
        group = picked[t * CHUNK + 16 : (t + 1) * CHUNK]
        picked[t * CHUNK + 16 : (t + 1) * CHUNK] = jnp.where(sublane((8, 1)) < 4, group, pltpu.roll(group, turn, 1))
    out[...] = picked[...].astype(BF16)


def tile_kernel(control, mate, out, held):
    even = lax.rem(lax.axis_index("tile"), 2) == 0
    size = control.shape[0]
    out[0:size] = control[...].astype(BF16)
    for r in range(size // 16):
        held[r * 2 : (r + 1) * 2] = jnp.where(
            even, mate[r * 16 : r * 16 + 2], mate[r * 16 + 14 : (r + 1) * 16]
        )
    out[size:] = held[...].astype(BF16)


def relay_kernel(control, mate, oth, out, near4, wide, edge):
    even = lax.rem(lax.axis_index("tile"), 2) == 0
    size = mate.shape[0]
    out[0:size] = control[...].astype(BF16)
    wide[...] = oth[0:size].astype(F32)
    for r in range(size // 16):
        a, b = r * 16, (r + 1) * 16
        edge[r * 2 : (r + 1) * 2] = jnp.where(even, wide[b - 2 : b], wide[a : a + 2])
        near4[r * 4 : (r + 1) * 4] = jnp.where(even, mate[a : a + 4], mate[b - 4 : b])
        start = size // 8 + r * 2
        edge[start : start + 2] = jnp.where(even, mate[a : a + 2], mate[b - 2 : b])
    out[size:] = edge[...].astype(BF16)


def forward_kernel(
    gain_hbm, ws_hbm, wn_hbm, wo_hbm, readout_hbm, error_hbm, background_hbm, control, mate, oth,
    edge0, u1x, d0x, d1x, f2x, field, final, wo, readout, gain, error, background,
    ua, ub, n, act, pre, edge, states, weights, sems,
):
    channels = wo.shape[0]
    halves = weights.at[pl.ds(0, channels)], weights.at[pl.ds(channels, channels)]
    pairs = (
        (gain_hbm, gain), (ws_hbm, halves[0]), (wn_hbm, halves[1]), (wo_hbm, wo), (readout_hbm, readout),
        (error_hbm, error), (background_hbm, background),
    )
    copies = [pltpu.make_async_copy(source, to, sems.at[i]) for i, (source, to) in enumerate(pairs)]
    for copy in copies:
        copy.start()
    members = final.shape[0] // 32
    even = lax.rem(lax.axis_index("tile"), 2) == 0
    tile_at = jnp.where(even, 24, 16)
    edge_at = jnp.where(even, 16, 32)
    far = oth[members * 32 :].astype(F32)
    for r in range(2 * members):
        ua[r * WIDE : r * WIDE + 16] = control[r * 16 : (r + 1) * 16]
        ua[pl.ds(pl.multiple_of(r * WIDE + tile_at, 8), 16)] = oth[r * 16 : (r + 1) * 16].astype(F32)
        near4 = mate[r * 4 : (r + 1) * 4]
        far2 = far[r * 2 : (r + 1) * 2]
        edge[...] = jnp.zeros_like(edge)
        edge[0:4] = near4
        edge[6:8] = far2
        edge[8:10] = far2
        edge[12:16] = near4
        ua[pl.ds(pl.multiple_of(r * WIDE + edge_at, 8), 8)] = jnp.where(even, edge[0:8], edge[8:16])
    for r in range(2 * members):
        edge0[r * 8 : (r + 1) * 8] = slim_edge(ua, r)
    copies[0].wait()
    g = gain[...]

    def keep(ref):
        def store(r, value):
            ref[r * WIDE : (r + 1) * WIDE] = value

        return store

    def keep_states(ref, k):
        own = k * members * 32
        away = (2 + k) * members * 32
        for r in range(2 * members):
            states[own + r * 16 : own + (r + 1) * 16] = ref[r * WIDE : r * WIDE + 16].astype(BF16)
            taken = ref[pl.ds(pl.multiple_of(r * WIDE + tile_at, 8), 16)]
            states[away + r * 16 : away + (r + 1) * 16] = taken.astype(BF16)

    forward_step(ua, n, act, pre, d0x, g, weights, wo, WIDE, members, keep(ub), copies[1:])
    for m in range(members):
        slim_copy(u1x, ub, m)
    keep_states(ub, 0)
    forward_step(ub, n, act, pre, d1x, g, weights, wo, WIDE, members, keep(ua))
    for m in range(members):
        slim_copy(f2x, ua, m)
    keep_states(ua, 1)
    final[...] = states[members * 32 : 2 * members * 32]
    read = dot(states[...], readout[...])
    for q in range(4):
        for m in range(members):
            start = (q * members + m) * 32
            at = slice(m * LANES, (m + 1) * LANES)
            field[q * 32 : (q + 1) * 32, at], field[LANES + q * 32 : LANES + (q + 1) * 32, at] = split(
                read[start : start + 32]
            )


def split(x):
    high = x.astype(BF16)
    return high, (x - high.astype(F32)).astype(BF16)


def spread_of(first, th, tl, scaled, taken, field, pp, spread):
    lane = lax.broadcasted_iota(jnp.int32, (1, LANES), 1)
    members = field.shape[1] // LANES
    for p in range(th.shape[1] // LANES):
        at = slice(p * LANES, (p + 1) * LANES)
        slot = (lane + p * LANES) % CHUNK
        table_of = jnp.where(slot < SLOTS, slot // CAP, -1)
        for q in range(2):
            kept = jnp.where(table_of == first + q, scaled[:, at], 0.0)
            pp[q * 32 : (q + 1) * 32, at], pp[64 + q * 32 : 96 + q * 32, at] = split(kept)
    cross = dot_t(pp[...], th[...])
    cross = cross[:64] + cross[64:] + dot_t(pp[0:64], tl[...])
    block = jnp.concatenate([cross] * 2, axis=1)
    on_block = sublane(block.shape) // 32 == lax.broadcasted_iota(jnp.int32, block.shape, 1) // 32
    target = dot(pp[...], taken[...])
    target = target[:64] + target[64:]
    ch, cl = split(jnp.where(on_block, block, 0.0))
    high = field[first * 32 : (first + 2) * 32]
    low = field[LANES + first * 32 : LANES + (first + 2) * 32]
    mixed = dot(jnp.concatenate([ch, cl], axis=0), high)
    mixed = mixed[:64] + mixed[64:] + dot(ch, low)
    for q in range(2):
        for m in range(members):
            start = (q * members + m) * 32
            value = mixed[q * 32 : (q + 1) * 32, m * LANES : (m + 1) * LANES] - target[q * 32 : (q + 1) * 32]
            spread[start : start + 32] = value.astype(BF16)


def observe_kernel(
    tiles, arrived, field,
    spread, message, th, tl, scaled,
    pp,
):
    steps = 2
    members = field.shape[1] // LANES
    even = lax.rem(lax.axis_index("tile"), 2) == 0
    cells = sublane((32, LANES)).astype(F32)
    lane = lax.broadcasted_iota(jnp.int32, (8, LANES), 1)
    packs = th.shape[1] // LANES
    sums = [[jnp.zeros((8, LANES), F32)] * 3 for _ in range(packs)]
    for d in range(tiles):
        p, start = divmod(d * CHUNK, LANES)
        window = (d * CHUNK + 16) // 16 * 16
        group = arrived[window : window + 16].astype(F32)
        group = group[8:] if d % 2 else group[:8]
        for b in range(3):
            first = start + b * APART
            place = lane - first % LANES
            place = jnp.where(place < 0, place + LANES, place)
            ends = min(LANES - start, SLOTS)
            sums[p][b] = sums[p][b] + jnp.where(place < ends, group, 0.0)
            if ends < SLOTS:
                rest = jnp.logical_and(place >= ends, place < SLOTS)
                sums[p + 1][b] = sums[p + 1][b] + jnp.where(rest, group, 0.0)
    for p in range(packs):
        kinds = [pltpu.roll(sums[p][b], (LANES - b * APART) % LANES, 1) if b else sums[p][b] for b in range(3)]
        entry = [kinds[i % 3][4 + i // 3 : 5 + i // 3] for i in range(9)]
        weight = jnp.zeros((32, LANES), F32)
        for i in range(4):
            weight += jnp.where(cells == entry[i], entry[4 + i], 0.0)
        at = slice(p * LANES, (p + 1) * LANES)
        th[:, at], tl[:, at] = split(weight)
        scaled[:, at] = weight * entry[8]
    spread_of(0, th, tl, scaled, arrived, field, pp, spread)
    size = members * 32
    for k in range(steps):
        for m in range(members):
            start = k * size + m * 32
            pair = spread[start : start + 32].astype(F32)
            near = [jnp.where(even, pair[i + 8 : i + 16], pair[i : i + 8]) for i in (0, 16)]
            start = k * size // 2 + m * 16
            message[start : start + 16] = jnp.concatenate(near, axis=0).astype(BF16)


def adjoint_step(u, cot, gb, gm, flat, d, out, gain, ws, wn, wo, members):
    both = 2 * SLIM
    gb[...] = cot[...].astype(BF16)
    flat[...] = dot_t(gb[...], wo[...])
    gb[...] = (flat[...] * d[...]).astype(BF16)
    gm[...] = dot_t(gb[...], wn[...])
    flat[...] = dot_t(gb[...], ws[...])
    for m in range(members):
        base = m * both
        rows = []
        for lat in range(2):
            start = base + lat * SLIM
            rows.append(gm[start : start + SLIM].astype(BF16).astype(F32))
        around = neighbours(rows)
        for lat in range(2):
            start = base + lat * SLIM
            x = u[start : start + SLIM]
            s = inverse_rms(x)
            scaled = gain * (flat[start : start + SLIM] + around[lat])
            inner = jnp.mean(x * scaled, axis=-1, keepdims=True)
            out(2 * m + lat, cot[start : start + SLIM] + s * scaled - x * (s * s * s * inner))


def edges(nxt, size, edge, r):
    even = lax.rem(lax.axis_index("tile"), 2) == 0
    start = size + r * 2
    far = nxt[start : start + 2]
    start = size + size // 8 + r * 2
    near = nxt[start : start + 2]
    edge[...] = jnp.zeros_like(edge)
    edge[0:2] = near
    edge[6:8] = far
    edge[8:10] = far
    edge[14:16] = near
    return jnp.where(even, edge[0:8], edge[8:16])


def pull_kernel(
    wn_hbm, ws_hbm, spread_own, readout, th, tl, scaled, arrived, field,
    pulled, away, wn, ws,
    pp, spread, near, sems,
):
    pairs = ((wn_hbm, wn), (ws_hbm, ws))
    copies = [pltpu.make_async_copy(source, to, sems.at[i]) for i, (source, to) in enumerate(pairs)]
    for copy in copies:
        copy.start()
    even = lax.rem(lax.axis_index("tile"), 2) == 0
    pulled[...] = dot_t(spread_own[...], readout[...])
    spread_of(2, th, tl, scaled, arrived, field, pp, spread)
    for start in range(0, spread.shape[0], 32):
        pair = spread[start : start + 32].astype(F32)
        rows = [jnp.where(even, pair[i + 8 : i + 16], pair[i : i + 8]) for i in (0, 16)]
        near[start // 2 : start // 2 + 16] = jnp.concatenate(rows, axis=0).astype(BF16)
    away[...] = dot_t(near[...], readout[...])
    for copy in copies:
        copy.wait()


def backward_kernel(
    pulled, away, wn, ws, gain, control, edge0, message16, f2x, wo, readout, error, message,
    u1x, d0x, d1x,
    result,
    cot2, cot1, gb, gm, flat, mate_pull, edge, u0x, final, nxt,
):
    size = result.shape[0]
    members = size // 32
    even = lax.rem(lax.axis_index("tile"), 2) == 0
    nxt[...] = message16[...].astype(F32)
    weight = jnp.where(lax.axis_index("slot") == lax.axis_size("slot") - 1, 0.0, 1.0) * error[...]
    row8 = sublane((8, 1))
    mate_side = jnp.where(even, 1, 0) == jnp.where(row8 < 4, 1, 0)
    mate_pull[...] = dot_t(message[...], readout[...])
    final[...] = f2x[...].astype(F32)

    def pulls(k, r):
        own = k * size + r * 16
        near = k * size // 2 + r * 8
        group = jnp.where(mate_side, mate_pull[near : near + 8], away[near : near + 8])
        return pulled[own : own + 16], group

    for r in range(2 * members):
        own, group = pulls(1, r)
        a, b = r * SLIM, r * SLIM + 16
        cot2[a:b] = own - weight * (nxt[r * 16 : (r + 1) * 16] - final[a:b])
        u0x[a:b] = control[r * 16 : (r + 1) * 16]
        a, b = b, b + 8
        cot2[a:b] = group - weight * (edges(nxt, size, edge, r) - final[a:b])
        u0x[a:b] = edge0[r * 8 : (r + 1) * 8]

    def keep(r, value):
        cot1[r * SLIM : (r + 1) * SLIM] = value + jnp.concatenate(pulls(0, r), axis=0)

    def finish(r, value):
        a, b = r * SLIM, r * SLIM + 16
        result[r * 16 : (r + 1) * 16] = value[0:16] + error[...] * u0x[a:b]

    adjoint_step(u1x, cot2, gb, gm, flat, d1x, keep, gain[...], ws, wn, wo, members)
    adjoint_step(u0x, cot1, gb, gm, flat, d0x, finish, gain[...], ws, wn, wo, members)


def last_kernel(base, background, before, error, result, held, sems):
    first = lax.axis_index("slot") == 0
    count = base.shape[0] // sems.shape[0]
    copies = []
    for i in range(sems.shape[0]):
        at = slice(i * count, (i + 1) * count)
        taken = jnp.where(first, background[at].astype(F32), before[at].astype(F32))
        held[at] = base[at] - error[...] * taken
        rows = pl.ds(i * count, count)
        copies.append(pltpu.make_async_copy(held.at[rows], result.at[rows], sems.at[i]))
        copies[-1].start()
    for copy in copies:
        copy.wait()


def kernel_call(body, outs, scratch, flops, moved, hbm=0, out_places=None, aliases={}):
    def call(*operands):
        fixed = [i in range(hbm) and i not in aliases for i in range(len(operands))]
        operands = [
            pltpu.with_memory_space_constraint(x, pltpu.HBM) if fix else x for x, fix in zip(operands, fixed)
        ]
        places = [pltpu.HBM] * hbm + [pltpu.VMEM] * (len(operands) - hbm)
        given = {} if out_places is None else {"out_specs": [pl.BlockSpec(memory_space=p) for p in out_places]}
        return pl.pallas_call(
            body,
            out_shape=outs,
            in_specs=[pl.BlockSpec(memory_space=place) for place in places],
            **given,
            scratch_shapes=scratch,
            input_output_aliases=aliases,
            compiler_params=pltpu.CompilerParams(vmem_limit_bytes=VMEM_LIMIT),
            cost_estimate=pl.CostEstimate(flops=flops, bytes_accessed=moved, transcendentals=0),
        )(*operands)

    return call


def per_device(
    control,
    background,
    self_weight,
    neighbour_weight,
    output_weight,
    norm_gain,
    readout,
    error_weight,
    report_owner,
    report_stencil,
    report_weights,
    report_values,
    report_precision,
):
    tiles = lax.axis_size("tile")
    slots = lax.axis_size("slot")
    members, lats, cols, channels = control.shape[1:]
    groups = members * lats
    size = groups * cols
    steps = report_owner.shape[1]
    rows = report_owner.shape[2]
    gain = norm_gain.reshape(1, channels)
    error = error_weight.reshape(1, channels)
    flat = control.reshape(size, channels)

    def spec(count, dtype=F32, width=channels):
        return jax.ShapeDtypeStruct((count, width), dtype)

    def scratch(count, dtype=F32, width=channels):
        return pltpu.VMEM((count, width), dtype)

    mate_of = [(i, i ^ 1) for i in range(tiles)]
    other_of = [(i, (i - 1) % tiles if i % 2 == 0 else (i + 1) % tiles) for i in range(tiles)]

    def across(block, shift):
        pairs = [
            ((s + shift) % slots * tiles + i, s * tiles + i) for s in range(slots) for i in range(tiles)
        ]
        return lax.ppermute(block, ("slot", "tile"), pairs)

    mate = lax.ppermute(flat, "tile", mate_of)
    listed = (
        jnp.transpose(report_owner[0], (0, 2, 1)),
        jnp.transpose(report_stencil[0], (0, 2, 1)),
        jnp.transpose(report_weights[0], (0, 2, 1)),
        report_precision[0],
        report_values[0].reshape(steps * rows, LANES),
    )
    work = [
        pltpu.VMEM((1, steps * rows), jnp.int32),
        scratch(24, F32, steps * rows),
        scratch(tiles * CHUNK, F32, LANES),
        scratch(tiles * CHUNK, BF16, LANES),
    ]
    held, packed, *listed = kernel_call(
        first_kernel,
        [spec(size), spec(tiles * CHUNK, BF16, LANES)]
        + [jax.ShapeDtypeStruct(block.shape, block.dtype) for block in listed],
        work + [pltpu.SemaphoreType.DMA((7,))],
        10**7,
        200000,
        hbm=6,
        out_places=[pltpu.VMEM, pltpu.HBM] + [pltpu.VMEM] * 5,
    )(flat, *listed)
    sent = kernel_call(
        tile_kernel, spec(groups * (cols + 2), BF16), [scratch(groups * 2)], 1000, 400000
    )(held, mate)
    oth = lax.ppermute(sent, "tile", other_of)
    (packed,) = kernel_call(
        later_kernel,
        [spec(tiles * CHUNK, BF16, LANES)],
        work + [pltpu.SemaphoreType.DMA],
        10**7,
        200000,
        hbm=1,
        out_places=[pltpu.HBM],
        aliases={0: 0},
    )(packed, *listed, sent)
    arrived = lax.all_to_all(packed, "tile", split_axis=0, concat_axis=0, tiled=True)

    message, near4 = kernel_call(
        relay_kernel,
        [spec(size + 4 * groups, BF16), spec(4 * groups)],
        [scratch(size), scratch(4 * groups)],
        1000,
        700000,
    )(held, mate, oth)
    nxt = across(message, 1)
    wide = groups * WIDE
    slim = groups * SLIM
    (
        edge0, u1x, d0x, d1x, f2x, field, final, wo, readout_held, gain_held, error_held, background_held,
    ) = kernel_call(
        forward_kernel,
        [spec(groups * 8), spec(slim)] + [spec(slim, BF16)] * 3
        + [spec(8 * lats * cols, BF16, members * LANES), spec(size, BF16)]
        + [spec(channels, BF16), spec(channels, BF16, LANES), spec(1), spec(1), spec(size, BF16)],
        [scratch(wide), scratch(wide), scratch(wide, BF16, 2 * channels), scratch(wide, BF16)]
        + [scratch(wide), scratch(16), scratch(4 * size, BF16)]
        + [scratch(2 * channels, BF16), pltpu.SemaphoreType.DMA((7,))],
        10**11,
        4000000,
        hbm=7,
    )(
        gain, self_weight, neighbour_weight, output_weight, readout, error, background.reshape(size, channels),
        held, near4, oth,
    )
    before = across(final, -1)
    total = tiles * CHUNK
    tables = [scratch(128, BF16, total)]
    spread, near_spread, *reports_held = kernel_call(
        functools.partial(observe_kernel, tiles),
        [spec(2 * size, BF16, LANES), spec(size, BF16, LANES)]
        + [spec(32, BF16, total), spec(32, BF16, total), spec(32, F32, total)],
        tables,
        10**9,
        2000000,
    )(arrived, field)
    from_mate = lax.ppermute(near_spread, "tile", mate_of)
    handed = kernel_call(
        pull_kernel,
        [spec(2 * size), spec(size), spec(channels, BF16), spec(channels, BF16)],
        tables + [scratch(2 * size, BF16, LANES), scratch(size, BF16, LANES), pltpu.SemaphoreType.DMA((2,))],
        10**9,
        3000000,
        hbm=2,
    )(neighbour_weight, self_weight, spread, readout_held, *reports_held, arrived, field)
    base = kernel_call(
        backward_kernel,
        spec(size),
        [scratch(slim), scratch(slim), scratch(slim, BF16), scratch(slim), scratch(slim)]
        + [scratch(size), scratch(16), scratch(slim), scratch(slim), scratch(size + 4 * groups)],
        12 * slim * channels * channels,
        6000000,
    )(
        *handed, gain_held, held, edge0, nxt, f2x, wo, readout_held, error_held, from_mate,
        u1x, d0x, d1x,
    )
    (result,) = kernel_call(
        last_kernel,
        [spec(size)],
        [scratch(size), pltpu.SemaphoreType.DMA((4,))],
        10**6,
        900000,
        out_places=[pltpu.HBM],
    )(base, background_held, before, error_held)
    return result.reshape(control.shape)


def solution(mesh):
    in_specs = (
        P("slot", None, None, "tile", None),
        P(None, None, "tile", None),
        P(),
        P(),
        P(),
        P(),
        P(),
        P(),
        P("slot", None, "tile", None),
        P("slot", None, "tile", None),
        P("slot", None, "tile", None),
        P("slot", None, "tile", None),
        P("slot", None, "tile"),
    )
    out_specs = P("slot", None, None, "tile", None)
    return jax.shard_map(
        per_device, mesh=mesh, in_specs=in_specs, out_specs=out_specs, check_vma=False
    )
```
